32 devices in a mesh: section: 4 (over y, x), seq: 4 (over z), rep: 2 (over core).
Axes of the slice: x: 2, y: 2, z: 4, core: 2. Of those that a mesh axis runs over, the one named last changes fastest.
Arguments:
- char_queries: bfloat16 [2, 4, 1024, 2048], P('rep', 'section', 'seq'), may hold values from -34 to 34
- char_keys: bfloat16 [2, 4, 1024, 2048], P('rep', 'section', 'seq'), may hold values from -6 to 6
- char_values: bfloat16 [2, 4, 1024, 2048], P('rep', 'section', 'seq'), may hold values from -48 to 48
- doc_starts: int32 [2, 4, 8], P('rep', 'section'), may hold values from 0 to 1023, as said below
- key_weight: bfloat16 [4, 2048, 1024], P('section'), may hold values from -0.125 to 0.125
- norm_gain: float32 [4, 2048], P('section'), may hold values from 0.25 to 1.75
- stashed: bfloat16 [2, 4, 2, 256, 2048], P('rep', 'section', None, 'seq'), may hold values from -48 to 48
- cotangent: bfloat16 [2, 4, 256, 1024], P('rep', 'section', 'seq'), may hold values from -6 to 6
- plan_slot: int32 [2, 4], P('rep', 'section'), may hold values from 0 to 1
Outputs:
- mol_keys: bfloat16 [2, 4, 256, 1024], P('rep', 'section', 'seq')
- upstream_grad: bfloat16 [2, 4, 256, 2048], P('rep', 'section', 'seq')
- gain_update: float32 [4, 2048], P('section')
The draws below stay inside these ranges and needn't reach their ends.
Inputs may be any that keep to these rules, and one draw needn't show every extreme that they name: `doc_starts`: each row of offsets rises strictly, begins with 0 and ends with 1023.
All inputs are finite; a program needn't handle non-finite values.
Results may differ from the reference program's by a relative error of at most 0.012.
Values may be sent and summed in bfloat16 or wider, within the bound.
No kernel may reach another device: no remote copies, remote signals or barrier semaphores. Data moves between devices by JAX's collectives and lax.ppermute only.
A program may use at most 64 MiB of HBM per device.

```python
import math
import jax
import jax.numpy as jnp
from jax import lax

HEADS = 32
HEAD_DIM = 64
D = 2048
KEY_WIDTH = 1024
POOL = 4
CH_DEV = 256
WINDOW = 128
SLOTS = 2
REPLICAS = 2
SECTIONS = 4
CHARS = 1024
MOL = 256
DOCS = 8
N_SEQ = 4


def doc_offsets(key):
    row_keys = jax.random.split(jax.random.fold_in(key, 7), REPLICAS * SECTIONS)

    def one_row(row_key):
        chosen = jax.random.permutation(row_key, CHARS - 2)[:DOCS - 2] + 1
        return jnp.concatenate([jnp.zeros((1,), jnp.int32), jnp.sort(chosen).astype(jnp.int32), jnp.full((1,), CHARS - 1, jnp.int32)])
    return jax.vmap(one_row)(row_keys).reshape(REPLICAS, SECTIONS, DOCS)


def draw_doc_starts(key, part):
    return doc_offsets(key)


def draw_char_queries(key, part):
    gaussian = jnp.clip(jax.random.normal(jax.random.fold_in(key, 23), (REPLICAS, SECTIONS, CHARS, D)), -6.0, 6.0)
    return gaussian.astype(jnp.bfloat16)


def draw_char_keys(key, part):
    gaussian = jnp.clip(jax.random.normal(jax.random.fold_in(key, 19), (REPLICAS, SECTIONS, CHARS, D)), -6.0, 6.0)
    return gaussian.astype(jnp.bfloat16)


def scaled_noise(key, full_shape):
    column_shape = full_shape[:-2] + (1, full_shape[-1])
    row_shape = full_shape[:-1] + (1,)
    gaussian = jnp.clip(jax.random.normal(jax.random.fold_in(key, 29), full_shape), -4.0, 4.0)
    column_scale = jnp.exp(jax.random.uniform(jax.random.fold_in(key, 31), column_shape, jnp.float32, 0.0, math.log(10.0)))
    row_scale = jnp.exp(jax.random.uniform(jax.random.fold_in(key, 37), row_shape, jnp.float32, 0.0, math.log(4.0)))
    return 0.3 * gaussian * column_scale * row_scale


def draw_char_values(key, part):
    return scaled_noise(jax.random.fold_in(key, 41), (REPLICAS, SECTIONS, CHARS, D)).astype(jnp.bfloat16)


def draw_stashed(key, part):
    return scaled_noise(jax.random.fold_in(key, 43), (REPLICAS, SECTIONS, SLOTS, MOL, D)).astype(jnp.bfloat16)


def place_ends(result, stream_key, least, top_value):
    shape = result.shape
    spot = [jax.random.randint(jax.random.fold_in(stream_key, axis), (), 0, shape[axis]) for axis in range(len(shape))]
    result = result.at[tuple(spot)].set(least)
    longest = shape.index(max(shape))
    spot[longest] = (spot[longest] + 1) % shape[longest]
    return result.at[tuple(spot)].set(top_value)


def shard_levels(key, shape, cuts, least, top_value):
    factor_of = 1.0
    for position, shards_of in cuts:
        heights = jax.random.uniform(jax.random.fold_in(jax.random.fold_in(key, 6), position), (shards_of,), jnp.float32, least / len(cuts), top_value / len(cuts))
        factor_of = factor_of * jnp.repeat(jnp.exp(heights), shape[position] // shards_of).reshape((-1,) + (1,) * (len(shape) - 1 - position))
    return factor_of


def scatter_about(rng, extent, scale, bound, shards=(), kind=jnp.bfloat16):
    result = jax.random.normal(rng, extent, jnp.float32) * scale
    if len(shards) > 0:
        result = shard_levels(rng, extent, shards, -0.22, 0.18) * result
    return jnp.clip(result, min=-bound, max=bound).astype(kind)


def setup_inputs(seed: int = 0) -> dict:
    key_list = jax.random.split(jax.random.key(seed), 10)
    return {
        "char_queries": draw_char_queries(jax.random.fold_in(key_list[9], 71), 0),
        "char_keys": draw_char_keys(jax.random.fold_in(key_list[9], 71), 0),
        "char_values": draw_char_values(jax.random.fold_in(key_list[9], 71), 0),
        "doc_starts": draw_doc_starts(jax.random.fold_in(key_list[9], 71), 0),
        "key_weight": scatter_about(key_list[4], (SECTIONS, D, KEY_WIDTH), D ** -0.5, 0.125, ((0, 4),)),
        "norm_gain": jnp.clip(1.0 + 0.15 * jax.random.normal(key_list[5], (SECTIONS, D), jnp.float32), 0.25, 1.75),
        "stashed": draw_stashed(jax.random.fold_in(key_list[9], 71), 0),
        "cotangent": scatter_about(key_list[7], (REPLICAS, SECTIONS, MOL, KEY_WIDTH), 1.0, 6.0, ((0, 2), (1, 4), (2, 4))),
        "plan_slot": place_ends(jax.random.randint(key_list[8], (REPLICAS, SECTIONS), 0, SLOTS), jax.random.fold_in(key_list[8], 1), 0, SLOTS - 1).astype(jnp.int32),
    }


EPS_NORM = 1e-05
EPS_STEP = 1e-06

def doc_index(positions, offsets):
    return lax.optimization_barrier(jnp.sum((offsets[None, :] <= positions[:, None]).astype(jnp.int32), axis=1))

def attend(block_queries, block_keys, block_values, query_pos, key_pos, offsets):
    row_count = block_queries.shape[0]
    key_count = block_keys.shape[0]
    query_doc = doc_index(query_pos, offsets)
    key_doc = doc_index(key_pos, offsets)
    allowed = (key_doc[None, :] == query_doc[:, None]) & (key_pos[None, :] <= query_pos[:, None]) & (key_pos[None, :] > query_pos[:, None] - WINDOW)
    heads_query = block_queries.astype(jnp.float32).reshape(row_count, HEADS, HEAD_DIM)
    heads_key = block_keys.astype(jnp.float32).reshape(key_count, HEADS, HEAD_DIM)
    heads_value = block_values.astype(jnp.float32).reshape(key_count, HEADS, HEAD_DIM)
    scores = jnp.einsum('qhd,khd->hqk', heads_query, heads_key) * (1.0 / math.sqrt(HEAD_DIM))
    scores = jnp.where(allowed[None, :, :], scores, -1e+30)
    row_max = lax.optimization_barrier(jnp.max(scores, axis=2, keepdims=True))
    weights = jnp.exp(scores - row_max)
    row_total = lax.optimization_barrier(jnp.sum(weights, axis=2, keepdims=True))
    rounded = lax.optimization_barrier(weights.astype(jnp.bfloat16)).astype(jnp.float32)
    mixed_heads = jnp.einsum('hqk,khd->qhd', rounded, heads_value)
    return (mixed_heads / jnp.transpose(row_total, (1, 0, 2))).reshape(row_count, D).astype(jnp.bfloat16)

def character_row(row_queries, row_keys, row_values, offsets):
    padded_keys = jnp.concatenate([jnp.zeros((WINDOW, D), row_keys.dtype), row_keys], axis=0)
    padded_values = jnp.concatenate([jnp.zeros((WINDOW, D), row_values.dtype), row_values], axis=0)

    def block(block_index):
        block_start = block_index * CH_DEV
        block_queries = lax.dynamic_slice_in_dim(row_queries, block_start, CH_DEV, 0)
        block_keys = lax.dynamic_slice_in_dim(padded_keys, block_start, CH_DEV + WINDOW, 0)
        block_values = lax.dynamic_slice_in_dim(padded_values, block_start, CH_DEV + WINDOW, 0)
        query_pos = block_start + jnp.arange(CH_DEV, dtype=jnp.int32)
        key_pos = block_start - WINDOW + jnp.arange(CH_DEV + WINDOW, dtype=jnp.int32)
        return attend(block_queries, block_keys, block_values, query_pos, key_pos, offsets)
    blocks = lax.map(block, jnp.arange(N_SEQ, dtype=jnp.int32))
    return blocks.reshape(CHARS, D)

def reference(char_queries, char_keys, char_values, doc_starts, key_weight, norm_gain, stashed, cotangent, plan_slot):

    def one_row(row_index):
        rep_index = row_index // SECTIONS
        section_index = row_index % SECTIONS
        return character_row(char_queries[rep_index, section_index], char_keys[rep_index, section_index], char_values[rep_index, section_index], doc_starts[rep_index, section_index])
    attended = lax.map(one_row, jnp.arange(REPLICAS * SECTIONS, dtype=jnp.int32)).reshape(REPLICAS, SECTIONS, CHARS, D)
    pooled = lax.optimization_barrier(jnp.mean(attended.astype(jnp.float32).reshape(REPLICAS, SECTIONS, MOL, POOL, D), axis=3)).astype(jnp.bfloat16)
    arrived = jnp.roll(pooled, 1, axis=1)
    as_float = arrived.astype(jnp.float32)
    inv_norm = lax.rsqrt(lax.optimization_barrier(jnp.mean(as_float * as_float, axis=3, keepdims=True)) + EPS_NORM)
    normed = (as_float * inv_norm * norm_gain[None, :, None, :]).astype(jnp.bfloat16)
    mol_keys = jnp.einsum('rsmd,sdk->rsmk', normed.astype(jnp.float32), key_weight.astype(jnp.float32)).astype(jnp.bfloat16)
    chooser = jnp.arange(SLOTS, dtype=jnp.int32)[None, None, :] == plan_slot[:, :, None]
    held_rows = lax.optimization_barrier(jnp.sum(jnp.where(chooser[:, :, :, None, None], stashed.astype(jnp.float32), jnp.float32(0.0)), axis=2))
    back_grad = jnp.einsum('rsmk,sdk->rsmd', cotangent.astype(jnp.float32), key_weight.astype(jnp.float32))
    inv_rms = lax.rsqrt(lax.optimization_barrier(jnp.mean(held_rows * held_rows, axis=3, keepdims=True)) + EPS_NORM)
    whitened = held_rows * inv_rms
    gain_sum = lax.optimization_barrier(jnp.sum(back_grad * whitened, axis=(0, 2)))
    gain_update = gain_sum / jnp.sqrt(lax.optimization_barrier(jnp.mean(gain_sum * gain_sum, axis=1, keepdims=True)) + EPS_STEP)
    scaled = back_grad * norm_gain[None, :, None, :]
    dinput = (inv_rms * (scaled - whitened * lax.optimization_barrier(jnp.mean(scaled * whitened, axis=3, keepdims=True)))).astype(jnp.bfloat16)
    upstream_grad = jnp.roll(dinput, -1, axis=1)
    return (mol_keys, upstream_grad, gain_update)
```

```python
import functools
import math

import jax
import jax.numpy as jnp
from jax import lax
from jax.experimental import pallas as pl
from jax.experimental.pallas import tpu as pltpu
from jax.sharding import PartitionSpec as P

HEAD_DIM = 64
POOL = 4
WINDOW = 128
LANES = 128
EPS_NORM = 1e-05
EPS_STEP = 1e-06
MASKED = -1e30

NT = (((1,), (1,)), ((), ()))


def dot_nt(a, b):
    return lax.dot_general(a, b, NT, preferred_element_type=jnp.float32)


def dot_nn(a, b):
    return jnp.dot(a, b, preferred_element_type=jnp.float32)


def shifted(value, axis, steps):
    count = lax.axis_size(axis)
    first, last = max(0, -steps), min(count, count - steps)
    return lax.ppermute(value, axis, [(i, i + steps) for i in range(first, last)])


def passed_along(value, axis, steps):
    count = lax.axis_size(axis)
    return lax.ppermute(value, axis, [(i, (i + steps) % count) for i in range(count)])


def earliest_key(offsets_ref, query_pos):
    start = jnp.zeros_like(query_pos)
    for d in range(offsets_ref.shape[1]):
        offset = offsets_ref[0, d]
        start = jnp.where(query_pos >= offset, offset, start)
    return jnp.maximum(start, query_pos - (WINDOW - 1))


def mask_bias(offsets_ref, key_start, key_count, query_start, query_count):
    query_pos = query_start + lax.broadcasted_iota(jnp.int32, (1, query_count), 1)
    lowest = earliest_key(offsets_ref, query_pos)
    key_pos = key_start + lax.broadcasted_iota(jnp.int32, (key_count, query_count), 0)
    allowed = (key_pos >= lowest) & (key_pos <= query_pos)
    return jnp.where(allowed, 0.0, MASKED).astype(jnp.float32)


def split_heads(queries):
    rows = queries.shape[0]
    lane = lax.broadcasted_iota(jnp.int32, (rows, LANES), 1)
    scaled = queries.astype(jnp.float32) * (1.0 / math.sqrt(HEAD_DIM))
    first = jnp.where(lane < HEAD_DIM, scaled, 0.0)
    second = jnp.where(lane < HEAD_DIM, 0.0, scaled)
    return jnp.concatenate([first, second], axis=0).astype(jnp.bfloat16)


def pool_matrix(queries):
    molecule = lax.broadcasted_iota(jnp.int32, (queries // POOL, queries), 0)
    query = lax.broadcasted_iota(jnp.int32, (queries // POOL, queries), 1)
    return jnp.where(query // POOL == molecule, 1.0 / POOL, 0.0).astype(jnp.bfloat16)


def own_heads(mixed, scale):
    count = mixed.shape[1] // 2
    return jnp.concatenate(
        [
            mixed[:HEAD_DIM, :count] * scale[:, :count],
            mixed[HEAD_DIM:, count:] * scale[:, count:],
        ],
        axis=0,
    )


def twice(bias):
    return jnp.concatenate([bias, bias], axis=1)


def softmax_parts(scores):
    top = jnp.max(scores, axis=0, keepdims=True)
    weights = jnp.exp(scores - top)
    total = jnp.sum(weights, axis=0, keepdims=True)
    return top, weights.astype(jnp.bfloat16), total


def own_kernel(rows, offsets_ref, q_ref, k_ref, v_ref, late_ref, early_ref, lse_ref, bias0, bias1):
    half = rows // 2
    shard_start = lax.axis_index("seq") * rows

    @pl.when(pl.program_id(0) == 0)
    def _():
        bias0[...] = mask_bias(offsets_ref, shard_start, half, shard_start, half)
        bias1[...] = mask_bias(offsets_ref, shard_start, rows, shard_start + half, half)

    pooling = pool_matrix(half)
    for pair in range(q_ref.shape[1] // LANES):
        columns = pl.ds(pair * LANES, LANES)
        keys = k_ref[:, columns]
        values_t = jnp.transpose(v_ref[:, columns])
        scores = dot_nt(keys[:half], split_heads(q_ref[:half, columns])) + twice(bias0[...])
        top, weights, total = softmax_parts(scores)
        mixed = dot_nn(values_t[:, :half], weights)
        early_ref[columns, :] = own_heads(mixed, 1.0 / total).astype(jnp.bfloat16)
        lse = top + jnp.log(total)
        lse_ref[0:1, columns] = lse[:, :half]
        lse_ref[1:2, columns] = lse[:, half:]
        scores = dot_nt(keys, split_heads(q_ref[half:, columns])) + twice(bias1[...])
        _, weights, total = softmax_parts(scores)
        mixed = dot_nn(values_t, weights)
        attended = own_heads(mixed, 1.0 / total).astype(jnp.bfloat16)
        late_ref[:, columns] = dot_nt(pooling, attended).astype(jnp.bfloat16)


def halo_kernel(rows, offsets_ref, q_ref, k_ref, v_ref, lse_ref, out_ref, bias):
    half = rows // 2
    next_start = (lax.axis_index("seq") + 1) * rows

    @pl.when(pl.program_id(0) == 0)
    def _():
        bias[...] = mask_bias(offsets_ref, next_start - half, half, next_start, half)

    pooling = pool_matrix(half)
    molecules = half // POOL
    for pair in range(q_ref.shape[1] // LANES):
        columns = pl.ds(pair * LANES, LANES)
        scores = dot_nt(k_ref[:, columns], split_heads(q_ref[:, columns])) + twice(bias[...])
        lse = jnp.concatenate([lse_ref[0:1, columns], lse_ref[1:2, columns]], axis=1)
        top = jnp.maximum(jnp.max(scores, axis=0, keepdims=True), lse)
        weights = jnp.exp(scores - top)
        rest = jnp.exp(lse - top)
        inverse = 1.0 / (jnp.sum(weights, axis=0, keepdims=True) + rest)
        mixed = dot_nn(jnp.transpose(v_ref[:, columns]), weights.astype(jnp.bfloat16))
        part = own_heads(mixed, inverse).astype(jnp.bfloat16)
        pooled = dot_nt(pooling, part).astype(jnp.bfloat16)
        share = rest * inverse
        high = share.astype(jnp.bfloat16)
        low = (share - high.astype(jnp.float32)).astype(jnp.bfloat16)
        out_ref[:molecules, columns] = pooled
        out_ref[molecules:, columns] = jnp.concatenate(
            [
                high[:, :half].astype(jnp.float32),
                low[:, :half].astype(jnp.float32),
                high[:, half:].astype(jnp.float32),
                low[:, half:].astype(jnp.float32),
                jnp.zeros((12, LANES), jnp.float32),
            ],
            axis=0,
        ).astype(jnp.bfloat16)


def combine_kernel(early_ref, halo_ref, out_ref):
    half = early_ref.shape[1]
    molecules = half // POOL
    pooling = pool_matrix(half)
    first = lax.axis_index("seq") == 0
    for pair in range(out_ref.shape[1] // LANES):
        columns = pl.ds(pair * LANES, LANES)
        shares = halo_ref[molecules:, columns].astype(jnp.float32)
        share_a = jnp.where(first, 1.0, shares[0:1] + shares[1:2])
        share_b = jnp.where(first, 1.0, shares[2:3] + shares[3:4])
        early = early_ref[columns, :].astype(jnp.float32)
        scaled = jnp.concatenate([early[:HEAD_DIM] * share_a, early[HEAD_DIM:] * share_b], axis=0)
        pooled = dot_nt(pooling, scaled.astype(jnp.bfloat16))
        out_ref[:, columns] = (pooled + halo_ref[:molecules, columns].astype(jnp.float32)).astype(
            jnp.bfloat16
        )


def back_kernel(slot_ref, cotangent_ref, weight_ref, gain_ref, held_ref, dinput_ref, term_ref, grad, stats):
    step = pl.program_id(0)
    width = weight_ref.shape[0]
    columns = pl.ds(pl.multiple_of(step * width, width), width)

    @pl.when(step == 0)
    def _():
        held = held_ref[0].astype(jnp.float32)
        mean = jnp.sum(held * held, axis=1, keepdims=True) / held.shape[1]
        stats[0] = jnp.broadcast_to(lax.rsqrt(mean + EPS_NORM), stats.shape[1:])
        stats[1] = jnp.zeros(stats.shape[1:], jnp.float32)

    inv_rms = stats[0, :, 0:1]
    back = dot_nt(cotangent_ref[...], weight_ref[...])
    whitened = held_ref[0, :, columns].astype(jnp.float32) * inv_rms
    product = back * whitened
    term_ref[:, columns] = jnp.sum(product, axis=0, keepdims=True)
    gain = gain_ref[:, columns]
    stats[1] += jnp.broadcast_to(jnp.sum(product * gain, axis=1, keepdims=True), stats.shape[1:])
    grad[:, columns] = back * gain

    @pl.when(step == pl.num_programs(0) - 1)
    def _():
        mean = stats[1, :, 0:1] / grad.shape[1]
        held = held_ref[0].astype(jnp.float32)
        dinput_ref[...] = (inv_rms * (grad[...] - held * inv_rms * mean)).astype(jnp.bfloat16)


def project_kernel(early_ref, late_ref, gain_ref, weight_ref, terms_ref, out_ref, update_ref):
    features = gain_ref.shape[1]
    arrived = jnp.concatenate([early_ref[...], late_ref[...]], axis=0).astype(jnp.float32)
    mean = jnp.sum(arrived * arrived, axis=1, keepdims=True) / features
    normed = (arrived * lax.rsqrt(mean + EPS_NORM) * gain_ref[...]).astype(jnp.bfloat16)
    out_ref[...] = dot_nn(normed, weight_ref[...]).astype(jnp.bfloat16)
    total = jnp.sum(terms_ref[...], axis=0, keepdims=True)
    mean = jnp.sum(total * total, axis=1, keepdims=True) / features
    update_ref[...] = total / jnp.sqrt(mean + EPS_STEP)


def cost(flops, read, exps=0):
    return pl.CostEstimate(flops=flops, bytes_accessed=read, transcendentals=exps)


SMEM = pl.BlockSpec(memory_space=pltpu.SMEM)
VMEM = pl.BlockSpec(memory_space=pltpu.VMEM)


def attend_own(queries, keys, values, offsets, steps):
    rows, width = queries.shape
    half, block = rows // 2, width // steps
    shard = pl.BlockSpec((rows, block), lambda i: (0, i))
    return pl.pallas_call(
        functools.partial(own_kernel, rows),
        grid=(steps,),
        in_specs=[SMEM, shard, shard, shard],
        out_specs=[
            pl.BlockSpec((half // POOL, block), lambda i: (0, i)),
            pl.BlockSpec((block, half), lambda i: (i, 0)),
            pl.BlockSpec((2, block), lambda i: (0, i)),
        ],
        out_shape=[
            jax.ShapeDtypeStruct((half // POOL, width), jnp.bfloat16),
            jax.ShapeDtypeStruct((width, half), jnp.bfloat16),
            jax.ShapeDtypeStruct((2, width), jnp.float32),
        ],
        scratch_shapes=[
            pltpu.VMEM((half, half), jnp.float32),
            pltpu.VMEM((rows, half), jnp.float32),
        ],
        cost_estimate=cost(12 * half * half * width, 6 * rows * width, 3 * half * half * width // 64),
        compiler_params=pltpu.CompilerParams(vmem_limit_bytes=24 * 2**20),
        name="attend_own",
    )(offsets, queries, keys, values)


def attend_halo(queries, keys, values, lse, offsets, steps):
    half, width = queries.shape
    rows, block = 2 * half, width // steps
    shard = pl.BlockSpec((half, block), lambda i: (0, i))
    tail = pl.BlockSpec((half, block), lambda i: (1, i))
    return pl.pallas_call(
        functools.partial(halo_kernel, rows),
        grid=(steps,),
        in_specs=[SMEM, shard, tail, tail, pl.BlockSpec((2, block), lambda i: (0, i))],
        out_specs=pl.BlockSpec((half // POOL + 16, block), lambda i: (0, i)),
        out_shape=jax.ShapeDtypeStruct((half // POOL + 16, width), jnp.bfloat16),
        scratch_shapes=[pltpu.VMEM((half, half), jnp.float32)],
        cost_estimate=cost(4 * half * half * width, 6 * half * width, half * half * width // 64),
        compiler_params=pltpu.CompilerParams(vmem_limit_bytes=24 * 2**20),
        name="attend_halo",
    )(offsets, queries, keys, values, lse)


def combine(early, halo):
    width, half = early.shape
    return pl.pallas_call(
        combine_kernel,
        in_specs=[VMEM, VMEM],
        out_specs=VMEM,
        out_shape=jax.ShapeDtypeStruct((half // POOL, width), jnp.bfloat16),
        cost_estimate=cost(half * half * width, 2 * half * width),
        name="combine",
    )(early, halo)


def backward(slot, cotangent, weight, gain, stashed, steps):
    rows, depth = cotangent.shape
    width = weight.shape[0]
    return pl.pallas_call(
        back_kernel,
        grid_spec=pltpu.PrefetchScalarGridSpec(
            num_scalar_prefetch=1,
            grid=(steps,),
            in_specs=[
                pl.BlockSpec((rows, depth), lambda i, slot: (0, 0)),
                pl.BlockSpec((width // steps, depth), lambda i, slot: (i, 0)),
                pl.BlockSpec((1, width), lambda i, slot: (0, 0)),
                pl.BlockSpec((1, rows, width), lambda i, slot: (slot[0], 0, 0)),
            ],
            out_specs=[
                pl.BlockSpec((rows, width), lambda i, slot: (0, 0)),
                pl.BlockSpec((1, width), lambda i, slot: (0, 0)),
            ],
            scratch_shapes=[
                pltpu.VMEM((rows, width), jnp.float32),
                pltpu.VMEM((2, rows, LANES), jnp.float32),
            ],
        ),
        out_shape=[
            jax.ShapeDtypeStruct((rows, width), jnp.bfloat16),
            jax.ShapeDtypeStruct((1, width), jnp.float32),
        ],
        cost_estimate=cost(2 * rows * width * depth, 2 * width * depth),
        compiler_params=pltpu.CompilerParams(vmem_limit_bytes=24 * 2**20),
        name="backward",
    )(slot, cotangent, weight, gain, stashed)


def project(early, late, gain, weight, terms):
    rows = early.shape[0] + late.shape[0]
    width, depth = weight.shape
    return pl.pallas_call(
        project_kernel,
        in_specs=[VMEM] * 5,
        out_specs=[VMEM] * 2,
        out_shape=[
            jax.ShapeDtypeStruct((rows, depth), jnp.bfloat16),
            jax.ShapeDtypeStruct((1, width), jnp.float32),
        ],
        cost_estimate=cost(2 * rows * width * depth, 2 * width * depth),
        compiler_params=pltpu.CompilerParams(vmem_limit_bytes=24 * 2**20),
        name="project",
    )(early, late, gain, weight, terms)


def local(queries, keys, values, doc_starts, weight, gain, stashed, cotangent, slot):
    queries, keys, values, offsets = queries[0, 0], keys[0, 0], values[0, 0], doc_starts[0]
    half = queries.shape[0] // 2
    next_queries = shifted(queries[:half], "seq", -1)
    late, early, lse = attend_own(queries, keys, values, offsets, 4)
    next_lse = shifted(lse, "seq", -1)
    late_arrived = passed_along(late, "section", 1)
    dinput, term = backward(slot[0], cotangent[0, 0], weight[0], gain, stashed[0, 0], 4)
    upstream = passed_along(dinput, "section", -1)
    terms = lax.all_gather(term, ("rep", "seq"), axis=0, tiled=True)
    halo = shifted(attend_halo(next_queries, keys, values, next_lse, offsets, 2), "seq", 1)
    early_arrived = passed_along(combine(early, halo), "section", 1)
    mol_keys, update = project(early_arrived, late_arrived, gain, weight[0], terms)
    return mol_keys[None, None], upstream[None, None], update


def solution(mesh):
    in_specs = (
        P("rep", "section", "seq", None),
        P("rep", "section", "seq", None),
        P("rep", "section", "seq", None),
        P("rep", "section", None),
        P("section", None, None),
        P("section", None),
        P("rep", "section", None, "seq", None),
        P("rep", "section", "seq", None),
        P("rep", "section"),
    )
    out_specs = (
        P("rep", "section", "seq", None),
        P("rep", "section", "seq", None),
        P("section", None),
    )
    return jax.shard_map(local, mesh=mesh, in_specs=in_specs, out_specs=out_specs, check_vma=False)
```

```python
import functools
import math

import jax
import jax.numpy as jnp
from jax import lax
from jax.experimental import pallas as pl
from jax.experimental.pallas import tpu as pltpu
from jax.sharding import PartitionSpec as P

HEAD_DIM = 64
POOL = 4
WINDOW = 128
LANES = 128
EPS_NORM = 1e-05
EPS_STEP = 1e-06
MASKED = -1e30
AHEAD = 2

NT = (((1,), (1,)), ((), ()))


def dot_nt(a, b):
    return lax.dot_general(a, b, NT, preferred_element_type=jnp.float32)


def dot_nn(a, b):
    return jnp.dot(a, b, preferred_element_type=jnp.float32)


def shifted(value, axis, steps):
    count = lax.axis_size(axis)
    first, last = max(0, -steps), min(count, count - steps)
    return lax.ppermute(value, axis, [(i, i + steps) for i in range(first, last)])


def passed_along(value, axis, steps):
    count = lax.axis_size(axis)
    return lax.ppermute(value, axis, [(i, (i + steps) % count) for i in range(count)])


def earliest_key(offsets_ref, query_pos):
    start = jnp.zeros_like(query_pos)
    for d in range(offsets_ref.shape[1]):
        offset = offsets_ref[0, d]
        start = jnp.where(query_pos >= offset, offset, start)
    return jnp.maximum(start, query_pos - (WINDOW - 1))


def mask_bias(offsets_ref, key_start, key_count, query_start, query_count):
    query_pos = query_start + lax.broadcasted_iota(jnp.int32, (1, query_count), 1)
    lowest = earliest_key(offsets_ref, query_pos)
    key_pos = key_start + lax.broadcasted_iota(jnp.int32, (key_count, query_count), 0)
    allowed = (key_pos >= lowest) & (key_pos <= query_pos)
    return jnp.where(allowed, 0.0, MASKED).astype(jnp.float32)


def split_heads(queries):
    lane = lax.broadcasted_iota(jnp.int32, (1, LANES), 1)
    scale = 1.0 / math.sqrt(HEAD_DIM)
    first = jnp.where(lane < HEAD_DIM, scale, 0.0).astype(jnp.bfloat16)
    second = jnp.where(lane < HEAD_DIM, 0.0, scale).astype(jnp.bfloat16)
    return jnp.concatenate([queries * first, queries * second], axis=0)


def pool_matrix(queries):
    molecule = lax.broadcasted_iota(jnp.int32, (queries // POOL, queries), 0)
    query = lax.broadcasted_iota(jnp.int32, (queries // POOL, queries), 1)
    return jnp.where(query // POOL == molecule, 1.0 / POOL, 0.0).astype(jnp.bfloat16)


def own_heads(mixed, scale):
    count = mixed.shape[1] // 2
    return jnp.concatenate(
        [
            mixed[:HEAD_DIM, :count] * scale[:, :count],
            mixed[HEAD_DIM:, count:] * scale[:, count:],
        ],
        axis=0,
    )


def twice(bias):
    return jnp.concatenate([bias, bias], axis=1)


def softmax_parts(scores):
    top = jnp.max(scores, axis=0, keepdims=True)
    weights = jnp.exp(scores - top)
    total = jnp.sum(weights, axis=0, keepdims=True)
    return top, weights.astype(jnp.bfloat16), total


def load(source, target, sem):
    copy = pltpu.make_async_copy(source, target, sem)
    copy.start()
    return copy


def own_kernel(
    rows, chunks, offsets_hbm, q_hbm, k_hbm, v_hbm, late_ref, early_ref, lse_ref,
    offsets_ref, q_ref, k_ref, v_ref, bias0, bias1, sems, offsets_sem,
):
    half = rows // 2
    block = q_ref.shape[1] // chunks
    offsets_copy = load(offsets_hbm, offsets_ref, offsets_sem)
    arrays = ((k_hbm, k_ref), (q_hbm, q_ref), (v_hbm, v_ref))
    for chunk in range(chunks):
        columns = pl.ds(chunk * block, block)
        for i, (source, target) in enumerate(arrays):
            load(source.at[:, columns], target.at[:, columns], sems.at[i, chunk])
    offsets_copy.wait()
    shard_start = lax.axis_index("seq") * rows
    bias0[...] = mask_bias(offsets_ref, shard_start, half, shard_start, half)
    bias1[...] = mask_bias(offsets_ref, shard_start, rows, shard_start + half, half)
    pooling = pool_matrix(half)

    @pl.loop(0, chunks)
    def _(chunk):
        begin = pl.multiple_of(chunk * block, block)
        whole = pl.ds(begin, block)
        for i, (source, target) in enumerate(arrays):
            pltpu.make_async_copy(source.at[:, whole], target.at[:, whole], sems.at[i, chunk]).wait()
        pairs = block // LANES

        def at(pair):
            return pl.ds(pl.multiple_of(begin + pair * LANES, LANES), LANES)

        def scores_of(pair):
            keys = k_ref[:, at(pair)]
            return (
                dot_nt(keys[:half], split_heads(q_ref[:half, at(pair)])),
                dot_nt(keys, split_heads(q_ref[half:, at(pair)])),
            )

        scores = {pair: scores_of(pair) for pair in range(min(AHEAD, pairs))}
        late = []
        for pair in range(pairs):
            if pair + AHEAD < pairs:
                scores[pair + AHEAD] = scores_of(pair + AHEAD)
            first, second = scores.pop(pair)
            values_t = jnp.transpose(v_ref[:, at(pair)])
            top, weights, total = softmax_parts(first + twice(bias0[...]))
            mixed = dot_nn(values_t[:, :half], weights)
            _, weights1, total1 = softmax_parts(second + twice(bias1[...]))
            mixed1 = dot_nn(values_t, weights1)
            early_ref[at(pair), :] = own_heads(mixed, 1.0 / total).astype(jnp.bfloat16)
            lse = top + jnp.log(total)
            lse_ref[0:1, at(pair)] = lse[:, :half]
            lse_ref[1:2, at(pair)] = lse[:, half:]
            late.append(own_heads(mixed1, 1.0 / total1).astype(jnp.bfloat16))
        late_ref[:, whole] = dot_nt(pooling, jnp.concatenate(late, axis=0)).astype(jnp.bfloat16)


def halo_kernel(
    rows, chunks, offsets_hbm, q_ref, k_hbm, v_hbm, lse_ref, term_ref, other_ref, *rest
):
    out_ref, sum_ref, offsets_ref, k_ref, v_ref, bias, sems, offsets_sem = rest[-8:]
    half = rows // 2
    block = q_ref.shape[1] // chunks
    offsets_copy = load(offsets_hbm, offsets_ref, offsets_sem)
    arrays = ((k_hbm, k_ref), (v_hbm, v_ref))
    copies = []
    for chunk in range(chunks):
        columns = pl.ds(chunk * block, block)
        for i, (source, target) in enumerate(arrays):
            tail = source.at[pl.ds(half, half), columns]
            copies.append(load(tail, target.at[:, columns], sems.at[i, chunk]))
    sum_ref[...] = term_ref[...] + other_ref[...]
    offsets_copy.wait()
    next_start = (lax.axis_index("seq") + 1) * rows
    bias[...] = mask_bias(offsets_ref, next_start - half, half, next_start, half)
    pooling = pool_matrix(half)
    molecules = half // POOL
    for copy in copies:
        copy.wait()
    pairs = q_ref.shape[1] // LANES

    def at(pair):
        return pl.ds(pair * LANES, LANES)

    def scores_of(pair):
        return dot_nt(k_ref[:, at(pair)], split_heads(q_ref[:, at(pair)]))

    scores = {pair: scores_of(pair) for pair in range(min(AHEAD, pairs))}
    parts = []
    for pair in range(pairs):
        if pair + AHEAD < pairs:
            scores[pair + AHEAD] = scores_of(pair + AHEAD)
        masked = scores.pop(pair) + twice(bias[...])
        lse = jnp.concatenate([lse_ref[0:1, at(pair)], lse_ref[1:2, at(pair)]], axis=1)
        top = jnp.maximum(jnp.max(masked, axis=0, keepdims=True), lse)
        weights = jnp.exp(masked - top)
        kept = jnp.exp(lse - top)
        inverse = 1.0 / (jnp.sum(weights, axis=0, keepdims=True) + kept)
        mixed = dot_nn(jnp.transpose(v_ref[:, at(pair)]), weights.astype(jnp.bfloat16))
        parts.append(own_heads(mixed, inverse).astype(jnp.bfloat16))
        share = kept * inverse
        high = share.astype(jnp.bfloat16).astype(jnp.float32)
        low = share - high
        out_ref[molecules:, at(pair)] = jnp.concatenate(
            [
                high[:, :half],
                low[:, :half],
                high[:, half:],
                low[:, half:],
                jnp.zeros((12, LANES), jnp.float32),
            ],
            axis=0,
        ).astype(jnp.bfloat16)
        if len(parts) == 4 or pair == pairs - 1:
            begin = (pair + 1 - len(parts)) * LANES
            pooled = dot_nt(pooling, jnp.concatenate(parts, axis=0)).astype(jnp.bfloat16)
            out_ref[:molecules, begin : (pair + 1) * LANES] = pooled
            parts = []


def combine_kernel(early_ref, halo_ref, term_ref, other_ref, out_ref, sum_ref):
    half = early_ref.shape[1]
    molecules = half // POOL
    pooling = pool_matrix(half)
    first = lax.axis_index("seq") == 0
    sum_ref[...] = term_ref[...] + other_ref[...]
    parts = []
    for pair in range(out_ref.shape[1] // LANES):
        columns = pl.ds(pair * LANES, LANES)
        shares = halo_ref[molecules:, columns].astype(jnp.float32)
        share_a = jnp.where(first, 1.0, shares[0:1] + shares[1:2])
        share_b = jnp.where(first, 1.0, shares[2:3] + shares[3:4])
        early = early_ref[columns, :].astype(jnp.float32)
        parts += [early[:HEAD_DIM] * share_a, early[HEAD_DIM:] * share_b]
        if len(parts) == 8:
            begin = (pair + 1) * LANES - 8 * HEAD_DIM
            columns = pl.ds(begin, 8 * HEAD_DIM)
            pooled = dot_nt(pooling, jnp.concatenate(parts, axis=0).astype(jnp.bfloat16))
            arrived = halo_ref[:molecules, columns].astype(jnp.float32)
            out_ref[:, columns] = (pooled + arrived).astype(jnp.bfloat16)
            parts = []


def back_kernel(
    slot_ref, cotangent_hbm, weight_ref, gain_ref, stashed_hbm, after_ref, dinput_ref, term_ref,
    cotangent_ref, held_ref, grad, sems,
):
    cotangent_copy = load(cotangent_hbm, cotangent_ref, sems.at[1])
    held_copy = load(stashed_hbm.at[slot_ref[0, 0]], held_ref, sems.at[0])
    cotangent_copy.wait()
    features = weight_ref.shape[0]
    block = 512
    for begin in range(0, features, block):
        columns = pl.ds(begin, block)
        grad[:, columns] = dot_nt(cotangent_ref[...], weight_ref[columns, :])
    held_copy.wait()
    held = held_ref[...].astype(jnp.float32)
    inv_rms = lax.rsqrt(jnp.sum(held * held, axis=1, keepdims=True) / features + EPS_NORM)
    along = jnp.zeros_like(inv_rms)
    for begin in range(0, features, block):
        columns = pl.ds(begin, block)
        product = grad[:, columns] * (held_ref[:, columns].astype(jnp.float32) * inv_rms)
        term_ref[:, columns] = jnp.sum(product, axis=0, keepdims=True)
        along += jnp.sum(product * gain_ref[:, columns], axis=1, keepdims=True)
    along = along / features
    for begin in range(0, features, block):
        columns = pl.ds(begin, block)
        whitened = held_ref[:, columns].astype(jnp.float32) * inv_rms
        scaled = grad[:, columns] * gain_ref[:, columns]
        dinput_ref[:, columns] = (inv_rms * (scaled - whitened * along)).astype(jnp.bfloat16)


def project_kernel(
    early_ref, late_ref, gain_ref, weight_ref, term_ref, other_ref, out_ref, update_ref
):
    features = gain_ref.shape[1]
    arrived = jnp.concatenate([early_ref[...], late_ref[...]], axis=0).astype(jnp.float32)
    mean = jnp.sum(arrived * arrived, axis=1, keepdims=True) / features
    normed = (arrived * lax.rsqrt(mean + EPS_NORM) * gain_ref[...]).astype(jnp.bfloat16)
    out_ref[...] = dot_nn(normed, weight_ref[...]).astype(jnp.bfloat16)
    total = term_ref[...] + other_ref[...]
    mean = jnp.sum(total * total, axis=1, keepdims=True) / features
    update_ref[...] = total / jnp.sqrt(mean + EPS_STEP)


def cost(flops, read, exps=0):
    return pl.CostEstimate(flops=flops, bytes_accessed=read, transcendentals=exps)


SMEM = pl.BlockSpec(memory_space=pltpu.SMEM)
HBM = pl.BlockSpec(memory_space=pltpu.HBM)
ANY = pl.BlockSpec(memory_space=pl.ANY)
VMEM = pl.BlockSpec(memory_space=pltpu.VMEM)


def in_hbm(*arrays):
    return [pltpu.with_memory_space_constraint(x, pltpu.HBM) for x in arrays]


def attend_own(queries, keys, values, offsets, chunks):
    rows, width = queries.shape
    half = rows // 2
    return pl.pallas_call(
        functools.partial(own_kernel, rows, chunks),
        in_specs=[HBM] * 4,
        out_specs=[VMEM] * 3,
        out_shape=[
            jax.ShapeDtypeStruct((half // POOL, width), jnp.bfloat16),
            jax.ShapeDtypeStruct((width, half), jnp.bfloat16),
            jax.ShapeDtypeStruct((2, width), jnp.float32),
        ],
        scratch_shapes=[
            pltpu.SMEM(offsets.shape, jnp.int32),
            pltpu.VMEM((rows, width), jnp.bfloat16),
            pltpu.VMEM((rows, width), jnp.bfloat16),
            pltpu.VMEM((rows, width), jnp.bfloat16),
            pltpu.VMEM((half, half), jnp.float32),
            pltpu.VMEM((rows, half), jnp.float32),
            pltpu.SemaphoreType.DMA((3, chunks)),
            pltpu.SemaphoreType.DMA,
        ],
        cost_estimate=cost(12 * half * half * width, 6 * rows * width, 3 * half * half * width // 64),
        compiler_params=pltpu.CompilerParams(vmem_limit_bytes=24 * 2**20),
        name="attend_own",
    )(*in_hbm(offsets, queries, keys, values))


def attend_halo(queries, keys, values, lse, offsets, term, other, after, chunks):
    half, width = queries.shape
    return pl.pallas_call(
        functools.partial(halo_kernel, 2 * half, chunks),
        in_specs=[HBM, VMEM, HBM, HBM, VMEM, VMEM, VMEM] + [ANY] * len(after),
        out_specs=[VMEM] * 2,
        out_shape=[
            jax.ShapeDtypeStruct((half // POOL + 16, width), jnp.bfloat16),
            jax.ShapeDtypeStruct(term.shape, term.dtype),
        ],
        scratch_shapes=[
            pltpu.SMEM(offsets.shape, jnp.int32),
            pltpu.VMEM((half, width), jnp.bfloat16),
            pltpu.VMEM((half, width), jnp.bfloat16),
            pltpu.VMEM((half, half), jnp.float32),
            pltpu.SemaphoreType.DMA((2, chunks)),
            pltpu.SemaphoreType.DMA,
        ],
        cost_estimate=cost(4 * half * half * width, 6 * half * width, half * half * width // 64),
        compiler_params=pltpu.CompilerParams(vmem_limit_bytes=24 * 2**20),
        name="attend_halo",
    )(*in_hbm(offsets), queries, *in_hbm(keys, values), lse, term, other, *after)


def combine(early, halo, term, other):
    width, half = early.shape
    return pl.pallas_call(
        combine_kernel,
        in_specs=[VMEM] * 4,
        out_specs=[VMEM] * 2,
        out_shape=[
            jax.ShapeDtypeStruct((half // POOL, width), jnp.bfloat16),
            jax.ShapeDtypeStruct(term.shape, term.dtype),
        ],
        cost_estimate=cost(half * half * width, 2 * half * width),
        compiler_params=pltpu.CompilerParams(vmem_limit_bytes=24 * 2**20),
        name="combine",
    )(early, halo, term, other)


def backward(slot, cotangent, weight, gain, stashed, after):
    rows, depth = cotangent.shape
    width = weight.shape[0]
    return pl.pallas_call(
        back_kernel,
        in_specs=[SMEM, HBM, VMEM, VMEM, HBM, ANY],
        out_specs=[VMEM] * 2,
        scratch_shapes=[
            pltpu.VMEM((rows, depth), jnp.bfloat16),
            pltpu.VMEM((rows, width), jnp.bfloat16),
            pltpu.VMEM((rows, width), jnp.float32),
            pltpu.SemaphoreType.DMA((2,)),
        ],
        out_shape=[
            jax.ShapeDtypeStruct((rows, width), jnp.bfloat16),
            jax.ShapeDtypeStruct((1, width), jnp.float32),
        ],
        cost_estimate=cost(2 * rows * width * depth, 2 * width * depth),
        compiler_params=pltpu.CompilerParams(vmem_limit_bytes=24 * 2**20),
        name="backward",
    )(slot, *in_hbm(cotangent), weight, gain, *in_hbm(stashed), after)


def project(early, late, gain, weight, term, other):
    rows = early.shape[0] + late.shape[0]
    width, depth = weight.shape
    return pl.pallas_call(
        project_kernel,
        in_specs=[VMEM] * 6,
        out_specs=[VMEM] * 2,
        out_shape=[
            jax.ShapeDtypeStruct((rows, depth), jnp.bfloat16),
            jax.ShapeDtypeStruct((1, width), jnp.float32),
        ],
        cost_estimate=cost(2 * rows * width * depth, 2 * width * depth),
        compiler_params=pltpu.CompilerParams(vmem_limit_bytes=24 * 2**20),
        name="project",
    )(early, late, gain, weight, term, other)


def swapped(value, axis, distance):
    return lax.ppermute(value, axis, [(i, i ^ distance) for i in range(lax.axis_size(axis))])


def sum_rounds():
    rounds = []
    for axis in ("rep", "seq"):
        count = lax.axis_size(axis)
        if count & (count - 1):
            return []
        rounds += [(axis, 1 << i) for i in range(count.bit_length() - 1)]
    return rounds if len(rounds) == 3 else []


def local(queries, keys, values, doc_starts, weight, gain, stashed, cotangent, slot):
    queries, keys, values, offsets = queries[0, 0], keys[0, 0], values[0, 0], doc_starts[0]
    half = queries.shape[0] // 2
    rounds = sum_rounds()

    def partner(term, index):
        return swapped(term, *rounds[index]) if rounds else jnp.zeros_like(term)

    next_queries = shifted(queries[:half], "seq", -1)
    late, early, lse = attend_own(queries, keys, values, offsets, 2)
    next_lse = shifted(lse, "seq", -1)
    late_arrived = passed_along(late, "section", 1)
    dinput, term = backward(slot, cotangent[0, 0], weight[0], gain, stashed[0, 0], lse)
    upstream = passed_along(dinput, "section", -1)
    term = term if rounds else lax.psum(term, ("rep", "seq"))
    halo, term = attend_halo(
        next_queries, keys, values, next_lse, offsets, term, partner(term, 0), (upstream, late_arrived), 4
    )
    halo = shifted(halo, "seq", 1)
    pooled, term = combine(early, halo, term, partner(term, 1))
    early_arrived = passed_along(pooled, "section", 1)
    mol_keys, update = project(early_arrived, late_arrived, gain, weight[0], term, partner(term, 2))
    return mol_keys[None, None], upstream[None, None], update


def solution(mesh):
    in_specs = (
        P("rep", "section", "seq", None),
        P("rep", "section", "seq", None),
        P("rep", "section", "seq", None),
        P("rep", "section", None),
        P("section", None, None),
        P("section", None),
        P("rep", "section", None, "seq", None),
        P("rep", "section", "seq", None),
        P("rep", "section"),
    )
    out_specs = (
        P("rep", "section", "seq", None),
        P("rep", "section", "seq", None),
        P("section", None),
    )
    return jax.shard_map(local, mesh=mesh, in_specs=in_specs, out_specs=out_specs, check_vma=False)
```

```python
import functools
import math

import jax
import jax.numpy as jnp
from jax import lax
from jax.experimental import pallas as pl
from jax.experimental.pallas import tpu as pltpu
from jax.sharding import PartitionSpec as P

HEAD_DIM = 64
POOL = 4
WINDOW = 128
LANES = 128
EPS_NORM = 1e-05
EPS_STEP = 1e-06
MASKED = -1e30
AHEAD = 2

NT = (((1,), (1,)), ((), ()))


def dot_nt(a, b):
    return lax.dot_general(a, b, NT, preferred_element_type=jnp.float32)


def dot_nn(a, b):
    return jnp.dot(a, b, preferred_element_type=jnp.float32)


def shifted(value, axis, steps):
    count = lax.axis_size(axis)
    first, last = max(0, -steps), min(count, count - steps)
    return lax.ppermute(value, axis, [(i, i + steps) for i in range(first, last)])


def passed_along(value, axis, steps):
    count = lax.axis_size(axis)
    return lax.ppermute(value, axis, [(i, (i + steps) % count) for i in range(count)])


def earliest_key(offsets_ref, query_pos):
    start = jnp.zeros_like(query_pos)
    for d in range(offsets_ref.shape[1]):
        offset = offsets_ref[0, d]
        start = jnp.where(query_pos >= offset, offset, start)
    return jnp.maximum(start, query_pos - (WINDOW - 1))


def mask_bias(offsets_ref, key_start, key_count, query_start, query_count):
    query_pos = query_start + lax.broadcasted_iota(jnp.int32, (1, query_count), 1)
    lowest = earliest_key(offsets_ref, query_pos)
    key_pos = key_start + lax.broadcasted_iota(jnp.int32, (key_count, query_count), 0)
    allowed = (key_pos >= lowest) & (key_pos <= query_pos)
    return jnp.where(allowed, 0.0, MASKED).astype(jnp.float32)


def split_heads(queries):
    lane = lax.broadcasted_iota(jnp.int32, (1, LANES), 1)
    scale = 1.0 / math.sqrt(HEAD_DIM)
    first = jnp.where(lane < HEAD_DIM, scale, 0.0).astype(jnp.bfloat16)
    second = jnp.where(lane < HEAD_DIM, 0.0, scale).astype(jnp.bfloat16)
    return jnp.concatenate([queries * first, queries * second], axis=0)


def pool_matrix(queries):
    molecule = lax.broadcasted_iota(jnp.int32, (queries // POOL, queries), 0)
    query = lax.broadcasted_iota(jnp.int32, (queries // POOL, queries), 1)
    return jnp.where(query // POOL == molecule, 1.0 / POOL, 0.0).astype(jnp.bfloat16)


def own_heads(mixed, scale):
    count = mixed.shape[1] // 2
    return jnp.concatenate(
        [
            mixed[:HEAD_DIM, :count] * scale[:, :count],
            mixed[HEAD_DIM:, count:] * scale[:, count:],
        ],
        axis=0,
    )


def twice(bias):
    return jnp.concatenate([bias, bias], axis=1)


def load(source, target, sem):
    copy = pltpu.make_async_copy(source, target, sem)
    copy.start()
    return copy


def load_chunks(arrays, chunks, sems):
    block = arrays[0][1].shape[1] // chunks
    return [
        [
            load(source.at[:, pl.ds(chunk * block, block)], target.at[:, pl.ds(chunk * block, block)], sems.at[i, chunk])
            for i, (source, target) in enumerate(arrays)
        ]
        for chunk in range(chunks)
    ]


def at(pair):
    return pl.ds(pair * LANES, LANES)


def over_pairs(pairs, first, second, third, copies):
    ready, pending = {}, None
    per_chunk = pairs // len(copies)
    for step in range(pairs + AHEAD):
        if step < pairs:
            if step % per_chunk == 0:
                for copy in copies[step // per_chunk]:
                    copy.wait()
            ready[step] = first(step)
        pair = step - AHEAD
        if pair >= 0:
            result = second(pair, *ready.pop(pair))
            if pending is not None:
                third(pair - 1, *pending)
            pending = result
    third(pairs - 1, *pending)


def pool_into(pooling, out_ref, rows, parts, pair, last):
    if len(parts) == 4 or last:
        columns = pl.ds((pair + 1 - len(parts)) * LANES, len(parts) * LANES)
        pooled = dot_nt(pooling, jnp.concatenate(parts, axis=0))
        out_ref[pl.ds(0, rows), columns] = pooled.astype(jnp.bfloat16)
        parts.clear()


def three_terms(value):
    high = value.astype(jnp.bfloat16).astype(jnp.float32)
    middle = (value - high).astype(jnp.bfloat16).astype(jnp.float32)
    return [high, middle, value - high - middle]


def early_kernel(
    rows, chunks, offsets_hbm, q_hbm, k_hbm, v_hbm, sent_ref, early_ref,
    offsets_ref, k_ref, v_ref, bias, sems, offsets_sem,
):
    half = rows // 2
    head = pl.ds(0, half)
    offsets_copy = load(offsets_hbm, offsets_ref, offsets_sem)
    arrays = (
        (k_hbm.at[head], k_ref),
        (q_hbm.at[head], sent_ref.at[head]),
        (v_hbm.at[head], v_ref),
    )
    copies = load_chunks(arrays, chunks, sems)
    offsets_copy.wait()
    start = lax.axis_index("seq") * rows
    bias[...] = mask_bias(offsets_ref, start, half, start, half)

    def score(pair):
        return dot_nt(k_ref[:, at(pair)], split_heads(sent_ref[head, at(pair)])), jnp.transpose(
            v_ref[:, at(pair)]
        )

    def weigh(pair, scores, values_t):
        scores = scores + twice(bias[...])
        top = jnp.max(scores, axis=0, keepdims=True)
        weights = jnp.exp(scores - top)
        total = jnp.sum(weights, axis=0, keepdims=True)
        mixed = dot_nn(values_t, weights.astype(jnp.bfloat16))
        lse = top + jnp.log(total)
        terms = three_terms(lse[:, :half]) + three_terms(lse[:, half:])
        terms.append(jnp.zeros((10, LANES), jnp.float32))
        sent_ref[pl.ds(half, 16), at(pair)] = jnp.concatenate(terms, axis=0).astype(jnp.bfloat16)
        return mixed, 1.0 / total

    def finish(pair, mixed, inverse):
        early_ref[at(pair), :] = own_heads(mixed, inverse).astype(jnp.bfloat16)

    over_pairs(k_ref.shape[1] // LANES, score, weigh, finish, copies)


def late_kernel(
    rows, chunks, offsets_hbm, q_hbm, k_hbm, v_hbm, after_ref, late_ref,
    offsets_ref, q_ref, k_ref, v_ref, bias, own, other, sems, offsets_sem,
):
    half = rows // 2
    offsets_copy = load(offsets_hbm, offsets_ref, offsets_sem)
    arrays = ((k_hbm, k_ref), (q_hbm.at[pl.ds(half, half)], q_ref), (v_hbm, v_ref))
    copies = load_chunks(arrays, chunks, sems)
    offsets_copy.wait()
    start = lax.axis_index("seq") * rows
    key = lax.broadcasted_iota(jnp.int32, (half, half), 0)
    query = lax.broadcasted_iota(jnp.int32, (half, half), 1)
    lowest = earliest_key(
        offsets_ref, start + half + lax.broadcasted_iota(jnp.int32, (1, half), 1)
    )
    key_pos = start + key + jnp.where(key <= query, half, 0)
    bias[...] = jnp.where(key_pos >= lowest, 0.0, MASKED).astype(jnp.float32)
    own[...] = jnp.where(key <= query, 1.0, 0.0).astype(jnp.bfloat16)
    other[...] = jnp.where(key <= query, 0.0, 1.0).astype(jnp.bfloat16)
    pooling = pool_matrix(half)
    pairs = k_ref.shape[1] // LANES
    parts = []

    def score(pair):
        queries = split_heads(q_ref[:, at(pair)])
        return dot_nt(k_ref[:, at(pair)], queries), jnp.transpose(v_ref[:, at(pair)])

    def weigh(pair, scores, values_t):
        scores = jnp.where(twice(key <= query), scores[half:], scores[:half]) + twice(bias[...])
        top = jnp.max(scores, axis=0, keepdims=True)
        weights = jnp.exp(scores - top)
        total = jnp.sum(weights, axis=0, keepdims=True)
        weights = weights.astype(jnp.bfloat16)
        weights = jnp.concatenate([weights * twice(other[...]), weights * twice(own[...])], axis=0)
        return dot_nn(values_t, weights), 1.0 / total

    def finish(pair, mixed, inverse):
        parts.append(own_heads(mixed, inverse).astype(jnp.bfloat16))
        pool_into(pooling, late_ref, half // POOL, parts, pair, pair == pairs - 1)

    over_pairs(pairs, score, weigh, finish, copies)


def halo_kernel(rows, chunks, offsets_hbm, q_ref, k_hbm, v_hbm, *rest):
    out_ref, offsets_ref, k_ref, v_ref, bias, sems, offsets_sem = rest[-7:]
    half = rows // 2
    molecules = half // POOL
    offsets_copy = load(offsets_hbm, offsets_ref, offsets_sem)
    tail = pl.ds(half, half)
    copies = load_chunks(((k_hbm.at[tail], k_ref), (v_hbm.at[tail], v_ref)), chunks, sems)
    offsets_copy.wait()
    start = (lax.axis_index("seq") + 1) * rows
    bias[...] = mask_bias(offsets_ref, start - half, half, start, half)
    pooling = pool_matrix(half)
    pairs = k_ref.shape[1] // LANES
    parts = []

    def score(pair):
        queries = split_heads(q_ref[pl.ds(0, half), at(pair)])
        return dot_nt(k_ref[:, at(pair)], queries), jnp.transpose(v_ref[:, at(pair)])

    def weigh(pair, scores, values_t):
        terms = q_ref[pl.ds(half, 16), at(pair)].astype(jnp.float32)
        lse = jnp.concatenate(
            [terms[0:1] + terms[1:2] + terms[2:3], terms[3:4] + terms[4:5] + terms[5:6]], axis=1
        )
        scores = scores + twice(bias[...])
        top = jnp.maximum(jnp.max(scores, axis=0, keepdims=True), lse)
        weights = jnp.exp(scores - top)
        kept = jnp.exp(lse - top)
        inverse = 1.0 / (jnp.sum(weights, axis=0, keepdims=True) + kept)
        mixed = dot_nn(values_t, weights.astype(jnp.bfloat16))
        share = kept * inverse
        high = share.astype(jnp.bfloat16).astype(jnp.float32)
        low = share - high
        shares = [high[:, :half], low[:, :half], high[:, half:], low[:, half:]]
        shares.append(jnp.zeros((12, LANES), jnp.float32))
        out_ref[pl.ds(molecules, 16), at(pair)] = jnp.concatenate(shares, axis=0).astype(jnp.bfloat16)
        return mixed, inverse

    def finish(pair, mixed, inverse):
        parts.append(own_heads(mixed, inverse).astype(jnp.bfloat16))
        pool_into(pooling, out_ref, molecules, parts, pair, pair == pairs - 1)

    over_pairs(pairs, score, weigh, finish, copies)


def combine_kernel(early_ref, halo_ref, *rest):
    out_ref = rest[-1]
    half = early_ref.shape[1]
    molecules = half // POOL
    pooling = pool_matrix(half)
    first = lax.axis_index("seq") == 0
    parts = []
    for pair in range(out_ref.shape[1] // LANES):
        shares = halo_ref[molecules:, at(pair)].astype(jnp.float32)
        share_a = jnp.where(first, 1.0, shares[0:1] + shares[1:2])
        share_b = jnp.where(first, 1.0, shares[2:3] + shares[3:4])
        early = early_ref[at(pair), :].astype(jnp.float32)
        parts += [early[:HEAD_DIM] * share_a, early[HEAD_DIM:] * share_b]
        if len(parts) == 8:
            columns = pl.ds((pair - 3) * LANES, 4 * LANES)
            pooled = dot_nt(pooling, jnp.concatenate(parts, axis=0).astype(jnp.bfloat16))
            arrived = halo_ref[:molecules, columns].astype(jnp.float32)
            out_ref[:, columns] = (pooled + arrived).astype(jnp.bfloat16)
            parts = []


def back_kernel(
    slot_ref, cotangent_hbm, weight_ref, gain_ref, stashed_hbm, after_ref, dinput_ref, terms_ref,
    cotangent_ref, held_ref, grad, sems,
):
    cotangent_copy = load(cotangent_hbm, cotangent_ref, sems.at[1])
    held_copy = load(stashed_hbm.at[slot_ref[0, 0]], held_ref, sems.at[0])
    cotangent_copy.wait()
    features = weight_ref.shape[0]
    block = 512
    for begin in range(0, features, block):
        columns = pl.ds(begin, block)
        grad[:, columns] = dot_nt(cotangent_ref[...], weight_ref[columns, :])
    held_copy.wait()
    held = held_ref[...].astype(jnp.float32)
    inv_rms = lax.rsqrt(jnp.sum(held * held, axis=1, keepdims=True) / features + EPS_NORM)
    along = jnp.zeros_like(inv_rms)
    for begin in range(0, features, block):
        columns = pl.ds(begin, block)
        product = grad[:, columns] * (held_ref[:, columns].astype(jnp.float32) * inv_rms)
        total = jnp.sum(product, axis=0, keepdims=True)
        terms_ref[:, columns] = jnp.broadcast_to(total, (terms_ref.shape[0], block))
        along += jnp.sum(product * gain_ref[:, columns], axis=1, keepdims=True)
    along = along / features
    for begin in range(0, features, block):
        columns = pl.ds(begin, block)
        whitened = held_ref[:, columns].astype(jnp.float32) * inv_rms
        scaled = grad[:, columns] * gain_ref[:, columns]
        dinput_ref[:, columns] = (inv_rms * (scaled - whitened * along)).astype(jnp.bfloat16)


def project_kernel(
    early_ref, late_ref, gain_ref, weight_ref, terms_ref, out_ref, update_ref
):
    features = gain_ref.shape[1]
    arrived = jnp.concatenate([early_ref[...], late_ref[...]], axis=0).astype(jnp.float32)
    mean = jnp.sum(arrived * arrived, axis=1, keepdims=True) / features
    normed = (arrived * lax.rsqrt(mean + EPS_NORM) * gain_ref[...]).astype(jnp.bfloat16)
    out_ref[...] = dot_nn(normed, weight_ref[...]).astype(jnp.bfloat16)
    total = jnp.sum(terms_ref[...], axis=0, keepdims=True)
    mean = jnp.sum(total * total, axis=1, keepdims=True) / features
    update_ref[...] = total / jnp.sqrt(mean + EPS_STEP)


def cost(flops, read, exps=0):
    return pl.CostEstimate(flops=flops, bytes_accessed=read, transcendentals=exps)


SMEM = pl.BlockSpec(memory_space=pltpu.SMEM)
HBM = pl.BlockSpec(memory_space=pltpu.HBM)
ANY = pl.BlockSpec(memory_space=pl.ANY)
VMEM = pl.BlockSpec(memory_space=pltpu.VMEM)


def in_hbm(*arrays):
    return [pltpu.with_memory_space_constraint(x, pltpu.HBM) for x in arrays]


def params():
    return pltpu.CompilerParams(vmem_limit_bytes=24 * 2**20)


def attend_early(queries, keys, values, offsets, chunks):
    rows, width = queries.shape
    half = rows // 2
    return pl.pallas_call(
        functools.partial(early_kernel, rows, chunks),
        in_specs=[HBM] * 4,
        out_specs=[VMEM] * 2,
        out_shape=[
            jax.ShapeDtypeStruct((half + 16, width), jnp.bfloat16),
            jax.ShapeDtypeStruct((width, half), jnp.bfloat16),
        ],
        scratch_shapes=[
            pltpu.SMEM(offsets.shape, jnp.int32),
            pltpu.VMEM((half, width), jnp.bfloat16),
            pltpu.VMEM((half, width), jnp.bfloat16),
            pltpu.VMEM((half, half), jnp.float32),
            pltpu.SemaphoreType.DMA((3, chunks)),
            pltpu.SemaphoreType.DMA,
        ],
        cost_estimate=cost(4 * half * half * width, 6 * half * width, half * half * width // 64),
        compiler_params=params(),
        name="attend_early",
    )(*in_hbm(offsets, queries, keys, values))


def attend_late(queries, keys, values, offsets, after, chunks):
    rows, width = queries.shape
    half = rows // 2
    return pl.pallas_call(
        functools.partial(late_kernel, rows, chunks),
        in_specs=[HBM] * 4 + [ANY],
        out_specs=VMEM,
        out_shape=jax.ShapeDtypeStruct((half // POOL, width), jnp.bfloat16),
        scratch_shapes=[
            pltpu.SMEM(offsets.shape, jnp.int32),
            pltpu.VMEM((half, width), jnp.bfloat16),
            pltpu.VMEM((rows, width), jnp.bfloat16),
            pltpu.VMEM((rows, width), jnp.bfloat16),
            pltpu.VMEM((half, half), jnp.float32),
            pltpu.VMEM((half, half), jnp.bfloat16),
            pltpu.VMEM((half, half), jnp.bfloat16),
            pltpu.SemaphoreType.DMA((3, chunks)),
            pltpu.SemaphoreType.DMA,
        ],
        cost_estimate=cost(8 * half * half * width, 5 * rows * width, half * half * width // 64),
        compiler_params=params(),
        name="attend_late",
    )(*in_hbm(offsets, queries, keys, values), after)


def attend_halo(sent, keys, values, offsets, after, chunks):
    rows, width = keys.shape
    half = rows // 2
    return pl.pallas_call(
        functools.partial(halo_kernel, rows, chunks),
        in_specs=[HBM, VMEM, HBM, HBM] + [ANY] * len(after),
        out_specs=VMEM,
        out_shape=jax.ShapeDtypeStruct((half // POOL + 16, width), jnp.bfloat16),
        scratch_shapes=[
            pltpu.SMEM(offsets.shape, jnp.int32),
            pltpu.VMEM((half, width), jnp.bfloat16),
            pltpu.VMEM((half, width), jnp.bfloat16),
            pltpu.VMEM((half, half), jnp.float32),
            pltpu.SemaphoreType.DMA((2, chunks)),
            pltpu.SemaphoreType.DMA,
        ],
        cost_estimate=cost(4 * half * half * width, 6 * half * width, half * half * width // 64),
        compiler_params=params(),
        name="attend_halo",
    )(*in_hbm(offsets), sent, *in_hbm(keys, values), *after)


def combine(early, halo, after):
    width, half = early.shape
    return pl.pallas_call(
        combine_kernel,
        in_specs=[VMEM] * 2 + [ANY] * len(after),
        out_specs=VMEM,
        out_shape=jax.ShapeDtypeStruct((half // POOL, width), jnp.bfloat16),
        cost_estimate=cost(half * half * width, 2 * half * width),
        compiler_params=params(),
        name="combine",
    )(early, halo, *after)


def backward(slot, cotangent, weight, gain, stashed, copies, after):
    rows, depth = cotangent.shape
    width = weight.shape[0]
    return pl.pallas_call(
        back_kernel,
        in_specs=[SMEM, HBM, VMEM, VMEM, HBM, ANY],
        out_specs=[VMEM] * 2,
        scratch_shapes=[
            pltpu.VMEM((rows, depth), jnp.bfloat16),
            pltpu.VMEM((rows, width), jnp.bfloat16),
            pltpu.VMEM((rows, width), jnp.float32),
            pltpu.SemaphoreType.DMA((2,)),
        ],
        out_shape=[
            jax.ShapeDtypeStruct((rows, width), jnp.bfloat16),
            jax.ShapeDtypeStruct((copies, width), jnp.float32),
        ],
        cost_estimate=cost(2 * rows * width * depth, 2 * width * depth),
        compiler_params=params(),
        name="backward",
    )(slot, *in_hbm(cotangent), weight, gain, *in_hbm(stashed), after)


def project(early, late, gain, weight, terms):
    rows = early.shape[0] + late.shape[0]
    width, depth = weight.shape
    return pl.pallas_call(
        project_kernel,
        in_specs=[VMEM] * 5,
        out_specs=[VMEM] * 2,
        out_shape=[
            jax.ShapeDtypeStruct((rows, depth), jnp.bfloat16),
            jax.ShapeDtypeStruct((1, width), jnp.float32),
        ],
        cost_estimate=cost(2 * rows * width * depth, 2 * width * depth),
        compiler_params=params(),
        name="project",
    )(early, late, gain, weight, terms)


def local(queries, keys, values, doc_starts, weight, gain, stashed, cotangent, slot):
    queries, keys, values, offsets = queries[0, 0], keys[0, 0], values[0, 0], doc_starts[0]
    group = ("rep", "seq")
    sent, early = attend_early(queries, keys, values, offsets, 4)
    arrived = shifted(sent, "seq", -1)
    late = attend_late(queries, keys, values, offsets, early, 4)
    late_arrived = passed_along(late, "section", 1)
    copies = lax.axis_size(group)
    dinput, terms = backward(slot, cotangent[0, 0], weight[0], gain, stashed[0, 0], copies, late)
    upstream = passed_along(dinput, "section", -1)
    terms = lax.all_to_all(terms, group, 0, 0, tiled=True)
    halo = attend_halo(arrived, keys, values, offsets, (late_arrived,), 4)
    pooled = combine(early, shifted(halo, "seq", 1), (upstream, terms))
    early_arrived = passed_along(pooled, "section", 1)
    mol_keys, update = project(early_arrived, late_arrived, gain, weight[0], terms)
    return mol_keys[None, None], upstream[None, None], update


def solution(mesh):
    in_specs = (
        P("rep", "section", "seq", None),
        P("rep", "section", "seq", None),
        P("rep", "section", "seq", None),
        P("rep", "section", None),
        P("section", None, None),
        P("section", None),
        P("rep", "section", None, "seq", None),
        P("rep", "section", "seq", None),
        P("rep", "section"),
    )
    out_specs = (
        P("rep", "section", "seq", None),
        P("rep", "section", "seq", None),
        P("section", None),
    )
    return jax.shard_map(local, mesh=mesh, in_specs=in_specs, out_specs=out_specs, check_vma=False)
```

```python
import functools
import math

import jax
import jax.numpy as jnp
from jax import lax
from jax.experimental import pallas as pl
from jax.experimental.pallas import tpu as pltpu
from jax.sharding import PartitionSpec as P

HEAD_DIM = 64
POOL = 4
WINDOW = 128
LANES = 128
EPS_NORM = 1e-05
EPS_STEP = 1e-06
MASKED = -1e30
LAGS = (0, 2, 3, 4)

NT = (((1,), (1,)), ((), ()))


def dot_nt(a, b):
    return lax.dot_general(a, b, NT, preferred_element_type=jnp.float32)


def dot_nn(a, b):
    return jnp.dot(a, b, preferred_element_type=jnp.float32)


def shifted(value, axis, steps):
    count = lax.axis_size(axis)
    first, last = max(0, -steps), min(count, count - steps)
    return lax.ppermute(value, axis, [(i, i + steps) for i in range(first, last)])


def passed_along(value, axis, steps):
    count = lax.axis_size(axis)
    return lax.ppermute(value, axis, [(i, (i + steps) % count) for i in range(count)])


def earliest_key(offsets_ref, query_pos):
    start = jnp.zeros_like(query_pos)
    for d in range(offsets_ref.shape[1]):
        offset = offsets_ref[0, d]
        start = jnp.where(query_pos >= offset, offset, start)
    return jnp.maximum(start, query_pos - (WINDOW - 1))


def mask_bias(offsets_ref, query_start, key_start, keep):
    key = lax.broadcasted_iota(jnp.int32, (WINDOW, 2 * WINDOW), 0)
    query = lax.broadcasted_iota(jnp.int32, (WINDOW, 2 * WINDOW), 1) % WINDOW
    lane = lax.broadcasted_iota(jnp.int32, (1, 2 * WINDOW), 1) % WINDOW
    lowest = earliest_key(offsets_ref, query_start + lane)
    allowed = (key_start + key >= lowest) & keep(key, query)
    return jnp.where(allowed, 0.0, MASKED).astype(jnp.float32)


def split_heads(queries):
    lane = lax.broadcasted_iota(jnp.int32, (1, LANES), 1)
    scale = 1.0 / math.sqrt(HEAD_DIM)
    first = jnp.where(lane < HEAD_DIM, scale, 0.0).astype(jnp.bfloat16)
    second = jnp.where(lane < HEAD_DIM, 0.0, scale).astype(jnp.bfloat16)
    return jnp.concatenate([queries * first, queries * second], axis=0)


def pool_matrix(queries):
    molecule = lax.broadcasted_iota(jnp.int32, (queries // POOL, queries), 0)
    query = lax.broadcasted_iota(jnp.int32, (queries // POOL, queries), 1)
    return jnp.where(query // POOL == molecule, 1.0 / POOL, 0.0).astype(jnp.bfloat16)


def own_heads(mixed, scale):
    count = mixed.shape[1] // 2
    return jnp.concatenate(
        [
            mixed[:HEAD_DIM, :count] * scale[:, :count],
            mixed[HEAD_DIM:LANES, count:] * scale[:, count:],
        ],
        axis=0,
    )


def load(source, target, sem):
    copy = pltpu.make_async_copy(source, target, sem)
    copy.start()
    return copy


def load_chunks(arrays, chunks, sems):
    block = arrays[0][1].shape[1] // chunks
    return [
        [
            load(source.at[:, pl.ds(chunk * block, block)], target.at[:, pl.ds(chunk * block, block)], sems.at[i, chunk])
            for i, (source, target) in enumerate(arrays)
        ]
        for chunk in range(chunks)
    ]


def at(pair):
    return pl.ds(pair * LANES, LANES)


def over_pairs(pairs, stages, lags, before):
    results = {}
    for step in range(pairs + lags[-1]):
        if step < pairs:
            before(step)
        for stage, lag in zip(stages, lags):
            pair = step - lag
            if 0 <= pair < pairs:
                results[pair] = stage(pair, *results.get(pair, ()))


def tops(scores):
    rows = scores.shape[0]
    while rows > 8:
        rows //= 2
        scores = jnp.maximum(scores[:rows], scores[rows:])
    return jnp.max(scores, axis=0, keepdims=True)


def with_ones(values_t):
    return jnp.concatenate([values_t, jnp.ones((16, values_t.shape[1]), jnp.bfloat16)], axis=0)


def pool_into(pooling, out_ref, rows, parts, pair, last):
    if len(parts) == 4 or last:
        columns = pl.ds((pair + 1 - len(parts)) * LANES, len(parts) * LANES)
        pooled = dot_nt(pooling, jnp.concatenate(parts, axis=0))
        out_ref[pl.ds(0, rows), columns] = pooled.astype(jnp.bfloat16)
        parts.clear()


def three_terms(value):
    high = value.astype(jnp.bfloat16).astype(jnp.float32)
    middle = (value - high).astype(jnp.bfloat16).astype(jnp.float32)
    return [high, middle, value - high - middle]


def early_kernel(
    rows, chunks, offsets_hbm, q_hbm, k_hbm, v_hbm,
    sent_ref, early_ref, q_late_ref, k_ref, v_ref, own_ref, other_ref, next_ref,
    offsets_ref, bias, sems, offsets_sem,
):
    half = rows // 2
    head, tail = pl.ds(0, half), pl.ds(half, half)
    offsets_copy = load(offsets_hbm, offsets_ref, offsets_sem.at[0])
    arrays = (
        (k_hbm.at[head], k_ref.at[head]),
        (q_hbm.at[head], sent_ref.at[head]),
        (v_hbm.at[head], v_ref.at[head]),
    )
    copies = load_chunks(arrays, chunks, sems)
    rest = [
        load(k_hbm.at[tail], k_ref.at[tail], offsets_sem.at[1]),
        load(v_hbm.at[tail], v_ref.at[tail], offsets_sem.at[2]),
        load(q_hbm.at[tail], q_late_ref, offsets_sem.at[3]),
    ]
    offsets_copy.wait()
    start = lax.axis_index("seq") * rows
    bias[...] = mask_bias(offsets_ref, start, start, lambda key, query: key <= query)
    pairs = k_ref.shape[1] // LANES

    def arrive(pair):
        per_chunk = pairs // chunks
        if pair % per_chunk == 0:
            for copy in copies[pair // per_chunk]:
                copy.wait()

    def score(pair):
        scores = dot_nt(k_ref[head, at(pair)], split_heads(sent_ref[head, at(pair)]))
        return scores, with_ones(jnp.transpose(v_ref[head, at(pair)]))

    def top(pair, scores, values_t):
        scores = scores + bias[...]
        return scores, tops(scores), values_t

    def weigh(pair, scores, top, values_t):
        return top, dot_nn(values_t, jnp.exp(scores - top).astype(jnp.bfloat16))

    def finish(pair, top, mixed):
        total = mixed[LANES : LANES + 1]
        early_ref[at(pair), :] = own_heads(mixed, 1.0 / total).astype(jnp.bfloat16)
        lse = top + jnp.log(total)
        terms = three_terms(lse[:, :half]) + three_terms(lse[:, half:])
        terms.append(jnp.zeros((10, LANES), jnp.float32))
        sent_ref[pl.ds(half, 16), at(pair)] = jnp.concatenate(terms, axis=0).astype(jnp.bfloat16)
        return ()

    over_pairs(pairs, (score, top, weigh, finish), LAGS, arrive)
    own_ref[...] = mask_bias(offsets_ref, start + half, start + half, lambda key, query: key <= query)
    other_ref[...] = mask_bias(offsets_ref, start + half, start, lambda key, query: key > query)
    next_ref[...] = mask_bias(offsets_ref, start + rows, start + half, lambda key, query: key > query)
    for copy in rest:
        copy.wait()


def late_kernel(q_ref, k_ref, v_ref, own_bias, other_bias, late_ref, own, other):
    half = q_ref.shape[0]
    key = lax.broadcasted_iota(jnp.int32, own.shape, 0)
    query = lax.broadcasted_iota(jnp.int32, own.shape, 1) % half
    own[...] = jnp.where(key <= query, 1.0, 0.0).astype(jnp.bfloat16)
    other[...] = jnp.where(key <= query, 0.0, 1.0).astype(jnp.bfloat16)
    pooling = pool_matrix(half)
    pairs = k_ref.shape[1] // LANES
    parts = []

    def score(pair):
        scores = dot_nt(k_ref[:, at(pair)], split_heads(q_ref[:, at(pair)]))
        return scores, with_ones(jnp.transpose(v_ref[:, at(pair)]))

    def top(pair, scores, values_t):
        scores = jnp.maximum(scores[:half] + other_bias[...], scores[half:] + own_bias[...])
        return scores, tops(scores), values_t

    def weigh(pair, scores, top, values_t):
        weights = jnp.exp(scores - top).astype(jnp.bfloat16)
        weights = jnp.concatenate([weights * other[...], weights * own[...]], axis=0)
        return (dot_nn(values_t, weights),)

    def finish(pair, mixed):
        inverse = 1.0 / mixed[LANES : LANES + 1]
        parts.append(own_heads(mixed, inverse).astype(jnp.bfloat16))
        pool_into(pooling, late_ref, half // POOL, parts, pair, pair == pairs - 1)
        return ()

    over_pairs(pairs, (score, top, weigh, finish), LAGS, lambda pair: None)


def halo_kernel(q_ref, k_ref, v_ref, bias, term_ref, other_ref, *rest):
    out_ref, sum_ref = rest[-2:]
    sum_ref[...] = term_ref[...] + other_ref[...]
    half = bias.shape[0]
    molecules = half // POOL
    tail = pl.ds(half, half)
    pooling = pool_matrix(half)
    pairs = k_ref.shape[1] // LANES
    parts = []

    def score(pair):
        queries = split_heads(q_ref[pl.ds(0, half), at(pair)])
        scores = dot_nt(k_ref[tail, at(pair)], queries)
        return scores, with_ones(jnp.transpose(v_ref[tail, at(pair)]))

    def top(pair, scores, values_t):
        terms = q_ref[pl.ds(half, 16), at(pair)].astype(jnp.float32)
        lse = jnp.concatenate(
            [terms[0:1] + terms[1:2] + terms[2:3], terms[3:4] + terms[4:5] + terms[5:6]], axis=1
        )
        scores = scores + bias[...]
        return scores, jnp.maximum(tops(scores), lse), lse, values_t

    def weigh(pair, scores, top, lse, values_t):
        mixed = dot_nn(values_t, jnp.exp(scores - top).astype(jnp.bfloat16))
        return mixed, jnp.exp(lse - top)

    def finish(pair, mixed, kept):
        inverse = 1.0 / (mixed[LANES : LANES + 1] + kept)
        parts.append(own_heads(mixed, inverse).astype(jnp.bfloat16))
        pool_into(pooling, out_ref, molecules, parts, pair, pair == pairs - 1)
        share = kept * inverse
        high = share.astype(jnp.bfloat16).astype(jnp.float32)
        low = share - high
        shares = [high[:, :half], low[:, :half], high[:, half:], low[:, half:]]
        shares.append(jnp.zeros((12, LANES), jnp.float32))
        out_ref[pl.ds(molecules, 16), at(pair)] = jnp.concatenate(shares, axis=0).astype(jnp.bfloat16)
        return ()

    over_pairs(pairs, (score, top, weigh, finish), LAGS, lambda pair: None)


def back_kernel(
    slot_ref, cotangent_hbm, weight_ref, gain_ref, stashed_hbm, after_ref, dinput_ref, term_ref,
    cotangent_ref, held_ref, grad, sems,
):
    cotangent_copy = load(cotangent_hbm, cotangent_ref, sems.at[1])
    held_copy = load(stashed_hbm.at[slot_ref[0, 0]], held_ref, sems.at[0])
    cotangent_copy.wait()
    features = weight_ref.shape[0]
    block = 512
    for begin in range(0, features, block):
        columns = pl.ds(begin, block)
        grad[:, columns] = dot_nt(cotangent_ref[...], weight_ref[columns, :])
    held_copy.wait()
    held = held_ref[...].astype(jnp.float32)
    inv_rms = lax.rsqrt(jnp.sum(held * held, axis=1, keepdims=True) / features + EPS_NORM)
    along = jnp.zeros_like(inv_rms)
    for begin in range(0, features, block):
        columns = pl.ds(begin, block)
        product = grad[:, columns] * (held_ref[:, columns].astype(jnp.float32) * inv_rms)
        term_ref[:, columns] = jnp.sum(product, axis=0, keepdims=True)
        along += jnp.sum(product * gain_ref[:, columns], axis=1, keepdims=True)
    along = along / features
    for begin in range(0, features, block):
        columns = pl.ds(begin, block)
        whitened = held_ref[:, columns].astype(jnp.float32) * inv_rms
        scaled = grad[:, columns] * gain_ref[:, columns]
        dinput_ref[:, columns] = (inv_rms * (scaled - whitened * along)).astype(jnp.bfloat16)


def project_kernel(
    early_ref, late_ref, halo_ref, gain_ref, weight_ref, term_ref, other_ref, upstream_hbm,
    out_ref, update_ref, passed_hbm, pooled, sem,
):
    passing = load(upstream_hbm, passed_hbm, sem)
    half = early_ref.shape[1]
    molecules = half // POOL
    pooling = pool_matrix(half)
    first = lax.axis_index("seq") == 0
    parts = []
    for pair in range(early_ref.shape[0] // LANES):
        shares = halo_ref[molecules:, at(pair)].astype(jnp.float32)
        share_a = jnp.where(first, 1.0, shares[0:1] + shares[1:2])
        share_b = jnp.where(first, 1.0, shares[2:3] + shares[3:4])
        early = early_ref[at(pair), :].astype(jnp.float32)
        parts += [early[:HEAD_DIM] * share_a, early[HEAD_DIM:] * share_b]
        if len(parts) == 8:
            columns = pl.ds((pair - 3) * LANES, 4 * LANES)
            mean = dot_nt(pooling, jnp.concatenate(parts, axis=0).astype(jnp.bfloat16))
            arrived = halo_ref[:molecules, columns].astype(jnp.float32)
            pooled[pl.ds(0, molecules), columns] = (mean + arrived).astype(jnp.bfloat16)
            parts = []
    pooled[pl.ds(molecules, molecules), :] = late_ref[...]
    features = gain_ref.shape[1]
    arrived = pooled[...].astype(jnp.float32)
    mean = jnp.sum(arrived * arrived, axis=1, keepdims=True) / features
    normed = (arrived * lax.rsqrt(mean + EPS_NORM) * gain_ref[...]).astype(jnp.bfloat16)
    out_ref[...] = dot_nn(normed, weight_ref[...]).astype(jnp.bfloat16)
    total = term_ref[...] + other_ref[...]
    mean = jnp.sum(total * total, axis=1, keepdims=True) / features
    update_ref[...] = total / jnp.sqrt(mean + EPS_STEP)
    passing.wait()


def cost(flops, read, exps=0):
    return pl.CostEstimate(flops=flops, bytes_accessed=read, transcendentals=exps)


SMEM = pl.BlockSpec(memory_space=pltpu.SMEM)
HBM = pl.BlockSpec(memory_space=pltpu.HBM)
ANY = pl.BlockSpec(memory_space=pl.ANY)
VMEM = pl.BlockSpec(memory_space=pltpu.VMEM)


def in_hbm(*arrays):
    return [pltpu.with_memory_space_constraint(x, pltpu.HBM) for x in arrays]


def params():
    return pltpu.CompilerParams(vmem_limit_bytes=24 * 2**20)


def attend_early(queries, keys, values, offsets, chunks):
    rows, width = queries.shape
    half = rows // 2
    masks = [jax.ShapeDtypeStruct((half, 2 * half), jnp.float32)] * 3
    return pl.pallas_call(
        functools.partial(early_kernel, rows, chunks),
        in_specs=[HBM] * 4,
        out_specs=[VMEM] * 8,
        out_shape=[
            jax.ShapeDtypeStruct((half + 16, width), jnp.bfloat16),
            jax.ShapeDtypeStruct((width, half), jnp.bfloat16),
            jax.ShapeDtypeStruct((half, width), jnp.bfloat16),
            jax.ShapeDtypeStruct((rows, width), jnp.bfloat16),
            jax.ShapeDtypeStruct((rows, width), jnp.bfloat16),
        ]
        + masks,
        scratch_shapes=[
            pltpu.SMEM(offsets.shape, jnp.int32),
            pltpu.VMEM((half, 2 * half), jnp.float32),
            pltpu.SemaphoreType.DMA((3, chunks)),
            pltpu.SemaphoreType.DMA((4,)),
        ],
        cost_estimate=cost(4 * half * half * width, 6 * rows * width, half * half * width // 64),
        compiler_params=params(),
        name="attend_early",
    )(*in_hbm(offsets, queries, keys, values))


def attend_late(queries, keys, values, own_bias, other_bias):
    half, width = queries.shape
    return pl.pallas_call(
        late_kernel,
        in_specs=[VMEM] * 5,
        out_specs=VMEM,
        out_shape=jax.ShapeDtypeStruct((half // POOL, width), jnp.bfloat16),
        scratch_shapes=[pltpu.VMEM((half, 2 * half), jnp.bfloat16)] * 2,
        cost_estimate=cost(8 * half * half * width, 10 * half * width, half * half * width // 64),
        compiler_params=params(),
        name="attend_late",
    )(queries, keys, values, own_bias, other_bias)


def attend_halo(sent, keys, values, bias, term, other, after):
    half, width = bias.shape[0], keys.shape[1]
    return pl.pallas_call(
        halo_kernel,
        in_specs=[VMEM] * 6 + [ANY] * len(after),
        out_specs=[VMEM] * 2,
        out_shape=[
            jax.ShapeDtypeStruct((half // POOL + 16, width), jnp.bfloat16),
            jax.ShapeDtypeStruct(term.shape, term.dtype),
        ],
        cost_estimate=cost(4 * half * half * width, 6 * half * width, half * half * width // 64),
        compiler_params=params(),
        name="attend_halo",
    )(sent, keys, values, bias, term, other, *after)


def backward(slot, cotangent, weight, gain, stashed, after):
    rows, depth = cotangent.shape
    width = weight.shape[0]
    return pl.pallas_call(
        back_kernel,
        in_specs=[SMEM, HBM, VMEM, VMEM, HBM, ANY],
        out_specs=[VMEM] * 2,
        scratch_shapes=[
            pltpu.VMEM((rows, depth), jnp.bfloat16),
            pltpu.VMEM((rows, width), jnp.bfloat16),
            pltpu.VMEM((rows, width), jnp.float32),
            pltpu.SemaphoreType.DMA((2,)),
        ],
        out_shape=[
            jax.ShapeDtypeStruct((rows, width), jnp.bfloat16),
            jax.ShapeDtypeStruct((1, width), jnp.float32),
        ],
        cost_estimate=cost(2 * rows * width * depth, 2 * width * depth),
        compiler_params=params(),
        name="backward",
    )(slot, *in_hbm(cotangent), weight, gain, *in_hbm(stashed), after)


def project(early, late, halo, gain, weight, term, other, upstream):
    rows = 2 * late.shape[0]
    width, depth = weight.shape
    return pl.pallas_call(
        project_kernel,
        in_specs=[VMEM] * 7 + [ANY],
        out_specs=[VMEM, VMEM, HBM],
        out_shape=[
            jax.ShapeDtypeStruct((rows, depth), jnp.bfloat16),
            jax.ShapeDtypeStruct((1, width), jnp.float32),
            jax.ShapeDtypeStruct(upstream.shape, upstream.dtype),
        ],
        scratch_shapes=[pltpu.VMEM((rows, width), jnp.bfloat16), pltpu.SemaphoreType.DMA],
        cost_estimate=cost(2 * rows * width * depth, 2 * width * depth),
        compiler_params=params(),
        name="project",
    )(early, late, halo, gain, weight, term, other, upstream)


def swapped(value, axis, distance):
    return lax.ppermute(value, axis, [(i, i ^ distance) for i in range(lax.axis_size(axis))])


def sum_rounds():
    rounds = []
    for axis in ("rep", "seq"):
        count = lax.axis_size(axis)
        if count & (count - 1):
            return []
        rounds += [(axis, 1 << i) for i in range(count.bit_length() - 1)]
    return rounds if len(rounds) == 3 else []


def onward(value):
    sections, shards = lax.axis_size("section"), lax.axis_size("seq")
    route = [
        (s * shards + k, (s + 1) % sections * shards + k + 1)
        for s in range(sections)
        for k in range(shards - 1)
    ]
    return lax.ppermute(value, ("section", "seq"), route)


def local(queries, keys, values, doc_starts, weight, gain, stashed, cotangent, slot):
    queries, keys, values, offsets = queries[0, 0], keys[0, 0], values[0, 0], doc_starts[0]
    rounds = sum_rounds()

    def partner(term, index):
        return swapped(term, *rounds[index]) if rounds else jnp.zeros_like(term)

    sent, early, q_late, keys, values, own_bias, other_bias, next_bias = attend_early(
        queries, keys, values, offsets, 4
    )
    arrived = shifted(sent, "seq", -1)
    early = passed_along(early, "section", 1)
    late = attend_late(q_late, keys, values, own_bias, other_bias)
    late_arrived = passed_along(late, "section", 1)
    dinput, term = backward(slot, cotangent[0, 0], weight[0], gain, stashed[0, 0], late)
    upstream = passed_along(dinput, "section", -1)
    term = term if rounds else lax.psum(term, ("rep", "seq"))
    halo, term = attend_halo(arrived, keys, values, next_bias, term, partner(term, 0), (late_arrived,))
    halo = onward(halo)
    term = term + partner(term, 1)
    mol_keys, update, upstream = project(
        early, late_arrived, halo, gain, weight[0], term, partner(term, 2), upstream
    )
    return mol_keys[None, None], upstream[None, None], update


def solution(mesh):
    in_specs = (
        P("rep", "section", "seq", None),
        P("rep", "section", "seq", None),
        P("rep", "section", "seq", None),
        P("rep", "section", None),
        P("section", None, None),
        P("section", None),
        P("rep", "section", None, "seq", None),
        P("rep", "section", "seq", None),
        P("rep", "section"),
    )
    out_specs = (
        P("rep", "section", "seq", None),
        P("rep", "section", "seq", None),
        P("section", None),
    )
    return jax.shard_map(local, mesh=mesh, in_specs=in_specs, out_specs=out_specs, check_vma=False)
```

```python
import functools
import math

import jax
import jax.numpy as jnp
from jax import lax
from jax.experimental import pallas as pl
from jax.experimental.pallas import tpu as pltpu
from jax.sharding import PartitionSpec as P

HEAD_DIM = 64
POOL = 4
WINDOW = 128
LANES = 128
EPS_NORM = 1e-05
EPS_STEP = 1e-06
MASKED = -1e30
LAGS = (0, 2, 3, 4)
EXTRA = 8

NT = (((1,), (1,)), ((), ()))


def dot_nt(a, b):
    return lax.dot_general(a, b, NT, preferred_element_type=jnp.float32)


def dot_nn(a, b):
    return jnp.dot(a, b, preferred_element_type=jnp.float32)


def shifted(value, axis, steps):
    count = lax.axis_size(axis)
    first, last = max(0, -steps), min(count, count - steps)
    return lax.ppermute(value, axis, [(i, i + steps) for i in range(first, last)])


def passed_along(value, axis, steps):
    count = lax.axis_size(axis)
    return lax.ppermute(value, axis, [(i, (i + steps) % count) for i in range(count)])


def earliest_key(offsets_ref, query_pos):
    start = jnp.zeros_like(query_pos)
    for d in range(offsets_ref.shape[1]):
        offset = offsets_ref[0, d]
        start = jnp.where(query_pos >= offset, offset, start)
    return jnp.maximum(start, query_pos - (WINDOW - 1))


def mask_bias(offsets_ref, query_start, key_start, keep):
    key = lax.broadcasted_iota(jnp.int32, (WINDOW, 2 * WINDOW), 0)
    query = lax.broadcasted_iota(jnp.int32, (WINDOW, 2 * WINDOW), 1) % WINDOW
    lane = lax.broadcasted_iota(jnp.int32, (1, 2 * WINDOW), 1) % WINDOW
    lowest = earliest_key(offsets_ref, query_start + lane)
    allowed = (key_start + key >= lowest) & keep(key, query)
    return jnp.where(allowed, 0.0, MASKED).astype(jnp.float32)


def split_heads(queries):
    lane = lax.broadcasted_iota(jnp.int32, (1, LANES), 1)
    scale = 1.0 / math.sqrt(HEAD_DIM)
    first = jnp.where(lane < HEAD_DIM, scale, 0.0).astype(jnp.bfloat16)
    second = jnp.where(lane < HEAD_DIM, 0.0, scale).astype(jnp.bfloat16)
    return jnp.concatenate([queries * first, queries * second], axis=0)


def pool_matrix(queries):
    molecule = lax.broadcasted_iota(jnp.int32, (queries // POOL, queries), 0)
    query = lax.broadcasted_iota(jnp.int32, (queries // POOL, queries), 1)
    return jnp.where(query // POOL == molecule, 1.0 / POOL, 0.0).astype(jnp.bfloat16)


def own_heads(mixed, scale):
    count = mixed.shape[1] // 2
    return jnp.concatenate(
        [
            mixed[:HEAD_DIM, :count] * scale[:, :count],
            mixed[HEAD_DIM:LANES, count:] * scale[:, count:],
        ],
        axis=0,
    )


def load(source, target, sem):
    copy = pltpu.make_async_copy(source, target, sem)
    copy.start()
    return copy


def load_chunks(arrays, chunks, sems):
    block = arrays[0][1].shape[1] // chunks
    return [
        [
            load(source.at[:, pl.ds(chunk * block, block)], target.at[:, pl.ds(chunk * block, block)], sems.at[i, chunk])
            for i, (source, target) in enumerate(arrays)
        ]
        for chunk in range(chunks)
    ]


def at(pair):
    return pl.ds(pair * LANES, LANES)


def over_pairs(pairs, stages, lags, before):
    results = {}
    for step in range(pairs + lags[-1]):
        if step < pairs:
            before(step)
        for stage, lag in zip(stages, lags):
            pair = step - lag
            if 0 <= pair < pairs:
                results[pair] = stage(pair, *results.get(pair, ()))


def tops(scores):
    rows = scores.shape[0]
    while rows > 8:
        rows //= 2
        scores = jnp.maximum(scores[:rows], scores[rows:])
    return jnp.max(scores, axis=0, keepdims=True)


def with_ones(values_t):
    return jnp.concatenate([values_t, jnp.ones((16, values_t.shape[1]), jnp.bfloat16)], axis=0)


def three_terms(value):
    high = value.astype(jnp.bfloat16).astype(jnp.float32)
    middle = (value - high).astype(jnp.bfloat16).astype(jnp.float32)
    return [high, middle, value - high - middle]


def early_kernel(
    rows, chunks, offsets_hbm, q_hbm, k_hbm, v_hbm, sent_ref, early_ref,
    offsets_ref, k_ref, v_ref, bias, sems, offsets_sem,
):
    half = rows // 2
    head = pl.ds(0, half)
    offsets_copy = load(offsets_hbm, offsets_ref, offsets_sem)
    arrays = (
        (k_hbm.at[head], k_ref),
        (q_hbm.at[head], sent_ref.at[head]),
        (v_hbm.at[head], v_ref),
    )
    copies = load_chunks(arrays, chunks, sems)
    offsets_copy.wait()
    start = lax.axis_index("seq") * rows
    bias[...] = mask_bias(offsets_ref, start, start, lambda key, query: key <= query)
    pairs = k_ref.shape[1] // LANES

    def arrive(pair):
        per_chunk = pairs // chunks
        if pair % per_chunk == 0:
            for copy in copies[pair // per_chunk]:
                copy.wait()

    def score(pair):
        scores = dot_nt(k_ref[:, at(pair)], split_heads(sent_ref[head, at(pair)]))
        return scores, with_ones(jnp.transpose(v_ref[:, at(pair)]))

    def top(pair, scores, values_t):
        scores = scores + bias[...]
        return scores, tops(scores), values_t

    def weigh(pair, scores, top, values_t):
        return top, dot_nn(values_t, jnp.exp(scores - top).astype(jnp.bfloat16))

    def finish(pair, top, mixed):
        total = mixed[LANES : LANES + 1]
        early_ref[at(pair), :] = own_heads(mixed, 1.0 / total).astype(jnp.bfloat16)
        lse = top + jnp.log(total)
        terms = three_terms(lse[:, :half]) + three_terms(lse[:, half:])
        terms.append(jnp.zeros((EXTRA - 6, LANES), jnp.float32))
        sent_ref[pl.ds(half, EXTRA), at(pair)] = jnp.concatenate(terms, axis=0).astype(jnp.bfloat16)
        return ()

    over_pairs(pairs, (score, top, weigh, finish), LAGS, arrive)


def late_kernel(
    rows, chunks, offsets_hbm, q_hbm, k_hbm, v_hbm, early_ref,
    both_ref, k_tail_ref, v_tail_ref, next_ref,
    offsets_ref, q_ref, k_ref, v_ref, own_bias, other_bias, own, other, sems, offsets_sem,
):
    half = rows // 2
    head, tail = pl.ds(0, half), pl.ds(half, half)
    offsets_copy = load(offsets_hbm, offsets_ref, offsets_sem)
    arrays = (
        (k_hbm.at[head], k_ref),
        (k_hbm.at[tail], k_tail_ref),
        (q_hbm.at[tail], q_ref),
        (v_hbm.at[head], v_ref),
        (v_hbm.at[tail], v_tail_ref),
    )
    copies = load_chunks(arrays, chunks, sems)
    features = early_ref.shape[0]
    both_ref[pl.ds(0, features), :] = early_ref[...]
    key = lax.broadcasted_iota(jnp.int32, own.shape, 0)
    query = lax.broadcasted_iota(jnp.int32, own.shape, 1) % half
    own[...] = jnp.where(key <= query, 1.0, 0.0).astype(jnp.bfloat16)
    other[...] = jnp.where(key <= query, 0.0, 1.0).astype(jnp.bfloat16)
    pooling = pool_matrix(half)
    molecules = half // POOL
    offsets_copy.wait()
    start = lax.axis_index("seq") * rows
    own_bias[...] = mask_bias(offsets_ref, start + half, start + half, lambda key, query: key <= query)
    other_bias[...] = mask_bias(offsets_ref, start + half, start, lambda key, query: key > query)
    next_ref[...] = mask_bias(offsets_ref, start + rows, start + half, lambda key, query: key > query)
    pairs = k_ref.shape[1] // LANES
    parts = []

    def arrive(pair):
        per_chunk = pairs // chunks
        if pair % per_chunk == 0:
            for copy in copies[pair // per_chunk]:
                copy.wait()

    def score(pair):
        queries = split_heads(q_ref[:, at(pair)])
        values = jnp.concatenate([v_ref[:, at(pair)], v_tail_ref[:, at(pair)]], axis=0)
        keys = jnp.concatenate([k_ref[:, at(pair)], k_tail_ref[:, at(pair)]], axis=0)
        return dot_nt(keys, queries), with_ones(jnp.transpose(values))

    def top(pair, scores, values_t):
        scores = jnp.maximum(scores[:half] + other_bias[...], scores[half:] + own_bias[...])
        return scores, tops(scores), values_t

    def weigh(pair, scores, top, values_t):
        weights = jnp.exp(scores - top).astype(jnp.bfloat16)
        weights = jnp.concatenate([weights * other[...], weights * own[...]], axis=0)
        return (dot_nn(values_t, weights),)

    def finish(pair, mixed):
        inverse = 1.0 / mixed[LANES : LANES + 1]
        parts.append(own_heads(mixed, inverse).astype(jnp.bfloat16))
        if len(parts) == 4:
            pooled = dot_nt(pooling, jnp.concatenate(parts, axis=0)).astype(jnp.bfloat16)
            for i in range(4):
                place = features + (pair - 3 + i) * molecules
                both_ref[pl.ds(place, molecules), :] = pooled[:, i * LANES : (i + 1) * LANES]
            parts.clear()
        return ()

    over_pairs(pairs, (score, top, weigh, finish), LAGS, arrive)


def halo_kernel(q_ref, k_ref, v_ref, bias, after_ref, out_ref):
    half = bias.shape[0]
    molecules = half // POOL
    pooling = pool_matrix(half)
    pairs = k_ref.shape[1] // LANES
    parts = []

    def score(pair):
        queries = split_heads(q_ref[pl.ds(0, half), at(pair)])
        scores = dot_nt(k_ref[:, at(pair)], queries)
        return scores, with_ones(jnp.transpose(v_ref[:, at(pair)]))

    def top(pair, scores, values_t):
        terms = q_ref[pl.ds(half, EXTRA), at(pair)].astype(jnp.float32)
        lse = jnp.concatenate(
            [terms[0:1] + terms[1:2] + terms[2:3], terms[3:4] + terms[4:5] + terms[5:6]], axis=1
        )
        scores = scores + bias[...]
        return scores, jnp.maximum(tops(scores), lse), lse, values_t

    def weigh(pair, scores, top, lse, values_t):
        mixed = dot_nn(values_t, jnp.exp(scores - top).astype(jnp.bfloat16))
        return mixed, jnp.exp(lse - top)

    def finish(pair, mixed, kept):
        inverse = 1.0 / (mixed[LANES : LANES + 1] + kept)
        parts.append(own_heads(mixed, inverse).astype(jnp.bfloat16))
        if len(parts) == 4:
            pooled = dot_nt(pooling, jnp.concatenate(parts, axis=0)).astype(jnp.bfloat16)
            out_ref[pl.ds(0, molecules), pl.ds((pair - 3) * LANES, 4 * LANES)] = pooled
            parts.clear()
        share = kept * inverse
        high = share.astype(jnp.bfloat16).astype(jnp.float32)
        low = share - high
        shares = [high[:, :half], low[:, :half], high[:, half:], low[:, half:]]
        shares.append(jnp.zeros((EXTRA - 4, LANES), jnp.float32))
        out_ref[pl.ds(molecules, EXTRA), at(pair)] = jnp.concatenate(shares, axis=0).astype(jnp.bfloat16)
        return ()

    over_pairs(pairs, (score, top, weigh, finish), LAGS, lambda pair: None)


def back_kernel(
    slot_ref, cotangent_hbm, weight_ref, gain_ref, stashed_hbm, after_ref, dinput_ref, term_ref,
    cotangent_ref, held_ref, grad, sems,
):
    cotangent_copy = load(cotangent_hbm, cotangent_ref, sems.at[1])
    held_copy = load(stashed_hbm.at[slot_ref[0, 0]], held_ref, sems.at[0])
    cotangent_copy.wait()
    features = weight_ref.shape[0]
    block = 512
    for begin in range(0, features, block):
        columns = pl.ds(begin, block)
        grad[:, columns] = dot_nt(cotangent_ref[...], weight_ref[columns, :])
    held_copy.wait()
    held = held_ref[...].astype(jnp.float32)
    inv_rms = lax.rsqrt(jnp.sum(held * held, axis=1, keepdims=True) / features + EPS_NORM)
    along = jnp.zeros_like(inv_rms)
    for begin in range(0, features, block):
        columns = pl.ds(begin, block)
        product = grad[:, columns] * (held_ref[:, columns].astype(jnp.float32) * inv_rms)
        term_ref[:, columns] = jnp.sum(product, axis=0, keepdims=True)
        along += jnp.sum(product * gain_ref[:, columns], axis=1, keepdims=True)
    along = along / features
    for begin in range(0, features, block):
        columns = pl.ds(begin, block)
        whitened = held_ref[:, columns].astype(jnp.float32) * inv_rms
        scaled = grad[:, columns] * gain_ref[:, columns]
        dinput_ref[:, columns] = (inv_rms * (scaled - whitened * along)).astype(jnp.bfloat16)


def project_kernel(
    both_ref, halo_ref, gain_ref, weight_ref, term_ref, other_ref, upstream_hbm,
    out_ref, update_ref, passed_hbm, pooled, sem,
):
    passing = load(upstream_hbm, passed_hbm, sem)
    half = both_ref.shape[1]
    features = gain_ref.shape[1]
    molecules = half // POOL
    pooling = pool_matrix(half)
    first = lax.axis_index("seq") == 0
    parts = []
    for pair in range(features // LANES):
        shares = halo_ref[molecules:, at(pair)].astype(jnp.float32)
        share_a = jnp.where(first, 1.0, shares[0:1] + shares[1:2])
        share_b = jnp.where(first, 1.0, shares[2:3] + shares[3:4])
        early = both_ref[at(pair), :].astype(jnp.float32)
        place = pl.ds(features + pair * molecules, molecules)
        pooled[pl.ds(molecules, molecules), at(pair)] = both_ref[place, :]
        parts += [early[:HEAD_DIM] * share_a, early[HEAD_DIM:] * share_b]
        if len(parts) == 8:
            columns = pl.ds((pair - 3) * LANES, 4 * LANES)
            mean = dot_nt(pooling, jnp.concatenate(parts, axis=0).astype(jnp.bfloat16))
            arrived = halo_ref[:molecules, columns].astype(jnp.float32)
            pooled[pl.ds(0, molecules), columns] = (mean + arrived).astype(jnp.bfloat16)
            parts = []
    arrived = pooled[...].astype(jnp.float32)
    mean = jnp.sum(arrived * arrived, axis=1, keepdims=True) / features
    normed = (arrived * lax.rsqrt(mean + EPS_NORM) * gain_ref[...]).astype(jnp.bfloat16)
    out_ref[...] = dot_nn(normed, weight_ref[...]).astype(jnp.bfloat16)
    total = term_ref[...] + other_ref[...]
    mean = jnp.sum(total * total, axis=1, keepdims=True) / features
    update_ref[...] = total / jnp.sqrt(mean + EPS_STEP)
    passing.wait()


def cost(flops, read, exps=0):
    return pl.CostEstimate(flops=flops, bytes_accessed=read, transcendentals=exps)


SMEM = pl.BlockSpec(memory_space=pltpu.SMEM)
HBM = pl.BlockSpec(memory_space=pltpu.HBM)
ANY = pl.BlockSpec(memory_space=pl.ANY)
VMEM = pl.BlockSpec(memory_space=pltpu.VMEM)


def in_hbm(*arrays):
    return [pltpu.with_memory_space_constraint(x, pltpu.HBM) for x in arrays]


def params():
    return pltpu.CompilerParams(vmem_limit_bytes=24 * 2**20)


def attend_early(queries, keys, values, offsets, chunks):
    rows, width = queries.shape
    half = rows // 2
    return pl.pallas_call(
        functools.partial(early_kernel, rows, chunks),
        in_specs=[HBM] * 4,
        out_specs=[VMEM] * 2,
        out_shape=[
            jax.ShapeDtypeStruct((half + EXTRA, width), jnp.bfloat16),
            jax.ShapeDtypeStruct((width, half), jnp.bfloat16),
        ],
        scratch_shapes=[
            pltpu.SMEM(offsets.shape, jnp.int32),
            pltpu.VMEM((half, width), jnp.bfloat16),
            pltpu.VMEM((half, width), jnp.bfloat16),
            pltpu.VMEM((half, 2 * half), jnp.float32),
            pltpu.SemaphoreType.DMA((3, chunks)),
            pltpu.SemaphoreType.DMA,
        ],
        cost_estimate=cost(4 * half * half * width, 6 * half * width, half * half * width // 64),
        compiler_params=params(),
        name="attend_early",
    )(*in_hbm(offsets, queries, keys, values))


def attend_late(queries, keys, values, offsets, early, chunks):
    rows, width = queries.shape
    half = rows // 2
    return pl.pallas_call(
        functools.partial(late_kernel, rows, chunks),
        in_specs=[HBM] * 4 + [VMEM],
        out_specs=[VMEM] * 4,
        out_shape=[
            jax.ShapeDtypeStruct((width + width // POOL, half), jnp.bfloat16),
            jax.ShapeDtypeStruct((half, width), jnp.bfloat16),
            jax.ShapeDtypeStruct((half, width), jnp.bfloat16),
            jax.ShapeDtypeStruct((half, 2 * half), jnp.float32),
        ],
        scratch_shapes=[
            pltpu.SMEM(offsets.shape, jnp.int32),
            pltpu.VMEM((half, width), jnp.bfloat16),
            pltpu.VMEM((half, width), jnp.bfloat16),
            pltpu.VMEM((half, width), jnp.bfloat16),
            pltpu.VMEM((half, 2 * half), jnp.float32),
            pltpu.VMEM((half, 2 * half), jnp.float32),
            pltpu.VMEM((half, 2 * half), jnp.bfloat16),
            pltpu.VMEM((half, 2 * half), jnp.bfloat16),
            pltpu.SemaphoreType.DMA((5, chunks)),
            pltpu.SemaphoreType.DMA,
        ],
        cost_estimate=cost(8 * half * half * width, 10 * half * width, half * half * width // 64),
        compiler_params=params(),
        name="attend_late",
    )(*in_hbm(offsets, queries, keys, values), early)


def attend_halo(sent, keys, values, bias, after):
    half, width = keys.shape
    return pl.pallas_call(
        halo_kernel,
        in_specs=[VMEM] * 4 + [ANY],
        out_specs=VMEM,
        out_shape=jax.ShapeDtypeStruct((half // POOL + EXTRA, width), jnp.bfloat16),
        cost_estimate=cost(4 * half * half * width, 6 * half * width, half * half * width // 64),
        compiler_params=params(),
        name="attend_halo",
    )(sent, keys, values, bias, after)


def backward(slot, cotangent, weight, gain, stashed, after):
    rows, depth = cotangent.shape
    width = weight.shape[0]
    return pl.pallas_call(
        back_kernel,
        in_specs=[SMEM, HBM, VMEM, VMEM, HBM, ANY],
        out_specs=[VMEM] * 2,
        scratch_shapes=[
            pltpu.VMEM((rows, depth), jnp.bfloat16),
            pltpu.VMEM((rows, width), jnp.bfloat16),
            pltpu.VMEM((rows, width), jnp.float32),
            pltpu.SemaphoreType.DMA((2,)),
        ],
        out_shape=[
            jax.ShapeDtypeStruct((rows, width), jnp.bfloat16),
            jax.ShapeDtypeStruct((1, width), jnp.float32),
        ],
        cost_estimate=cost(2 * rows * width * depth, 2 * width * depth),
        compiler_params=params(),
        name="backward",
    )(slot, *in_hbm(cotangent), weight, gain, *in_hbm(stashed), after)


def project(both, halo, gain, weight, term, other, upstream):
    rows = upstream.shape[0]
    width, depth = weight.shape
    return pl.pallas_call(
        project_kernel,
        in_specs=[VMEM] * 6 + [ANY],
        out_specs=[VMEM, VMEM, HBM],
        out_shape=[
            jax.ShapeDtypeStruct((rows, depth), jnp.bfloat16),
            jax.ShapeDtypeStruct((1, width), jnp.float32),
            jax.ShapeDtypeStruct(upstream.shape, upstream.dtype),
        ],
        scratch_shapes=[pltpu.VMEM((rows, width), jnp.bfloat16), pltpu.SemaphoreType.DMA],
        cost_estimate=cost(2 * rows * width * depth, 2 * width * depth),
        compiler_params=params(),
        name="project",
    )(both, halo, gain, weight, term, other, upstream)


def swapped(value, axis, distance):
    return lax.ppermute(value, axis, [(i, i ^ distance) for i in range(lax.axis_size(axis))])


def sum_rounds():
    rounds = []
    for axis in ("rep", "seq"):
        count = lax.axis_size(axis)
        if count & (count - 1):
            return []
        rounds += [(axis, 1 << i) for i in range(count.bit_length() - 1)]
    return rounds if len(rounds) == 3 else []


def onward(value):
    sections, shards = lax.axis_size("section"), lax.axis_size("seq")
    route = [
        (s * shards + k, (s + 1) % sections * shards + k + 1)
        for s in range(sections)
        for k in range(shards - 1)
    ]
    return lax.ppermute(value, ("section", "seq"), route)


def local(queries, keys, values, doc_starts, weight, gain, stashed, cotangent, slot):
    queries, keys, values, offsets = queries[0, 0], keys[0, 0], values[0, 0], doc_starts[0]
    rounds = sum_rounds()

    def partner(term, index):
        return swapped(term, *rounds[index]) if rounds else jnp.zeros_like(term)

    sent, early = attend_early(queries, keys, values, offsets, 4)
    arrived = shifted(sent, "seq", -1)
    both, k_tail, v_tail, next_bias = attend_late(queries, keys, values, offsets, early, 4)
    both_arrived = passed_along(both, "section", 1)
    dinput, term = backward(slot, cotangent[0, 0], weight[0], gain, stashed[0, 0], both)
    upstream = passed_along(dinput, "section", -1)
    term = term if rounds else lax.psum(term, ("rep", "seq"))
    term = term + partner(term, 0)
    term = term + partner(term, 1)
    halo = onward(attend_halo(arrived, k_tail, v_tail, next_bias, term))
    mol_keys, update, upstream = project(
        both_arrived, halo, gain, weight[0], term, partner(term, 2), upstream
    )
    return mol_keys[None, None], upstream[None, None], update


def solution(mesh):
    in_specs = (
        P("rep", "section", "seq", None),
        P("rep", "section", "seq", None),
        P("rep", "section", "seq", None),
        P("rep", "section", None),
        P("section", None, None),
        P("section", None),
        P("rep", "section", None, "seq", None),
        P("rep", "section", "seq", None),
        P("rep", "section"),
    )
    out_specs = (
        P("rep", "section", "seq", None),
        P("rep", "section", "seq", None),
        P("section", None),
    )
    return jax.shard_map(local, mesh=mesh, in_specs=in_specs, out_specs=out_specs, check_vma=False)
```

```python
import functools
import math

import jax
import jax.numpy as jnp
from jax import lax
from jax.experimental import pallas as pl
from jax.experimental.pallas import tpu as pltpu
from jax.sharding import PartitionSpec as P

HEAD_DIM = 64
POOL = 4
WINDOW = 128
LANES = 128
EPS_NORM = 1e-05
EPS_STEP = 1e-06
MASKED = -1e30
LAGS = (0, 2, 3, 4)
EXTRA = 8

NT = (((1,), (1,)), ((), ()))


def dot_nt(a, b):
    return lax.dot_general(a, b, NT, preferred_element_type=jnp.float32)


def dot_nn(a, b):
    return jnp.dot(a, b, preferred_element_type=jnp.float32)


def shifted(value, axis, steps):
    count = lax.axis_size(axis)
    first, last = max(0, -steps), min(count, count - steps)
    return lax.ppermute(value, axis, [(i, i + steps) for i in range(first, last)])


def passed_along(value, axis, steps):
    count = lax.axis_size(axis)
    return lax.ppermute(value, axis, [(i, (i + steps) % count) for i in range(count)])


def earliest_key(offsets_ref, query_pos):
    start = jnp.zeros_like(query_pos)
    for d in range(offsets_ref.shape[1]):
        offset = offsets_ref[0, d]
        start = jnp.where(query_pos >= offset, offset, start)
    return jnp.maximum(start, query_pos - (WINDOW - 1))


def mask_bias(offsets_ref, query_start, key_start, keep):
    key = lax.broadcasted_iota(jnp.int32, (WINDOW, 2 * WINDOW), 0)
    query = lax.broadcasted_iota(jnp.int32, (WINDOW, 2 * WINDOW), 1) % WINDOW
    lane = lax.broadcasted_iota(jnp.int32, (1, 2 * WINDOW), 1) % WINDOW
    lowest = earliest_key(offsets_ref, query_start + lane)
    allowed = (key_start + key >= lowest) & keep(key, query)
    return jnp.where(allowed, 0.0, MASKED).astype(jnp.float32)


def split_heads(queries):
    lane = lax.broadcasted_iota(jnp.int32, (1, LANES), 1)
    scale = 1.0 / math.sqrt(HEAD_DIM)
    first = jnp.where(lane < HEAD_DIM, scale, 0.0).astype(jnp.bfloat16)
    second = jnp.where(lane < HEAD_DIM, 0.0, scale).astype(jnp.bfloat16)
    return jnp.concatenate([queries * first, queries * second], axis=0)


def pool_matrix(queries):
    molecule = lax.broadcasted_iota(jnp.int32, (queries // POOL, queries), 0)
    query = lax.broadcasted_iota(jnp.int32, (queries // POOL, queries), 1)
    return jnp.where(query // POOL == molecule, 1.0 / POOL, 0.0).astype(jnp.bfloat16)


def own_heads(mixed, scale):
    count = mixed.shape[1] // 2
    return jnp.concatenate(
        [
            mixed[:HEAD_DIM, :count] * scale[:, :count],
            mixed[HEAD_DIM:LANES, count:] * scale[:, count:],
        ],
        axis=0,
    )


def load(source, target, sem):
    copy = pltpu.make_async_copy(source, target, sem)
    copy.start()
    return copy


def load_chunks(arrays, chunks, sems):
    block = arrays[0][1].shape[1] // chunks
    return [
        [
            load(source.at[:, pl.ds(chunk * block, block)], target.at[:, pl.ds(chunk * block, block)], sems.at[i, chunk])
            for i, (source, target) in enumerate(arrays)
        ]
        for chunk in range(chunks)
    ]


def at(pair):
    return pl.ds(pair * LANES, LANES)


def over_pairs(pairs, stages, lags, before):
    results = {}
    for step in range(pairs + lags[-1]):
        if step < pairs:
            before(step)
        for stage, lag in zip(stages, lags):
            pair = step - lag
            if 0 <= pair < pairs:
                results[pair] = stage(pair, *results.get(pair, ()))


def tops(scores):
    rows = scores.shape[0]
    while rows > 8:
        rows //= 2
        scores = jnp.maximum(scores[:rows], scores[rows:])
    return jnp.max(scores, axis=0, keepdims=True)


def with_ones(values_t):
    return jnp.concatenate([values_t, jnp.ones((16, values_t.shape[1]), jnp.bfloat16)], axis=0)


def three_terms(value):
    high = value.astype(jnp.bfloat16).astype(jnp.float32)
    middle = (value - high).astype(jnp.bfloat16).astype(jnp.float32)
    return [high, middle, value - high - middle]


def early_kernel(
    rows, chunks, offsets_hbm, q_hbm, k_hbm, v_hbm,
    sent_ref, early_ref, q_late_ref, k_ref, v_ref, own_ref, other_ref, next_ref,
    offsets_ref, bias, sems, offsets_sem,
):
    half = rows // 2
    head, tail = pl.ds(0, half), pl.ds(half, half)
    offsets_copy = load(offsets_hbm, offsets_ref, offsets_sem.at[0])
    arrays = (
        (k_hbm.at[head], k_ref.at[head]),
        (q_hbm.at[head], sent_ref.at[head]),
        (v_hbm.at[head], v_ref.at[head]),
    )
    copies = load_chunks(arrays, chunks, sems)
    rest = [
        load(k_hbm.at[tail], k_ref.at[tail], offsets_sem.at[1]),
        load(v_hbm.at[tail], v_ref.at[tail], offsets_sem.at[2]),
        load(q_hbm.at[tail], q_late_ref, offsets_sem.at[3]),
    ]
    offsets_copy.wait()
    start = lax.axis_index("seq") * rows
    bias[...] = mask_bias(offsets_ref, start, start, lambda key, query: key <= query)
    pairs = k_ref.shape[1] // LANES

    def arrive(pair):
        per_chunk = pairs // chunks
        if pair % per_chunk == 0:
            for copy in copies[pair // per_chunk]:
                copy.wait()

    def score(pair):
        scores = dot_nt(k_ref[head, at(pair)], split_heads(sent_ref[head, at(pair)]))
        return scores, with_ones(jnp.transpose(v_ref[head, at(pair)]))

    def top(pair, scores, values_t):
        scores = scores + bias[...]
        return scores, tops(scores), values_t

    def weigh(pair, scores, top, values_t):
        return top, dot_nn(values_t, jnp.exp(scores - top).astype(jnp.bfloat16))

    def finish(pair, top, mixed):
        total = mixed[LANES : LANES + 1]
        early_ref[at(pair), :] = own_heads(mixed, 1.0 / total).astype(jnp.bfloat16)
        lse = top + jnp.log(total)
        terms = three_terms(lse[:, :half]) + three_terms(lse[:, half:])
        terms.append(jnp.zeros((EXTRA - 6, LANES), jnp.float32))
        sent_ref[pl.ds(half, EXTRA), at(pair)] = jnp.concatenate(terms, axis=0).astype(jnp.bfloat16)
        return ()

    over_pairs(pairs, (score, top, weigh, finish), LAGS, arrive)
    own_ref[...] = mask_bias(offsets_ref, start + half, start + half, lambda key, query: key <= query)
    other_ref[...] = mask_bias(offsets_ref, start + half, start, lambda key, query: key > query)
    next_ref[...] = mask_bias(offsets_ref, start + rows, start + half, lambda key, query: key > query)
    for copy in rest:
        copy.wait()


def late_kernel(
    q_ref, k_ref, v_ref, own_bias, other_bias, slot_ref, weight_hbm, cotangent_hbm, stashed_hbm,
    late_ref, weight_ref, cotangent_ref, held_ref, own, other, sems,
):
    copies = [
        load(cotangent_hbm, cotangent_ref, sems.at[0]),
        load(stashed_hbm.at[slot_ref[0, 0]], held_ref, sems.at[1]),
        load(weight_hbm, weight_ref, sems.at[2]),
    ]
    half = q_ref.shape[0]
    key = lax.broadcasted_iota(jnp.int32, own.shape, 0)
    query = lax.broadcasted_iota(jnp.int32, own.shape, 1) % half
    own[...] = jnp.where(key <= query, 1.0, 0.0).astype(jnp.bfloat16)
    other[...] = jnp.where(key <= query, 0.0, 1.0).astype(jnp.bfloat16)
    pooling = pool_matrix(half)
    pairs = k_ref.shape[1] // LANES
    parts = []

    def score(pair):
        scores = dot_nt(k_ref[:, at(pair)], split_heads(q_ref[:, at(pair)]))
        return scores, with_ones(jnp.transpose(v_ref[:, at(pair)]))

    def top(pair, scores, values_t):
        scores = jnp.maximum(scores[:half] + other_bias[...], scores[half:] + own_bias[...])
        return scores, tops(scores), values_t

    def weigh(pair, scores, top, values_t):
        weights = jnp.exp(scores - top).astype(jnp.bfloat16)
        weights = jnp.concatenate([weights * other[...], weights * own[...]], axis=0)
        return (dot_nn(values_t, weights),)

    def finish(pair, mixed):
        inverse = 1.0 / mixed[LANES : LANES + 1]
        parts.append(own_heads(mixed, inverse).astype(jnp.bfloat16))
        if len(parts) == 4:
            pooled = dot_nt(pooling, jnp.concatenate(parts, axis=0)).astype(jnp.bfloat16)
            late_ref[:, pl.ds((pair - 3) * LANES, 4 * LANES)] = pooled
            parts.clear()
        return ()

    over_pairs(pairs, (score, top, weigh, finish), LAGS, lambda pair: None)
    for copy in copies:
        copy.wait()


def halo_kernel(q_ref, k_ref, v_ref, bias, after_ref, out_ref):
    half = bias.shape[0]
    molecules = half // POOL
    tail = pl.ds(half, half)
    pooling = pool_matrix(half)
    pairs = k_ref.shape[1] // LANES
    parts = []

    def score(pair):
        queries = split_heads(q_ref[pl.ds(0, half), at(pair)])
        scores = dot_nt(k_ref[tail, at(pair)], queries)
        return scores, with_ones(jnp.transpose(v_ref[tail, at(pair)]))

    def top(pair, scores, values_t):
        terms = q_ref[pl.ds(half, EXTRA), at(pair)].astype(jnp.float32)
        lse = jnp.concatenate(
            [terms[0:1] + terms[1:2] + terms[2:3], terms[3:4] + terms[4:5] + terms[5:6]], axis=1
        )
        scores = scores + bias[...]
        return scores, jnp.maximum(tops(scores), lse), lse, values_t

    def weigh(pair, scores, top, lse, values_t):
        mixed = dot_nn(values_t, jnp.exp(scores - top).astype(jnp.bfloat16))
        return mixed, jnp.exp(lse - top)

    def finish(pair, mixed, kept):
        inverse = 1.0 / (mixed[LANES : LANES + 1] + kept)
        parts.append(own_heads(mixed, inverse).astype(jnp.bfloat16))
        if len(parts) == 4:
            pooled = dot_nt(pooling, jnp.concatenate(parts, axis=0)).astype(jnp.bfloat16)
            out_ref[pl.ds(0, molecules), pl.ds((pair - 3) * LANES, 4 * LANES)] = pooled
            parts.clear()
        share = kept * inverse
        high = share.astype(jnp.bfloat16).astype(jnp.float32)
        low = share - high
        shares = [high[:, :half], low[:, :half], high[:, half:], low[:, half:]]
        shares.append(jnp.zeros((EXTRA - 4, LANES), jnp.float32))
        out_ref[pl.ds(molecules, EXTRA), at(pair)] = jnp.concatenate(shares, axis=0).astype(jnp.bfloat16)
        return ()

    over_pairs(pairs, (score, top, weigh, finish), LAGS, lambda pair: None)


def back_kernel(cotangent_ref, weight_ref, gain_ref, held_ref, dinput_ref, term_ref, grad):
    features = weight_ref.shape[0]
    block = 512
    for begin in range(0, features, block):
        columns = pl.ds(begin, block)
        grad[:, columns] = dot_nt(cotangent_ref[...], weight_ref[columns, :])
    held = held_ref[...].astype(jnp.float32)
    inv_rms = lax.rsqrt(jnp.sum(held * held, axis=1, keepdims=True) / features + EPS_NORM)
    along = jnp.zeros_like(inv_rms)
    for begin in range(0, features, block):
        columns = pl.ds(begin, block)
        product = grad[:, columns] * (held_ref[:, columns].astype(jnp.float32) * inv_rms)
        term_ref[:, columns] = jnp.sum(product, axis=0, keepdims=True)
        along += jnp.sum(product * gain_ref[:, columns], axis=1, keepdims=True)
    along = along / features
    for begin in range(0, features, block):
        columns = pl.ds(begin, block)
        whitened = held_ref[:, columns].astype(jnp.float32) * inv_rms
        scaled = grad[:, columns] * gain_ref[:, columns]
        dinput_ref[:, columns] = (inv_rms * (scaled - whitened * along)).astype(jnp.bfloat16)


def project_kernel(
    early_ref, late_ref, halo_ref, gain_ref, weight_ref, term_ref, other_ref, upstream_hbm,
    out_ref, update_ref, passed_hbm, pooled, sem,
):
    passing = load(upstream_hbm, passed_hbm, sem)
    half = early_ref.shape[1]
    features = gain_ref.shape[1]
    molecules = half // POOL
    pooling = pool_matrix(half)
    first = lax.axis_index("seq") == 0
    parts = []
    for pair in range(features // LANES):
        shares = halo_ref[molecules:, at(pair)].astype(jnp.float32)
        share_a = jnp.where(first, 1.0, shares[0:1] + shares[1:2])
        share_b = jnp.where(first, 1.0, shares[2:3] + shares[3:4])
        early = early_ref[at(pair), :].astype(jnp.float32)
        parts += [early[:HEAD_DIM] * share_a, early[HEAD_DIM:] * share_b]
        if len(parts) == 8:
            columns = pl.ds((pair - 3) * LANES, 4 * LANES)
            mean = dot_nt(pooling, jnp.concatenate(parts, axis=0).astype(jnp.bfloat16))
            arrived = halo_ref[:molecules, columns].astype(jnp.float32)
            pooled[pl.ds(0, molecules), columns] = (mean + arrived).astype(jnp.bfloat16)
            parts = []
    pooled[pl.ds(molecules, molecules), :] = late_ref[...]
    arrived = pooled[...].astype(jnp.float32)
    mean = jnp.sum(arrived * arrived, axis=1, keepdims=True) / features
    normed = (arrived * lax.rsqrt(mean + EPS_NORM) * gain_ref[...]).astype(jnp.bfloat16)
    out_ref[...] = dot_nn(normed, weight_ref[...]).astype(jnp.bfloat16)
    total = term_ref[...] + other_ref[...]
    mean = jnp.sum(total * total, axis=1, keepdims=True) / features
    update_ref[...] = total / jnp.sqrt(mean + EPS_STEP)
    passing.wait()


def cost(flops, read, exps=0):
    return pl.CostEstimate(flops=flops, bytes_accessed=read, transcendentals=exps)


SMEM = pl.BlockSpec(memory_space=pltpu.SMEM)
HBM = pl.BlockSpec(memory_space=pltpu.HBM)
ANY = pl.BlockSpec(memory_space=pl.ANY)
VMEM = pl.BlockSpec(memory_space=pltpu.VMEM)


def in_hbm(*arrays):
    return [pltpu.with_memory_space_constraint(x, pltpu.HBM) for x in arrays]


def params():
    return pltpu.CompilerParams(vmem_limit_bytes=24 * 2**20)


def attend_early(queries, keys, values, offsets, chunks):
    rows, width = queries.shape
    half = rows // 2
    masks = [jax.ShapeDtypeStruct((half, 2 * half), jnp.float32)] * 3
    return pl.pallas_call(
        functools.partial(early_kernel, rows, chunks),
        in_specs=[HBM] * 4,
        out_specs=[VMEM] * 8,
        out_shape=[
            jax.ShapeDtypeStruct((half + EXTRA, width), jnp.bfloat16),
            jax.ShapeDtypeStruct((width, half), jnp.bfloat16),
            jax.ShapeDtypeStruct((half, width), jnp.bfloat16),
            jax.ShapeDtypeStruct((rows, width), jnp.bfloat16),
            jax.ShapeDtypeStruct((rows, width), jnp.bfloat16),
        ]
        + masks,
        scratch_shapes=[
            pltpu.SMEM(offsets.shape, jnp.int32),
            pltpu.VMEM((half, 2 * half), jnp.float32),
            pltpu.SemaphoreType.DMA((3, chunks)),
            pltpu.SemaphoreType.DMA((4,)),
        ],
        cost_estimate=cost(4 * half * half * width, 6 * rows * width, half * half * width // 64),
        compiler_params=params(),
        name="attend_early",
    )(*in_hbm(offsets, queries, keys, values))


def attend_late(queries, keys, values, own_bias, other_bias, slot, weight, cotangent, stashed):
    half, width = queries.shape
    return pl.pallas_call(
        late_kernel,
        in_specs=[VMEM] * 5 + [SMEM] + [HBM] * 3,
        out_specs=[VMEM] * 4,
        out_shape=[
            jax.ShapeDtypeStruct((half // POOL, width), jnp.bfloat16),
            jax.ShapeDtypeStruct(weight.shape, weight.dtype),
            jax.ShapeDtypeStruct(cotangent.shape, cotangent.dtype),
            jax.ShapeDtypeStruct(stashed.shape[1:], stashed.dtype),
        ],
        scratch_shapes=[
            pltpu.VMEM((half, 2 * half), jnp.bfloat16),
            pltpu.VMEM((half, 2 * half), jnp.bfloat16),
            pltpu.SemaphoreType.DMA((3,)),
        ],
        cost_estimate=cost(8 * half * half * width, 30 * half * width, half * half * width // 64),
        compiler_params=params(),
        name="attend_late",
    )(queries, keys, values, own_bias, other_bias, slot, *in_hbm(weight, cotangent, stashed))


def attend_halo(sent, keys, values, bias, after):
    half, width = bias.shape[0], keys.shape[1]
    return pl.pallas_call(
        halo_kernel,
        in_specs=[VMEM] * 4 + [ANY],
        out_specs=VMEM,
        out_shape=jax.ShapeDtypeStruct((half // POOL + EXTRA, width), jnp.bfloat16),
        cost_estimate=cost(4 * half * half * width, 6 * half * width, half * half * width // 64),
        compiler_params=params(),
        name="attend_halo",
    )(sent, keys, values, bias, after)


def backward(cotangent, weight, gain, held):
    rows, width = held.shape
    depth = weight.shape[1]
    return pl.pallas_call(
        back_kernel,
        in_specs=[VMEM] * 4,
        out_specs=[VMEM] * 2,
        scratch_shapes=[pltpu.VMEM((rows, width), jnp.float32)],
        out_shape=[
            jax.ShapeDtypeStruct((rows, width), jnp.bfloat16),
            jax.ShapeDtypeStruct((1, width), jnp.float32),
        ],
        cost_estimate=cost(2 * rows * width * depth, 2 * width * depth),
        compiler_params=params(),
        name="backward",
    )(cotangent, weight, gain, held)


def project(early, late, halo, gain, weight, term, other, upstream):
    rows = upstream.shape[0]
    width, depth = weight.shape
    return pl.pallas_call(
        project_kernel,
        in_specs=[VMEM] * 7 + [ANY],
        out_specs=[VMEM, VMEM, HBM],
        out_shape=[
            jax.ShapeDtypeStruct((rows, depth), jnp.bfloat16),
            jax.ShapeDtypeStruct((1, width), jnp.float32),
            jax.ShapeDtypeStruct(upstream.shape, upstream.dtype),
        ],
        scratch_shapes=[pltpu.VMEM((rows, width), jnp.bfloat16), pltpu.SemaphoreType.DMA],
        cost_estimate=cost(2 * rows * width * depth, 2 * width * depth),
        compiler_params=params(),
        name="project",
    )(early, late, halo, gain, weight, term, other, upstream)


def swapped(value, axis, distance):
    return lax.ppermute(value, axis, [(i, i ^ distance) for i in range(lax.axis_size(axis))])


def sum_rounds():
    rounds = []
    for axis in ("rep", "seq"):
        count = lax.axis_size(axis)
        if count & (count - 1):
            return []
        rounds += [(axis, 1 << i) for i in range(count.bit_length() - 1)]
    return rounds if len(rounds) == 3 else []


def onward(value):
    sections, shards = lax.axis_size("section"), lax.axis_size("seq")
    route = [
        (s * shards + k, (s + 1) % sections * shards + k + 1)
        for s in range(sections)
        for k in range(shards - 1)
    ]
    return lax.ppermute(value, ("section", "seq"), route)


def local(queries, keys, values, doc_starts, weight, gain, stashed, cotangent, slot):
    queries, keys, values, offsets = queries[0, 0], keys[0, 0], values[0, 0], doc_starts[0]
    rounds = sum_rounds()

    def partner(term, index):
        return swapped(term, *rounds[index]) if rounds else jnp.zeros_like(term)

    sent, early, q_late, keys, values, own_bias, other_bias, next_bias = attend_early(
        queries, keys, values, offsets, 4
    )
    arrived = shifted(sent, "seq", -1)
    early = passed_along(early, "section", 1)
    late, weight, cotangent, held = attend_late(
        q_late, keys, values, own_bias, other_bias, slot, weight[0], cotangent[0, 0], stashed[0, 0]
    )
    dinput, term = backward(cotangent, weight, gain, held)
    upstream = passed_along(dinput, "section", -1)
    term = term if rounds else lax.psum(term, ("rep", "seq"))
    term = term + partner(term, 0)
    term = term + partner(term, 1)
    late = passed_along(late, "section", 1)
    halo = onward(attend_halo(arrived, keys, values, next_bias, term))
    mol_keys, update, upstream = project(
        early, late, halo, gain, weight, term, partner(term, 2), upstream
    )
    return mol_keys[None, None], upstream[None, None], update


def solution(mesh):
    in_specs = (
        P("rep", "section", "seq", None),
        P("rep", "section", "seq", None),
        P("rep", "section", "seq", None),
        P("rep", "section", None),
        P("section", None, None),
        P("section", None),
        P("rep", "section", None, "seq", None),
        P("rep", "section", "seq", None),
        P("rep", "section"),
    )
    out_specs = (
        P("rep", "section", "seq", None),
        P("rep", "section", "seq", None),
        P("section", None),
    )
    return jax.shard_map(local, mesh=mesh, in_specs=in_specs, out_specs=out_specs, check_vma=False)
```

```python
import functools
import math

import jax
import jax.numpy as jnp
from jax import lax
from jax.experimental import pallas as pl
from jax.experimental.pallas import tpu as pltpu
from jax.sharding import PartitionSpec as P

HEAD_DIM = 64
POOL = 4
WINDOW = 128
LANES = 128
EPS_NORM = 1e-05
EPS_STEP = 1e-06
MASKED = -1e30
LAGS = (0, 2, 3, 4)
EXTRA = 8

NT = (((1,), (1,)), ((), ()))


def dot_nt(a, b):
    return lax.dot_general(a, b, NT, preferred_element_type=jnp.float32)


def dot_nn(a, b):
    return jnp.dot(a, b, preferred_element_type=jnp.float32)


def shifted(value, axis, steps):
    count = lax.axis_size(axis)
    first, last = max(0, -steps), min(count, count - steps)
    return lax.ppermute(value, axis, [(i, i + steps) for i in range(first, last)])


def passed_along(value, axis, steps):
    count = lax.axis_size(axis)
    return lax.ppermute(value, axis, [(i, (i + steps) % count) for i in range(count)])


def earliest_key(offsets_ref, query_pos):
    start = jnp.zeros_like(query_pos)
    for d in range(offsets_ref.shape[1]):
        offset = offsets_ref[0, d]
        start = jnp.where(query_pos >= offset, offset, start)
    return jnp.maximum(start, query_pos - (WINDOW - 1))


def mask_bias(offsets_ref, query_start, key_start, keep):
    key = lax.broadcasted_iota(jnp.int32, (WINDOW, 2 * WINDOW), 0)
    query = lax.broadcasted_iota(jnp.int32, (WINDOW, 2 * WINDOW), 1) % WINDOW
    lane = lax.broadcasted_iota(jnp.int32, (1, 2 * WINDOW), 1) % WINDOW
    lowest = earliest_key(offsets_ref, query_start + lane)
    allowed = (key_start + key >= lowest) & keep(key, query)
    return jnp.where(allowed, 0.0, MASKED).astype(jnp.float32)


def split_heads(queries):
    lane = lax.broadcasted_iota(jnp.int32, (1, LANES), 1)
    scale = 1.0 / math.sqrt(HEAD_DIM)
    first = jnp.where(lane < HEAD_DIM, scale, 0.0).astype(jnp.bfloat16)
    second = jnp.where(lane < HEAD_DIM, 0.0, scale).astype(jnp.bfloat16)
    return jnp.concatenate([queries * first, queries * second], axis=0)


def pool_matrix(queries):
    molecule = lax.broadcasted_iota(jnp.int32, (queries // POOL, queries), 0)
    query = lax.broadcasted_iota(jnp.int32, (queries // POOL, queries), 1)
    return jnp.where(query // POOL == molecule, 1.0 / POOL, 0.0).astype(jnp.bfloat16)


def own_heads(mixed, scale):
    count = mixed.shape[1] // 2
    return jnp.concatenate(
        [
            mixed[:HEAD_DIM, :count] * scale[:, :count],
            mixed[HEAD_DIM:LANES, count:] * scale[:, count:],
        ],
        axis=0,
    )


def load(source, target, sem):
    copy = pltpu.make_async_copy(source, target, sem)
    copy.start()
    return copy


def load_chunks(arrays, chunks, sems):
    block = arrays[0][1].shape[1] // chunks
    return [
        [
            load(source.at[:, pl.ds(chunk * block, block)], target.at[:, pl.ds(chunk * block, block)], sems.at[i, chunk])
            for i, (source, target) in enumerate(arrays)
        ]
        for chunk in range(chunks)
    ]


def at(pair):
    return pl.ds(pair * LANES, LANES)


def over_pairs(pairs, stages, lags, before):
    results = {}
    for step in range(pairs + lags[-1]):
        if step < pairs:
            before(step)
        for stage, lag in zip(stages, lags):
            pair = step - lag
            if 0 <= pair < pairs:
                results[pair] = stage(pair, *results.get(pair, ()))


def tops(scores):
    rows = scores.shape[0]
    while rows > 8:
        rows //= 2
        scores = jnp.maximum(scores[:rows], scores[rows:])
    return jnp.max(scores, axis=0, keepdims=True)


def with_ones(values_t):
    return jnp.concatenate([values_t, jnp.ones((16, values_t.shape[1]), jnp.bfloat16)], axis=0)


def three_terms(value):
    high = value.astype(jnp.bfloat16).astype(jnp.float32)
    middle = (value - high).astype(jnp.bfloat16).astype(jnp.float32)
    return [high, middle, value - high - middle]


def early_kernel(
    rows, chunks, offsets_hbm, q_hbm, k_hbm, v_hbm, cotangent_hbm, stashed_hbm,
    sent_ref, early_ref, q_late_ref, k_ref, v_ref, own_ref, other_ref, next_ref, cotangent_ref, stashed_ref,
    offsets_ref, bias, sems, offsets_sem,
):
    half = rows // 2
    head, tail = pl.ds(0, half), pl.ds(half, half)
    offsets_copy = load(offsets_hbm, offsets_ref, offsets_sem.at[0])
    arrays = (
        (k_hbm.at[head], k_ref.at[head]),
        (q_hbm.at[head], sent_ref.at[head]),
        (v_hbm.at[head], v_ref.at[head]),
    )
    copies = load_chunks(arrays, chunks, sems)
    rest = [
        load(k_hbm.at[tail], k_ref.at[tail], offsets_sem.at[1]),
        load(v_hbm.at[tail], v_ref.at[tail], offsets_sem.at[2]),
        load(q_hbm.at[tail], q_late_ref, offsets_sem.at[3]),
        load(cotangent_hbm, cotangent_ref, offsets_sem.at[4]),
        load(stashed_hbm, stashed_ref, offsets_sem.at[5]),
    ]
    start = lax.axis_index("seq") * rows
    pairs = k_ref.shape[1] // LANES

    def arrive(pair):
        per_chunk = pairs // chunks
        if pair % per_chunk == 0:
            for copy in copies[pair // per_chunk]:
                copy.wait()
        if pair == 1:
            offsets_copy.wait()
            bias[...] = mask_bias(offsets_ref, start, start, lambda key, query: key <= query)

    def score(pair):
        scores = dot_nt(k_ref[head, at(pair)], split_heads(sent_ref[head, at(pair)]))
        return scores, with_ones(jnp.transpose(v_ref[head, at(pair)]))

    def top(pair, scores, values_t):
        scores = scores + bias[...]
        return scores, tops(scores), values_t

    def weigh(pair, scores, top, values_t):
        return top, dot_nn(values_t, jnp.exp(scores - top).astype(jnp.bfloat16))

    def finish(pair, top, mixed):
        total = mixed[LANES : LANES + 1]
        early_ref[at(pair), :] = own_heads(mixed, 1.0 / total).astype(jnp.bfloat16)
        lse = top + jnp.log(total)
        terms = three_terms(lse[:, :half]) + three_terms(lse[:, half:])
        terms.append(jnp.zeros((EXTRA - 6, LANES), jnp.float32))
        sent_ref[pl.ds(half, EXTRA), at(pair)] = jnp.concatenate(terms, axis=0).astype(jnp.bfloat16)
        return ()

    over_pairs(pairs, (score, top, weigh, finish), LAGS, arrive)
    own_ref[...] = mask_bias(offsets_ref, start + half, start + half, lambda key, query: key <= query)
    other_ref[...] = mask_bias(offsets_ref, start + half, start, lambda key, query: key > query)
    next_ref[...] = mask_bias(offsets_ref, start + rows, start + half, lambda key, query: key > query)
    for copy in rest:
        copy.wait()


def late_kernel(
    q_ref, k_ref, v_ref, own_bias, other_bias, early_ref, both_ref, own, other
):
    half = q_ref.shape[0]
    key = lax.broadcasted_iota(jnp.int32, own.shape, 0)
    query = lax.broadcasted_iota(jnp.int32, own.shape, 1) % half
    own[...] = jnp.where(key <= query, 1.0, 0.0).astype(jnp.bfloat16)
    other[...] = jnp.where(key <= query, 0.0, 1.0).astype(jnp.bfloat16)
    pooling = pool_matrix(half)
    molecules = half // POOL
    features = early_ref.shape[0]
    both_ref[pl.ds(0, features), :] = early_ref[...]
    pairs = k_ref.shape[1] // LANES
    parts = []

    def score(pair):
        scores = dot_nt(k_ref[:, at(pair)], split_heads(q_ref[:, at(pair)]))
        return scores, with_ones(jnp.transpose(v_ref[:, at(pair)]))

    def top(pair, scores, values_t):
        scores = jnp.maximum(scores[:half] + other_bias[...], scores[half:] + own_bias[...])
        return scores, tops(scores), values_t

    def weigh(pair, scores, top, values_t):
        weights = jnp.exp(scores - top).astype(jnp.bfloat16)
        weights = jnp.concatenate([weights * other[...], weights * own[...]], axis=0)
        return (dot_nn(values_t, weights),)

    def finish(pair, mixed):
        inverse = 1.0 / mixed[LANES : LANES + 1]
        parts.append(own_heads(mixed, inverse).astype(jnp.bfloat16))
        if len(parts) == 4:
            pooled = dot_nt(pooling, jnp.concatenate(parts, axis=0)).astype(jnp.bfloat16)
            for i in range(4):
                place = features + (pair - 3 + i) * molecules
                both_ref[pl.ds(place, molecules), :] = pooled[:, i * LANES : (i + 1) * LANES]
            parts.clear()
        return ()

    over_pairs(pairs, (score, top, weigh, finish), LAGS, lambda pair: None)


def halo_kernel(q_ref, k_ref, v_ref, bias, after_ref, out_ref):
    half = bias.shape[0]
    molecules = half // POOL
    tail = pl.ds(half, half)
    pooling = pool_matrix(half)
    pairs = k_ref.shape[1] // LANES
    parts = []

    def score(pair):
        queries = split_heads(q_ref[pl.ds(0, half), at(pair)])
        scores = dot_nt(k_ref[tail, at(pair)], queries)
        return scores, with_ones(jnp.transpose(v_ref[tail, at(pair)]))

    def top(pair, scores, values_t):
        terms = q_ref[pl.ds(half, EXTRA), at(pair)].astype(jnp.float32)
        lse = jnp.concatenate(
            [terms[0:1] + terms[1:2] + terms[2:3], terms[3:4] + terms[4:5] + terms[5:6]], axis=1
        )
        scores = scores + bias[...]
        return scores, jnp.maximum(tops(scores), lse), lse, values_t

    def weigh(pair, scores, top, lse, values_t):
        mixed = dot_nn(values_t, jnp.exp(scores - top).astype(jnp.bfloat16))
        return mixed, jnp.exp(lse - top)

    def finish(pair, mixed, kept):
        inverse = 1.0 / (mixed[LANES : LANES + 1] + kept)
        parts.append(own_heads(mixed, inverse).astype(jnp.bfloat16))
        if len(parts) == 4:
            pooled = dot_nt(pooling, jnp.concatenate(parts, axis=0)).astype(jnp.bfloat16)
            out_ref[pl.ds(0, molecules), pl.ds((pair - 3) * LANES, 4 * LANES)] = pooled
            parts.clear()
        share = kept * inverse
        high = share.astype(jnp.bfloat16).astype(jnp.float32)
        low = share - high
        shares = [high[:, :half], low[:, :half], high[:, half:], low[:, half:]]
        shares.append(jnp.zeros((EXTRA - 4, LANES), jnp.float32))
        out_ref[pl.ds(molecules, EXTRA), at(pair)] = jnp.concatenate(shares, axis=0).astype(jnp.bfloat16)
        return ()

    over_pairs(pairs, (score, top, weigh, finish), LAGS, lambda pair: None)


def back_kernel(
    slot_ref, cotangent_ref, weight_ref, gain_ref, stashed_ref, after_ref, dinput_ref, term_ref, grad, held_ref
):
    held = stashed_ref[0]
    for i in range(1, stashed_ref.shape[0]):
        held = jnp.where(slot_ref[0:1, 0:1] == i, stashed_ref[i].astype(jnp.float32), held.astype(jnp.float32))
    held_ref[...] = held.astype(jnp.bfloat16)
    features = weight_ref.shape[0]
    block = 512
    for begin in range(0, features, block):
        columns = pl.ds(begin, block)
        grad[:, columns] = dot_nt(cotangent_ref[...], weight_ref[columns, :])
    held = held_ref[...].astype(jnp.float32)
    inv_rms = lax.rsqrt(jnp.sum(held * held, axis=1, keepdims=True) / features + EPS_NORM)
    along = jnp.zeros_like(inv_rms)
    for begin in range(0, features, block):
        columns = pl.ds(begin, block)
        product = grad[:, columns] * (held_ref[:, columns].astype(jnp.float32) * inv_rms)
        term_ref[:, columns] = jnp.sum(product, axis=0, keepdims=True)
        along += jnp.sum(product * gain_ref[:, columns], axis=1, keepdims=True)
    along = along / features
    for begin in range(0, features, block):
        columns = pl.ds(begin, block)
        whitened = held_ref[:, columns].astype(jnp.float32) * inv_rms
        scaled = grad[:, columns] * gain_ref[:, columns]
        dinput_ref[:, columns] = (inv_rms * (scaled - whitened * along)).astype(jnp.bfloat16)


def project_kernel(
    both_ref, halo_ref, gain_ref, weight_ref, term_ref, other_ref, upstream_hbm,
    out_ref, update_ref, passed_hbm, pooled, sem,
):
    passing = load(upstream_hbm, passed_hbm, sem)
    half = both_ref.shape[1]
    features = gain_ref.shape[1]
    molecules = half // POOL
    pooling = pool_matrix(half)
    first = lax.axis_index("seq") == 0
    parts = []
    for pair in range(features // LANES):
        shares = halo_ref[molecules:, at(pair)].astype(jnp.float32)
        share_a = jnp.where(first, 1.0, shares[0:1] + shares[1:2])
        share_b = jnp.where(first, 1.0, shares[2:3] + shares[3:4])
        early = both_ref[at(pair), :].astype(jnp.float32)
        place = pl.ds(features + pair * molecules, molecules)
        pooled[pl.ds(molecules, molecules), at(pair)] = both_ref[place, :]
        parts += [early[:HEAD_DIM] * share_a, early[HEAD_DIM:] * share_b]
        if len(parts) == 8:
            columns = pl.ds((pair - 3) * LANES, 4 * LANES)
            mean = dot_nt(pooling, jnp.concatenate(parts, axis=0).astype(jnp.bfloat16))
            arrived = halo_ref[:molecules, columns].astype(jnp.float32)
            pooled[pl.ds(0, molecules), columns] = (mean + arrived).astype(jnp.bfloat16)
            parts = []
    arrived = pooled[...].astype(jnp.float32)
    mean = jnp.sum(arrived * arrived, axis=1, keepdims=True) / features
    normed = (arrived * lax.rsqrt(mean + EPS_NORM) * gain_ref[...]).astype(jnp.bfloat16)
    out_ref[...] = dot_nn(normed, weight_ref[...]).astype(jnp.bfloat16)
    total = term_ref[...] + other_ref[...]
    mean = jnp.sum(total * total, axis=1, keepdims=True) / features
    update_ref[...] = total / jnp.sqrt(mean + EPS_STEP)
    passing.wait()


def cost(flops, read, exps=0):
    return pl.CostEstimate(flops=flops, bytes_accessed=read, transcendentals=exps)


SMEM = pl.BlockSpec(memory_space=pltpu.SMEM)
HBM = pl.BlockSpec(memory_space=pltpu.HBM)
ANY = pl.BlockSpec(memory_space=pl.ANY)
VMEM = pl.BlockSpec(memory_space=pltpu.VMEM)


def in_hbm(*arrays):
    return [pltpu.with_memory_space_constraint(x, pltpu.HBM) for x in arrays]


def params():
    return pltpu.CompilerParams(vmem_limit_bytes=24 * 2**20)


def attend_early(queries, keys, values, offsets, cotangent, stashed, chunks):
    rows, width = queries.shape
    half = rows // 2
    masks = [jax.ShapeDtypeStruct((half, 2 * half), jnp.float32)] * 3
    return pl.pallas_call(
        functools.partial(early_kernel, rows, chunks),
        in_specs=[HBM] * 6,
        out_specs=[VMEM] * 10,
        out_shape=[
            jax.ShapeDtypeStruct((half + EXTRA, width), jnp.bfloat16),
            jax.ShapeDtypeStruct((width, half), jnp.bfloat16),
            jax.ShapeDtypeStruct((half, width), jnp.bfloat16),
            jax.ShapeDtypeStruct((rows, width), jnp.bfloat16),
            jax.ShapeDtypeStruct((rows, width), jnp.bfloat16),
        ]
        + masks
        + [
            jax.ShapeDtypeStruct(cotangent.shape, cotangent.dtype),
            jax.ShapeDtypeStruct(stashed.shape, stashed.dtype),
        ],
        scratch_shapes=[
            pltpu.SMEM(offsets.shape, jnp.int32),
            pltpu.VMEM((half, 2 * half), jnp.float32),
            pltpu.SemaphoreType.DMA((3, chunks)),
            pltpu.SemaphoreType.DMA((6,)),
        ],
        cost_estimate=cost(4 * half * half * width, 6 * rows * width, half * half * width // 64),
        compiler_params=params(),
        name="attend_early",
    )(*in_hbm(offsets, queries, keys, values, cotangent, stashed))


def attend_late(queries, keys, values, own_bias, other_bias, early):
    half, width = queries.shape
    return pl.pallas_call(
        late_kernel,
        in_specs=[VMEM] * 6,
        out_specs=VMEM,
        out_shape=jax.ShapeDtypeStruct((width + width // POOL, half), jnp.bfloat16),
        scratch_shapes=[
            pltpu.VMEM((half, 2 * half), jnp.bfloat16),
            pltpu.VMEM((half, 2 * half), jnp.bfloat16),
        ],
        cost_estimate=cost(8 * half * half * width, 10 * half * width, half * half * width // 64),
        compiler_params=params(),
        name="attend_late",
    )(queries, keys, values, own_bias, other_bias, early)


def attend_halo(sent, keys, values, bias, after):
    half, width = bias.shape[0], keys.shape[1]
    return pl.pallas_call(
        halo_kernel,
        in_specs=[VMEM] * 4 + [ANY],
        out_specs=VMEM,
        out_shape=jax.ShapeDtypeStruct((half // POOL + EXTRA, width), jnp.bfloat16),
        cost_estimate=cost(4 * half * half * width, 6 * half * width, half * half * width // 64),
        compiler_params=params(),
        name="attend_halo",
    )(sent, keys, values, bias, after)


def backward(slot, cotangent, weight, gain, stashed, after):
    rows, width = stashed.shape[1:]
    depth = weight.shape[1]
    return pl.pallas_call(
        back_kernel,
        in_specs=[VMEM] * 5 + [ANY],
        out_specs=[VMEM] * 2,
        scratch_shapes=[
            pltpu.VMEM((rows, width), jnp.float32),
            pltpu.VMEM((rows, width), jnp.bfloat16),
        ],
        out_shape=[
            jax.ShapeDtypeStruct((rows, width), jnp.bfloat16),
            jax.ShapeDtypeStruct((1, width), jnp.float32),
        ],
        cost_estimate=cost(2 * rows * width * depth, 2 * width * depth),
        compiler_params=params(),
        name="backward",
    )(slot, cotangent, weight, gain, stashed, after)


def project(both, halo, gain, weight, term, other, upstream):
    rows = upstream.shape[0]
    width, depth = weight.shape
    return pl.pallas_call(
        project_kernel,
        in_specs=[VMEM] * 6 + [ANY],
        out_specs=[VMEM, VMEM, HBM],
        out_shape=[
            jax.ShapeDtypeStruct((rows, depth), jnp.bfloat16),
            jax.ShapeDtypeStruct((1, width), jnp.float32),
            jax.ShapeDtypeStruct(upstream.shape, upstream.dtype),
        ],
        scratch_shapes=[pltpu.VMEM((rows, width), jnp.bfloat16), pltpu.SemaphoreType.DMA],
        cost_estimate=cost(2 * rows * width * depth, 2 * width * depth),
        compiler_params=params(),
        name="project",
    )(both, halo, gain, weight, term, other, upstream)


def swapped(value, axis, distance):
    return lax.ppermute(value, axis, [(i, i ^ distance) for i in range(lax.axis_size(axis))])


def sum_rounds():
    rounds = []
    for axis in ("seq", "rep"):
        count = lax.axis_size(axis)
        if count & (count - 1):
            return []
        rounds += [(axis, 1 << i) for i in range(count.bit_length() - 1)]
    return rounds if len(rounds) == 3 else []


def onward(value):
    sections, shards = lax.axis_size("section"), lax.axis_size("seq")
    route = [
        (s * shards + k, (s + 1) % sections * shards + k + 1)
        for s in range(sections)
        for k in range(shards - 1)
    ]
    return lax.ppermute(value, ("section", "seq"), route)


def local(queries, keys, values, doc_starts, weight, gain, stashed, cotangent, slot):
    queries, keys, values, offsets = queries[0, 0], keys[0, 0], values[0, 0], doc_starts[0]
    rounds = sum_rounds()

    def partner(term, index):
        return swapped(term, *rounds[index]) if rounds else jnp.zeros_like(term)

    sent, early, q_late, keys, values, own_bias, other_bias, next_bias, cotangent, stashed = (
        attend_early(queries, keys, values, offsets, cotangent[0, 0], stashed[0, 0], 4)
    )
    arrived = shifted(sent, "seq", -1)
    both = attend_late(q_late, keys, values, own_bias, other_bias, early)
    slot = jnp.broadcast_to(slot, (1, LANES))
    dinput, term = backward(slot, cotangent, weight[0], gain, stashed, both)
    both = passed_along(both, "section", 1)
    upstream = passed_along(dinput, "section", -1)
    term = term if rounds else lax.psum(term, ("rep", "seq"))
    term = term + partner(term, 0)
    halo = onward(attend_halo(arrived, keys, values, next_bias, term))
    term = term + partner(term, 1)
    mol_keys, update, upstream = project(
        both, halo, gain, weight[0], term, partner(term, 2), upstream
    )
    return mol_keys[None, None], upstream[None, None], update


def solution(mesh):
    in_specs = (
        P("rep", "section", "seq", None),
        P("rep", "section", "seq", None),
        P("rep", "section", "seq", None),
        P("rep", "section", None),
        P("section", None, None),
        P("section", None),
        P("rep", "section", None, "seq", None),
        P("rep", "section", "seq", None),
        P("rep", "section"),
    )
    out_specs = (
        P("rep", "section", "seq", None),
        P("rep", "section", "seq", None),
        P("section", None),
    )
    return jax.shard_map(local, mesh=mesh, in_specs=in_specs, out_specs=out_specs, check_vma=False)
```

```python
import functools
import math

import jax
import jax.numpy as jnp
from jax import lax
from jax.experimental import pallas as pl
from jax.experimental.pallas import tpu as pltpu
from jax.sharding import PartitionSpec as P

HEAD_DIM = 64
POOL = 4
WINDOW = 128
LANES = 128
EPS_NORM = 1e-05
EPS_STEP = 1e-06
MASKED = -1e30
LAGS = (0, 2, 3, 4)
EXTRA = 8

NT = (((1,), (1,)), ((), ()))


def dot_nt(a, b):
    return lax.dot_general(a, b, NT, preferred_element_type=jnp.float32)


def dot_nn(a, b):
    return jnp.dot(a, b, preferred_element_type=jnp.float32)


def shifted(value, axis, steps):
    count = lax.axis_size(axis)
    first, last = max(0, -steps), min(count, count - steps)
    return lax.ppermute(value, axis, [(i, i + steps) for i in range(first, last)])


def passed_along(value, axis, steps):
    count = lax.axis_size(axis)
    return lax.ppermute(value, axis, [(i, (i + steps) % count) for i in range(count)])


def earliest_key(offsets_ref, query_pos):
    start = jnp.zeros_like(query_pos)
    for d in range(offsets_ref.shape[1]):
        offset = offsets_ref[0, d]
        start = jnp.where(query_pos >= offset, offset, start)
    return jnp.maximum(start, query_pos - (WINDOW - 1))


def mask_bias(offsets_ref, query_start, key_start, keep):
    key = lax.broadcasted_iota(jnp.int32, (WINDOW, 2 * WINDOW), 0)
    query = lax.broadcasted_iota(jnp.int32, (WINDOW, 2 * WINDOW), 1) % WINDOW
    lane = lax.broadcasted_iota(jnp.int32, (1, 2 * WINDOW), 1) % WINDOW
    lowest = earliest_key(offsets_ref, query_start + lane)
    allowed = (key_start + key >= lowest) & keep(key, query)
    return jnp.where(allowed, 0.0, MASKED).astype(jnp.float32)


def split_heads(queries):
    lane = lax.broadcasted_iota(jnp.int32, (1, LANES), 1)
    scale = 1.0 / math.sqrt(HEAD_DIM)
    first = jnp.where(lane < HEAD_DIM, scale, 0.0).astype(jnp.bfloat16)
    second = jnp.where(lane < HEAD_DIM, 0.0, scale).astype(jnp.bfloat16)
    return jnp.concatenate([queries * first, queries * second], axis=0)


def pool_matrix(queries):
    molecule = lax.broadcasted_iota(jnp.int32, (queries // POOL, queries), 0)
    query = lax.broadcasted_iota(jnp.int32, (queries // POOL, queries), 1)
    return jnp.where(query // POOL == molecule, 1.0 / POOL, 0.0).astype(jnp.bfloat16)


def own_heads(mixed, scale):
    count = mixed.shape[1] // 2
    return jnp.concatenate(
        [
            mixed[:HEAD_DIM, :count] * scale[:, :count],
            mixed[HEAD_DIM:LANES, count:] * scale[:, count:],
        ],
        axis=0,
    )


def load(source, target, sem):
    copy = pltpu.make_async_copy(source, target, sem)
    copy.start()
    return copy


def load_chunks(arrays, chunks, sems):
    block = arrays[0][1].shape[1] // chunks
    return [
        [
            load(source.at[:, pl.ds(chunk * block, block)], target.at[:, pl.ds(chunk * block, block)], sems.at[i, chunk])
            for i, (source, target) in enumerate(arrays)
        ]
        for chunk in range(chunks)
    ]


def at(pair):
    return pl.ds(pair * LANES, LANES)


def over_pairs(pairs, stages, lags, before):
    results = {}
    for step in range(pairs + lags[-1]):
        if step < pairs:
            before(step)
        for stage, lag in zip(stages, lags):
            pair = step - lag
            if 0 <= pair < pairs:
                results[pair] = stage(pair, *results.get(pair, ()))


def tops(scores):
    rows = scores.shape[0]
    while rows > 8:
        rows //= 2
        scores = jnp.maximum(scores[:rows], scores[rows:])
    return jnp.max(scores, axis=0, keepdims=True)


def with_ones(values_t):
    return jnp.concatenate([values_t, jnp.ones((16, values_t.shape[1]), jnp.bfloat16)], axis=0)


def three_terms(value):
    high = value.astype(jnp.bfloat16).astype(jnp.float32)
    middle = (value - high).astype(jnp.bfloat16).astype(jnp.float32)
    return [high, middle, value - high - middle]


def early_kernel(
    rows, chunks, offsets_hbm, q_hbm, k_hbm, v_hbm, cotangent_hbm, stashed_hbm,
    sent_ref, early_ref, q_own_ref, q_late_ref, k_ref, v_ref, forward_ref,
    first_ref, own_ref, other_ref, next_ref, last_ref, cotangent_ref, stashed_ref,
    offsets_ref, sems, rest_sems,
):
    half = rows // 2
    head, tail = pl.ds(0, half), pl.ds(half, half)
    width = sent_ref.shape[1]
    back, kept = pl.ds(0, width), pl.ds(width, k_ref.shape[1] - width)
    offsets_copy = load(offsets_hbm, offsets_ref, rest_sems.at[0])
    arrays = (
        (k_hbm.at[head, back], k_ref.at[head, back]),
        (q_hbm.at[head, back], sent_ref.at[head]),
        (v_hbm.at[head, back], v_ref.at[head, back]),
    )
    copies = load_chunks(arrays, chunks, sems)
    rest = [
        (k_hbm.at[tail, kept], forward_ref.at[head]),
        (v_hbm.at[tail, kept], forward_ref.at[tail]),
        (k_hbm.at[tail], k_ref.at[tail]),
        (v_hbm.at[tail], v_ref.at[tail]),
        (q_hbm.at[tail], q_late_ref),
        (k_hbm.at[head, kept], k_ref.at[head, kept]),
        (v_hbm.at[head, kept], v_ref.at[head, kept]),
        (q_hbm.at[head, kept], q_own_ref),
        (cotangent_hbm, cotangent_ref),
        (stashed_hbm, stashed_ref),
    ]
    rest = [load(source, target, rest_sems.at[i + 1]) for i, (source, target) in enumerate(rest)]
    start = lax.axis_index("seq") * rows
    pairs = width // LANES

    def arrive(pair):
        per_chunk = pairs // chunks
        if pair % per_chunk == 0:
            for copy in copies[pair // per_chunk]:
                copy.wait()
        if pair == 1:
            offsets_copy.wait()
            first_ref[...] = mask_bias(offsets_ref, start, start, lambda key, query: key <= query)

    def score(pair):
        scores = dot_nt(k_ref[head, at(pair)], split_heads(sent_ref[head, at(pair)]))
        return scores, with_ones(jnp.transpose(v_ref[head, at(pair)]))

    def top(pair, scores, values_t):
        scores = scores + first_ref[...]
        return scores, tops(scores), values_t

    def weigh(pair, scores, top, values_t):
        return top, dot_nn(values_t, jnp.exp(scores - top).astype(jnp.bfloat16))

    def finish(pair, top, mixed):
        total = mixed[LANES : LANES + 1]
        early_ref[at(pair), :] = own_heads(mixed, 1.0 / total).astype(jnp.bfloat16)
        lse = top + jnp.log(total)
        terms = three_terms(lse[:, :half]) + three_terms(lse[:, half:])
        terms.append(jnp.zeros((EXTRA - 6, LANES), jnp.float32))
        sent_ref[pl.ds(half, EXTRA), at(pair)] = jnp.concatenate(terms, axis=0).astype(jnp.bfloat16)
        return ()

    over_pairs(pairs, (score, top, weigh, finish), LAGS, arrive)
    own_ref[...] = mask_bias(offsets_ref, start + half, start + half, lambda key, query: key <= query)
    other_ref[...] = mask_bias(offsets_ref, start + half, start, lambda key, query: key > query)
    next_ref[...] = mask_bias(offsets_ref, start + rows, start + half, lambda key, query: key > query)
    last_ref[...] = mask_bias(offsets_ref, start, start - half, lambda key, query: key > query)
    for copy in rest:
        copy.wait()


def window_pairs(pairs, q_ref, blocks, biases, shares, emit):
    half = q_ref.shape[0]
    before_bias, own_bias = biases
    before, own = shares
    key = lax.broadcasted_iota(jnp.int32, own.shape, 0)
    query = lax.broadcasted_iota(jnp.int32, own.shape, 1) % half
    own[...] = jnp.where(key <= query, 1.0, 0.0).astype(jnp.bfloat16)
    before[...] = jnp.where(key <= query, 0.0, 1.0).astype(jnp.bfloat16)
    pooling = pool_matrix(half)
    parts = []

    def score(pair):
        keys, values = blocks(pair)
        return dot_nt(keys, split_heads(q_ref[:, at(pair)])), with_ones(jnp.transpose(values))

    def top(pair, scores, values_t):
        scores = jnp.maximum(scores[:half] + before_bias[...], scores[half:] + own_bias[...])
        return scores, tops(scores), values_t

    def weigh(pair, scores, top, values_t):
        weights = jnp.exp(scores - top).astype(jnp.bfloat16)
        weights = jnp.concatenate([weights * before[...], weights * own[...]], axis=0)
        return (dot_nn(values_t, weights),)

    def finish(pair, mixed):
        inverse = 1.0 / mixed[LANES : LANES + 1]
        parts.append(own_heads(mixed, inverse).astype(jnp.bfloat16))
        if len(parts) == 4:
            emit(pair, dot_nt(pooling, jnp.concatenate(parts, axis=0)).astype(jnp.bfloat16))
            parts.clear()
        return ()

    over_pairs(pairs, (score, top, weigh, finish), LAGS, lambda pair: None)


def late_kernel(q_ref, k_ref, v_ref, own_bias, other_bias, early_ref, both_ref, own, other):
    half = q_ref.shape[0]
    molecules = half // POOL
    features = early_ref.shape[0]
    both_ref[pl.ds(0, features), :] = early_ref[...]

    def emit(pair, pooled):
        for i in range(4):
            place = features + (pair - 3 + i) * molecules
            both_ref[pl.ds(place, molecules), :] = pooled[:, i * LANES : (i + 1) * LANES]

    window_pairs(
        q_ref.shape[1] // LANES,
        q_ref,
        lambda pair: (k_ref[:, at(pair)], v_ref[:, at(pair)]),
        (other_bias, own_bias),
        (other, own),
        emit,
    )


def kept_kernel(
    q_ref, k_ref, v_ref, arrived_ref, first_bias, last_bias, after_ref, out_ref, own, other
):
    half = q_ref.shape[0]
    head, tail = pl.ds(0, half), pl.ds(half, half)
    begin = k_ref.shape[1] - q_ref.shape[1]

    def blocks(pair):
        columns = pl.ds(begin + pair * LANES, LANES)
        return (
            jnp.concatenate([arrived_ref[head, at(pair)], k_ref[head, columns]], axis=0),
            jnp.concatenate([arrived_ref[tail, at(pair)], v_ref[head, columns]], axis=0),
        )

    def emit(pair, pooled):
        out_ref[:, pl.ds((pair - 3) * LANES, 4 * LANES)] = pooled

    pairs = q_ref.shape[1] // LANES
    window_pairs(pairs, q_ref, blocks, (last_bias, first_bias), (other, own), emit)


def halo_kernel(q_ref, k_ref, v_ref, bias, after_ref, out_ref):
    half = bias.shape[0]
    molecules = half // POOL
    tail = pl.ds(half, half)
    pooling = pool_matrix(half)
    pairs = q_ref.shape[1] // LANES
    parts = []

    def score(pair):
        queries = split_heads(q_ref[pl.ds(0, half), at(pair)])
        scores = dot_nt(k_ref[tail, at(pair)], queries)
        return scores, with_ones(jnp.transpose(v_ref[tail, at(pair)]))

    def top(pair, scores, values_t):
        terms = q_ref[pl.ds(half, EXTRA), at(pair)].astype(jnp.float32)
        lse = jnp.concatenate(
            [terms[0:1] + terms[1:2] + terms[2:3], terms[3:4] + terms[4:5] + terms[5:6]], axis=1
        )
        scores = scores + bias[...]
        return scores, jnp.maximum(tops(scores), lse), lse, values_t

    def weigh(pair, scores, top, lse, values_t):
        mixed = dot_nn(values_t, jnp.exp(scores - top).astype(jnp.bfloat16))
        return mixed, jnp.exp(lse - top)

    def finish(pair, mixed, kept):
        inverse = 1.0 / (mixed[LANES : LANES + 1] + kept)
        parts.append(own_heads(mixed, inverse).astype(jnp.bfloat16))
        if len(parts) == 4:
            pooled = dot_nt(pooling, jnp.concatenate(parts, axis=0)).astype(jnp.bfloat16)
            out_ref[pl.ds(0, molecules), pl.ds((pair - 3) * LANES, 4 * LANES)] = pooled
            parts.clear()
        share = kept * inverse
        high = share.astype(jnp.bfloat16).astype(jnp.float32)
        low = share - high
        shares = [high[:, :half], low[:, :half], high[:, half:], low[:, half:]]
        shares.append(jnp.zeros((EXTRA - 4, LANES), jnp.float32))
        out_ref[pl.ds(molecules, EXTRA), at(pair)] = jnp.concatenate(shares, axis=0).astype(jnp.bfloat16)
        return ()

    over_pairs(pairs, (score, top, weigh, finish), LAGS, lambda pair: None)


def back_kernel(
    slot_ref, cotangent_ref, weight_ref, gain_ref, stashed_ref, after_ref, dinput_ref, term_ref, grad, held_ref
):
    held = stashed_ref[0]
    for i in range(1, stashed_ref.shape[0]):
        held = jnp.where(slot_ref[0:1, 0:1] == i, stashed_ref[i].astype(jnp.float32), held.astype(jnp.float32))
    held_ref[...] = held.astype(jnp.bfloat16)
    features = weight_ref.shape[0]
    block = 512
    for begin in range(0, features, block):
        columns = pl.ds(begin, block)
        grad[:, columns] = dot_nt(cotangent_ref[...], weight_ref[columns, :])
    held = held_ref[...].astype(jnp.float32)
    inv_rms = lax.rsqrt(jnp.sum(held * held, axis=1, keepdims=True) / features + EPS_NORM)
    along = jnp.zeros_like(inv_rms)
    for begin in range(0, features, block):
        columns = pl.ds(begin, block)
        product = grad[:, columns] * (held_ref[:, columns].astype(jnp.float32) * inv_rms)
        term_ref[:, columns] = jnp.sum(product, axis=0, keepdims=True)
        along += jnp.sum(product * gain_ref[:, columns], axis=1, keepdims=True)
    along = along / features
    for begin in range(0, features, block):
        columns = pl.ds(begin, block)
        whitened = held_ref[:, columns].astype(jnp.float32) * inv_rms
        scaled = grad[:, columns] * gain_ref[:, columns]
        dinput_ref[:, columns] = (inv_rms * (scaled - whitened * along)).astype(jnp.bfloat16)


def project_kernel(
    both_ref, halo_ref, kept_ref, gain_ref, weight_ref, term_ref, other_ref, upstream_hbm,
    out_ref, update_ref, passed_hbm, pooled, sem,
):
    passing = load(upstream_hbm, passed_hbm, sem)
    half = both_ref.shape[1]
    features = gain_ref.shape[1]
    molecules = half // POOL
    pooling = pool_matrix(half)
    first = lax.axis_index("seq") == 0
    parts = []
    width = halo_ref.shape[1]
    for pair in range(features // LANES):
        place = pl.ds(width + pair * molecules, molecules)
        pooled[pl.ds(molecules, molecules), at(pair)] = both_ref[place, :]
        if pair * LANES >= width:
            continue
        shares = halo_ref[molecules:, at(pair)].astype(jnp.float32)
        share_a = jnp.where(first, 1.0, shares[0:1] + shares[1:2])
        share_b = jnp.where(first, 1.0, shares[2:3] + shares[3:4])
        early = both_ref[at(pair), :].astype(jnp.float32)
        parts += [early[:HEAD_DIM] * share_a, early[HEAD_DIM:] * share_b]
        if len(parts) == 8:
            columns = pl.ds((pair - 3) * LANES, 4 * LANES)
            mean = dot_nt(pooling, jnp.concatenate(parts, axis=0).astype(jnp.bfloat16))
            arrived = halo_ref[:molecules, columns].astype(jnp.float32)
            pooled[pl.ds(0, molecules), columns] = (mean + arrived).astype(jnp.bfloat16)
            parts = []
    pooled[pl.ds(0, molecules), pl.ds(width, features - width)] = kept_ref[...]
    arrived = pooled[...].astype(jnp.float32)
    mean = jnp.sum(arrived * arrived, axis=1, keepdims=True) / features
    normed = (arrived * lax.rsqrt(mean + EPS_NORM) * gain_ref[...]).astype(jnp.bfloat16)
    out_ref[...] = dot_nn(normed, weight_ref[...]).astype(jnp.bfloat16)
    total = term_ref[...] + other_ref[...]
    mean = jnp.sum(total * total, axis=1, keepdims=True) / features
    update_ref[...] = total / jnp.sqrt(mean + EPS_STEP)
    passing.wait()


def cost(flops, read, exps=0):
    return pl.CostEstimate(flops=flops, bytes_accessed=read, transcendentals=exps)


SMEM = pl.BlockSpec(memory_space=pltpu.SMEM)
HBM = pl.BlockSpec(memory_space=pltpu.HBM)
ANY = pl.BlockSpec(memory_space=pl.ANY)
VMEM = pl.BlockSpec(memory_space=pltpu.VMEM)


def in_hbm(*arrays):
    return [pltpu.with_memory_space_constraint(x, pltpu.HBM) for x in arrays]


def params():
    return pltpu.CompilerParams(vmem_limit_bytes=24 * 2**20)


def attend_early(queries, keys, values, offsets, cotangent, stashed, kept):
    rows, width = queries.shape
    half, back = rows // 2, width - kept
    chunks = back // (4 * LANES)
    bf16 = lambda *shape: jax.ShapeDtypeStruct(shape, jnp.bfloat16)
    return pl.pallas_call(
        functools.partial(early_kernel, rows, chunks),
        in_specs=[HBM] * 6,
        out_specs=[VMEM] * 14,
        out_shape=[
            bf16(half + EXTRA, back),
            bf16(back, half),
            bf16(half, kept),
            bf16(half, width),
            bf16(rows, width),
            bf16(rows, width),
            bf16(rows, kept),
        ]
        + [jax.ShapeDtypeStruct((half, 2 * half), jnp.float32)] * 5
        + [bf16(*cotangent.shape), bf16(*stashed.shape)],
        scratch_shapes=[
            pltpu.SMEM(offsets.shape, jnp.int32),
            pltpu.SemaphoreType.DMA((3, chunks)),
            pltpu.SemaphoreType.DMA((11,)),
        ],
        cost_estimate=cost(4 * half * half * back, 6 * rows * width, half * half * back // 64),
        compiler_params=params(),
        name="attend_early",
    )(*in_hbm(offsets, queries, keys, values, cotangent, stashed))


def share_masks(half):
    return [pltpu.VMEM((half, 2 * half), jnp.bfloat16)] * 2


def attend_late(queries, keys, values, own_bias, other_bias, early):
    half, width = queries.shape
    return pl.pallas_call(
        late_kernel,
        in_specs=[VMEM] * 6,
        out_specs=VMEM,
        out_shape=jax.ShapeDtypeStruct((early.shape[0] + width // POOL, half), jnp.bfloat16),
        scratch_shapes=share_masks(half),
        cost_estimate=cost(8 * half * half * width, 10 * half * width, half * half * width // 64),
        compiler_params=params(),
        name="attend_late",
    )(queries, keys, values, own_bias, other_bias, early)


def attend_kept(queries, keys, values, arrived, first_bias, last_bias, after):
    half, width = queries.shape
    return pl.pallas_call(
        kept_kernel,
        in_specs=[VMEM] * 6 + [ANY],
        out_specs=VMEM,
        out_shape=jax.ShapeDtypeStruct((half // POOL, width), jnp.bfloat16),
        scratch_shapes=share_masks(half),
        cost_estimate=cost(8 * half * half * width, 10 * half * width, half * half * width // 64),
        compiler_params=params(),
        name="attend_kept",
    )(queries, keys, values, arrived, first_bias, last_bias, after)


def attend_halo(sent, keys, values, bias, after):
    half, width = bias.shape[0], sent.shape[1]
    return pl.pallas_call(
        halo_kernel,
        in_specs=[VMEM] * 4 + [ANY],
        out_specs=VMEM,
        out_shape=jax.ShapeDtypeStruct((half // POOL + EXTRA, width), jnp.bfloat16),
        cost_estimate=cost(4 * half * half * width, 6 * half * width, half * half * width // 64),
        compiler_params=params(),
        name="attend_halo",
    )(sent, keys, values, bias, after)


def backward(slot, cotangent, weight, gain, stashed, after):
    rows, width = stashed.shape[1:]
    depth = weight.shape[1]
    return pl.pallas_call(
        back_kernel,
        in_specs=[VMEM] * 5 + [ANY],
        out_specs=[VMEM] * 2,
        scratch_shapes=[
            pltpu.VMEM((rows, width), jnp.float32),
            pltpu.VMEM((rows, width), jnp.bfloat16),
        ],
        out_shape=[
            jax.ShapeDtypeStruct((rows, width), jnp.bfloat16),
            jax.ShapeDtypeStruct((1, width), jnp.float32),
        ],
        cost_estimate=cost(2 * rows * width * depth, 2 * width * depth),
        compiler_params=params(),
        name="backward",
    )(slot, cotangent, weight, gain, stashed, after)


def project(both, halo, kept, gain, weight, term, other, upstream):
    rows = upstream.shape[0]
    width, depth = weight.shape
    return pl.pallas_call(
        project_kernel,
        in_specs=[VMEM] * 7 + [ANY],
        out_specs=[VMEM, VMEM, HBM],
        out_shape=[
            jax.ShapeDtypeStruct((rows, depth), jnp.bfloat16),
            jax.ShapeDtypeStruct((1, width), jnp.float32),
            jax.ShapeDtypeStruct(upstream.shape, upstream.dtype),
        ],
        scratch_shapes=[pltpu.VMEM((rows, width), jnp.bfloat16), pltpu.SemaphoreType.DMA],
        cost_estimate=cost(2 * rows * width * depth, 2 * width * depth),
        compiler_params=params(),
        name="project",
    )(both, halo, kept, gain, weight, term, other, upstream)


def swapped(value, axis, distance):
    return lax.ppermute(value, axis, [(i, i ^ distance) for i in range(lax.axis_size(axis))])


def sum_rounds():
    rounds = []
    for axis in ("seq", "rep"):
        count = lax.axis_size(axis)
        if count & (count - 1):
            return []
        rounds += [(axis, 1 << i) for i in range(count.bit_length() - 1)]
    return rounds if len(rounds) == 3 else []


def onward(value):
    sections, shards = lax.axis_size("section"), lax.axis_size("seq")
    route = [
        (s * shards + k, (s + 1) % sections * shards + k + 1)
        for s in range(sections)
        for k in range(shards - 1)
    ]
    return lax.ppermute(value, ("section", "seq"), route)


def local(queries, keys, values, doc_starts, weight, gain, stashed, cotangent, slot):
    queries, keys, values, offsets = queries[0, 0], keys[0, 0], values[0, 0], doc_starts[0]
    rounds = sum_rounds()

    def partner(term, index):
        return swapped(term, *rounds[index]) if rounds else jnp.zeros_like(term)

    kept = queries.shape[1] // LANES // 4 * LANES
    sent, early, q_own, q_late, keys, values, forward, *rest = attend_early(
        queries, keys, values, offsets, cotangent[0, 0], stashed[0, 0], kept
    )
    first_bias, own_bias, other_bias, next_bias, last_bias, cotangent, stashed = rest
    arrived = shifted(sent, "seq", -1)
    forward = shifted(forward, "seq", 1)
    both = attend_late(q_late, keys, values, own_bias, other_bias, early)
    slot = jnp.broadcast_to(slot, (1, LANES))
    dinput, term = backward(slot, cotangent, weight[0], gain, stashed, both)
    both = passed_along(both, "section", 1)
    upstream = passed_along(dinput, "section", -1)
    term = term if rounds else lax.psum(term, ("rep", "seq"))
    term = term + partner(term, 0)
    halo = attend_halo(arrived, keys, values, next_bias, term)
    own = attend_kept(q_own, keys, values, forward, first_bias, last_bias, halo)
    halo = onward(halo)
    own = passed_along(own, "section", 1)
    term = term + partner(term, 1)
    mol_keys, update, upstream = project(
        both, halo, own, gain, weight[0], term, partner(term, 2), upstream
    )
    return mol_keys[None, None], upstream[None, None], update


def solution(mesh):
    in_specs = (
        P("rep", "section", "seq", None),
        P("rep", "section", "seq", None),
        P("rep", "section", "seq", None),
        P("rep", "section", None),
        P("section", None, None),
        P("section", None),
        P("rep", "section", None, "seq", None),
        P("rep", "section", "seq", None),
        P("rep", "section"),
    )
    out_specs = (
        P("rep", "section", "seq", None),
        P("rep", "section", "seq", None),
        P("section", None),
    )
    return jax.shard_map(local, mesh=mesh, in_specs=in_specs, out_specs=out_specs, check_vma=False)
```

```python
import functools
import math

import jax
import jax.numpy as jnp
from jax import lax
from jax.experimental import pallas as pl
from jax.experimental.pallas import tpu as pltpu
from jax.sharding import PartitionSpec as P

HEAD_DIM = 64
POOL = 4
WINDOW = 128
LANES = 128
EPS_NORM = 1e-05
EPS_STEP = 1e-06
MASKED = -1e30
LAGS = (0, 2, 3, 4)
EXTRA = 8

NT = (((1,), (1,)), ((), ()))


def dot_nt(a, b):
    return lax.dot_general(a, b, NT, preferred_element_type=jnp.float32)


def dot_nn(a, b):
    return jnp.dot(a, b, preferred_element_type=jnp.float32)


def shifted(value, axis, steps):
    count = lax.axis_size(axis)
    first, last = max(0, -steps), min(count, count - steps)
    return lax.ppermute(value, axis, [(i, i + steps) for i in range(first, last)])


def passed_along(value, axis, steps):
    count = lax.axis_size(axis)
    return lax.ppermute(value, axis, [(i, (i + steps) % count) for i in range(count)])


def earliest_key(offsets_ref, query_pos):
    start = jnp.zeros_like(query_pos)
    for d in range(offsets_ref.shape[1]):
        offset = offsets_ref[0, d]
        start = jnp.where(query_pos >= offset, offset, start)
    return jnp.maximum(start, query_pos - (WINDOW - 1))


def mask_bias(offsets_ref, query_start, key_start, keep):
    key = lax.broadcasted_iota(jnp.int32, (WINDOW, 2 * WINDOW), 0)
    query = lax.broadcasted_iota(jnp.int32, (WINDOW, 2 * WINDOW), 1) % WINDOW
    lane = lax.broadcasted_iota(jnp.int32, (1, 2 * WINDOW), 1) % WINDOW
    lowest = earliest_key(offsets_ref, query_start + lane)
    allowed = (key_start + key >= lowest) & keep(key, query)
    return jnp.where(allowed, 0.0, MASKED).astype(jnp.float32)


def split_heads(queries):
    lane = lax.broadcasted_iota(jnp.int32, (1, LANES), 1)
    scale = 1.0 / math.sqrt(HEAD_DIM)
    first = jnp.where(lane < HEAD_DIM, scale, 0.0).astype(jnp.bfloat16)
    second = jnp.where(lane < HEAD_DIM, 0.0, scale).astype(jnp.bfloat16)
    return jnp.concatenate([queries * first, queries * second], axis=0)


def pool_matrix(queries):
    molecule = lax.broadcasted_iota(jnp.int32, (queries // POOL, queries), 0)
    query = lax.broadcasted_iota(jnp.int32, (queries // POOL, queries), 1)
    return jnp.where(query // POOL == molecule, 1.0 / POOL, 0.0).astype(jnp.bfloat16)


def own_heads(mixed, scale):
    count = mixed.shape[1] // 2
    return jnp.concatenate(
        [
            mixed[:HEAD_DIM, :count] * scale[:, :count],
            mixed[HEAD_DIM:LANES, count:] * scale[:, count:],
        ],
        axis=0,
    )


def load(source, target, sem):
    copy = pltpu.make_async_copy(source, target, sem)
    copy.start()
    return copy


def load_chunks(arrays, chunks, sems):
    block = arrays[0][1].shape[1] // chunks
    return [
        [
            load(source.at[:, pl.ds(chunk * block, block)], target.at[:, pl.ds(chunk * block, block)], sems.at[i, chunk])
            for i, (source, target) in enumerate(arrays)
        ]
        for chunk in range(chunks)
    ]


def at(pair):
    return pl.ds(pair * LANES, LANES)


def over_pairs(pairs, stages, lags, before):
    results = {}
    for step in range(pairs + lags[-1]):
        if step < pairs:
            before(step)
        for stage, lag in zip(stages, lags):
            pair = step - lag
            if 0 <= pair < pairs:
                results[pair] = stage(pair, *results.get(pair, ()))


def tops(scores):
    rows = scores.shape[0]
    while rows > 8:
        rows //= 2
        scores = jnp.maximum(scores[:rows], scores[rows:])
    return jnp.max(scores, axis=0, keepdims=True)


def with_ones(values_t):
    return jnp.concatenate([values_t, jnp.ones((16, values_t.shape[1]), jnp.bfloat16)], axis=0)


def three_terms(value):
    high = value.astype(jnp.bfloat16).astype(jnp.float32)
    middle = (value - high).astype(jnp.bfloat16).astype(jnp.float32)
    return [high, middle, value - high - middle]


def early_kernel(
    rows, chunks, offsets_hbm, q_hbm, k_hbm, v_hbm, cotangent_hbm, stashed_hbm,
    sent_ref, early_ref, more_ref, q_late_ref, k_ref, v_ref, own_ref, other_ref, next_ref, cotangent_ref, stashed_ref,
    offsets_ref, bias, sems, offsets_sem,
):
    half = rows // 2
    head, tail = pl.ds(0, half), pl.ds(half, half)
    offsets_copy = load(offsets_hbm, offsets_ref, offsets_sem.at[0])
    arrays = (
        (k_hbm.at[head], k_ref.at[head]),
        (q_hbm.at[head], sent_ref.at[head]),
        (v_hbm.at[head], v_ref.at[head]),
    )
    copies = load_chunks(arrays, chunks, sems)
    rest = [
        load(k_hbm.at[tail], k_ref.at[tail], offsets_sem.at[1]),
        load(v_hbm.at[tail], v_ref.at[tail], offsets_sem.at[2]),
        load(q_hbm.at[tail], q_late_ref, offsets_sem.at[3]),
        load(cotangent_hbm, cotangent_ref, offsets_sem.at[4]),
        load(stashed_hbm, stashed_ref, offsets_sem.at[5]),
    ]
    start = lax.axis_index("seq") * rows
    pairs = k_ref.shape[1] // LANES
    split = early_ref.shape[0] // LANES

    def arrive(pair):
        per_chunk = pairs // chunks
        if pair % per_chunk == 0:
            for copy in copies[pair // per_chunk]:
                copy.wait()
        if pair == 1:
            offsets_copy.wait()
            bias[...] = mask_bias(offsets_ref, start, start, lambda key, query: key <= query)

    def score(pair):
        scores = dot_nt(k_ref[head, at(pair)], split_heads(sent_ref[head, at(pair)]))
        return scores, with_ones(jnp.transpose(v_ref[head, at(pair)]))

    def top(pair, scores, values_t):
        scores = scores + bias[...]
        return scores, tops(scores), values_t

    def weigh(pair, scores, top, values_t):
        return top, dot_nn(values_t, jnp.exp(scores - top).astype(jnp.bfloat16))

    def finish(pair, top, mixed):
        total = mixed[LANES : LANES + 1]
        target, place = (early_ref, pair) if pair < split else (more_ref, pair - split)
        target[at(place), :] = own_heads(mixed, 1.0 / total).astype(jnp.bfloat16)
        lse = top + jnp.log(total)
        terms = three_terms(lse[:, :half]) + three_terms(lse[:, half:])
        terms.append(jnp.zeros((EXTRA - 6, LANES), jnp.float32))
        sent_ref[pl.ds(half, EXTRA), at(pair)] = jnp.concatenate(terms, axis=0).astype(jnp.bfloat16)
        return ()

    over_pairs(pairs, (score, top, weigh, finish), LAGS, arrive)
    own_ref[...] = mask_bias(offsets_ref, start + half, start + half, lambda key, query: key <= query)
    other_ref[...] = mask_bias(offsets_ref, start + half, start, lambda key, query: key > query)
    next_ref[...] = mask_bias(offsets_ref, start + rows, start + half, lambda key, query: key > query)
    for copy in rest:
        copy.wait()


def late_kernel(
    q_ref, k_ref, v_ref, own_bias, other_bias, early_ref, both_ref, own, other
):
    half = q_ref.shape[0]
    key = lax.broadcasted_iota(jnp.int32, own.shape, 0)
    query = lax.broadcasted_iota(jnp.int32, own.shape, 1) % half
    own[...] = jnp.where(key <= query, 1.0, 0.0).astype(jnp.bfloat16)
    other[...] = jnp.where(key <= query, 0.0, 1.0).astype(jnp.bfloat16)
    pooling = pool_matrix(half)
    molecules = half // POOL
    features = early_ref.shape[0]
    both_ref[pl.ds(0, features), :] = early_ref[...]
    pairs = k_ref.shape[1] // LANES
    parts = []

    def score(pair):
        scores = dot_nt(k_ref[:, at(pair)], split_heads(q_ref[:, at(pair)]))
        return scores, with_ones(jnp.transpose(v_ref[:, at(pair)]))

    def top(pair, scores, values_t):
        scores = jnp.maximum(scores[:half] + other_bias[...], scores[half:] + own_bias[...])
        return scores, tops(scores), values_t

    def weigh(pair, scores, top, values_t):
        weights = jnp.exp(scores - top).astype(jnp.bfloat16)
        weights = jnp.concatenate([weights * other[...], weights * own[...]], axis=0)
        return (dot_nn(values_t, weights),)

    def finish(pair, mixed):
        inverse = 1.0 / mixed[LANES : LANES + 1]
        parts.append(own_heads(mixed, inverse).astype(jnp.bfloat16))
        if len(parts) == 4:
            pooled = dot_nt(pooling, jnp.concatenate(parts, axis=0)).astype(jnp.bfloat16)
            for i in range(4):
                place = features + (pair - 3 + i) * molecules
                both_ref[pl.ds(place, molecules), :] = pooled[:, i * LANES : (i + 1) * LANES]
            parts.clear()
        return ()

    over_pairs(pairs, (score, top, weigh, finish), LAGS, lambda pair: None)


def halo_kernel(q_ref, k_ref, v_ref, bias, after_ref, out_ref):
    half = bias.shape[0]
    molecules = half // POOL
    tail = pl.ds(half, half)
    pooling = pool_matrix(half)
    pairs = k_ref.shape[1] // LANES
    parts = []

    def score(pair):
        queries = split_heads(q_ref[pl.ds(0, half), at(pair)])
        scores = dot_nt(k_ref[tail, at(pair)], queries)
        return scores, with_ones(jnp.transpose(v_ref[tail, at(pair)]))

    def top(pair, scores, values_t):
        terms = q_ref[pl.ds(half, EXTRA), at(pair)].astype(jnp.float32)
        lse = jnp.concatenate(
            [terms[0:1] + terms[1:2] + terms[2:3], terms[3:4] + terms[4:5] + terms[5:6]], axis=1
        )
        scores = scores + bias[...]
        return scores, jnp.maximum(tops(scores), lse), lse, values_t

    def weigh(pair, scores, top, lse, values_t):
        mixed = dot_nn(values_t, jnp.exp(scores - top).astype(jnp.bfloat16))
        return mixed, jnp.exp(lse - top)

    def finish(pair, mixed, kept):
        inverse = 1.0 / (mixed[LANES : LANES + 1] + kept)
        parts.append(own_heads(mixed, inverse).astype(jnp.bfloat16))
        if len(parts) == 4:
            pooled = dot_nt(pooling, jnp.concatenate(parts, axis=0)).astype(jnp.bfloat16)
            out_ref[pl.ds(0, molecules), pl.ds((pair - 3) * LANES, 4 * LANES)] = pooled
            parts.clear()
        share = kept * inverse
        high = share.astype(jnp.bfloat16).astype(jnp.float32)
        low = share - high
        shares = [high[:, :half], low[:, :half], high[:, half:], low[:, half:]]
        shares.append(jnp.zeros((EXTRA - 4, LANES), jnp.float32))
        out_ref[pl.ds(molecules, EXTRA), at(pair)] = jnp.concatenate(shares, axis=0).astype(jnp.bfloat16)
        return ()

    over_pairs(pairs, (score, top, weigh, finish), LAGS, lambda pair: None)


def back_kernel(
    slot_ref, cotangent_ref, weight_ref, gain_ref, stashed_ref, after_ref, dinput_ref, term_ref, grad, held_ref
):
    held = stashed_ref[0]
    for i in range(1, stashed_ref.shape[0]):
        held = jnp.where(slot_ref[0:1, 0:1] == i, stashed_ref[i].astype(jnp.float32), held.astype(jnp.float32))
    held_ref[...] = held.astype(jnp.bfloat16)
    features = weight_ref.shape[0]
    block = 512
    for begin in range(0, features, block):
        columns = pl.ds(begin, block)
        grad[:, columns] = dot_nt(cotangent_ref[...], weight_ref[columns, :])
    held = held_ref[...].astype(jnp.float32)
    inv_rms = lax.rsqrt(jnp.sum(held * held, axis=1, keepdims=True) / features + EPS_NORM)
    along = jnp.zeros_like(inv_rms)
    for begin in range(0, features, block):
        columns = pl.ds(begin, block)
        product = grad[:, columns] * (held_ref[:, columns].astype(jnp.float32) * inv_rms)
        term_ref[:, columns] = jnp.sum(product, axis=0, keepdims=True)
        along += jnp.sum(product * gain_ref[:, columns], axis=1, keepdims=True)
    along = along / features
    for begin in range(0, features, block):
        columns = pl.ds(begin, block)
        whitened = held_ref[:, columns].astype(jnp.float32) * inv_rms
        scaled = grad[:, columns] * gain_ref[:, columns]
        dinput_ref[:, columns] = (inv_rms * (scaled - whitened * along)).astype(jnp.bfloat16)


def project_kernel(
    early_ref, both_ref, halo_ref, gain_ref, weight_ref, upstream_hbm, out_ref, passed_hbm, squares_ref, sem
):
    passing = load(upstream_hbm, passed_hbm, sem)
    half = both_ref.shape[1]
    features = gain_ref.shape[1]
    first_part = early_ref.shape[0]
    molecules = half // POOL
    pooling = pool_matrix(half)
    first = lax.axis_index("seq") == 0
    squares, product, parts = 0.0, 0.0, []
    for pair in range(features // LANES):
        shares = halo_ref[molecules:, at(pair)].astype(jnp.float32)
        share_a = jnp.where(first, 1.0, shares[0:1] + shares[1:2])
        share_b = jnp.where(first, 1.0, shares[2:3] + shares[3:4])
        begin = pair * LANES
        if begin < first_part:
            early = early_ref[pl.ds(begin, LANES), :].astype(jnp.float32)
        else:
            early = both_ref[pl.ds(begin - first_part, LANES), :].astype(jnp.float32)
        parts += [early[:HEAD_DIM] * share_a, early[HEAD_DIM:] * share_b]
        if len(parts) == 8:
            columns = pl.ds((pair - 3) * LANES, 4 * LANES)
            mean = dot_nt(pooling, jnp.concatenate(parts, axis=0).astype(jnp.bfloat16))
            upper = mean + halo_ref[:molecules, columns].astype(jnp.float32)
            place = features - first_part + (pair - 3) * molecules
            lower = [both_ref[pl.ds(place + i * molecules, molecules), :] for i in range(4)]
            lower = jnp.concatenate(lower, axis=1)
            arrived = jnp.concatenate([upper.astype(jnp.bfloat16), lower], axis=0).astype(jnp.float32)
            squares += jnp.sum(arrived * arrived, axis=1, keepdims=True)
            scaled = (arrived * gain_ref[:, columns]).astype(jnp.bfloat16)
            product += dot_nn(scaled, weight_ref[columns, :])
            parts = []
    squares_ref[...] = squares
    out_ref[...] = (product * lax.rsqrt(squares / features + EPS_NORM)).astype(jnp.bfloat16)
    passing.wait()


def update_kernel(term_ref, other_ref, after_ref, update_ref):
    total = term_ref[...] + other_ref[...]
    mean = jnp.sum(total * total, axis=1, keepdims=True) / total.shape[1]
    update_ref[...] = total / jnp.sqrt(mean + EPS_STEP)


def cost(flops, read, exps=0):
    return pl.CostEstimate(flops=flops, bytes_accessed=read, transcendentals=exps)


SMEM = pl.BlockSpec(memory_space=pltpu.SMEM)
HBM = pl.BlockSpec(memory_space=pltpu.HBM)
ANY = pl.BlockSpec(memory_space=pl.ANY)
VMEM = pl.BlockSpec(memory_space=pltpu.VMEM)


def in_hbm(*arrays):
    return [pltpu.with_memory_space_constraint(x, pltpu.HBM) for x in arrays]


def params():
    return pltpu.CompilerParams(vmem_limit_bytes=24 * 2**20)


def attend_early(queries, keys, values, offsets, cotangent, stashed, chunks):
    rows, width = queries.shape
    half = rows // 2
    soon = width // (4 * LANES) * 3 // 4 * 4 * LANES
    masks = [jax.ShapeDtypeStruct((half, 2 * half), jnp.float32)] * 3
    return pl.pallas_call(
        functools.partial(early_kernel, rows, chunks),
        in_specs=[HBM] * 6,
        out_specs=[VMEM] * 11,
        out_shape=[
            jax.ShapeDtypeStruct((half + EXTRA, width), jnp.bfloat16),
            jax.ShapeDtypeStruct((soon, half), jnp.bfloat16),
            jax.ShapeDtypeStruct((width - soon, half), jnp.bfloat16),
            jax.ShapeDtypeStruct((half, width), jnp.bfloat16),
            jax.ShapeDtypeStruct((rows, width), jnp.bfloat16),
            jax.ShapeDtypeStruct((rows, width), jnp.bfloat16),
        ]
        + masks
        + [
            jax.ShapeDtypeStruct(cotangent.shape, cotangent.dtype),
            jax.ShapeDtypeStruct(stashed.shape, stashed.dtype),
        ],
        scratch_shapes=[
            pltpu.SMEM(offsets.shape, jnp.int32),
            pltpu.VMEM((half, 2 * half), jnp.float32),
            pltpu.SemaphoreType.DMA((3, chunks)),
            pltpu.SemaphoreType.DMA((6,)),
        ],
        cost_estimate=cost(4 * half * half * width, 6 * rows * width, half * half * width // 64),
        compiler_params=params(),
        name="attend_early",
    )(*in_hbm(offsets, queries, keys, values, cotangent, stashed))


def attend_late(queries, keys, values, own_bias, other_bias, early):
    half, width = queries.shape
    return pl.pallas_call(
        late_kernel,
        in_specs=[VMEM] * 6,
        out_specs=VMEM,
        out_shape=jax.ShapeDtypeStruct((early.shape[0] + width // POOL, half), jnp.bfloat16),
        scratch_shapes=[
            pltpu.VMEM((half, 2 * half), jnp.bfloat16),
            pltpu.VMEM((half, 2 * half), jnp.bfloat16),
        ],
        cost_estimate=cost(8 * half * half * width, 10 * half * width, half * half * width // 64),
        compiler_params=params(),
        name="attend_late",
    )(queries, keys, values, own_bias, other_bias, early)


def attend_halo(sent, keys, values, bias, after):
    half, width = bias.shape[0], keys.shape[1]
    return pl.pallas_call(
        halo_kernel,
        in_specs=[VMEM] * 4 + [ANY],
        out_specs=VMEM,
        out_shape=jax.ShapeDtypeStruct((half // POOL + EXTRA, width), jnp.bfloat16),
        cost_estimate=cost(4 * half * half * width, 6 * half * width, half * half * width // 64),
        compiler_params=params(),
        name="attend_halo",
    )(sent, keys, values, bias, after)


def backward(slot, cotangent, weight, gain, stashed, after):
    rows, width = stashed.shape[1:]
    depth = weight.shape[1]
    return pl.pallas_call(
        back_kernel,
        in_specs=[VMEM] * 5 + [ANY],
        out_specs=[VMEM] * 2,
        scratch_shapes=[
            pltpu.VMEM((rows, width), jnp.float32),
            pltpu.VMEM((rows, width), jnp.bfloat16),
        ],
        out_shape=[
            jax.ShapeDtypeStruct((rows, width), jnp.bfloat16),
            jax.ShapeDtypeStruct((1, width), jnp.float32),
        ],
        cost_estimate=cost(2 * rows * width * depth, 2 * width * depth),
        compiler_params=params(),
        name="backward",
    )(slot, cotangent, weight, gain, stashed, after)


def project(early, both, halo, gain, weight, upstream):
    rows = upstream.shape[0]
    width, depth = weight.shape
    return pl.pallas_call(
        project_kernel,
        in_specs=[VMEM] * 5 + [ANY],
        out_specs=[VMEM, HBM, VMEM],
        out_shape=[
            jax.ShapeDtypeStruct((rows, depth), jnp.bfloat16),
            jax.ShapeDtypeStruct(upstream.shape, upstream.dtype),
            jax.ShapeDtypeStruct((rows, 1), jnp.float32),
        ],
        scratch_shapes=[pltpu.SemaphoreType.DMA],
        cost_estimate=cost(2 * rows * width * depth, 2 * width * depth),
        compiler_params=params(),
        name="project",
    )(early, both, halo, gain, weight, upstream)


def updated(term, other, after):
    return pl.pallas_call(
        update_kernel,
        in_specs=[VMEM] * 2 + [ANY],
        out_specs=VMEM,
        out_shape=jax.ShapeDtypeStruct(term.shape, term.dtype),
        cost_estimate=cost(8 * term.size, 12 * term.size),
        name="update",
    )(term, other, after)


def swapped(value, axis, distance):
    return lax.ppermute(value, axis, [(i, i ^ distance) for i in range(lax.axis_size(axis))])


def sum_rounds():
    rounds = []
    for axis in ("rep", "seq"):
        count = lax.axis_size(axis)
        if count & (count - 1):
            return []
        rounds += [(axis, 1 << i) for i in range(count.bit_length() - 1)]
    return rounds if len(rounds) == 3 else []


def onward(value):
    sections, shards = lax.axis_size("section"), lax.axis_size("seq")
    route = [
        (s * shards + k, (s + 1) % sections * shards + k + 1)
        for s in range(sections)
        for k in range(shards - 1)
    ]
    return lax.ppermute(value, ("section", "seq"), route)


def local(queries, keys, values, doc_starts, weight, gain, stashed, cotangent, slot):
    queries, keys, values, offsets = queries[0, 0], keys[0, 0], values[0, 0], doc_starts[0]
    rounds = sum_rounds()

    def partner(term, index):
        return swapped(term, *rounds[index]) if rounds else jnp.zeros_like(term)

    sent, early, more, q_late, keys, values, *rest = attend_early(
        queries, keys, values, offsets, cotangent[0, 0], stashed[0, 0], 4
    )
    own_bias, other_bias, next_bias, cotangent, stashed = rest
    arrived = shifted(sent, "seq", -1)
    early = passed_along(early, "section", 1)
    both = attend_late(q_late, keys, values, own_bias, other_bias, more)
    slot = jnp.broadcast_to(slot, (1, LANES))
    dinput, term = backward(slot, cotangent, weight[0], gain, stashed, both)
    both = passed_along(both, "section", 1)
    upstream = passed_along(dinput, "section", -1)
    term = term if rounds else lax.psum(term, ("rep", "seq"))
    term = term + partner(term, 0)
    term = term + partner(term, 1)
    halo = onward(attend_halo(arrived, keys, values, next_bias, term))
    mol_keys, upstream, squares = project(early, both, halo, gain, weight[0], upstream)
    update = updated(term, partner(term, 2), squares)
    return mol_keys[None, None], upstream[None, None], update


def solution(mesh):
    in_specs = (
        P("rep", "section", "seq", None),
        P("rep", "section", "seq", None),
        P("rep", "section", "seq", None),
        P("rep", "section", None),
        P("section", None, None),
        P("section", None),
        P("rep", "section", None, "seq", None),
        P("rep", "section", "seq", None),
        P("rep", "section"),
    )
    out_specs = (
        P("rep", "section", "seq", None),
        P("rep", "section", "seq", None),
        P("section", None),
    )
    return jax.shard_map(local, mesh=mesh, in_specs=in_specs, out_specs=out_specs, check_vma=False)
```

```python
import functools
import math

import jax
import jax.numpy as jnp
from jax import lax
from jax.experimental import pallas as pl
from jax.experimental.pallas import tpu as pltpu
from jax.sharding import PartitionSpec as P

HEAD_DIM = 64
POOL = 4
WINDOW = 128
LANES = 128
EPS_NORM = 1e-05
EPS_STEP = 1e-06
MASKED = -1e30
LAGS = (0, 2, 3, 4)
EXTRA = 8

NT = (((1,), (1,)), ((), ()))


def dot_nt(a, b):
    return lax.dot_general(a, b, NT, preferred_element_type=jnp.float32)


def dot_nn(a, b):
    return jnp.dot(a, b, preferred_element_type=jnp.float32)


def shifted(value, axis, steps):
    count = lax.axis_size(axis)
    first, last = max(0, -steps), min(count, count - steps)
    return lax.ppermute(value, axis, [(i, i + steps) for i in range(first, last)])


def passed_along(value, axis, steps):
    count = lax.axis_size(axis)
    return lax.ppermute(value, axis, [(i, (i + steps) % count) for i in range(count)])


def earliest_key(offsets_ref, query_pos):
    start = jnp.zeros_like(query_pos)
    for d in range(offsets_ref.shape[1]):
        offset = offsets_ref[0, d]
        start = jnp.where(query_pos >= offset, offset, start)
    return jnp.maximum(start, query_pos - (WINDOW - 1))


def mask_bias(offsets_ref, query_start, key_start, keep):
    key = lax.broadcasted_iota(jnp.int32, (WINDOW, 2 * WINDOW), 0)
    query = lax.broadcasted_iota(jnp.int32, (WINDOW, 2 * WINDOW), 1) % WINDOW
    lane = lax.broadcasted_iota(jnp.int32, (1, 2 * WINDOW), 1) % WINDOW
    lowest = earliest_key(offsets_ref, query_start + lane)
    allowed = (key_start + key >= lowest) & keep(key, query)
    return jnp.where(allowed, 0.0, MASKED).astype(jnp.float32)


def split_heads(queries):
    lane = lax.broadcasted_iota(jnp.int32, (1, LANES), 1)
    scale = 1.0 / math.sqrt(HEAD_DIM)
    first = jnp.where(lane < HEAD_DIM, scale, 0.0).astype(jnp.bfloat16)
    second = jnp.where(lane < HEAD_DIM, 0.0, scale).astype(jnp.bfloat16)
    return jnp.concatenate([queries * first, queries * second], axis=0)


def pool_matrix(queries):
    molecule = lax.broadcasted_iota(jnp.int32, (queries // POOL, queries), 0)
    query = lax.broadcasted_iota(jnp.int32, (queries // POOL, queries), 1)
    return jnp.where(query // POOL == molecule, 1.0 / POOL, 0.0).astype(jnp.bfloat16)


def own_heads(mixed, scale):
    count = mixed.shape[1] // 2
    return jnp.concatenate(
        [
            mixed[:HEAD_DIM, :count] * scale[:, :count],
            mixed[HEAD_DIM:LANES, count:] * scale[:, count:],
        ],
        axis=0,
    )


def load(source, target, sem):
    copy = pltpu.make_async_copy(source, target, sem)
    copy.start()
    return copy


def load_chunks(arrays, chunks, sems):
    block = arrays[0][1].shape[1] // chunks
    return [
        [
            load(source.at[:, pl.ds(chunk * block, block)], target.at[:, pl.ds(chunk * block, block)], sems.at[i, chunk])
            for i, (source, target) in enumerate(arrays)
        ]
        for chunk in range(chunks)
    ]


def at(pair):
    return pl.ds(pair * LANES, LANES)


def over_pairs(pairs, stages, lags, before):
    results = {}
    for step in range(pairs + lags[-1]):
        if step < pairs:
            before(step)
        for stage, lag in zip(stages, lags):
            pair = step - lag
            if 0 <= pair < pairs:
                results[pair] = stage(pair, *results.get(pair, ()))


def tops(scores):
    rows = scores.shape[0]
    while rows > 8:
        rows //= 2
        scores = jnp.maximum(scores[:rows], scores[rows:])
    return jnp.max(scores, axis=0, keepdims=True)


def with_ones(values_t):
    return jnp.concatenate([values_t, jnp.ones((16, values_t.shape[1]), jnp.bfloat16)], axis=0)


def three_terms(value):
    high = value.astype(jnp.bfloat16).astype(jnp.float32)
    middle = (value - high).astype(jnp.bfloat16).astype(jnp.float32)
    return [high, middle, value - high - middle]


def early_kernel(
    rows, chunks, offsets_hbm, q_hbm, k_hbm, v_hbm, cotangent_hbm, stashed_hbm,
    sent_ref, early_ref, more_ref, q_late_ref, k_ref, v_ref, cotangent_ref, stashed_ref,
    offsets_ref, bias, sems, offsets_sem,
):
    half = rows // 2
    head, tail = pl.ds(0, half), pl.ds(half, half)
    offsets_copy = load(offsets_hbm, offsets_ref, offsets_sem.at[0])
    arrays = (
        (k_hbm.at[head], k_ref.at[head]),
        (q_hbm.at[head], sent_ref.at[head]),
        (v_hbm.at[head], v_ref.at[head]),
    )
    copies = load_chunks(arrays, chunks, sems)
    later = (
        (k_hbm.at[tail], k_ref.at[tail]),
        (v_hbm.at[tail], v_ref.at[tail]),
        (q_hbm.at[tail], q_late_ref),
        (cotangent_hbm, cotangent_ref),
        (stashed_hbm, stashed_ref),
    )
    rest = []
    offsets_copy.wait()
    start = lax.axis_index("seq") * rows
    bias[...] = mask_bias(offsets_ref, start, start, lambda key, query: key <= query)
    pairs = k_ref.shape[1] // LANES
    split = early_ref.shape[0] // LANES

    def arrive(pair):
        per_chunk = pairs // chunks
        if pair % per_chunk == 0:
            for copy in copies[pair // per_chunk]:
                copy.wait()
        if pair == per_chunk:
            for i, (source, target) in enumerate(later):
                rest.append(load(source, target, offsets_sem.at[i + 1]))

    def score(pair):
        scores = dot_nt(k_ref[head, at(pair)], split_heads(sent_ref[head, at(pair)]))
        return scores, with_ones(jnp.transpose(v_ref[head, at(pair)]))

    def top(pair, scores, values_t):
        return scores, tops(scores + bias[...]), values_t

    def weigh(pair, scores, top, values_t):
        weights = jnp.exp((scores + bias[...]) - top).astype(jnp.bfloat16)
        return top, dot_nn(values_t, weights)

    def finish(pair, top, mixed):
        total = mixed[LANES : LANES + 1]
        target, place = (early_ref, pair) if pair < split else (more_ref, pair - split)
        target[at(place), :] = own_heads(mixed, 1.0 / total).astype(jnp.bfloat16)
        lse = top + jnp.log(total)
        terms = three_terms(lse[:, :half]) + three_terms(lse[:, half:])
        terms.append(jnp.zeros((EXTRA - 6, LANES), jnp.float32))
        sent_ref[pl.ds(half, EXTRA), at(pair)] = jnp.concatenate(terms, axis=0).astype(jnp.bfloat16)
        return ()

    over_pairs(pairs, (score, top, weigh, finish), LAGS, arrive)
    for copy in rest:
        copy.wait()


def late_kernel(
    rows, offsets_hbm, weight_hbm, q_ref, k_ref, v_ref, early_ref, both_ref, next_ref, weight_ref,
    offsets_ref, own_bias, other_bias, own, other, sems,
):
    offsets_copy = load(offsets_hbm, offsets_ref, sems.at[8])
    block = weight_ref.shape[0] // 8
    copies = []
    for i in range(8):
        place = pl.ds(i * block, block)
        copies.append(load(weight_hbm.at[place], weight_ref.at[place], sems.at[i]))
    half = q_ref.shape[0]
    key = lax.broadcasted_iota(jnp.int32, own.shape, 0)
    query = lax.broadcasted_iota(jnp.int32, own.shape, 1) % half
    own[...] = jnp.where(key <= query, 1.0, 0.0).astype(jnp.bfloat16)
    other[...] = jnp.where(key <= query, 0.0, 1.0).astype(jnp.bfloat16)
    pooling = pool_matrix(half)
    molecules = half // POOL
    features = early_ref.shape[0]
    both_ref[pl.ds(0, features), :] = early_ref[...]
    pairs = k_ref.shape[1] // LANES
    offsets_copy.wait()
    start = lax.axis_index("seq") * rows
    own_bias[...] = mask_bias(offsets_ref, start + half, start + half, lambda key, query: key <= query)
    other_bias[...] = mask_bias(offsets_ref, start + half, start, lambda key, query: key > query)
    next_ref[...] = mask_bias(offsets_ref, start + rows, start + half, lambda key, query: key > query)
    parts = []

    def score(pair):
        scores = dot_nt(k_ref[:, at(pair)], split_heads(q_ref[:, at(pair)]))
        return scores, with_ones(jnp.transpose(v_ref[:, at(pair)]))

    def top(pair, scores, values_t):
        scores = jnp.maximum(scores[:half] + other_bias[...], scores[half:] + own_bias[...])
        return scores, tops(scores), values_t

    def weigh(pair, scores, top, values_t):
        weights = jnp.exp(scores - top).astype(jnp.bfloat16)
        weights = jnp.concatenate([weights * other[...], weights * own[...]], axis=0)
        return (dot_nn(values_t, weights),)

    def finish(pair, mixed):
        inverse = 1.0 / mixed[LANES : LANES + 1]
        parts.append(own_heads(mixed, inverse).astype(jnp.bfloat16))
        if len(parts) == 4:
            pooled = dot_nt(pooling, jnp.concatenate(parts, axis=0)).astype(jnp.bfloat16)
            for i in range(4):
                place = features + (pair - 3 + i) * molecules
                both_ref[pl.ds(place, molecules), :] = pooled[:, i * LANES : (i + 1) * LANES]
            parts.clear()
        return ()

    over_pairs(pairs, (score, top, weigh, finish), LAGS, lambda pair: None)
    for copy in copies:
        copy.wait()


def halo_kernel(q_ref, k_ref, v_ref, bias, after_ref, out_ref):
    half = bias.shape[0]
    molecules = half // POOL
    tail = pl.ds(half, half)
    pooling = pool_matrix(half)
    pairs = k_ref.shape[1] // LANES
    parts = []

    def score(pair):
        queries = split_heads(q_ref[pl.ds(0, half), at(pair)])
        scores = dot_nt(k_ref[tail, at(pair)], queries)
        return scores, with_ones(jnp.transpose(v_ref[tail, at(pair)]))

    def top(pair, scores, values_t):
        terms = q_ref[pl.ds(half, EXTRA), at(pair)].astype(jnp.float32)
        lse = jnp.concatenate(
            [terms[0:1] + terms[1:2] + terms[2:3], terms[3:4] + terms[4:5] + terms[5:6]], axis=1
        )
        return scores, jnp.maximum(tops(scores + bias[...]), lse), lse, values_t

    def weigh(pair, scores, top, lse, values_t):
        weights = jnp.exp((scores + bias[...]) - top).astype(jnp.bfloat16)
        mixed = dot_nn(values_t, weights)
        return mixed, jnp.exp(lse - top)

    def finish(pair, mixed, kept):
        inverse = 1.0 / (mixed[LANES : LANES + 1] + kept)
        parts.append(own_heads(mixed, inverse).astype(jnp.bfloat16))
        if len(parts) == 4:
            pooled = dot_nt(pooling, jnp.concatenate(parts, axis=0)).astype(jnp.bfloat16)
            out_ref[pl.ds(0, molecules), pl.ds((pair - 3) * LANES, 4 * LANES)] = pooled
            parts.clear()
        share = kept * inverse
        high = share.astype(jnp.bfloat16).astype(jnp.float32)
        low = share - high
        shares = [high[:, :half], low[:, :half], high[:, half:], low[:, half:]]
        shares.append(jnp.zeros((EXTRA - 4, LANES), jnp.float32))
        out_ref[pl.ds(molecules, EXTRA), at(pair)] = jnp.concatenate(shares, axis=0).astype(jnp.bfloat16)
        return ()

    over_pairs(pairs, (score, top, weigh, finish), LAGS, lambda pair: None)


def back_kernel(
    slot_ref, cotangent_ref, weight_ref, gain_ref, stashed_ref, after_ref, dinput_ref, term_ref, grad, held_ref
):
    held = stashed_ref[0]
    for i in range(1, stashed_ref.shape[0]):
        held = jnp.where(slot_ref[0:1, 0:1] == i, stashed_ref[i].astype(jnp.float32), held.astype(jnp.float32))
    held_ref[...] = held.astype(jnp.bfloat16)
    features = weight_ref.shape[0]
    block = 512
    for begin in range(0, features, block):
        columns = pl.ds(begin, block)
        grad[:, columns] = dot_nt(cotangent_ref[...], weight_ref[columns, :])
    held = held_ref[...].astype(jnp.float32)
    inv_rms = lax.rsqrt(jnp.sum(held * held, axis=1, keepdims=True) / features + EPS_NORM)
    along = jnp.zeros_like(inv_rms)
    for begin in range(0, features, block):
        columns = pl.ds(begin, block)
        product = grad[:, columns] * (held_ref[:, columns].astype(jnp.float32) * inv_rms)
        term_ref[:, columns] = jnp.sum(product, axis=0, keepdims=True)
        along += jnp.sum(product * gain_ref[:, columns], axis=1, keepdims=True)
    along = along / features
    for begin in range(0, features, block):
        columns = pl.ds(begin, block)
        whitened = held_ref[:, columns].astype(jnp.float32) * inv_rms
        scaled = grad[:, columns] * gain_ref[:, columns]
        dinput_ref[:, columns] = (inv_rms * (scaled - whitened * along)).astype(jnp.bfloat16)


def project_kernel(
    early_ref, both_ref, halo_ref, gain_ref, weight_ref, term_ref, other_ref, upstream_hbm,
    out_ref, update_ref, passed_hbm, sem,
):
    passing = load(upstream_hbm, passed_hbm, sem)
    half = both_ref.shape[1]
    features = gain_ref.shape[1]
    first_part = early_ref.shape[0]
    molecules = half // POOL
    pooling = pool_matrix(half)
    first = lax.axis_index("seq") == 0
    squares, product, parts = 0.0, 0.0, []
    for pair in range(features // LANES):
        shares = halo_ref[molecules:, at(pair)].astype(jnp.float32)
        share_a = jnp.where(first, 1.0, shares[0:1] + shares[1:2])
        share_b = jnp.where(first, 1.0, shares[2:3] + shares[3:4])
        begin = pair * LANES
        if begin < first_part:
            early = early_ref[pl.ds(begin, LANES), :].astype(jnp.float32)
        else:
            early = both_ref[pl.ds(begin - first_part, LANES), :].astype(jnp.float32)
        parts += [early[:HEAD_DIM] * share_a, early[HEAD_DIM:] * share_b]
        if len(parts) == 8:
            columns = pl.ds((pair - 3) * LANES, 4 * LANES)
            mean = dot_nt(pooling, jnp.concatenate(parts, axis=0).astype(jnp.bfloat16))
            upper = mean + halo_ref[:molecules, columns].astype(jnp.float32)
            place = features - first_part + (pair - 3) * molecules
            lower = [both_ref[pl.ds(place + i * molecules, molecules), :] for i in range(4)]
            lower = jnp.concatenate(lower, axis=1)
            arrived = jnp.concatenate([upper.astype(jnp.bfloat16), lower], axis=0).astype(jnp.float32)
            squares += jnp.sum(arrived * arrived, axis=1, keepdims=True)
            scaled = (arrived * gain_ref[:, columns]).astype(jnp.bfloat16)
            product += dot_nn(scaled, weight_ref[columns, :])
            parts = []
    out_ref[...] = (product * lax.rsqrt(squares / features + EPS_NORM)).astype(jnp.bfloat16)
    total = term_ref[...] + other_ref[...]
    mean = jnp.sum(total * total, axis=1, keepdims=True) / features
    update_ref[...] = total / jnp.sqrt(mean + EPS_STEP)
    passing.wait()


def cost(flops, read, exps=0):
    return pl.CostEstimate(flops=flops, bytes_accessed=read, transcendentals=exps)


SMEM = pl.BlockSpec(memory_space=pltpu.SMEM)
HBM = pl.BlockSpec(memory_space=pltpu.HBM)
ANY = pl.BlockSpec(memory_space=pl.ANY)
VMEM = pl.BlockSpec(memory_space=pltpu.VMEM)


def in_hbm(*arrays):
    return [pltpu.with_memory_space_constraint(x, pltpu.HBM) for x in arrays]


def params():
    return pltpu.CompilerParams(vmem_limit_bytes=24 * 2**20)


def attend_early(queries, keys, values, offsets, cotangent, stashed, chunks):
    rows, width = queries.shape
    half = rows // 2
    soon = width // (4 * LANES) * 3 // 4 * 4 * LANES
    bf16 = lambda *shape: jax.ShapeDtypeStruct(shape, jnp.bfloat16)
    return pl.pallas_call(
        functools.partial(early_kernel, rows, chunks),
        in_specs=[HBM] * 6,
        out_specs=[VMEM] * 8,
        out_shape=[
            bf16(half + EXTRA, width),
            bf16(soon, half),
            bf16(width - soon, half),
            bf16(half, width),
            bf16(rows, width),
            bf16(rows, width),
            bf16(*cotangent.shape),
            bf16(*stashed.shape),
        ],
        scratch_shapes=[
            pltpu.SMEM(offsets.shape, jnp.int32),
            pltpu.VMEM((half, 2 * half), jnp.float32),
            pltpu.SemaphoreType.DMA((3, chunks)),
            pltpu.SemaphoreType.DMA((6,)),
        ],
        cost_estimate=cost(4 * half * half * width, 6 * rows * width, half * half * width // 64),
        compiler_params=params(),
        name="attend_early",
    )(*in_hbm(offsets, queries, keys, values, cotangent, stashed))


def attend_late(queries, keys, values, offsets, weight, early):
    half, width = queries.shape
    rows = 2 * half
    return pl.pallas_call(
        functools.partial(late_kernel, rows),
        in_specs=[HBM] * 2 + [VMEM] * 4,
        out_specs=[VMEM] * 3,
        out_shape=[
            jax.ShapeDtypeStruct((early.shape[0] + width // POOL, half), jnp.bfloat16),
            jax.ShapeDtypeStruct((half, rows), jnp.float32),
            jax.ShapeDtypeStruct(weight.shape, weight.dtype),
        ],
        scratch_shapes=[
            pltpu.SMEM(offsets.shape, jnp.int32),
            pltpu.VMEM((half, rows), jnp.float32),
            pltpu.VMEM((half, rows), jnp.float32),
            pltpu.VMEM((half, rows), jnp.bfloat16),
            pltpu.VMEM((half, rows), jnp.bfloat16),
            pltpu.SemaphoreType.DMA((9,)),
        ],
        cost_estimate=cost(8 * half * half * width, 10 * half * width, half * half * width // 64),
        compiler_params=params(),
        name="attend_late",
    )(*in_hbm(offsets, weight), queries, keys, values, early)


def attend_halo(sent, keys, values, bias, after):
    half, width = bias.shape[0], keys.shape[1]
    return pl.pallas_call(
        halo_kernel,
        in_specs=[VMEM] * 4 + [ANY],
        out_specs=VMEM,
        out_shape=jax.ShapeDtypeStruct((half // POOL + EXTRA, width), jnp.bfloat16),
        cost_estimate=cost(4 * half * half * width, 6 * half * width, half * half * width // 64),
        compiler_params=params(),
        name="attend_halo",
    )(sent, keys, values, bias, after)


def backward(slot, cotangent, weight, gain, stashed, after):
    rows, width = stashed.shape[1:]
    depth = weight.shape[1]
    return pl.pallas_call(
        back_kernel,
        in_specs=[VMEM] * 5 + [ANY],
        out_specs=[VMEM] * 2,
        scratch_shapes=[
            pltpu.VMEM((rows, width), jnp.float32),
            pltpu.VMEM((rows, width), jnp.bfloat16),
        ],
        out_shape=[
            jax.ShapeDtypeStruct((rows, width), jnp.bfloat16),
            jax.ShapeDtypeStruct((1, width), jnp.float32),
        ],
        cost_estimate=cost(2 * rows * width * depth, 2 * width * depth),
        compiler_params=params(),
        name="backward",
    )(slot, cotangent, weight, gain, stashed, after)


def project(early, both, halo, gain, weight, term, other, upstream):
    rows = upstream.shape[0]
    width, depth = weight.shape
    return pl.pallas_call(
        project_kernel,
        in_specs=[VMEM] * 7 + [ANY],
        out_specs=[VMEM, VMEM, HBM],
        out_shape=[
            jax.ShapeDtypeStruct((rows, depth), jnp.bfloat16),
            jax.ShapeDtypeStruct(term.shape, term.dtype),
            jax.ShapeDtypeStruct(upstream.shape, upstream.dtype),
        ],
        scratch_shapes=[pltpu.SemaphoreType.DMA],
        cost_estimate=cost(2 * rows * width * depth, 2 * width * depth),
        compiler_params=params(),
        name="project",
    )(early, both, halo, gain, weight, term, other, upstream)


def swapped(value, axis, distance):
    return lax.ppermute(value, axis, [(i, i ^ distance) for i in range(lax.axis_size(axis))])


def sum_rounds():
    rounds = []
    for axis in ("rep", "seq"):
        count = lax.axis_size(axis)
        if count & (count - 1):
            return []
        rounds += [(axis, 1 << i) for i in range(count.bit_length() - 1)]
    return rounds if len(rounds) == 3 else []


def onward(value):
    sections, shards = lax.axis_size("section"), lax.axis_size("seq")
    route = [
        (s * shards + k, (s + 1) % sections * shards + k + 1)
        for s in range(sections)
        for k in range(shards - 1)
    ]
    return lax.ppermute(value, ("section", "seq"), route)


def local(queries, keys, values, doc_starts, weight, gain, stashed, cotangent, slot):
    queries, keys, values, offsets = queries[0, 0], keys[0, 0], values[0, 0], doc_starts[0]
    rounds = sum_rounds()

    def partner(term, index):
        return swapped(term, *rounds[index]) if rounds else jnp.zeros_like(term)

    sent, early, more, q_late, keys, values, cotangent, stashed = attend_early(
        queries, keys, values, offsets, cotangent[0, 0], stashed[0, 0], 4
    )
    arrived = shifted(sent, "seq", -1)
    early = passed_along(early, "section", 1)
    both, next_bias, weight = attend_late(q_late, keys, values, offsets, weight[0], more)
    slot = jnp.broadcast_to(slot, (1, LANES))
    dinput, term = backward(slot, cotangent, weight, gain, stashed, both)
    both = passed_along(both, "section", 1)
    upstream = passed_along(dinput, "section", -1)
    term = term if rounds else lax.psum(term, ("rep", "seq"))
    term = term + partner(term, 0)
    term = term + partner(term, 1)
    halo = onward(attend_halo(arrived, keys, values, next_bias, term))
    mol_keys, update, upstream = project(
        early, both, halo, gain, weight, term, partner(term, 2), upstream
    )
    return mol_keys[None, None], upstream[None, None], update


def solution(mesh):
    in_specs = (
        P("rep", "section", "seq", None),
        P("rep", "section", "seq", None),
        P("rep", "section", "seq", None),
        P("rep", "section", None),
        P("section", None, None),
        P("section", None),
        P("rep", "section", None, "seq", None),
        P("rep", "section", "seq", None),
        P("rep", "section"),
    )
    out_specs = (
        P("rep", "section", "seq", None),
        P("rep", "section", "seq", None),
        P("section", None),
    )
    return jax.shard_map(local, mesh=mesh, in_specs=in_specs, out_specs=out_specs, check_vma=False)
```

```python
import functools
import math

import jax
import jax.numpy as jnp
from jax import lax
from jax.experimental import pallas as pl
from jax.experimental.pallas import tpu as pltpu
from jax.sharding import PartitionSpec as P

HEAD_DIM = 64
POOL = 4
WINDOW = 128
LANES = 128
EPS_NORM = 1e-05
EPS_STEP = 1e-06
MASKED = -1e30
LAGS = (0, 2, 3, 4)
EXTRA = 8

NT = (((1,), (1,)), ((), ()))


def dot_nt(a, b):
    return lax.dot_general(a, b, NT, preferred_element_type=jnp.float32)


def dot_nn(a, b):
    return jnp.dot(a, b, preferred_element_type=jnp.float32)


def shifted(value, axis, steps):
    count = lax.axis_size(axis)
    first, last = max(0, -steps), min(count, count - steps)
    return lax.ppermute(value, axis, [(i, i + steps) for i in range(first, last)])


def passed_along(value, axis, steps):
    count = lax.axis_size(axis)
    return lax.ppermute(value, axis, [(i, (i + steps) % count) for i in range(count)])


def earliest_key(offsets_ref, query_pos):
    start = jnp.zeros_like(query_pos)
    for d in range(offsets_ref.shape[1]):
        offset = offsets_ref[0, d]
        start = jnp.where(query_pos >= offset, offset, start)
    return jnp.maximum(start, query_pos - (WINDOW - 1))


def mask_bias(offsets_ref, query_start, key_start, keep):
    key = lax.broadcasted_iota(jnp.int32, (WINDOW, 2 * WINDOW), 0)
    query = lax.broadcasted_iota(jnp.int32, (WINDOW, 2 * WINDOW), 1) % WINDOW
    lane = lax.broadcasted_iota(jnp.int32, (1, 2 * WINDOW), 1) % WINDOW
    lowest = earliest_key(offsets_ref, query_start + lane)
    allowed = (key_start + key >= lowest) & keep(key, query)
    return jnp.where(allowed, 0.0, MASKED).astype(jnp.float32)


def split_heads(queries):
    lane = lax.broadcasted_iota(jnp.int32, (1, LANES), 1)
    scale = 1.0 / math.sqrt(HEAD_DIM)
    first = jnp.where(lane < HEAD_DIM, scale, 0.0).astype(jnp.bfloat16)
    second = jnp.where(lane < HEAD_DIM, 0.0, scale).astype(jnp.bfloat16)
    return jnp.concatenate([queries * first, queries * second], axis=0)


def pool_matrix(queries):
    molecule = lax.broadcasted_iota(jnp.int32, (queries // POOL, queries), 0)
    query = lax.broadcasted_iota(jnp.int32, (queries // POOL, queries), 1)
    return jnp.where(query // POOL == molecule, 1.0 / POOL, 0.0).astype(jnp.bfloat16)


def own_heads(mixed, scale):
    count = mixed.shape[1] // 2
    return jnp.concatenate(
        [
            mixed[:HEAD_DIM, :count] * scale[:, :count],
            mixed[HEAD_DIM:LANES, count:] * scale[:, count:],
        ],
        axis=0,
    )


def load(source, target, sem):
    copy = pltpu.make_async_copy(source, target, sem)
    copy.start()
    return copy


def load_chunks(arrays, chunks, sems):
    block = arrays[0][1].shape[1] // chunks
    return [
        [
            load(source.at[:, pl.ds(chunk * block, block)], target.at[:, pl.ds(chunk * block, block)], sems.at[i, chunk])
            for i, (source, target) in enumerate(arrays)
        ]
        for chunk in range(chunks)
    ]


def at(pair):
    return pl.ds(pair * LANES, LANES)


def over_pairs(pairs, stages, lags, before):
    results = {}
    for step in range(pairs + lags[-1]):
        if step < pairs:
            before(step)
        for stage, lag in zip(stages, lags):
            pair = step - lag
            if 0 <= pair < pairs:
                results[pair] = stage(pair, *results.get(pair, ()))


def tops(scores):
    rows = scores.shape[0]
    while rows > 8:
        rows //= 2
        scores = jnp.maximum(scores[:rows], scores[rows:])
    return jnp.max(scores, axis=0, keepdims=True)


def with_ones(values_t):
    return jnp.concatenate([values_t, jnp.ones((16, values_t.shape[1]), jnp.bfloat16)], axis=0)


def three_terms(value):
    high = value.astype(jnp.bfloat16).astype(jnp.float32)
    middle = (value - high).astype(jnp.bfloat16).astype(jnp.float32)
    return [high, middle, value - high - middle]


def early_kernel(
    rows, chunks, offsets_hbm, q_hbm, k_hbm, v_hbm, cotangent_hbm, stashed_hbm,
    sent_ref, early_ref, more_ref, q_late_ref, k_ref, v_ref, cotangent_ref, stashed_ref,
    offsets_ref, bias, sems, offsets_sem,
):
    half = rows // 2
    head, tail = pl.ds(0, half), pl.ds(half, half)
    offsets_copy = load(offsets_hbm, offsets_ref, offsets_sem.at[0])
    arrays = (
        (k_hbm.at[head], k_ref.at[head]),
        (q_hbm.at[head], sent_ref.at[head]),
        (v_hbm.at[head], v_ref.at[head]),
    )
    copies = load_chunks(arrays, chunks, sems)
    later = (
        (k_hbm.at[tail], k_ref.at[tail]),
        (v_hbm.at[tail], v_ref.at[tail]),
        (q_hbm.at[tail], q_late_ref),
        (cotangent_hbm, cotangent_ref),
        (stashed_hbm, stashed_ref),
    )
    rest = []
    offsets_copy.wait()
    start = lax.axis_index("seq") * rows
    bias[...] = mask_bias(offsets_ref, start, start, lambda key, query: key <= query)
    pairs = k_ref.shape[1] // LANES
    split = early_ref.shape[0] // LANES

    def arrive(pair):
        per_chunk = pairs // chunks
        if pair % per_chunk == 0:
            for copy in copies[pair // per_chunk]:
                copy.wait()
        if pair == per_chunk:
            for i, (source, target) in enumerate(later):
                rest.append(load(source, target, offsets_sem.at[i + 1]))

    def score(pair):
        scores = dot_nt(k_ref[head, at(pair)], split_heads(sent_ref[head, at(pair)]))
        return scores, with_ones(jnp.transpose(v_ref[head, at(pair)]))

    def top(pair, scores, values_t):
        return scores, tops(scores + bias[...]), values_t

    def weigh(pair, scores, top, values_t):
        weights = jnp.exp(((scores + bias[...]) - top).astype(jnp.bfloat16))
        return top, dot_nn(values_t, weights)

    def finish(pair, top, mixed):
        total = mixed[LANES : LANES + 1]
        target, place = (early_ref, pair) if pair < split else (more_ref, pair - split)
        target[at(place), :] = own_heads(mixed, 1.0 / total).astype(jnp.bfloat16)
        lse = top + jnp.log(total)
        terms = three_terms(lse[:, :half]) + three_terms(lse[:, half:])
        terms.append(jnp.zeros((EXTRA - 6, LANES), jnp.float32))
        sent_ref[pl.ds(half, EXTRA), at(pair)] = jnp.concatenate(terms, axis=0).astype(jnp.bfloat16)
        return ()

    over_pairs(pairs, (score, top, weigh, finish), LAGS, arrive)
    for copy in rest:
        copy.wait()


def late_kernel(
    rows, offsets_hbm, weight_hbm, q_ref, k_ref, v_ref, early_ref, both_ref, next_ref, weight_ref,
    offsets_ref, own_bias, other_bias, own, other, sems,
):
    offsets_copy = load(offsets_hbm, offsets_ref, sems.at[8])
    block = weight_ref.shape[0] // 8
    copies = []
    for i in range(8):
        place = pl.ds(i * block, block)
        copies.append(load(weight_hbm.at[place], weight_ref.at[place], sems.at[i]))
    half = q_ref.shape[0]
    key = lax.broadcasted_iota(jnp.int32, own.shape, 0)
    query = lax.broadcasted_iota(jnp.int32, own.shape, 1) % half
    own[...] = jnp.where(key <= query, 1.0, 0.0).astype(jnp.bfloat16)
    other[...] = jnp.where(key <= query, 0.0, 1.0).astype(jnp.bfloat16)
    pooling = pool_matrix(half)
    molecules = half // POOL
    features = early_ref.shape[0]
    both_ref[pl.ds(0, features), :] = early_ref[...]
    pairs = k_ref.shape[1] // LANES
    offsets_copy.wait()
    start = lax.axis_index("seq") * rows
    own_bias[...] = mask_bias(offsets_ref, start + half, start + half, lambda key, query: key <= query)
    other_bias[...] = mask_bias(offsets_ref, start + half, start, lambda key, query: key > query)
    next_ref[...] = mask_bias(offsets_ref, start + rows, start + half, lambda key, query: key > query)
    parts = []

    def score(pair):
        scores = dot_nt(k_ref[:, at(pair)], split_heads(q_ref[:, at(pair)]))
        return scores, with_ones(jnp.transpose(v_ref[:, at(pair)]))

    def top(pair, scores, values_t):
        scores = jnp.maximum(scores[:half] + other_bias[...], scores[half:] + own_bias[...])
        return scores, tops(scores), values_t

    def weigh(pair, scores, top, values_t):
        weights = jnp.exp((scores - top).astype(jnp.bfloat16))
        weights = jnp.concatenate([weights * other[...], weights * own[...]], axis=0)
        return (dot_nn(values_t, weights),)

    def finish(pair, mixed):
        inverse = 1.0 / mixed[LANES : LANES + 1]
        parts.append(own_heads(mixed, inverse).astype(jnp.bfloat16))
        if len(parts) == 4:
            pooled = dot_nt(pooling, jnp.concatenate(parts, axis=0)).astype(jnp.bfloat16)
            for i in range(4):
                place = features + (pair - 3 + i) * molecules
                both_ref[pl.ds(place, molecules), :] = pooled[:, i * LANES : (i + 1) * LANES]
            parts.clear()
        return ()

    over_pairs(pairs, (score, top, weigh, finish), LAGS, lambda pair: None)
    for copy in copies:
        copy.wait()


def halo_kernel(q_ref, k_ref, v_ref, bias, after_ref, out_ref):
    half = bias.shape[0]
    molecules = half // POOL
    tail = pl.ds(half, half)
    pooling = pool_matrix(half)
    pairs = k_ref.shape[1] // LANES
    parts = []

    def score(pair):
        queries = split_heads(q_ref[pl.ds(0, half), at(pair)])
        scores = dot_nt(k_ref[tail, at(pair)], queries)
        return scores, with_ones(jnp.transpose(v_ref[tail, at(pair)]))

    def top(pair, scores, values_t):
        terms = q_ref[pl.ds(half, EXTRA), at(pair)].astype(jnp.float32)
        lse = jnp.concatenate(
            [terms[0:1] + terms[1:2] + terms[2:3], terms[3:4] + terms[4:5] + terms[5:6]], axis=1
        )
        return scores, jnp.maximum(tops(scores + bias[...]), lse), lse, values_t

    def weigh(pair, scores, top, lse, values_t):
        weights = jnp.exp(((scores + bias[...]) - top).astype(jnp.bfloat16))
        mixed = dot_nn(values_t, weights)
        return mixed, jnp.exp(lse - top)

    def finish(pair, mixed, kept):
        inverse = 1.0 / (mixed[LANES : LANES + 1] + kept)
        parts.append(own_heads(mixed, inverse).astype(jnp.bfloat16))
        if len(parts) == 4:
            pooled = dot_nt(pooling, jnp.concatenate(parts, axis=0)).astype(jnp.bfloat16)
            out_ref[pl.ds(0, molecules), pl.ds((pair - 3) * LANES, 4 * LANES)] = pooled
            parts.clear()
        share = kept * inverse
        high = share.astype(jnp.bfloat16).astype(jnp.float32)
        low = share - high
        shares = [high[:, :half], low[:, :half], high[:, half:], low[:, half:]]
        shares.append(jnp.zeros((EXTRA - 4, LANES), jnp.float32))
        out_ref[pl.ds(molecules, EXTRA), at(pair)] = jnp.concatenate(shares, axis=0).astype(jnp.bfloat16)
        return ()

    over_pairs(pairs, (score, top, weigh, finish), LAGS, lambda pair: None)


def back_kernel(
    slot_ref, cotangent_ref, weight_ref, gain_ref, stashed_ref, after_ref, dinput_ref, term_ref, grad, held_ref
):
    held = stashed_ref[0]
    for i in range(1, stashed_ref.shape[0]):
        held = jnp.where(slot_ref[0:1, 0:1] == i, stashed_ref[i].astype(jnp.float32), held.astype(jnp.float32))
    held_ref[...] = held.astype(jnp.bfloat16)
    features = weight_ref.shape[0]
    block = 512
    for begin in range(0, features, block):
        columns = pl.ds(begin, block)
        grad[:, columns] = dot_nt(cotangent_ref[...], weight_ref[columns, :])
    held = held_ref[...].astype(jnp.float32)
    inv_rms = lax.rsqrt(jnp.sum(held * held, axis=1, keepdims=True) / features + EPS_NORM)
    along = jnp.zeros_like(inv_rms)
    for begin in range(0, features, block):
        columns = pl.ds(begin, block)
        product = grad[:, columns] * (held_ref[:, columns].astype(jnp.float32) * inv_rms)
        term_ref[:, columns] = jnp.sum(product, axis=0, keepdims=True)
        along += jnp.sum(product * gain_ref[:, columns], axis=1, keepdims=True)
    along = along / features
    for begin in range(0, features, block):
        columns = pl.ds(begin, block)
        whitened = held_ref[:, columns].astype(jnp.float32) * inv_rms
        scaled = grad[:, columns] * gain_ref[:, columns]
        dinput_ref[:, columns] = (inv_rms * (scaled - whitened * along)).astype(jnp.bfloat16)


def project_kernel(
    early_ref, both_ref, halo_ref, gain_ref, weight_ref, term_ref, other_ref, upstream_hbm,
    out_ref, update_ref, passed_hbm, sem,
):
    passing = load(upstream_hbm, passed_hbm, sem)
    half = both_ref.shape[1]
    features = gain_ref.shape[1]
    first_part = early_ref.shape[0]
    molecules = half // POOL
    pooling = pool_matrix(half)
    first = lax.axis_index("seq") == 0
    squares, product, ready = 0.0, 0.0, None
    group = 4
    for begin in range(0, features + group * LANES, group * LANES):
        following = ready
        if begin < features:
            parts = []
            for pair in range(begin // LANES, begin // LANES + group):
                shares = halo_ref[molecules:, at(pair)].astype(jnp.float32)
                share_a = jnp.where(first, 1.0, shares[0:1] + shares[1:2])
                share_b = jnp.where(first, 1.0, shares[2:3] + shares[3:4])
                if pair * LANES < first_part:
                    early = early_ref[at(pair), :].astype(jnp.float32)
                else:
                    early = both_ref[at(pair - first_part // LANES), :].astype(jnp.float32)
                parts += [early[:HEAD_DIM] * share_a, early[HEAD_DIM:] * share_b]
            columns = pl.ds(begin, group * LANES)
            mean = dot_nt(pooling, jnp.concatenate(parts, axis=0).astype(jnp.bfloat16))
            upper = mean + halo_ref[:molecules, columns].astype(jnp.float32)
            place = features - first_part + begin // LANES * molecules
            lower = [both_ref[pl.ds(place + i * molecules, molecules), :] for i in range(group)]
            lower = jnp.concatenate(lower, axis=1)
            arrived = jnp.concatenate([upper.astype(jnp.bfloat16), lower], axis=0).astype(jnp.float32)
            squares += jnp.sum(arrived * arrived, axis=1, keepdims=True)
            ready = (arrived * gain_ref[:, columns]).astype(jnp.bfloat16), columns
        if following is not None:
            scaled, columns = following
            product += dot_nn(scaled, weight_ref[columns, :])
    out_ref[...] = (product * lax.rsqrt(squares / features + EPS_NORM)).astype(jnp.bfloat16)
    total = term_ref[...] + other_ref[...]
    mean = jnp.sum(total * total, axis=1, keepdims=True) / features
    update_ref[...] = total / jnp.sqrt(mean + EPS_STEP)
    passing.wait()


def cost(flops, read, exps=0):
    return pl.CostEstimate(flops=flops, bytes_accessed=read, transcendentals=exps)


SMEM = pl.BlockSpec(memory_space=pltpu.SMEM)
HBM = pl.BlockSpec(memory_space=pltpu.HBM)
ANY = pl.BlockSpec(memory_space=pl.ANY)
VMEM = pl.BlockSpec(memory_space=pltpu.VMEM)


def in_hbm(*arrays):
    return [pltpu.with_memory_space_constraint(x, pltpu.HBM) for x in arrays]


def params():
    return pltpu.CompilerParams(vmem_limit_bytes=24 * 2**20)


def attend_early(queries, keys, values, offsets, cotangent, stashed, chunks):
    rows, width = queries.shape
    half = rows // 2
    soon = width // (4 * LANES) * 3 // 4 * 4 * LANES
    bf16 = lambda *shape: jax.ShapeDtypeStruct(shape, jnp.bfloat16)
    return pl.pallas_call(
        functools.partial(early_kernel, rows, chunks),
        in_specs=[HBM] * 6,
        out_specs=[VMEM] * 8,
        out_shape=[
            bf16(half + EXTRA, width),
            bf16(soon, half),
            bf16(width - soon, half),
            bf16(half, width),
            bf16(rows, width),
            bf16(rows, width),
            bf16(*cotangent.shape),
            bf16(*stashed.shape),
        ],
        scratch_shapes=[
            pltpu.SMEM(offsets.shape, jnp.int32),
            pltpu.VMEM((half, 2 * half), jnp.float32),
            pltpu.SemaphoreType.DMA((3, chunks)),
            pltpu.SemaphoreType.DMA((6,)),
        ],
        cost_estimate=cost(4 * half * half * width, 6 * rows * width, half * half * width // 64),
        compiler_params=params(),
        name="attend_early",
    )(*in_hbm(offsets, queries, keys, values, cotangent, stashed))


def attend_late(queries, keys, values, offsets, weight, early):
    half, width = queries.shape
    rows = 2 * half
    return pl.pallas_call(
        functools.partial(late_kernel, rows),
        in_specs=[HBM] * 2 + [VMEM] * 4,
        out_specs=[VMEM] * 3,
        out_shape=[
            jax.ShapeDtypeStruct((early.shape[0] + width // POOL, half), jnp.bfloat16),
            jax.ShapeDtypeStruct((half, rows), jnp.float32),
            jax.ShapeDtypeStruct(weight.shape, weight.dtype),
        ],
        scratch_shapes=[
            pltpu.SMEM(offsets.shape, jnp.int32),
            pltpu.VMEM((half, rows), jnp.float32),
            pltpu.VMEM((half, rows), jnp.float32),
            pltpu.VMEM((half, rows), jnp.bfloat16),
            pltpu.VMEM((half, rows), jnp.bfloat16),
            pltpu.SemaphoreType.DMA((9,)),
        ],
        cost_estimate=cost(8 * half * half * width, 10 * half * width, half * half * width // 64),
        compiler_params=params(),
        name="attend_late",
    )(*in_hbm(offsets, weight), queries, keys, values, early)


def attend_halo(sent, keys, values, bias, after):
    half, width = bias.shape[0], keys.shape[1]
    return pl.pallas_call(
        halo_kernel,
        in_specs=[VMEM] * 4 + [ANY],
        out_specs=VMEM,
        out_shape=jax.ShapeDtypeStruct((half // POOL + EXTRA, width), jnp.bfloat16),
        cost_estimate=cost(4 * half * half * width, 6 * half * width, half * half * width // 64),
        compiler_params=params(),
        name="attend_halo",
    )(sent, keys, values, bias, after)


def backward(slot, cotangent, weight, gain, stashed, after):
    rows, width = stashed.shape[1:]
    depth = weight.shape[1]
    return pl.pallas_call(
        back_kernel,
        in_specs=[VMEM] * 5 + [ANY],
        out_specs=[VMEM] * 2,
        scratch_shapes=[
            pltpu.VMEM((rows, width), jnp.float32),
            pltpu.VMEM((rows, width), jnp.bfloat16),
        ],
        out_shape=[
            jax.ShapeDtypeStruct((rows, width), jnp.bfloat16),
            jax.ShapeDtypeStruct((1, width), jnp.float32),
        ],
        cost_estimate=cost(2 * rows * width * depth, 2 * width * depth),
        compiler_params=params(),
        name="backward",
    )(slot, cotangent, weight, gain, stashed, after)


def project(early, both, halo, gain, weight, term, other, upstream):
    rows = upstream.shape[0]
    width, depth = weight.shape
    return pl.pallas_call(
        project_kernel,
        in_specs=[VMEM] * 7 + [ANY],
        out_specs=[VMEM, VMEM, HBM],
        out_shape=[
            jax.ShapeDtypeStruct((rows, depth), jnp.bfloat16),
            jax.ShapeDtypeStruct(term.shape, term.dtype),
            jax.ShapeDtypeStruct(upstream.shape, upstream.dtype),
        ],
        scratch_shapes=[pltpu.SemaphoreType.DMA],
        cost_estimate=cost(2 * rows * width * depth, 2 * width * depth),
        compiler_params=params(),
        name="project",
    )(early, both, halo, gain, weight, term, other, upstream)


def swapped(value, axis, distance):
    return lax.ppermute(value, axis, [(i, i ^ distance) for i in range(lax.axis_size(axis))])


def sum_rounds():
    rounds = []
    for axis in ("rep", "seq"):
        count = lax.axis_size(axis)
        if count & (count - 1):
            return []
        rounds += [(axis, 1 << i) for i in range(count.bit_length() - 1)]
    return rounds if len(rounds) == 3 else []


def onward(value):
    sections, shards = lax.axis_size("section"), lax.axis_size("seq")
    route = [
        (s * shards + k, (s + 1) % sections * shards + k + 1)
        for s in range(sections)
        for k in range(shards - 1)
    ]
    return lax.ppermute(value, ("section", "seq"), route)


def local(queries, keys, values, doc_starts, weight, gain, stashed, cotangent, slot):
    queries, keys, values, offsets = queries[0, 0], keys[0, 0], values[0, 0], doc_starts[0]
    rounds = sum_rounds()

    def partner(term, index):
        return swapped(term, *rounds[index]) if rounds else jnp.zeros_like(term)

    sent, early, more, q_late, keys, values, cotangent, stashed = attend_early(
        queries, keys, values, offsets, cotangent[0, 0], stashed[0, 0], 4
    )
    arrived = shifted(sent, "seq", -1)
    early = passed_along(early, "section", 1)
    both, next_bias, weight = attend_late(q_late, keys, values, offsets, weight[0], more)
    slot = jnp.broadcast_to(slot, (1, LANES))
    dinput, term = backward(slot, cotangent, weight, gain, stashed, both)
    both = passed_along(both, "section", 1)
    upstream = passed_along(dinput, "section", -1)
    term = term if rounds else lax.psum(term, ("rep", "seq"))
    term = term + partner(term, 0)
    term = term + partner(term, 1)
    halo = onward(attend_halo(arrived, keys, values, next_bias, term))
    mol_keys, update, upstream = project(
        early, both, halo, gain, weight, term, partner(term, 2), upstream
    )
    return mol_keys[None, None], upstream[None, None], update


def solution(mesh):
    in_specs = (
        P("rep", "section", "seq", None),
        P("rep", "section", "seq", None),
        P("rep", "section", "seq", None),
        P("rep", "section", None),
        P("section", None, None),
        P("section", None),
        P("rep", "section", None, "seq", None),
        P("rep", "section", "seq", None),
        P("rep", "section"),
    )
    out_specs = (
        P("rep", "section", "seq", None),
        P("rep", "section", "seq", None),
        P("section", None),
    )
    return jax.shard_map(local, mesh=mesh, in_specs=in_specs, out_specs=out_specs, check_vma=False)
```

```python
import functools
import math

import jax
import jax.numpy as jnp
from jax import lax
from jax.experimental import pallas as pl
from jax.experimental.pallas import tpu as pltpu
from jax.sharding import PartitionSpec as P

HEAD_DIM = 64
POOL = 4
WINDOW = 128
LANES = 128
EPS_NORM = 1e-05
EPS_STEP = 1e-06
MASKED = -1e30
LAGS = (0, 2, 3, 4)
EXTRA = 8

NT = (((1,), (1,)), ((), ()))


def dot_nt(a, b):
    return lax.dot_general(a, b, NT, preferred_element_type=jnp.float32)


def dot_nn(a, b):
    return jnp.dot(a, b, preferred_element_type=jnp.float32)


def shifted(value, axis, steps):
    count = lax.axis_size(axis)
    first, last = max(0, -steps), min(count, count - steps)
    return lax.ppermute(value, axis, [(i, i + steps) for i in range(first, last)])


def passed_along(value, axis, steps):
    count = lax.axis_size(axis)
    return lax.ppermute(value, axis, [(i, (i + steps) % count) for i in range(count)])


def earliest_key(offsets_ref, query_pos):
    start = jnp.zeros_like(query_pos)
    for d in range(offsets_ref.shape[1]):
        offset = offsets_ref[0, d]
        start = jnp.where(query_pos >= offset, offset, start)
    return jnp.maximum(start, query_pos - (WINDOW - 1))


def mask_bias(offsets_ref, query_start, key_start, keep):
    key = lax.broadcasted_iota(jnp.int32, (WINDOW, 2 * WINDOW), 0)
    query = lax.broadcasted_iota(jnp.int32, (WINDOW, 2 * WINDOW), 1) % WINDOW
    lane = lax.broadcasted_iota(jnp.int32, (1, 2 * WINDOW), 1) % WINDOW
    lowest = earliest_key(offsets_ref, query_start + lane)
    allowed = (key_start + key >= lowest) & keep(key, query)
    return jnp.where(allowed, 0.0, MASKED).astype(jnp.float32)


def split_heads(queries):
    lane = lax.broadcasted_iota(jnp.int32, (1, LANES), 1)
    scale = 1.0 / math.sqrt(HEAD_DIM)
    first = jnp.where(lane < HEAD_DIM, scale, 0.0).astype(jnp.bfloat16)
    second = jnp.where(lane < HEAD_DIM, 0.0, scale).astype(jnp.bfloat16)
    return jnp.concatenate([queries * first, queries * second], axis=0)


def pool_matrix(queries):
    molecule = lax.broadcasted_iota(jnp.int32, (queries // POOL, queries), 0)
    query = lax.broadcasted_iota(jnp.int32, (queries // POOL, queries), 1)
    return jnp.where(query // POOL == molecule, 1.0 / POOL, 0.0).astype(jnp.bfloat16)


def own_heads(mixed, scale):
    count = mixed.shape[1] // 2
    return jnp.concatenate(
        [
            mixed[:HEAD_DIM, :count] * scale[:, :count],
            mixed[HEAD_DIM:LANES, count:] * scale[:, count:],
        ],
        axis=0,
    )


def load(source, target, sem):
    copy = pltpu.make_async_copy(source, target, sem)
    copy.start()
    return copy


def load_chunks(arrays, chunks, sems):
    block = arrays[0][1].shape[1] // chunks
    return [
        [
            load(source.at[:, pl.ds(chunk * block, block)], target.at[:, pl.ds(chunk * block, block)], sems.at[i, chunk])
            for i, (source, target) in enumerate(arrays)
        ]
        for chunk in range(chunks)
    ]


def at(pair):
    return pl.ds(pair * LANES, LANES)


def over_pairs(pairs, stages, lags, before):
    results = {}
    for step in range(pairs + lags[-1]):
        if step < pairs:
            before(step)
        for stage, lag in zip(stages, lags):
            pair = step - lag
            if 0 <= pair < pairs:
                results[pair] = stage(pair, *results.get(pair, ()))


def tops(scores):
    rows = scores.shape[0]
    while rows > 8:
        rows //= 2
        scores = jnp.maximum(scores[:rows], scores[rows:])
    return jnp.max(scores, axis=0, keepdims=True)


def with_ones(values_t):
    return jnp.concatenate([values_t, jnp.ones((16, values_t.shape[1]), jnp.bfloat16)], axis=0)


def three_terms(value):
    high = value.astype(jnp.bfloat16).astype(jnp.float32)
    middle = (value - high).astype(jnp.bfloat16).astype(jnp.float32)
    return [high, middle, value - high - middle]


def early_pairs(pairs, arrive, q_at, k_at, v_at, bias, sent_ref, early_ref):
    half = bias.shape[0]

    def score(pair):
        return dot_nt(k_at(pair), split_heads(q_at(pair))), with_ones(jnp.transpose(v_at(pair)))

    def top(pair, scores, values_t):
        return scores, tops(scores + bias[...]), values_t

    def weigh(pair, scores, top, values_t):
        weights = jnp.exp((scores + bias[...]) - top).astype(jnp.bfloat16)
        return top, dot_nn(values_t, weights)

    def finish(pair, top, mixed):
        total = mixed[LANES : LANES + 1]
        early_ref[at(pair), :] = own_heads(mixed, 1.0 / total).astype(jnp.bfloat16)
        lse = top + jnp.log(total)
        terms = three_terms(lse[:, :half]) + three_terms(lse[:, half:])
        terms.append(jnp.zeros((EXTRA - 6, LANES), jnp.float32))
        sent_ref[pl.ds(half, EXTRA), at(pair)] = jnp.concatenate(terms, axis=0).astype(jnp.bfloat16)
        return ()

    over_pairs(pairs, (score, top, weigh, finish), LAGS, arrive)


def early_kernel(
    rows, chunk, offsets_hbm, q_hbm, k_hbm, v_hbm,
    sent_ref, early_ref, q_more_ref, k_ref, v_ref, bias,
    offsets_ref, sems, offsets_sem,
):
    half = rows // 2
    head = pl.ds(0, half)
    width = sent_ref.shape[1]
    offsets_copy = load(offsets_hbm, offsets_ref, offsets_sem)
    copies = []
    for i, begin in enumerate(range(0, k_ref.shape[1], chunk)):
        columns = pl.ds(begin, chunk)
        q_ref = sent_ref.at[head, columns] if begin < width else q_more_ref.at[:, pl.ds(begin - width, chunk)]
        copies.append(
            [
                load(k_hbm.at[head, columns], k_ref.at[:, columns], sems.at[0, i]),
                load(q_hbm.at[head, columns], q_ref, sems.at[1, i]),
                load(v_hbm.at[head, columns], v_ref.at[:, columns], sems.at[2, i]),
            ]
        )
    offsets_copy.wait()
    start = lax.axis_index("seq") * rows
    bias[...] = mask_bias(offsets_ref, start, start, lambda key, query: key <= query)

    def arrive(pair):
        if pair * LANES % chunk == 0:
            for copy in copies[pair * LANES // chunk]:
                copy.wait()

    early_pairs(
        width // LANES,
        arrive,
        lambda pair: sent_ref[head, at(pair)],
        lambda pair: k_ref[:, at(pair)],
        lambda pair: v_ref[:, at(pair)],
        bias,
        sent_ref,
        early_ref,
    )
    for group in copies[width // chunk :]:
        for copy in group:
            copy.wait()


def more_kernel(
    q_ref, k_ref, v_ref, bias, q_hbm, k_hbm, v_hbm, cotangent_hbm, stashed_hbm, after_ref,
    sent_ref, early_ref, q_late_ref, k_tail_ref, v_tail_ref, cotangent_ref, stashed_ref, sems,
):
    half, width = q_ref.shape
    tail = pl.ds(half, half)
    later = (
        (k_hbm.at[tail], k_tail_ref),
        (v_hbm.at[tail], v_tail_ref),
        (q_hbm.at[tail], q_late_ref),
        (cotangent_hbm, cotangent_ref),
        (stashed_hbm, stashed_ref),
    )
    copies = [load(source, target, sems.at[i]) for i, (source, target) in enumerate(later)]
    begin = k_ref.shape[1] - width
    sent_ref[pl.ds(0, half), :] = q_ref[...]
    early_pairs(
        width // LANES,
        lambda pair: None,
        lambda pair: q_ref[:, at(pair)],
        lambda pair: k_ref[:, pl.ds(begin + pair * LANES, LANES)],
        lambda pair: v_ref[:, pl.ds(begin + pair * LANES, LANES)],
        bias,
        sent_ref,
        early_ref,
    )
    for copy in copies:
        copy.wait()


def late_kernel(
    rows, offsets_hbm, weight_hbm, q_ref, k_ref, v_ref, k_tail_ref, v_tail_ref, early_ref,
    both_ref, next_ref, weight_ref,
    offsets_ref, own_bias, other_bias, own, other, sems,
):
    offsets_copy = load(offsets_hbm, offsets_ref, sems.at[8])
    block = weight_ref.shape[0] // 8
    copies = []
    for i in range(8):
        place = pl.ds(i * block, block)
        copies.append(load(weight_hbm.at[place], weight_ref.at[place], sems.at[i]))
    half = q_ref.shape[0]
    key = lax.broadcasted_iota(jnp.int32, own.shape, 0)
    query = lax.broadcasted_iota(jnp.int32, own.shape, 1) % half
    own[...] = jnp.where(key <= query, 1.0, 0.0).astype(jnp.bfloat16)
    other[...] = jnp.where(key <= query, 0.0, 1.0).astype(jnp.bfloat16)
    pooling = pool_matrix(half)
    molecules = half // POOL
    features = early_ref.shape[0]
    both_ref[pl.ds(0, features), :] = early_ref[...]
    pairs = k_ref.shape[1] // LANES
    offsets_copy.wait()
    start = lax.axis_index("seq") * rows
    own_bias[...] = mask_bias(offsets_ref, start + half, start + half, lambda key, query: key <= query)
    other_bias[...] = mask_bias(offsets_ref, start + half, start, lambda key, query: key > query)
    next_ref[...] = mask_bias(offsets_ref, start + rows, start + half, lambda key, query: key > query)
    parts = []

    def score(pair):
        keys = jnp.concatenate([k_ref[:, at(pair)], k_tail_ref[:, at(pair)]], axis=0)
        values = jnp.concatenate([v_ref[:, at(pair)], v_tail_ref[:, at(pair)]], axis=0)
        return dot_nt(keys, split_heads(q_ref[:, at(pair)])), with_ones(jnp.transpose(values))

    def top(pair, scores, values_t):
        scores = jnp.maximum(scores[:half] + other_bias[...], scores[half:] + own_bias[...])
        return scores, tops(scores), values_t

    def weigh(pair, scores, top, values_t):
        weights = jnp.exp(scores - top).astype(jnp.bfloat16)
        weights = jnp.concatenate([weights * other[...], weights * own[...]], axis=0)
        return (dot_nn(values_t, weights),)

    def finish(pair, mixed):
        inverse = 1.0 / mixed[LANES : LANES + 1]
        parts.append(own_heads(mixed, inverse).astype(jnp.bfloat16))
        if len(parts) == 4:
            pooled = dot_nt(pooling, jnp.concatenate(parts, axis=0)).astype(jnp.bfloat16)
            for i in range(4):
                place = features + (pair - 3 + i) * molecules
                both_ref[pl.ds(place, molecules), :] = pooled[:, i * LANES : (i + 1) * LANES]
            parts.clear()
        return ()

    over_pairs(pairs, (score, top, weigh, finish), LAGS, lambda pair: None)
    for copy in copies:
        copy.wait()


def halo_kernel(q_ref, q_more_ref, k_ref, v_ref, bias, term_ref, other_ref, out_ref, sum_ref):
    sum_ref[...] = term_ref[...] + other_ref[...]
    half = bias.shape[0]
    molecules = half // POOL
    pooling = pool_matrix(half)
    pairs = k_ref.shape[1] // LANES
    split = q_ref.shape[1] // LANES
    parts, shares = [], []

    def sent(pair, rows):
        return q_ref[rows, at(pair)] if pair < split else q_more_ref[rows, at(pair - split)]

    def score(pair):
        scores = dot_nt(k_ref[:, at(pair)], split_heads(sent(pair, pl.ds(0, half))))
        return scores, with_ones(jnp.transpose(v_ref[:, at(pair)]))

    def top(pair, scores, values_t):
        terms = sent(pair, pl.ds(half, EXTRA)).astype(jnp.float32)
        lse = jnp.concatenate(
            [terms[0:1] + terms[1:2] + terms[2:3], terms[3:4] + terms[4:5] + terms[5:6]], axis=1
        )
        return scores, jnp.maximum(tops(scores + bias[...]), lse), lse, values_t

    def weigh(pair, scores, top, lse, values_t):
        weights = jnp.exp((scores + bias[...]) - top).astype(jnp.bfloat16)
        return dot_nn(values_t, weights), jnp.exp(lse - top)

    def finish(pair, mixed, kept):
        inverse = 1.0 / (mixed[LANES : LANES + 1] + kept)
        parts.append(own_heads(mixed, inverse).astype(jnp.bfloat16))
        share = kept * inverse
        high = share.astype(jnp.bfloat16).astype(jnp.float32)
        low = share - high
        shares.extend([high[:, :half], low[:, :half], high[:, half:], low[:, half:]])
        if len(parts) == 4:
            pooled = dot_nt(pooling, jnp.concatenate(parts, axis=0)).astype(jnp.bfloat16)
            for i in range(4):
                place = pl.ds((pair - 3 + i) * molecules, molecules)
                out_ref[place, :] = pooled[:, i * LANES : (i + 1) * LANES]
            place = pl.ds(pairs * molecules + (pair - 3) * 4, 16)
            out_ref[place, :] = jnp.concatenate(shares, axis=0).astype(jnp.bfloat16)
            parts.clear()
            shares.clear()
        return ()

    over_pairs(pairs, (score, top, weigh, finish), LAGS, lambda pair: None)


def back_kernel(
    slot_ref, cotangent_ref, weight_ref, gain_ref, stashed_ref, after_ref, dinput_ref, term_ref, grad, held_ref
):
    held = stashed_ref[0]
    for i in range(1, stashed_ref.shape[0]):
        held = jnp.where(slot_ref[0:1, 0:1] == i, stashed_ref[i].astype(jnp.float32), held.astype(jnp.float32))
    held_ref[...] = held.astype(jnp.bfloat16)
    features = weight_ref.shape[0]
    block = 512
    for begin in range(0, features, block):
        columns = pl.ds(begin, block)
        grad[:, columns] = dot_nt(cotangent_ref[...], weight_ref[columns, :])
    held = held_ref[...].astype(jnp.float32)
    inv_rms = lax.rsqrt(jnp.sum(held * held, axis=1, keepdims=True) / features + EPS_NORM)
    along = jnp.zeros_like(inv_rms)
    for begin in range(0, features, block):
        columns = pl.ds(begin, block)
        product = grad[:, columns] * (held_ref[:, columns].astype(jnp.float32) * inv_rms)
        term_ref[:, columns] = jnp.sum(product, axis=0, keepdims=True)
        along += jnp.sum(product * gain_ref[:, columns], axis=1, keepdims=True)
    along = along / features
    for begin in range(0, features, block):
        columns = pl.ds(begin, block)
        whitened = held_ref[:, columns].astype(jnp.float32) * inv_rms
        scaled = grad[:, columns] * gain_ref[:, columns]
        dinput_ref[:, columns] = (inv_rms * (scaled - whitened * along)).astype(jnp.bfloat16)


def project_kernel(
    early_ref, both_ref, halo_ref, gain_ref, weight_ref, term_ref, other_ref, upstream_hbm,
    out_ref, update_ref, passed_hbm, sem,
):
    passing = load(upstream_hbm, passed_hbm, sem)
    half = both_ref.shape[1]
    features = gain_ref.shape[1]
    first_part = early_ref.shape[0]
    molecules = half // POOL
    pooling = pool_matrix(half)
    first = lax.axis_index("seq") == 0
    squares, product, parts = 0.0, 0.0, []
    for pair in range(features // LANES):
        if pair % 4 == 0:
            place = pl.ds(features // LANES * molecules + pair * 4, 16)
            shares = halo_ref[place, :].astype(jnp.float32)
        row = pair % 4 * 4
        share_a = jnp.where(first, 1.0, shares[row : row + 1] + shares[row + 1 : row + 2])
        share_b = jnp.where(first, 1.0, shares[row + 2 : row + 3] + shares[row + 3 : row + 4])
        begin = pair * LANES
        if begin < first_part:
            early = early_ref[pl.ds(begin, LANES), :].astype(jnp.float32)
        else:
            early = both_ref[pl.ds(begin - first_part, LANES), :].astype(jnp.float32)
        parts += [early[:HEAD_DIM] * share_a, early[HEAD_DIM:] * share_b]
        if len(parts) == 8:
            columns = pl.ds((pair - 3) * LANES, 4 * LANES)
            mean = dot_nt(pooling, jnp.concatenate(parts, axis=0).astype(jnp.bfloat16))
            place = pl.ds((pair - 3) * molecules, 4 * molecules)
            halo = halo_ref[place, :].astype(jnp.float32)
            halo = [halo[i * molecules : (i + 1) * molecules] for i in range(4)]
            upper = mean + jnp.concatenate(halo, axis=1)
            place = features - first_part + (pair - 3) * molecules
            lower = [both_ref[pl.ds(place + i * molecules, molecules), :] for i in range(4)]
            lower = jnp.concatenate(lower, axis=1)
            arrived = jnp.concatenate([upper.astype(jnp.bfloat16), lower], axis=0).astype(jnp.float32)
            squares += jnp.sum(arrived * arrived, axis=1, keepdims=True)
            scaled = (arrived * gain_ref[:, columns]).astype(jnp.bfloat16)
            product += dot_nn(scaled, weight_ref[columns, :])
            parts = []
    out_ref[...] = (product * lax.rsqrt(squares / features + EPS_NORM)).astype(jnp.bfloat16)
    total = term_ref[...] + other_ref[...]
    mean = jnp.sum(total * total, axis=1, keepdims=True) / features
    update_ref[...] = total / jnp.sqrt(mean + EPS_STEP)
    passing.wait()


def cost(flops, read, exps=0):
    return pl.CostEstimate(flops=flops, bytes_accessed=read, transcendentals=exps)


SMEM = pl.BlockSpec(memory_space=pltpu.SMEM)
HBM = pl.BlockSpec(memory_space=pltpu.HBM)
ANY = pl.BlockSpec(memory_space=pl.ANY)
VMEM = pl.BlockSpec(memory_space=pltpu.VMEM)


def in_hbm(*arrays):
    return [pltpu.with_memory_space_constraint(x, pltpu.HBM) for x in arrays]


def params():
    return pltpu.CompilerParams(vmem_limit_bytes=24 * 2**20)


def bf16(*shape):
    return jax.ShapeDtypeStruct(shape, jnp.bfloat16)


def attend_early(queries, keys, values, offsets, width):
    rows, features = queries.shape
    half, chunk = rows // 2, 2 * LANES
    return pl.pallas_call(
        functools.partial(early_kernel, rows, chunk),
        in_specs=[HBM] * 4,
        out_specs=[VMEM] * 6,
        out_shape=[
            bf16(half + EXTRA, width),
            bf16(width, half),
            bf16(half, features - width),
            bf16(half, features),
            bf16(half, features),
            jax.ShapeDtypeStruct((half, rows), jnp.float32),
        ],
        scratch_shapes=[
            pltpu.SMEM(offsets.shape, jnp.int32),
            pltpu.SemaphoreType.DMA((3, features // chunk)),
            pltpu.SemaphoreType.DMA,
        ],
        cost_estimate=cost(4 * half * half * width, 6 * half * features, half * half * width // 64),
        compiler_params=params(),
        name="attend_early",
    )(*in_hbm(offsets, queries, keys, values))


def attend_more(q_more, k_head, v_head, bias, queries, keys, values, cotangent, stashed, after):
    half, width = q_more.shape
    features = keys.shape[1]
    return pl.pallas_call(
        more_kernel,
        in_specs=[VMEM] * 4 + [HBM] * 5 + [ANY],
        out_specs=[VMEM] * 7,
        out_shape=[
            bf16(half + EXTRA, width),
            bf16(width, half),
            bf16(half, features),
            bf16(half, features),
            bf16(half, features),
            bf16(*cotangent.shape),
            bf16(*stashed.shape),
        ],
        scratch_shapes=[pltpu.SemaphoreType.DMA((5,))],
        cost_estimate=cost(4 * half * half * width, 6 * half * features, half * half * width // 64),
        compiler_params=params(),
        name="attend_more",
    )(q_more, k_head, v_head, bias, *in_hbm(queries, keys, values, cotangent, stashed), after)


def attend_late(queries, k_head, v_head, k_tail, v_tail, offsets, weight, early):
    half, width = queries.shape
    rows = 2 * half
    return pl.pallas_call(
        functools.partial(late_kernel, rows),
        in_specs=[HBM] * 2 + [VMEM] * 6,
        out_specs=[VMEM] * 3,
        out_shape=[
            bf16(early.shape[0] + width // POOL, half),
            jax.ShapeDtypeStruct((half, rows), jnp.float32),
            bf16(*weight.shape),
        ],
        scratch_shapes=[
            pltpu.SMEM(offsets.shape, jnp.int32),
            pltpu.VMEM((half, rows), jnp.float32),
            pltpu.VMEM((half, rows), jnp.float32),
            pltpu.VMEM((half, rows), jnp.bfloat16),
            pltpu.VMEM((half, rows), jnp.bfloat16),
            pltpu.SemaphoreType.DMA((9,)),
        ],
        cost_estimate=cost(8 * half * half * width, 10 * half * width, half * half * width // 64),
        compiler_params=params(),
        name="attend_late",
    )(*in_hbm(offsets, weight), queries, k_head, v_head, k_tail, v_tail, early)


def attend_halo(sent, sent_more, keys, values, bias, term, other):
    half, width = keys.shape
    return pl.pallas_call(
        halo_kernel,
        in_specs=[VMEM] * 7,
        out_specs=[VMEM] * 2,
        out_shape=[
            bf16(width // LANES * (half // POOL + 4), LANES),
            jax.ShapeDtypeStruct(term.shape, term.dtype),
        ],
        cost_estimate=cost(4 * half * half * width, 6 * half * width, half * half * width // 64),
        compiler_params=params(),
        name="attend_halo",
    )(sent, sent_more, keys, values, bias, term, other)


def backward(slot, cotangent, weight, gain, stashed, after):
    rows, width = stashed.shape[1:]
    depth = weight.shape[1]
    return pl.pallas_call(
        back_kernel,
        in_specs=[VMEM] * 5 + [ANY],
        out_specs=[VMEM] * 2,
        scratch_shapes=[
            pltpu.VMEM((rows, width), jnp.float32),
            pltpu.VMEM((rows, width), jnp.bfloat16),
        ],
        out_shape=[
            jax.ShapeDtypeStruct((rows, width), jnp.bfloat16),
            jax.ShapeDtypeStruct((1, width), jnp.float32),
        ],
        cost_estimate=cost(2 * rows * width * depth, 2 * width * depth),
        compiler_params=params(),
        name="backward",
    )(slot, cotangent, weight, gain, stashed, after)


def project(early, both, halo, gain, weight, term, other, upstream):
    rows = upstream.shape[0]
    width, depth = weight.shape
    return pl.pallas_call(
        project_kernel,
        in_specs=[VMEM] * 7 + [ANY],
        out_specs=[VMEM, VMEM, HBM],
        out_shape=[
            jax.ShapeDtypeStruct((rows, depth), jnp.bfloat16),
            jax.ShapeDtypeStruct(term.shape, term.dtype),
            jax.ShapeDtypeStruct(upstream.shape, upstream.dtype),
        ],
        scratch_shapes=[pltpu.SemaphoreType.DMA],
        cost_estimate=cost(2 * rows * width * depth, 2 * width * depth),
        compiler_params=params(),
        name="project",
    )(early, both, halo, gain, weight, term, other, upstream)


def swapped(value, axis, distance):
    return lax.ppermute(value, axis, [(i, i ^ distance) for i in range(lax.axis_size(axis))])


def sum_rounds():
    rounds = []
    for axis in ("seq", "rep"):
        count = lax.axis_size(axis)
        if count & (count - 1):
            return []
        rounds += [(axis, 1 << i) for i in range(count.bit_length() - 1)]
    return rounds if len(rounds) == 3 else []


def onward(value):
    sections, shards = lax.axis_size("section"), lax.axis_size("seq")
    route = [
        (s * shards + k, (s + 1) % sections * shards + k + 1)
        for s in range(sections)
        for k in range(shards - 1)
    ]
    return lax.ppermute(value, ("section", "seq"), route)


def local(queries, keys, values, doc_starts, weight, gain, stashed, cotangent, slot):
    queries, keys, values, offsets = queries[0, 0], keys[0, 0], values[0, 0], doc_starts[0]
    rounds = sum_rounds()

    def partner(term, index):
        return swapped(term, *rounds[index]) if rounds else jnp.zeros_like(term)

    features = queries.shape[1]
    width = features // LANES * 12 // 16 * LANES
    sent, early, q_more, k_head, v_head, bias = attend_early(queries, keys, values, offsets, width)
    arrived = shifted(sent, "seq", -1)
    early = passed_along(early, "section", 1)
    sent, more, q_late, k_tail, v_tail, cotangent, stashed = attend_more(
        q_more, k_head, v_head, bias, queries, keys, values, cotangent[0, 0], stashed[0, 0], sent
    )
    arrived_more = shifted(sent, "seq", -1)
    both, next_bias, weight = attend_late(
        q_late, k_head, v_head, k_tail, v_tail, offsets, weight[0], more
    )
    slot = jnp.broadcast_to(slot, (1, LANES))
    dinput, term = backward(slot, cotangent, weight, gain, stashed, both)
    both = passed_along(both, "section", 1)
    upstream = passed_along(dinput, "section", -1)
    term = term if rounds else lax.psum(term, ("rep", "seq"))
    halo, term = attend_halo(
        arrived, arrived_more, k_tail, v_tail, next_bias, term, partner(term, 0)
    )
    halo = onward(halo)
    term = term + partner(term, 1)
    mol_keys, update, upstream = project(
        early, both, halo, gain, weight, term, partner(term, 2), upstream
    )
    return mol_keys[None, None], upstream[None, None], update


def solution(mesh):
    in_specs = (
        P("rep", "section", "seq", None),
        P("rep", "section", "seq", None),
        P("rep", "section", "seq", None),
        P("rep", "section", None),
        P("section", None, None),
        P("section", None),
        P("rep", "section", None, "seq", None),
        P("rep", "section", "seq", None),
        P("rep", "section"),
    )
    out_specs = (
        P("rep", "section", "seq", None),
        P("rep", "section", "seq", None),
        P("section", None),
    )
    return jax.shard_map(local, mesh=mesh, in_specs=in_specs, out_specs=out_specs, check_vma=False)
```

```python
import functools
import math

import jax
import jax.numpy as jnp
from jax import lax
from jax.experimental import pallas as pl
from jax.experimental.pallas import tpu as pltpu
from jax.sharding import PartitionSpec as P

HEAD_DIM = 64
POOL = 4
WINDOW = 128
LANES = 128
EPS_NORM = 1e-05
EPS_STEP = 1e-06
MASKED = -1e30
LAGS = (0, 2, 3, 4)
EXTRA = 8

NT = (((1,), (1,)), ((), ()))


def dot_nt(a, b):
    return lax.dot_general(a, b, NT, preferred_element_type=jnp.float32)


def dot_nn(a, b):
    return jnp.dot(a, b, preferred_element_type=jnp.float32)


def shifted(value, axis, steps):
    count = lax.axis_size(axis)
    first, last = max(0, -steps), min(count, count - steps)
    return lax.ppermute(value, axis, [(i, i + steps) for i in range(first, last)])


def passed_along(value, axis, steps):
    count = lax.axis_size(axis)
    return lax.ppermute(value, axis, [(i, (i + steps) % count) for i in range(count)])


def earliest_key(offsets_ref, query_pos):
    start = jnp.zeros_like(query_pos)
    for d in range(offsets_ref.shape[1]):
        offset = offsets_ref[0, d]
        start = jnp.where(query_pos >= offset, offset, start)
    return jnp.maximum(start, query_pos - (WINDOW - 1))


def mask_bias(offsets_ref, query_start, key_start, keep):
    key = lax.broadcasted_iota(jnp.int32, (WINDOW, 2 * WINDOW), 0)
    query = lax.broadcasted_iota(jnp.int32, (WINDOW, 2 * WINDOW), 1) % WINDOW
    lane = lax.broadcasted_iota(jnp.int32, (1, 2 * WINDOW), 1) % WINDOW
    lowest = earliest_key(offsets_ref, query_start + lane)
    allowed = (key_start + key >= lowest) & keep(key, query)
    return jnp.where(allowed, 0.0, MASKED).astype(jnp.float32)


def split_heads(queries):
    lane = lax.broadcasted_iota(jnp.int32, (1, LANES), 1)
    scale = 1.0 / math.sqrt(HEAD_DIM)
    first = jnp.where(lane < HEAD_DIM, scale, 0.0).astype(jnp.bfloat16)
    second = jnp.where(lane < HEAD_DIM, 0.0, scale).astype(jnp.bfloat16)
    return jnp.concatenate([queries * first, queries * second], axis=0)


def pool_matrix(queries):
    molecule = lax.broadcasted_iota(jnp.int32, (queries // POOL, queries), 0)
    query = lax.broadcasted_iota(jnp.int32, (queries // POOL, queries), 1)
    return jnp.where(query // POOL == molecule, 1.0 / POOL, 0.0).astype(jnp.bfloat16)


def own_heads(mixed, scale):
    count = mixed.shape[1] // 2
    return jnp.concatenate(
        [
            mixed[:HEAD_DIM, :count] * scale[:, :count],
            mixed[HEAD_DIM:LANES, count:] * scale[:, count:],
        ],
        axis=0,
    )


def load(source, target, sem):
    copy = pltpu.make_async_copy(source, target, sem)
    copy.start()
    return copy


def load_chunks(arrays, chunks, sems):
    block = arrays[0][1].shape[1] // chunks
    return [
        [
            load(source.at[:, pl.ds(chunk * block, block)], target.at[:, pl.ds(chunk * block, block)], sems.at[i, chunk])
            for i, (source, target) in enumerate(arrays)
        ]
        for chunk in range(chunks)
    ]


def at(pair):
    return pl.ds(pair * LANES, LANES)


def over_pairs(pairs, stages, lags, before):
    results = {}
    for step in range(pairs + lags[-1]):
        if step < pairs:
            before(step)
        for stage, lag in zip(stages, lags):
            pair = step - lag
            if 0 <= pair < pairs:
                results[pair] = stage(pair, *results.get(pair, ()))


def tops(scores):
    rows = scores.shape[0]
    while rows > 8:
        rows //= 2
        scores = jnp.maximum(scores[:rows], scores[rows:])
    return jnp.max(scores, axis=0, keepdims=True)


def with_ones(values_t):
    return jnp.concatenate([values_t, jnp.ones((16, values_t.shape[1]), jnp.bfloat16)], axis=0)


def three_terms(value):
    high = value.astype(jnp.bfloat16).astype(jnp.float32)
    middle = (value - high).astype(jnp.bfloat16).astype(jnp.float32)
    return [high, middle, value - high - middle]


def put_terms(rows_ref, terms):
    blocks = [term[i : i + 8] for term in terms for i in range(0, term.shape[0], 8)]
    blocks.append(jnp.zeros((8, rows_ref.shape[1] - 256 * len(blocks)), jnp.float32))
    rows_ref[...] = jnp.concatenate(blocks, axis=1).astype(jnp.bfloat16)


def get_terms(rows_ref, pairs, count):
    per_term = pairs // 8
    sums = []
    for i in range(per_term):
        parts = [rows_ref[:, pl.ds((j * per_term + i) * 256, 256)] for j in range(count)]
        total = parts[0].astype(jnp.float32)
        for part in parts[1:]:
            total = total + part.astype(jnp.float32)
        sums.append(total)
    return jnp.concatenate(sums, axis=0)


def early_kernel(
    rows, chunks, offsets_hbm, q_hbm, k_hbm, v_hbm, cotangent_hbm, stashed_hbm,
    sent_ref, early_ref, more_ref, q_late_ref, k_ref, v_ref, cotangent_ref, stashed_ref,
    offsets_ref, bias, lse_ref, sems, offsets_sem,
):
    half = rows // 2
    head, tail = pl.ds(0, half), pl.ds(half, half)
    offsets_copy = load(offsets_hbm, offsets_ref, offsets_sem.at[0])
    arrays = (
        (k_hbm.at[head], k_ref.at[head]),
        (q_hbm.at[head], sent_ref.at[head]),
        (v_hbm.at[head], v_ref.at[head]),
    )
    copies = load_chunks(arrays, chunks, sems)
    later = (
        (k_hbm.at[tail], k_ref.at[tail]),
        (v_hbm.at[tail], v_ref.at[tail]),
        (q_hbm.at[tail], q_late_ref),
        (cotangent_hbm, cotangent_ref),
        (stashed_hbm, stashed_ref),
    )
    rest = []
    start = lax.axis_index("seq") * rows
    pairs = k_ref.shape[1] // LANES
    split = early_ref.shape[0] // LANES

    def arrive(pair):
        per_chunk = pairs // chunks
        if pair % per_chunk == 0:
            for copy in copies[pair // per_chunk]:
                copy.wait()
        if pair == 1:
            offsets_copy.wait()
            bias[...] = mask_bias(offsets_ref, start, start, lambda key, query: key <= query)
        if pair == per_chunk:
            for i, (source, target) in enumerate(later):
                rest.append(load(source, target, offsets_sem.at[i + 1]))

    def score(pair):
        scores = dot_nt(k_ref[head, at(pair)], split_heads(sent_ref[head, at(pair)]))
        return scores, with_ones(jnp.transpose(v_ref[head, at(pair)]))

    def top(pair, scores, values_t):
        return scores, tops(scores + bias[...]), values_t

    def weigh(pair, scores, top, values_t):
        weights = jnp.exp((scores + bias[...]) - top).astype(jnp.bfloat16)
        return top, dot_nn(values_t, weights)

    def finish(pair, top, mixed):
        total = mixed[LANES : LANES + 1]
        target, place = (early_ref, pair) if pair < split else (more_ref, pair - split)
        target[at(place), :] = own_heads(mixed, 1.0 / total).astype(jnp.bfloat16)
        lse_ref[pl.ds(pair, 1), :] = top + jnp.log(total)
        return ()

    over_pairs(pairs, (score, top, weigh, finish), LAGS, arrive)
    put_terms(sent_ref.at[pl.ds(half, EXTRA)], three_terms(lse_ref[...]))
    for copy in rest:
        copy.wait()


def late_kernel(
    rows, offsets_hbm, weight_hbm, q_ref, k_ref, v_ref, early_ref, both_ref, next_ref, weight_ref,
    offsets_ref, own_bias, other_bias, own, other, sems,
):
    offsets_copy = load(offsets_hbm, offsets_ref, sems.at[8])
    block = weight_ref.shape[0] // 8
    copies = []
    for i in range(8):
        place = pl.ds(i * block, block)
        copies.append(load(weight_hbm.at[place], weight_ref.at[place], sems.at[i]))
    half = q_ref.shape[0]
    key = lax.broadcasted_iota(jnp.int32, own.shape, 0)
    query = lax.broadcasted_iota(jnp.int32, own.shape, 1) % half
    own[...] = jnp.where(key <= query, 1.0, 0.0).astype(jnp.bfloat16)
    other[...] = jnp.where(key <= query, 0.0, 1.0).astype(jnp.bfloat16)
    pooling = pool_matrix(half)
    molecules = half // POOL
    features = early_ref.shape[0]
    both_ref[pl.ds(0, features), :] = early_ref[...]
    pairs = k_ref.shape[1] // LANES
    offsets_copy.wait()
    start = lax.axis_index("seq") * rows
    own_bias[...] = mask_bias(offsets_ref, start + half, start + half, lambda key, query: key <= query)
    other_bias[...] = mask_bias(offsets_ref, start + half, start, lambda key, query: key > query)
    next_ref[...] = mask_bias(offsets_ref, start + rows, start + half, lambda key, query: key > query)
    parts = []

    def score(pair):
        scores = dot_nt(k_ref[:, at(pair)], split_heads(q_ref[:, at(pair)]))
        return scores, with_ones(jnp.transpose(v_ref[:, at(pair)]))

    def top(pair, scores, values_t):
        scores = jnp.maximum(scores[:half] + other_bias[...], scores[half:] + own_bias[...])
        return scores, tops(scores), values_t

    def weigh(pair, scores, top, values_t):
        weights = jnp.exp(scores - top).astype(jnp.bfloat16)
        weights = jnp.concatenate([weights * other[...], weights * own[...]], axis=0)
        return (dot_nn(values_t, weights),)

    def finish(pair, mixed):
        inverse = 1.0 / mixed[LANES : LANES + 1]
        parts.append(own_heads(mixed, inverse).astype(jnp.bfloat16))
        if len(parts) == 4:
            pooled = dot_nt(pooling, jnp.concatenate(parts, axis=0)).astype(jnp.bfloat16)
            for i in range(4):
                place = features + (pair - 3 + i) * molecules
                both_ref[pl.ds(place, molecules), :] = pooled[:, i * LANES : (i + 1) * LANES]
            parts.clear()
        return ()

    over_pairs(pairs, (score, top, weigh, finish), LAGS, lambda pair: None)
    for copy in copies:
        copy.wait()


def halo_kernel(q_ref, k_ref, v_ref, bias, after_ref, out_ref, lse_ref, share_ref):
    half = bias.shape[0]
    molecules = half // POOL
    tail = pl.ds(half, half)
    pooling = pool_matrix(half)
    pairs = k_ref.shape[1] // LANES
    parts = []
    lse_ref[...] = get_terms(q_ref.at[pl.ds(half, EXTRA)], pairs, 3)

    def score(pair):
        queries = split_heads(q_ref[pl.ds(0, half), at(pair)])
        scores = dot_nt(k_ref[tail, at(pair)], queries)
        return scores, with_ones(jnp.transpose(v_ref[tail, at(pair)]))

    def top(pair, scores, values_t):
        lse = lse_ref[pl.ds(pair, 1), :]
        return scores, jnp.maximum(tops(scores + bias[...]), lse), lse, values_t

    def weigh(pair, scores, top, lse, values_t):
        weights = jnp.exp((scores + bias[...]) - top).astype(jnp.bfloat16)
        mixed = dot_nn(values_t, weights)
        return mixed, jnp.exp(lse - top)

    def finish(pair, mixed, kept):
        inverse = 1.0 / (mixed[LANES : LANES + 1] + kept)
        parts.append(own_heads(mixed, inverse).astype(jnp.bfloat16))
        if len(parts) == 4:
            pooled = dot_nt(pooling, jnp.concatenate(parts, axis=0)).astype(jnp.bfloat16)
            out_ref[pl.ds(0, molecules), pl.ds((pair - 3) * LANES, 4 * LANES)] = pooled
            parts.clear()
        share_ref[pl.ds(pair, 1), :] = kept * inverse
        return ()

    over_pairs(pairs, (score, top, weigh, finish), LAGS, lambda pair: None)
    share = share_ref[...]
    high = share.astype(jnp.bfloat16).astype(jnp.float32)
    put_terms(out_ref.at[pl.ds(molecules, EXTRA)], [high, share - high])


def back_kernel(
    slot_ref, cotangent_ref, weight_ref, gain_ref, stashed_ref, after_ref, dinput_ref, term_ref, grad, held_ref
):
    held = stashed_ref[0]
    for i in range(1, stashed_ref.shape[0]):
        held = jnp.where(slot_ref[0:1, 0:1] == i, stashed_ref[i].astype(jnp.float32), held.astype(jnp.float32))
    held_ref[...] = held.astype(jnp.bfloat16)
    features = weight_ref.shape[0]
    block = 512
    for begin in range(0, features, block):
        columns = pl.ds(begin, block)
        grad[:, columns] = dot_nt(cotangent_ref[...], weight_ref[columns, :])
    held = held_ref[...].astype(jnp.float32)
    inv_rms = lax.rsqrt(jnp.sum(held * held, axis=1, keepdims=True) / features + EPS_NORM)
    along = jnp.zeros_like(inv_rms)
    for begin in range(0, features, block):
        columns = pl.ds(begin, block)
        product = grad[:, columns] * (held_ref[:, columns].astype(jnp.float32) * inv_rms)
        term_ref[:, columns] = jnp.sum(product, axis=0, keepdims=True)
        along += jnp.sum(product * gain_ref[:, columns], axis=1, keepdims=True)
    along = along / features
    for begin in range(0, features, block):
        columns = pl.ds(begin, block)
        whitened = held_ref[:, columns].astype(jnp.float32) * inv_rms
        scaled = grad[:, columns] * gain_ref[:, columns]
        dinput_ref[:, columns] = (inv_rms * (scaled - whitened * along)).astype(jnp.bfloat16)


def project_kernel(
    early_ref, both_ref, halo_ref, gain_ref, weight_ref, term_ref, other_ref, upstream_hbm,
    out_ref, update_ref, passed_hbm, share_ref, sem,
):
    passing = load(upstream_hbm, passed_hbm, sem)
    half = both_ref.shape[1]
    features = gain_ref.shape[1]
    first_part = early_ref.shape[0]
    molecules = half // POOL
    pooling = pool_matrix(half)
    first = lax.axis_index("seq") == 0
    shares = get_terms(halo_ref.at[pl.ds(molecules, EXTRA)], features // LANES, 2)
    share_ref[...] = jnp.where(first, 1.0, shares)
    squares, product, parts = 0.0, 0.0, []
    for pair in range(features // LANES):
        share_a = share_ref[pl.ds(pair, 1), pl.ds(0, half)]
        share_b = share_ref[pl.ds(pair, 1), pl.ds(half, half)]
        begin = pair * LANES
        if begin < first_part:
            early = early_ref[pl.ds(begin, LANES), :].astype(jnp.float32)
        else:
            early = both_ref[pl.ds(begin - first_part, LANES), :].astype(jnp.float32)
        parts += [early[:HEAD_DIM] * share_a, early[HEAD_DIM:] * share_b]
        if len(parts) == 8:
            columns = pl.ds((pair - 3) * LANES, 4 * LANES)
            mean = dot_nt(pooling, jnp.concatenate(parts, axis=0).astype(jnp.bfloat16))
            upper = mean + halo_ref[:molecules, columns].astype(jnp.float32)
            place = features - first_part + (pair - 3) * molecules
            lower = [both_ref[pl.ds(place + i * molecules, molecules), :] for i in range(4)]
            lower = jnp.concatenate(lower, axis=1)
            arrived = jnp.concatenate([upper.astype(jnp.bfloat16), lower], axis=0).astype(jnp.float32)
            squares += jnp.sum(arrived * arrived, axis=1, keepdims=True)
            scaled = (arrived * gain_ref[:, columns]).astype(jnp.bfloat16)
            product += dot_nn(scaled, weight_ref[columns, :])
            parts = []
    out_ref[...] = (product * lax.rsqrt(squares / features + EPS_NORM)).astype(jnp.bfloat16)
    total = term_ref[...] + other_ref[...]
    mean = jnp.sum(total * total, axis=1, keepdims=True) / features
    update_ref[...] = total / jnp.sqrt(mean + EPS_STEP)
    passing.wait()


def cost(flops, read, exps=0):
    return pl.CostEstimate(flops=flops, bytes_accessed=read, transcendentals=exps)


SMEM = pl.BlockSpec(memory_space=pltpu.SMEM)
HBM = pl.BlockSpec(memory_space=pltpu.HBM)
ANY = pl.BlockSpec(memory_space=pl.ANY)
VMEM = pl.BlockSpec(memory_space=pltpu.VMEM)


def in_hbm(*arrays):
    return [pltpu.with_memory_space_constraint(x, pltpu.HBM) for x in arrays]


def params():
    return pltpu.CompilerParams(vmem_limit_bytes=24 * 2**20)


def attend_early(queries, keys, values, offsets, cotangent, stashed, chunks):
    rows, width = queries.shape
    half = rows // 2
    soon = width // (4 * LANES) * 3 // 4 * 4 * LANES
    bf16 = lambda *shape: jax.ShapeDtypeStruct(shape, jnp.bfloat16)
    return pl.pallas_call(
        functools.partial(early_kernel, rows, chunks),
        in_specs=[HBM] * 6,
        out_specs=[VMEM] * 8,
        out_shape=[
            bf16(half + EXTRA, width),
            bf16(soon, half),
            bf16(width - soon, half),
            bf16(half, width),
            bf16(rows, width),
            bf16(rows, width),
            bf16(*cotangent.shape),
            bf16(*stashed.shape),
        ],
        scratch_shapes=[
            pltpu.SMEM(offsets.shape, jnp.int32),
            pltpu.VMEM((half, 2 * half), jnp.float32),
            pltpu.VMEM((width // LANES, rows), jnp.float32),
            pltpu.SemaphoreType.DMA((3, chunks)),
            pltpu.SemaphoreType.DMA((6,)),
        ],
        cost_estimate=cost(4 * half * half * width, 6 * rows * width, half * half * width // 64),
        compiler_params=params(),
        name="attend_early",
    )(*in_hbm(offsets, queries, keys, values, cotangent, stashed))


def attend_late(queries, keys, values, offsets, weight, early):
    half, width = queries.shape
    rows = 2 * half
    return pl.pallas_call(
        functools.partial(late_kernel, rows),
        in_specs=[HBM] * 2 + [VMEM] * 4,
        out_specs=[VMEM] * 3,
        out_shape=[
            jax.ShapeDtypeStruct((early.shape[0] + width // POOL, half), jnp.bfloat16),
            jax.ShapeDtypeStruct((half, rows), jnp.float32),
            jax.ShapeDtypeStruct(weight.shape, weight.dtype),
        ],
        scratch_shapes=[
            pltpu.SMEM(offsets.shape, jnp.int32),
            pltpu.VMEM((half, rows), jnp.float32),
            pltpu.VMEM((half, rows), jnp.float32),
            pltpu.VMEM((half, rows), jnp.bfloat16),
            pltpu.VMEM((half, rows), jnp.bfloat16),
            pltpu.SemaphoreType.DMA((9,)),
        ],
        cost_estimate=cost(8 * half * half * width, 10 * half * width, half * half * width // 64),
        compiler_params=params(),
        name="attend_late",
    )(*in_hbm(offsets, weight), queries, keys, values, early)


def attend_halo(sent, keys, values, bias, after):
    half, width = bias.shape[0], keys.shape[1]
    return pl.pallas_call(
        halo_kernel,
        in_specs=[VMEM] * 4 + [ANY],
        out_specs=VMEM,
        out_shape=jax.ShapeDtypeStruct((half // POOL + EXTRA, width), jnp.bfloat16),
        scratch_shapes=[pltpu.VMEM((width // LANES, 2 * half), jnp.float32)] * 2,
        cost_estimate=cost(4 * half * half * width, 6 * half * width, half * half * width // 64),
        compiler_params=params(),
        name="attend_halo",
    )(sent, keys, values, bias, after)


def backward(slot, cotangent, weight, gain, stashed, after):
    rows, width = stashed.shape[1:]
    depth = weight.shape[1]
    return pl.pallas_call(
        back_kernel,
        in_specs=[VMEM] * 5 + [ANY],
        out_specs=[VMEM] * 2,
        scratch_shapes=[
            pltpu.VMEM((rows, width), jnp.float32),
            pltpu.VMEM((rows, width), jnp.bfloat16),
        ],
        out_shape=[
            jax.ShapeDtypeStruct((rows, width), jnp.bfloat16),
            jax.ShapeDtypeStruct((1, width), jnp.float32),
        ],
        cost_estimate=cost(2 * rows * width * depth, 2 * width * depth),
        compiler_params=params(),
        name="backward",
    )(slot, cotangent, weight, gain, stashed, after)


def project(early, both, halo, gain, weight, term, other, upstream):
    rows = upstream.shape[0]
    width, depth = weight.shape
    return pl.pallas_call(
        project_kernel,
        in_specs=[VMEM] * 7 + [ANY],
        out_specs=[VMEM, VMEM, HBM],
        out_shape=[
            jax.ShapeDtypeStruct((rows, depth), jnp.bfloat16),
            jax.ShapeDtypeStruct(term.shape, term.dtype),
            jax.ShapeDtypeStruct(upstream.shape, upstream.dtype),
        ],
        scratch_shapes=[
            pltpu.VMEM((width // LANES, 2 * WINDOW), jnp.float32),
            pltpu.SemaphoreType.DMA,
        ],
        cost_estimate=cost(2 * rows * width * depth, 2 * width * depth),
        compiler_params=params(),
        name="project",
    )(early, both, halo, gain, weight, term, other, upstream)


def swapped(value, axis, distance):
    return lax.ppermute(value, axis, [(i, i ^ distance) for i in range(lax.axis_size(axis))])


def sum_rounds():
    rounds = []
    for axis in ("rep", "seq"):
        count = lax.axis_size(axis)
        if count & (count - 1):
            return []
        rounds += [(axis, 1 << i) for i in range(count.bit_length() - 1)]
    return rounds if len(rounds) == 3 else []


def onward(value):
    sections, shards = lax.axis_size("section"), lax.axis_size("seq")
    route = [
        (s * shards + k, (s + 1) % sections * shards + k + 1)
        for s in range(sections)
        for k in range(shards - 1)
    ]
    return lax.ppermute(value, ("section", "seq"), route)


def local(queries, keys, values, doc_starts, weight, gain, stashed, cotangent, slot):
    queries, keys, values, offsets = queries[0, 0], keys[0, 0], values[0, 0], doc_starts[0]
    rounds = sum_rounds()

    def partner(term, index):
        return swapped(term, *rounds[index]) if rounds else jnp.zeros_like(term)

    sent, early, more, q_late, keys, values, cotangent, stashed = attend_early(
        queries, keys, values, offsets, cotangent[0, 0], stashed[0, 0], 4
    )
    arrived = shifted(sent, "seq", -1)
    early = passed_along(early, "section", 1)
    both, next_bias, weight = attend_late(q_late, keys, values, offsets, weight[0], more)
    slot = jnp.broadcast_to(slot, (1, LANES))
    dinput, term = backward(slot, cotangent, weight, gain, stashed, both)
    both = passed_along(both, "section", 1)
    upstream = passed_along(dinput, "section", -1)
    term = term if rounds else lax.psum(term, ("rep", "seq"))
    term = term + partner(term, 0)
    term = term + partner(term, 1)
    halo = onward(attend_halo(arrived, keys, values, next_bias, term))
    mol_keys, update, upstream = project(
        early, both, halo, gain, weight, term, partner(term, 2), upstream
    )
    return mol_keys[None, None], upstream[None, None], update


def solution(mesh):
    in_specs = (
        P("rep", "section", "seq", None),
        P("rep", "section", "seq", None),
        P("rep", "section", "seq", None),
        P("rep", "section", None),
        P("section", None, None),
        P("section", None),
        P("rep", "section", None, "seq", None),
        P("rep", "section", "seq", None),
        P("rep", "section"),
    )
    out_specs = (
        P("rep", "section", "seq", None),
        P("rep", "section", "seq", None),
        P("section", None),
    )
    return jax.shard_map(local, mesh=mesh, in_specs=in_specs, out_specs=out_specs, check_vma=False)
```

```python
import functools
import math

import jax
import jax.numpy as jnp
from jax import lax
from jax.experimental import pallas as pl
from jax.experimental.pallas import tpu as pltpu
from jax.sharding import PartitionSpec as P

HEAD_DIM = 64
POOL = 4
WINDOW = 128
LANES = 128
EPS_NORM = 1e-05
EPS_STEP = 1e-06
MASKED = -1e30
LAGS = (0, 2, 3, 4, 5)
EXTRA = 8

NT = (((1,), (1,)), ((), ()))


def dot_nt(a, b):
    return lax.dot_general(a, b, NT, preferred_element_type=jnp.float32)


def dot_nn(a, b):
    return jnp.dot(a, b, preferred_element_type=jnp.float32)


def shifted(value, axis, steps):
    count = lax.axis_size(axis)
    first, last = max(0, -steps), min(count, count - steps)
    return lax.ppermute(value, axis, [(i, i + steps) for i in range(first, last)])


def passed_along(value, axis, steps):
    count = lax.axis_size(axis)
    return lax.ppermute(value, axis, [(i, (i + steps) % count) for i in range(count)])


def earliest_key(offsets_ref, query_pos):
    start = jnp.zeros_like(query_pos)
    for d in range(offsets_ref.shape[1]):
        offset = offsets_ref[0, d]
        start = jnp.where(query_pos >= offset, offset, start)
    return jnp.maximum(start, query_pos - (WINDOW - 1))


def mask_bias(offsets_ref, query_start, key_start, keep):
    key = lax.broadcasted_iota(jnp.int32, (WINDOW, 2 * WINDOW), 0)
    query = lax.broadcasted_iota(jnp.int32, (WINDOW, 2 * WINDOW), 1) % WINDOW
    lane = lax.broadcasted_iota(jnp.int32, (1, 2 * WINDOW), 1) % WINDOW
    lowest = earliest_key(offsets_ref, query_start + lane)
    allowed = (key_start + key >= lowest) & keep(key, query)
    return jnp.where(allowed, 0.0, MASKED).astype(jnp.float32)


def split_heads(queries):
    lane = lax.broadcasted_iota(jnp.int32, (1, LANES), 1)
    scale = 1.0 / math.sqrt(HEAD_DIM)
    first = jnp.where(lane < HEAD_DIM, scale, 0.0).astype(jnp.bfloat16)
    second = jnp.where(lane < HEAD_DIM, 0.0, scale).astype(jnp.bfloat16)
    return jnp.concatenate([queries * first, queries * second], axis=0)


def pool_matrix(queries):
    molecule = lax.broadcasted_iota(jnp.int32, (queries // POOL, queries), 0)
    query = lax.broadcasted_iota(jnp.int32, (queries // POOL, queries), 1)
    return jnp.where(query // POOL == molecule, 1.0 / POOL, 0.0).astype(jnp.bfloat16)


def own_heads(mixed, scale):
    count = mixed.shape[1] // 2
    return jnp.concatenate(
        [
            mixed[:HEAD_DIM, :count] * scale[:, :count],
            mixed[HEAD_DIM:LANES, count:] * scale[:, count:],
        ],
        axis=0,
    )


def load(source, target, sem):
    copy = pltpu.make_async_copy(source, target, sem)
    copy.start()
    return copy


def load_chunks(arrays, chunks, sems):
    block = arrays[0][1].shape[1] // chunks
    return [
        [
            load(source.at[:, pl.ds(chunk * block, block)], target.at[:, pl.ds(chunk * block, block)], sems.at[i, chunk])
            for i, (source, target) in enumerate(arrays)
        ]
        for chunk in range(chunks)
    ]


def at(pair):
    return pl.ds(pair * LANES, LANES)


def over_pairs(pairs, stages, lags, before):
    results = {}
    for step in range(pairs + lags[-1]):
        if step < pairs:
            before(step)
        for stage, lag in zip(stages, lags):
            pair = step - lag
            if 0 <= pair < pairs:
                results[pair] = stage(pair, *results.get(pair, ()))


def tops(scores):
    rows = scores.shape[0]
    while rows > 8:
        rows //= 2
        scores = jnp.maximum(scores[:rows], scores[rows:])
    return jnp.max(scores, axis=0, keepdims=True)


def with_ones(values_t):
    return jnp.concatenate([values_t, jnp.ones((16, values_t.shape[1]), jnp.bfloat16)], axis=0)


def three_terms(value):
    high = value.astype(jnp.bfloat16).astype(jnp.float32)
    middle = (value - high).astype(jnp.bfloat16).astype(jnp.float32)
    return [high, middle, value - high - middle]


def early_kernel(
    rows, chunks, offsets_hbm, q_hbm, k_hbm, v_hbm, cotangent_hbm, stashed_hbm,
    sent_ref, early_ref, more_ref, q_late_ref, k_ref, v_ref, cotangent_ref, stashed_ref,
    offsets_ref, bias, sems, offsets_sem,
):
    half = rows // 2
    head, tail = pl.ds(0, half), pl.ds(half, half)
    offsets_copy = load(offsets_hbm, offsets_ref, offsets_sem.at[0])
    arrays = (
        (k_hbm.at[head], k_ref.at[head]),
        (q_hbm.at[head], sent_ref.at[head]),
        (v_hbm.at[head], v_ref.at[head]),
    )
    copies = load_chunks(arrays, chunks, sems)
    later = (
        (k_hbm.at[tail], k_ref.at[tail]),
        (v_hbm.at[tail], v_ref.at[tail]),
        (q_hbm.at[tail], q_late_ref),
        (cotangent_hbm, cotangent_ref),
        (stashed_hbm, stashed_ref),
    )
    rest = []
    offsets_copy.wait()
    start = lax.axis_index("seq") * rows
    bias[...] = mask_bias(offsets_ref, start, start, lambda key, query: key <= query)
    pairs = k_ref.shape[1] // LANES
    split = early_ref.shape[0] // LANES

    def arrive(pair):
        per_chunk = pairs // chunks
        if pair % per_chunk == 0:
            for copy in copies[pair // per_chunk]:
                copy.wait()
        if pair == per_chunk:
            for i, (source, target) in enumerate(later):
                rest.append(load(source, target, offsets_sem.at[i + 1]))

    def score(pair):
        scores = dot_nt(k_ref[head, at(pair)], split_heads(sent_ref[head, at(pair)]))
        return scores, with_ones(jnp.transpose(v_ref[head, at(pair)]))

    def top(pair, scores, values_t):
        return scores, tops(scores + bias[...]), values_t

    def weigh(pair, scores, top, values_t):
        return top, jnp.exp((scores + bias[...]) - top).astype(jnp.bfloat16), values_t

    def mix(pair, top, weights, values_t):
        return top, dot_nn(values_t, weights)

    def finish(pair, top, mixed):
        total = mixed[LANES : LANES + 1]
        target, place = (early_ref, pair) if pair < split else (more_ref, pair - split)
        target[at(place), :] = own_heads(mixed, 1.0 / total).astype(jnp.bfloat16)
        lse = top + jnp.log(total)
        terms = three_terms(lse[:, :half]) + three_terms(lse[:, half:])
        terms.append(jnp.zeros((EXTRA - 6, LANES), jnp.float32))
        sent_ref[pl.ds(half, EXTRA), at(pair)] = jnp.concatenate(terms, axis=0).astype(jnp.bfloat16)
        return ()

    over_pairs(pairs, (score, top, weigh, mix, finish), LAGS, arrive)
    for copy in rest:
        copy.wait()


def late_kernel(
    rows, offsets_hbm, weight_hbm, q_ref, k_ref, v_ref, early_ref, both_ref, next_ref, weight_ref,
    offsets_ref, own_bias, other_bias, own, other, sems,
):
    offsets_copy = load(offsets_hbm, offsets_ref, sems.at[8])
    block = weight_ref.shape[0] // 8
    copies = []
    for i in range(8):
        place = pl.ds(i * block, block)
        copies.append(load(weight_hbm.at[place], weight_ref.at[place], sems.at[i]))
    half = q_ref.shape[0]
    key = lax.broadcasted_iota(jnp.int32, own.shape, 0)
    query = lax.broadcasted_iota(jnp.int32, own.shape, 1) % half
    own[...] = jnp.where(key <= query, 1.0, 0.0).astype(jnp.bfloat16)
    other[...] = jnp.where(key <= query, 0.0, 1.0).astype(jnp.bfloat16)
    pooling = pool_matrix(half)
    molecules = half // POOL
    features = early_ref.shape[0]
    both_ref[pl.ds(0, features), :] = early_ref[...]
    pairs = k_ref.shape[1] // LANES
    offsets_copy.wait()
    start = lax.axis_index("seq") * rows
    own_bias[...] = mask_bias(offsets_ref, start + half, start + half, lambda key, query: key <= query)
    other_bias[...] = mask_bias(offsets_ref, start + half, start, lambda key, query: key > query)
    next_ref[...] = mask_bias(offsets_ref, start + rows, start + half, lambda key, query: key > query)
    parts = []

    def score(pair):
        scores = dot_nt(k_ref[:, at(pair)], split_heads(q_ref[:, at(pair)]))
        return scores, with_ones(jnp.transpose(v_ref[:, at(pair)]))

    def top(pair, scores, values_t):
        scores = jnp.maximum(scores[:half] + other_bias[...], scores[half:] + own_bias[...])
        return scores, tops(scores), values_t

    def weigh(pair, scores, top, values_t):
        weights = jnp.exp(scores - top).astype(jnp.bfloat16)
        return jnp.concatenate([weights * other[...], weights * own[...]], axis=0), values_t

    def mix(pair, weights, values_t):
        return (dot_nn(values_t, weights),)

    def finish(pair, mixed):
        inverse = 1.0 / mixed[LANES : LANES + 1]
        parts.append(own_heads(mixed, inverse).astype(jnp.bfloat16))
        if len(parts) == 4:
            pooled = dot_nt(pooling, jnp.concatenate(parts, axis=0)).astype(jnp.bfloat16)
            for i in range(4):
                place = features + (pair - 3 + i) * molecules
                both_ref[pl.ds(place, molecules), :] = pooled[:, i * LANES : (i + 1) * LANES]
            parts.clear()
        return ()

    over_pairs(pairs, (score, top, weigh, mix, finish), LAGS, lambda pair: None)
    for copy in copies:
        copy.wait()


def halo_kernel(q_ref, k_ref, v_ref, bias, after_ref, out_ref):
    half = bias.shape[0]
    molecules = half // POOL
    tail = pl.ds(half, half)
    pooling = pool_matrix(half)
    pairs = k_ref.shape[1] // LANES
    parts = []

    def score(pair):
        queries = split_heads(q_ref[pl.ds(0, half), at(pair)])
        scores = dot_nt(k_ref[tail, at(pair)], queries)
        return scores, with_ones(jnp.transpose(v_ref[tail, at(pair)]))

    def top(pair, scores, values_t):
        terms = q_ref[pl.ds(half, EXTRA), at(pair)].astype(jnp.float32)
        lse = jnp.concatenate(
            [terms[0:1] + terms[1:2] + terms[2:3], terms[3:4] + terms[4:5] + terms[5:6]], axis=1
        )
        return scores, jnp.maximum(tops(scores + bias[...]), lse), lse, values_t

    def weigh(pair, scores, top, lse, values_t):
        weights = jnp.exp((scores + bias[...]) - top).astype(jnp.bfloat16)
        return weights, jnp.exp(lse - top), values_t

    def mix(pair, weights, kept, values_t):
        return dot_nn(values_t, weights), kept

    def finish(pair, mixed, kept):
        inverse = 1.0 / (mixed[LANES : LANES + 1] + kept)
        parts.append(own_heads(mixed, inverse).astype(jnp.bfloat16))
        if len(parts) == 4:
            pooled = dot_nt(pooling, jnp.concatenate(parts, axis=0)).astype(jnp.bfloat16)
            out_ref[pl.ds(0, molecules), pl.ds((pair - 3) * LANES, 4 * LANES)] = pooled
            parts.clear()
        share = kept * inverse
        high = share.astype(jnp.bfloat16).astype(jnp.float32)
        low = share - high
        shares = [high[:, :half], low[:, :half], high[:, half:], low[:, half:]]
        shares.append(jnp.zeros((EXTRA - 4, LANES), jnp.float32))
        out_ref[pl.ds(molecules, EXTRA), at(pair)] = jnp.concatenate(shares, axis=0).astype(jnp.bfloat16)
        return ()

    over_pairs(pairs, (score, top, weigh, mix, finish), LAGS, lambda pair: None)


def back_kernel(
    slot_ref, cotangent_ref, weight_ref, gain_ref, stashed_ref, after_ref, dinput_ref, term_ref, grad, held_ref
):
    held = stashed_ref[0]
    for i in range(1, stashed_ref.shape[0]):
        held = jnp.where(slot_ref[0:1, 0:1] == i, stashed_ref[i].astype(jnp.float32), held.astype(jnp.float32))
    held_ref[...] = held.astype(jnp.bfloat16)
    features = weight_ref.shape[0]
    block = 512
    for begin in range(0, features, block):
        columns = pl.ds(begin, block)
        grad[:, columns] = dot_nt(cotangent_ref[...], weight_ref[columns, :])
    held = held_ref[...].astype(jnp.float32)
    inv_rms = lax.rsqrt(jnp.sum(held * held, axis=1, keepdims=True) / features + EPS_NORM)
    along = jnp.zeros_like(inv_rms)
    for begin in range(0, features, block):
        columns = pl.ds(begin, block)
        product = grad[:, columns] * (held_ref[:, columns].astype(jnp.float32) * inv_rms)
        term_ref[:, columns] = jnp.sum(product, axis=0, keepdims=True)
        along += jnp.sum(product * gain_ref[:, columns], axis=1, keepdims=True)
    along = along / features
    for begin in range(0, features, block):
        columns = pl.ds(begin, block)
        whitened = held_ref[:, columns].astype(jnp.float32) * inv_rms
        scaled = grad[:, columns] * gain_ref[:, columns]
        dinput_ref[:, columns] = (inv_rms * (scaled - whitened * along)).astype(jnp.bfloat16)


def project_kernel(
    early_ref, both_ref, halo_ref, gain_ref, weight_ref, term_ref, other_ref, upstream_hbm,
    out_ref, update_ref, passed_hbm, sem,
):
    passing = load(upstream_hbm, passed_hbm, sem)
    half = both_ref.shape[1]
    features = gain_ref.shape[1]
    first_part = early_ref.shape[0]
    molecules = half // POOL
    pooling = pool_matrix(half)
    first = lax.axis_index("seq") == 0
    squares, product, parts = 0.0, 0.0, []
    for pair in range(features // LANES):
        shares = halo_ref[molecules:, at(pair)].astype(jnp.float32)
        share_a = jnp.where(first, 1.0, shares[0:1] + shares[1:2])
        share_b = jnp.where(first, 1.0, shares[2:3] + shares[3:4])
        begin = pair * LANES
        if begin < first_part:
            early = early_ref[pl.ds(begin, LANES), :].astype(jnp.float32)
        else:
            early = both_ref[pl.ds(begin - first_part, LANES), :].astype(jnp.float32)
        parts += [early[:HEAD_DIM] * share_a, early[HEAD_DIM:] * share_b]
        if len(parts) == 8:
            columns = pl.ds((pair - 3) * LANES, 4 * LANES)
            mean = dot_nt(pooling, jnp.concatenate(parts, axis=0).astype(jnp.bfloat16))
            upper = mean + halo_ref[:molecules, columns].astype(jnp.float32)
            place = features - first_part + (pair - 3) * molecules
            lower = [both_ref[pl.ds(place + i * molecules, molecules), :] for i in range(4)]
            lower = jnp.concatenate(lower, axis=1)
            arrived = jnp.concatenate([upper.astype(jnp.bfloat16), lower], axis=0).astype(jnp.float32)
            squares += jnp.sum(arrived * arrived, axis=1, keepdims=True)
            scaled = (arrived * gain_ref[:, columns]).astype(jnp.bfloat16)
            product += dot_nn(scaled, weight_ref[columns, :])
            parts = []
    out_ref[...] = (product * lax.rsqrt(squares / features + EPS_NORM)).astype(jnp.bfloat16)
    total = term_ref[...] + other_ref[...]
    mean = jnp.sum(total * total, axis=1, keepdims=True) / features
    update_ref[...] = total / jnp.sqrt(mean + EPS_STEP)
    passing.wait()


def cost(flops, read, exps=0):
    return pl.CostEstimate(flops=flops, bytes_accessed=read, transcendentals=exps)


SMEM = pl.BlockSpec(memory_space=pltpu.SMEM)
HBM = pl.BlockSpec(memory_space=pltpu.HBM)
ANY = pl.BlockSpec(memory_space=pl.ANY)
VMEM = pl.BlockSpec(memory_space=pltpu.VMEM)


def in_hbm(*arrays):
    return [pltpu.with_memory_space_constraint(x, pltpu.HBM) for x in arrays]


def params():
    return pltpu.CompilerParams(vmem_limit_bytes=24 * 2**20)


def attend_early(queries, keys, values, offsets, cotangent, stashed, chunks):
    rows, width = queries.shape
    half = rows // 2
    soon = width // (4 * LANES) * 3 // 4 * 4 * LANES
    bf16 = lambda *shape: jax.ShapeDtypeStruct(shape, jnp.bfloat16)
    return pl.pallas_call(
        functools.partial(early_kernel, rows, chunks),
        in_specs=[HBM] * 6,
        out_specs=[VMEM] * 8,
        out_shape=[
            bf16(half + EXTRA, width),
            bf16(soon, half),
            bf16(width - soon, half),
            bf16(half, width),
            bf16(rows, width),
            bf16(rows, width),
            bf16(*cotangent.shape),
            bf16(*stashed.shape),
        ],
        scratch_shapes=[
            pltpu.SMEM(offsets.shape, jnp.int32),
            pltpu.VMEM((half, 2 * half), jnp.float32),
            pltpu.SemaphoreType.DMA((3, chunks)),
            pltpu.SemaphoreType.DMA((6,)),
        ],
        cost_estimate=cost(4 * half * half * width, 6 * rows * width, half * half * width // 64),
        compiler_params=params(),
        name="attend_early",
    )(*in_hbm(offsets, queries, keys, values, cotangent, stashed))


def attend_late(queries, keys, values, offsets, weight, early):
    half, width = queries.shape
    rows = 2 * half
    return pl.pallas_call(
        functools.partial(late_kernel, rows),
        in_specs=[HBM] * 2 + [VMEM] * 4,
        out_specs=[VMEM] * 3,
        out_shape=[
            jax.ShapeDtypeStruct((early.shape[0] + width // POOL, half), jnp.bfloat16),
            jax.ShapeDtypeStruct((half, rows), jnp.float32),
            jax.ShapeDtypeStruct(weight.shape, weight.dtype),
        ],
        scratch_shapes=[
            pltpu.SMEM(offsets.shape, jnp.int32),
            pltpu.VMEM((half, rows), jnp.float32),
            pltpu.VMEM((half, rows), jnp.float32),
            pltpu.VMEM((half, rows), jnp.bfloat16),
            pltpu.VMEM((half, rows), jnp.bfloat16),
            pltpu.SemaphoreType.DMA((9,)),
        ],
        cost_estimate=cost(8 * half * half * width, 10 * half * width, half * half * width // 64),
        compiler_params=params(),
        name="attend_late",
    )(*in_hbm(offsets, weight), queries, keys, values, early)


def attend_halo(sent, keys, values, bias, after):
    half, width = bias.shape[0], keys.shape[1]
    return pl.pallas_call(
        halo_kernel,
        in_specs=[VMEM] * 4 + [ANY],
        out_specs=VMEM,
        out_shape=jax.ShapeDtypeStruct((half // POOL + EXTRA, width), jnp.bfloat16),
        cost_estimate=cost(4 * half * half * width, 6 * half * width, half * half * width // 64),
        compiler_params=params(),
        name="attend_halo",
    )(sent, keys, values, bias, after)


def backward(slot, cotangent, weight, gain, stashed, after):
    rows, width = stashed.shape[1:]
    depth = weight.shape[1]
    return pl.pallas_call(
        back_kernel,
        in_specs=[VMEM] * 5 + [ANY],
        out_specs=[VMEM] * 2,
        scratch_shapes=[
            pltpu.VMEM((rows, width), jnp.float32),
            pltpu.VMEM((rows, width), jnp.bfloat16),
        ],
        out_shape=[
            jax.ShapeDtypeStruct((rows, width), jnp.bfloat16),
            jax.ShapeDtypeStruct((1, width), jnp.float32),
        ],
        cost_estimate=cost(2 * rows * width * depth, 2 * width * depth),
        compiler_params=params(),
        name="backward",
    )(slot, cotangent, weight, gain, stashed, after)


def project(early, both, halo, gain, weight, term, other, upstream):
    rows = upstream.shape[0]
    width, depth = weight.shape
    return pl.pallas_call(
        project_kernel,
        in_specs=[VMEM] * 7 + [ANY],
        out_specs=[VMEM, VMEM, HBM],
        out_shape=[
            jax.ShapeDtypeStruct((rows, depth), jnp.bfloat16),
            jax.ShapeDtypeStruct(term.shape, term.dtype),
            jax.ShapeDtypeStruct(upstream.shape, upstream.dtype),
        ],
        scratch_shapes=[pltpu.SemaphoreType.DMA],
        cost_estimate=cost(2 * rows * width * depth, 2 * width * depth),
        compiler_params=params(),
        name="project",
    )(early, both, halo, gain, weight, term, other, upstream)


def swapped(value, axis, distance):
    return lax.ppermute(value, axis, [(i, i ^ distance) for i in range(lax.axis_size(axis))])


def sum_rounds():
    rounds = []
    for axis in ("rep", "seq"):
        count = lax.axis_size(axis)
        if count & (count - 1):
            return []
        rounds += [(axis, 1 << i) for i in range(count.bit_length() - 1)]
    return rounds if len(rounds) == 3 else []


def onward(value):
    sections, shards = lax.axis_size("section"), lax.axis_size("seq")
    route = [
        (s * shards + k, (s + 1) % sections * shards + k + 1)
        for s in range(sections)
        for k in range(shards - 1)
    ]
    return lax.ppermute(value, ("section", "seq"), route)


def local(queries, keys, values, doc_starts, weight, gain, stashed, cotangent, slot):
    queries, keys, values, offsets = queries[0, 0], keys[0, 0], values[0, 0], doc_starts[0]
    rounds = sum_rounds()

    def partner(term, index):
        return swapped(term, *rounds[index]) if rounds else jnp.zeros_like(term)

    sent, early, more, q_late, keys, values, cotangent, stashed = attend_early(
        queries, keys, values, offsets, cotangent[0, 0], stashed[0, 0], 4
    )
    arrived = shifted(sent, "seq", -1)
    early = passed_along(early, "section", 1)
    both, next_bias, weight = attend_late(q_late, keys, values, offsets, weight[0], more)
    slot = jnp.broadcast_to(slot, (1, LANES))
    dinput, term = backward(slot, cotangent, weight, gain, stashed, both)
    both = passed_along(both, "section", 1)
    upstream = passed_along(dinput, "section", -1)
    term = term if rounds else lax.psum(term, ("rep", "seq"))
    term = term + partner(term, 0)
    term = term + partner(term, 1)
    halo = onward(attend_halo(arrived, keys, values, next_bias, term))
    mol_keys, update, upstream = project(
        early, both, halo, gain, weight, term, partner(term, 2), upstream
    )
    return mol_keys[None, None], upstream[None, None], update


def solution(mesh):
    in_specs = (
        P("rep", "section", "seq", None),
        P("rep", "section", "seq", None),
        P("rep", "section", "seq", None),
        P("rep", "section", None),
        P("section", None, None),
        P("section", None),
        P("rep", "section", None, "seq", None),
        P("rep", "section", "seq", None),
        P("rep", "section"),
    )
    out_specs = (
        P("rep", "section", "seq", None),
        P("rep", "section", "seq", None),
        P("section", None),
    )
    return jax.shard_map(local, mesh=mesh, in_specs=in_specs, out_specs=out_specs, check_vma=False)
```

```python
import functools
import math

import jax
import jax.numpy as jnp
from jax import lax
from jax.experimental import pallas as pl
from jax.experimental.pallas import tpu as pltpu
from jax.sharding import PartitionSpec as P

HEAD_DIM = 64
POOL = 4
WINDOW = 128
LANES = 128
EPS_NORM = 1e-05
EPS_STEP = 1e-06
MASKED = -1e30
LAGS = (0, 3, 5, 6, 8)
EXTRA = 8

NT = (((1,), (1,)), ((), ()))


def dot_nt(a, b):
    return lax.dot_general(a, b, NT, preferred_element_type=jnp.float32)


def dot_nn(a, b):
    return jnp.dot(a, b, preferred_element_type=jnp.float32)


def shifted(value, axis, steps):
    count = lax.axis_size(axis)
    first, last = max(0, -steps), min(count, count - steps)
    return lax.ppermute(value, axis, [(i, i + steps) for i in range(first, last)])


def passed_along(value, axis, steps):
    count = lax.axis_size(axis)
    return lax.ppermute(value, axis, [(i, (i + steps) % count) for i in range(count)])


def earliest_key(offsets_ref, query_pos):
    start = jnp.zeros_like(query_pos)
    for d in range(offsets_ref.shape[1]):
        offset = offsets_ref[0, d]
        start = jnp.where(query_pos >= offset, offset, start)
    return jnp.maximum(start, query_pos - (WINDOW - 1))


def mask_bias(offsets_ref, query_start, key_start, keep):
    key = lax.broadcasted_iota(jnp.int32, (WINDOW, 2 * WINDOW), 0)
    query = lax.broadcasted_iota(jnp.int32, (WINDOW, 2 * WINDOW), 1) % WINDOW
    lane = lax.broadcasted_iota(jnp.int32, (1, 2 * WINDOW), 1) % WINDOW
    lowest = earliest_key(offsets_ref, query_start + lane)
    allowed = (key_start + key >= lowest) & keep(key, query)
    return jnp.where(allowed, 0.0, MASKED).astype(jnp.float32)


def split_heads(queries):
    lane = lax.broadcasted_iota(jnp.int32, (1, LANES), 1)
    scale = 1.0 / math.sqrt(HEAD_DIM)
    first = jnp.where(lane < HEAD_DIM, scale, 0.0).astype(jnp.bfloat16)
    second = jnp.where(lane < HEAD_DIM, 0.0, scale).astype(jnp.bfloat16)
    return jnp.concatenate([queries * first, queries * second], axis=0)


def pool_matrix(queries):
    molecule = lax.broadcasted_iota(jnp.int32, (queries // POOL, queries), 0)
    query = lax.broadcasted_iota(jnp.int32, (queries // POOL, queries), 1)
    return jnp.where(query // POOL == molecule, 1.0 / POOL, 0.0).astype(jnp.bfloat16)


def own_heads(mixed, scale):
    count = mixed.shape[1] // 2
    return jnp.concatenate(
        [
            mixed[:HEAD_DIM, :count] * scale[:, :count],
            mixed[HEAD_DIM:LANES, count:] * scale[:, count:],
        ],
        axis=0,
    )


def load(source, target, sem):
    copy = pltpu.make_async_copy(source, target, sem)
    copy.start()
    return copy


def load_chunks(arrays, chunks, sems):
    block = arrays[0][1].shape[1] // chunks
    return [
        [
            load(source.at[:, pl.ds(chunk * block, block)], target.at[:, pl.ds(chunk * block, block)], sems.at[i, chunk])
            for i, (source, target) in enumerate(arrays)
        ]
        for chunk in range(chunks)
    ]


def at(pair):
    return pl.ds(pair * LANES, LANES)


def over_pairs(pairs, stages, lags, before):
    results = {}
    for step in range(pairs + lags[-1]):
        if step < pairs:
            before(step)
        for stage, lag in zip(stages, lags):
            pair = step - lag
            if 0 <= pair < pairs:
                results[pair] = stage(pair, *results.get(pair, ()))


def tops(scores):
    rows = scores.shape[0]
    while rows > 8:
        rows //= 2
        scores = jnp.maximum(scores[:rows], scores[rows:])
    return jnp.max(scores, axis=0, keepdims=True)


def with_ones(values_t):
    return jnp.concatenate([values_t, jnp.ones((16, values_t.shape[1]), jnp.bfloat16)], axis=0)


def three_terms(value):
    high = value.astype(jnp.bfloat16).astype(jnp.float32)
    middle = (value - high).astype(jnp.bfloat16).astype(jnp.float32)
    return [high, middle, value - high - middle]


def early_kernel(
    rows, chunks, offsets_hbm, q_hbm, k_hbm, v_hbm, cotangent_hbm, stashed_hbm,
    sent_ref, early_ref, more_ref, q_late_ref, k_ref, v_ref, cotangent_ref, stashed_ref,
    offsets_ref, bias, sems, offsets_sem,
):
    half = rows // 2
    head, tail = pl.ds(0, half), pl.ds(half, half)
    offsets_copy = load(offsets_hbm, offsets_ref, offsets_sem.at[0])
    arrays = (
        (k_hbm.at[head], k_ref.at[head]),
        (q_hbm.at[head], sent_ref.at[head]),
        (v_hbm.at[head], v_ref.at[head]),
    )
    copies = load_chunks(arrays, chunks, sems)
    later = (
        (k_hbm.at[tail], k_ref.at[tail]),
        (v_hbm.at[tail], v_ref.at[tail]),
        (q_hbm.at[tail], q_late_ref),
        (cotangent_hbm, cotangent_ref),
        (stashed_hbm, stashed_ref),
    )
    rest = []
    offsets_copy.wait()
    start = lax.axis_index("seq") * rows
    bias[...] = mask_bias(offsets_ref, start, start, lambda key, query: key <= query)
    pairs = k_ref.shape[1] // LANES
    split = early_ref.shape[0] // LANES

    def arrive(pair):
        per_chunk = pairs // chunks
        if pair % per_chunk == 0:
            for copy in copies[pair // per_chunk]:
                copy.wait()
        if pair == per_chunk:
            for i, (source, target) in enumerate(later):
                rest.append(load(source, target, offsets_sem.at[i + 1]))

    def score(pair):
        scores = dot_nt(k_ref[head, at(pair)], split_heads(sent_ref[head, at(pair)]))
        return scores, with_ones(jnp.transpose(v_ref[head, at(pair)]))

    def top(pair, scores, values_t):
        return scores, tops(scores + bias[...]), values_t

    def weigh(pair, scores, top, values_t):
        return top, jnp.exp((scores + bias[...]) - top).astype(jnp.bfloat16), values_t

    def mix(pair, top, weights, values_t):
        return top, dot_nn(values_t, weights)

    def finish(pair, top, mixed):
        total = mixed[LANES : LANES + 1]
        target, place = (early_ref, pair) if pair < split else (more_ref, pair - split)
        target[at(place), :] = own_heads(mixed, 1.0 / total).astype(jnp.bfloat16)
        lse = top + jnp.log(total)
        terms = three_terms(lse[:, :half]) + three_terms(lse[:, half:])
        terms.append(jnp.zeros((EXTRA - 6, LANES), jnp.float32))
        sent_ref[pl.ds(half, EXTRA), at(pair)] = jnp.concatenate(terms, axis=0).astype(jnp.bfloat16)
        return ()

    over_pairs(pairs, (score, top, weigh, mix, finish), LAGS, arrive)
    for copy in rest:
        copy.wait()


def late_kernel(
    rows, offsets_hbm, weight_hbm, q_ref, k_ref, v_ref, early_ref, both_ref, next_ref, weight_ref,
    offsets_ref, own_bias, other_bias, own, other, sems,
):
    offsets_copy = load(offsets_hbm, offsets_ref, sems.at[8])
    block = weight_ref.shape[0] // 8
    copies = []
    for i in range(8):
        place = pl.ds(i * block, block)
        copies.append(load(weight_hbm.at[place], weight_ref.at[place], sems.at[i]))
    half = q_ref.shape[0]
    key = lax.broadcasted_iota(jnp.int32, own.shape, 0)
    query = lax.broadcasted_iota(jnp.int32, own.shape, 1) % half
    own[...] = jnp.where(key <= query, 1.0, 0.0).astype(jnp.bfloat16)
    other[...] = jnp.where(key <= query, 0.0, 1.0).astype(jnp.bfloat16)
    pooling = pool_matrix(half)
    molecules = half // POOL
    features = early_ref.shape[0]
    both_ref[pl.ds(0, features), :] = early_ref[...]
    pairs = k_ref.shape[1] // LANES
    offsets_copy.wait()
    start = lax.axis_index("seq") * rows
    own_bias[...] = mask_bias(offsets_ref, start + half, start + half, lambda key, query: key <= query)
    other_bias[...] = mask_bias(offsets_ref, start + half, start, lambda key, query: key > query)
    next_ref[...] = mask_bias(offsets_ref, start + rows, start + half, lambda key, query: key > query)
    parts = []

    def score(pair):
        scores = dot_nt(k_ref[:, at(pair)], split_heads(q_ref[:, at(pair)]))
        return scores, with_ones(jnp.transpose(v_ref[:, at(pair)]))

    def top(pair, scores, values_t):
        scores = jnp.maximum(scores[:half] + other_bias[...], scores[half:] + own_bias[...])
        return scores, tops(scores), values_t

    def weigh(pair, scores, top, values_t):
        weights = jnp.exp(scores - top).astype(jnp.bfloat16)
        return jnp.concatenate([weights * other[...], weights * own[...]], axis=0), values_t

    def mix(pair, weights, values_t):
        return (dot_nn(values_t, weights),)

    def finish(pair, mixed):
        inverse = 1.0 / mixed[LANES : LANES + 1]
        parts.append(own_heads(mixed, inverse).astype(jnp.bfloat16))
        if len(parts) == 4:
            pooled = dot_nt(pooling, jnp.concatenate(parts, axis=0)).astype(jnp.bfloat16)
            for i in range(4):
                place = features + (pair - 3 + i) * molecules
                both_ref[pl.ds(place, molecules), :] = pooled[:, i * LANES : (i + 1) * LANES]
            parts.clear()
        return ()

    over_pairs(pairs, (score, top, weigh, mix, finish), LAGS, lambda pair: None)
    for copy in copies:
        copy.wait()


def halo_kernel(q_ref, k_ref, v_ref, bias, after_ref, out_ref):
    half = bias.shape[0]
    molecules = half // POOL
    tail = pl.ds(half, half)
    pooling = pool_matrix(half)
    pairs = k_ref.shape[1] // LANES
    parts = []

    def score(pair):
        queries = split_heads(q_ref[pl.ds(0, half), at(pair)])
        scores = dot_nt(k_ref[tail, at(pair)], queries)
        return scores, with_ones(jnp.transpose(v_ref[tail, at(pair)]))

    def top(pair, scores, values_t):
        terms = q_ref[pl.ds(half, EXTRA), at(pair)].astype(jnp.float32)
        lse = jnp.concatenate(
            [terms[0:1] + terms[1:2] + terms[2:3], terms[3:4] + terms[4:5] + terms[5:6]], axis=1
        )
        return scores, jnp.maximum(tops(scores + bias[...]), lse), lse, values_t

    def weigh(pair, scores, top, lse, values_t):
        weights = jnp.exp((scores + bias[...]) - top).astype(jnp.bfloat16)
        return weights, jnp.exp(lse - top), values_t

    def mix(pair, weights, kept, values_t):
        return dot_nn(values_t, weights), kept

    def finish(pair, mixed, kept):
        inverse = 1.0 / (mixed[LANES : LANES + 1] + kept)
        parts.append(own_heads(mixed, inverse).astype(jnp.bfloat16))
        if len(parts) == 4:
            pooled = dot_nt(pooling, jnp.concatenate(parts, axis=0)).astype(jnp.bfloat16)
            out_ref[pl.ds(0, molecules), pl.ds((pair - 3) * LANES, 4 * LANES)] = pooled
            parts.clear()
        share = kept * inverse
        high = share.astype(jnp.bfloat16).astype(jnp.float32)
        low = share - high
        shares = [high[:, :half], low[:, :half], high[:, half:], low[:, half:]]
        shares.append(jnp.zeros((EXTRA - 4, LANES), jnp.float32))
        out_ref[pl.ds(molecules, EXTRA), at(pair)] = jnp.concatenate(shares, axis=0).astype(jnp.bfloat16)
        return ()

    over_pairs(pairs, (score, top, weigh, mix, finish), LAGS, lambda pair: None)


def back_kernel(
    slot_ref, cotangent_ref, weight_ref, gain_ref, stashed_ref, after_ref, dinput_ref, term_ref, grad, held_ref
):
    held = stashed_ref[0]
    for i in range(1, stashed_ref.shape[0]):
        held = jnp.where(slot_ref[0:1, 0:1] == i, stashed_ref[i].astype(jnp.float32), held.astype(jnp.float32))
    held_ref[...] = held.astype(jnp.bfloat16)
    features = weight_ref.shape[0]
    block = 512
    for begin in range(0, features, block):
        columns = pl.ds(begin, block)
        grad[:, columns] = dot_nt(cotangent_ref[...], weight_ref[columns, :])
    held = held_ref[...].astype(jnp.float32)
    inv_rms = lax.rsqrt(jnp.sum(held * held, axis=1, keepdims=True) / features + EPS_NORM)
    along = jnp.zeros_like(inv_rms)
    for begin in range(0, features, block):
        columns = pl.ds(begin, block)
        product = grad[:, columns] * (held_ref[:, columns].astype(jnp.float32) * inv_rms)
        term_ref[:, columns] = jnp.sum(product, axis=0, keepdims=True)
        along += jnp.sum(product * gain_ref[:, columns], axis=1, keepdims=True)
    along = along / features
    for begin in range(0, features, block):
        columns = pl.ds(begin, block)
        whitened = held_ref[:, columns].astype(jnp.float32) * inv_rms
        scaled = grad[:, columns] * gain_ref[:, columns]
        dinput_ref[:, columns] = (inv_rms * (scaled - whitened * along)).astype(jnp.bfloat16)


def project_kernel(
    early_ref, both_ref, halo_ref, gain_ref, weight_ref, term_ref, other_ref, upstream_hbm,
    out_ref, update_ref, passed_hbm, scaled_ref, sem,
):
    passing = load(upstream_hbm, passed_hbm, sem)
    half = both_ref.shape[1]
    features = gain_ref.shape[1]
    first_part = early_ref.shape[0]
    molecules = half // POOL
    pooling = pool_matrix(half)
    first = lax.axis_index("seq") == 0
    squares, parts = 0.0, []
    for pair in range(features // LANES):
        shares = halo_ref[molecules:, at(pair)].astype(jnp.float32)
        share_a = jnp.where(first, 1.0, shares[0:1] + shares[1:2])
        share_b = jnp.where(first, 1.0, shares[2:3] + shares[3:4])
        begin = pair * LANES
        if begin < first_part:
            early = early_ref[pl.ds(begin, LANES), :].astype(jnp.float32)
        else:
            early = both_ref[pl.ds(begin - first_part, LANES), :].astype(jnp.float32)
        parts += [early[:HEAD_DIM] * share_a, early[HEAD_DIM:] * share_b]
        if len(parts) == 8:
            columns = pl.ds((pair - 3) * LANES, 4 * LANES)
            mean = dot_nt(pooling, jnp.concatenate(parts, axis=0).astype(jnp.bfloat16))
            upper = mean + halo_ref[:molecules, columns].astype(jnp.float32)
            place = features - first_part + (pair - 3) * molecules
            lower = [both_ref[pl.ds(place + i * molecules, molecules), :] for i in range(4)]
            lower = jnp.concatenate(lower, axis=1)
            arrived = jnp.concatenate([upper.astype(jnp.bfloat16), lower], axis=0).astype(jnp.float32)
            squares += jnp.sum(arrived * arrived, axis=1, keepdims=True)
            scaled_ref[:, columns] = (arrived * gain_ref[:, columns]).astype(jnp.bfloat16)
            parts = []
    product = dot_nn(scaled_ref[...], weight_ref[...])
    out_ref[...] = (product * lax.rsqrt(squares / features + EPS_NORM)).astype(jnp.bfloat16)
    total = term_ref[...] + other_ref[...]
    mean = jnp.sum(total * total, axis=1, keepdims=True) / features
    update_ref[...] = total / jnp.sqrt(mean + EPS_STEP)
    passing.wait()


def cost(flops, read, exps=0):
    return pl.CostEstimate(flops=flops, bytes_accessed=read, transcendentals=exps)


SMEM = pl.BlockSpec(memory_space=pltpu.SMEM)
HBM = pl.BlockSpec(memory_space=pltpu.HBM)
ANY = pl.BlockSpec(memory_space=pl.ANY)
VMEM = pl.BlockSpec(memory_space=pltpu.VMEM)


def in_hbm(*arrays):
    return [pltpu.with_memory_space_constraint(x, pltpu.HBM) for x in arrays]


def params():
    return pltpu.CompilerParams(vmem_limit_bytes=24 * 2**20)


def attend_early(queries, keys, values, offsets, cotangent, stashed, chunks):
    rows, width = queries.shape
    half = rows // 2
    soon = width // (4 * LANES) * 3 // 4 * 4 * LANES
    bf16 = lambda *shape: jax.ShapeDtypeStruct(shape, jnp.bfloat16)
    return pl.pallas_call(
        functools.partial(early_kernel, rows, chunks),
        in_specs=[HBM] * 6,
        out_specs=[VMEM] * 8,
        out_shape=[
            bf16(half + EXTRA, width),
            bf16(soon, half),
            bf16(width - soon, half),
            bf16(half, width),
            bf16(rows, width),
            bf16(rows, width),
            bf16(*cotangent.shape),
            bf16(*stashed.shape),
        ],
        scratch_shapes=[
            pltpu.SMEM(offsets.shape, jnp.int32),
            pltpu.VMEM((half, 2 * half), jnp.float32),
            pltpu.SemaphoreType.DMA((3, chunks)),
            pltpu.SemaphoreType.DMA((6,)),
        ],
        cost_estimate=cost(4 * half * half * width, 6 * rows * width, half * half * width // 64),
        compiler_params=params(),
        name="attend_early",
    )(*in_hbm(offsets, queries, keys, values, cotangent, stashed))


def attend_late(queries, keys, values, offsets, weight, early):
    half, width = queries.shape
    rows = 2 * half
    return pl.pallas_call(
        functools.partial(late_kernel, rows),
        in_specs=[HBM] * 2 + [VMEM] * 4,
        out_specs=[VMEM] * 3,
        out_shape=[
            jax.ShapeDtypeStruct((early.shape[0] + width // POOL, half), jnp.bfloat16),
            jax.ShapeDtypeStruct((half, rows), jnp.float32),
            jax.ShapeDtypeStruct(weight.shape, weight.dtype),
        ],
        scratch_shapes=[
            pltpu.SMEM(offsets.shape, jnp.int32),
            pltpu.VMEM((half, rows), jnp.float32),
            pltpu.VMEM((half, rows), jnp.float32),
            pltpu.VMEM((half, rows), jnp.bfloat16),
            pltpu.VMEM((half, rows), jnp.bfloat16),
            pltpu.SemaphoreType.DMA((9,)),
        ],
        cost_estimate=cost(8 * half * half * width, 10 * half * width, half * half * width // 64),
        compiler_params=params(),
        name="attend_late",
    )(*in_hbm(offsets, weight), queries, keys, values, early)


def attend_halo(sent, keys, values, bias, after):
    half, width = bias.shape[0], keys.shape[1]
    return pl.pallas_call(
        halo_kernel,
        in_specs=[VMEM] * 4 + [ANY],
        out_specs=VMEM,
        out_shape=jax.ShapeDtypeStruct((half // POOL + EXTRA, width), jnp.bfloat16),
        cost_estimate=cost(4 * half * half * width, 6 * half * width, half * half * width // 64),
        compiler_params=params(),
        name="attend_halo",
    )(sent, keys, values, bias, after)


def backward(slot, cotangent, weight, gain, stashed, after):
    rows, width = stashed.shape[1:]
    depth = weight.shape[1]
    return pl.pallas_call(
        back_kernel,
        in_specs=[VMEM] * 5 + [ANY],
        out_specs=[VMEM] * 2,
        scratch_shapes=[
            pltpu.VMEM((rows, width), jnp.float32),
            pltpu.VMEM((rows, width), jnp.bfloat16),
        ],
        out_shape=[
            jax.ShapeDtypeStruct((rows, width), jnp.bfloat16),
            jax.ShapeDtypeStruct((1, width), jnp.float32),
        ],
        cost_estimate=cost(2 * rows * width * depth, 2 * width * depth),
        compiler_params=params(),
        name="backward",
    )(slot, cotangent, weight, gain, stashed, after)


def project(early, both, halo, gain, weight, term, other, upstream):
    rows = upstream.shape[0]
    width, depth = weight.shape
    return pl.pallas_call(
        project_kernel,
        in_specs=[VMEM] * 7 + [ANY],
        out_specs=[VMEM, VMEM, HBM],
        out_shape=[
            jax.ShapeDtypeStruct((rows, depth), jnp.bfloat16),
            jax.ShapeDtypeStruct(term.shape, term.dtype),
            jax.ShapeDtypeStruct(upstream.shape, upstream.dtype),
        ],
        scratch_shapes=[pltpu.VMEM((rows, width), jnp.bfloat16), pltpu.SemaphoreType.DMA],
        cost_estimate=cost(2 * rows * width * depth, 2 * width * depth),
        compiler_params=params(),
        name="project",
    )(early, both, halo, gain, weight, term, other, upstream)


def swapped(value, axis, distance):
    return lax.ppermute(value, axis, [(i, i ^ distance) for i in range(lax.axis_size(axis))])


def sum_rounds():
    rounds = []
    for axis in ("rep", "seq"):
        count = lax.axis_size(axis)
        if count & (count - 1):
            return []
        rounds += [(axis, 1 << i) for i in range(count.bit_length() - 1)]
    return rounds if len(rounds) == 3 else []


def onward(value):
    sections, shards = lax.axis_size("section"), lax.axis_size("seq")
    route = [
        (s * shards + k, (s + 1) % sections * shards + k + 1)
        for s in range(sections)
        for k in range(shards - 1)
    ]
    return lax.ppermute(value, ("section", "seq"), route)


def local(queries, keys, values, doc_starts, weight, gain, stashed, cotangent, slot):
    queries, keys, values, offsets = queries[0, 0], keys[0, 0], values[0, 0], doc_starts[0]
    rounds = sum_rounds()

    def partner(term, index):
        return swapped(term, *rounds[index]) if rounds else jnp.zeros_like(term)

    sent, early, more, q_late, keys, values, cotangent, stashed = attend_early(
        queries, keys, values, offsets, cotangent[0, 0], stashed[0, 0], 4
    )
    arrived = shifted(sent, "seq", -1)
    early = passed_along(early, "section", 1)
    both, next_bias, weight = attend_late(q_late, keys, values, offsets, weight[0], more)
    slot = jnp.broadcast_to(slot, (1, LANES))
    dinput, term = backward(slot, cotangent, weight, gain, stashed, both)
    both = passed_along(both, "section", 1)
    upstream = passed_along(dinput, "section", -1)
    term = term if rounds else lax.psum(term, ("rep", "seq"))
    term = term + partner(term, 0)
    term = term + partner(term, 1)
    halo = onward(attend_halo(arrived, keys, values, next_bias, term))
    mol_keys, update, upstream = project(
        early, both, halo, gain, weight, term, partner(term, 2), upstream
    )
    return mol_keys[None, None], upstream[None, None], update


def solution(mesh):
    in_specs = (
        P("rep", "section", "seq", None),
        P("rep", "section", "seq", None),
        P("rep", "section", "seq", None),
        P("rep", "section", None),
        P("section", None, None),
        P("section", None),
        P("rep", "section", None, "seq", None),
        P("rep", "section", "seq", None),
        P("rep", "section"),
    )
    out_specs = (
        P("rep", "section", "seq", None),
        P("rep", "section", "seq", None),
        P("section", None),
    )
    return jax.shard_map(local, mesh=mesh, in_specs=in_specs, out_specs=out_specs, check_vma=False)
```

```python
import functools
import math

import jax
import jax.numpy as jnp
from jax import lax
from jax.experimental import pallas as pl
from jax.experimental.pallas import tpu as pltpu
from jax.sharding import PartitionSpec as P

HEAD_DIM = 64
POOL = 4
WINDOW = 128
LANES = 128
EPS_NORM = 1e-05
EPS_STEP = 1e-06
MASKED = -1e30
LAGS = (0, 3, 5, 6, 8)
EXTRA = 8

NT = (((1,), (1,)), ((), ()))


def dot_nt(a, b):
    return lax.dot_general(a, b, NT, preferred_element_type=jnp.float32)


def dot_nn(a, b):
    return jnp.dot(a, b, preferred_element_type=jnp.float32)


def shifted(value, axis, steps):
    count = lax.axis_size(axis)
    first, last = max(0, -steps), min(count, count - steps)
    return lax.ppermute(value, axis, [(i, i + steps) for i in range(first, last)])


def passed_along(value, axis, steps):
    count = lax.axis_size(axis)
    return lax.ppermute(value, axis, [(i, (i + steps) % count) for i in range(count)])


def earliest_key(offsets_ref, query_pos):
    start = jnp.zeros_like(query_pos)
    for d in range(offsets_ref.shape[1]):
        offset = offsets_ref[0, d]
        start = jnp.where(query_pos >= offset, offset, start)
    return jnp.maximum(start, query_pos - (WINDOW - 1))


def mask_bias(offsets_ref, query_start, key_start, keep):
    key = lax.broadcasted_iota(jnp.int32, (WINDOW, 2 * WINDOW), 0)
    query = lax.broadcasted_iota(jnp.int32, (WINDOW, 2 * WINDOW), 1) % WINDOW
    lane = lax.broadcasted_iota(jnp.int32, (1, 2 * WINDOW), 1) % WINDOW
    lowest = earliest_key(offsets_ref, query_start + lane)
    allowed = (key_start + key >= lowest) & keep(key, query)
    return jnp.where(allowed, 0.0, MASKED).astype(jnp.float32)


def split_heads(queries):
    lane = lax.broadcasted_iota(jnp.int32, (1, LANES), 1)
    scale = 1.0 / math.sqrt(HEAD_DIM)
    first = jnp.where(lane < HEAD_DIM, scale, 0.0).astype(jnp.bfloat16)
    second = jnp.where(lane < HEAD_DIM, 0.0, scale).astype(jnp.bfloat16)
    return jnp.concatenate([queries * first, queries * second], axis=0)


def pool_matrix(queries):
    molecule = lax.broadcasted_iota(jnp.int32, (queries // POOL, queries), 0)
    query = lax.broadcasted_iota(jnp.int32, (queries // POOL, queries), 1)
    return jnp.where(query // POOL == molecule, 1.0 / POOL, 0.0).astype(jnp.bfloat16)


def own_heads(mixed, scale):
    count = mixed.shape[1] // 2
    return jnp.concatenate(
        [
            mixed[:HEAD_DIM, :count] * scale[:, :count],
            mixed[HEAD_DIM:LANES, count:] * scale[:, count:],
        ],
        axis=0,
    )


def load(source, target, sem):
    copy = pltpu.make_async_copy(source, target, sem)
    copy.start()
    return copy


def load_chunks(arrays, chunks, sems):
    block = arrays[0][1].shape[1] // chunks
    return [
        [
            load(source.at[:, pl.ds(chunk * block, block)], target.at[:, pl.ds(chunk * block, block)], sems.at[i, chunk])
            for i, (source, target) in enumerate(arrays)
        ]
        for chunk in range(chunks)
    ]


def at(pair):
    return pl.ds(pair * LANES, LANES)


def over_pairs(pairs, stages, lags, before):
    results = {}
    for step in range(pairs + lags[-1]):
        if step < pairs:
            before(step)
        for stage, lag in zip(stages, lags):
            pair = step - lag
            if 0 <= pair < pairs:
                results[pair] = stage(pair, *results.get(pair, ()))


def tops(scores):
    rows = scores.shape[0]
    while rows > 8:
        rows //= 2
        scores = jnp.maximum(scores[:rows], scores[rows:])
    return jnp.max(scores, axis=0, keepdims=True)


def with_ones(values_t):
    return jnp.concatenate([values_t, jnp.ones((16, values_t.shape[1]), jnp.bfloat16)], axis=0)


def three_terms(value):
    high = value.astype(jnp.bfloat16).astype(jnp.float32)
    middle = (value - high).astype(jnp.bfloat16).astype(jnp.float32)
    return [high, middle, value - high - middle]


def early_kernel(
    rows, chunks, offsets_hbm, q_hbm, k_hbm, v_hbm, cotangent_hbm, stashed_hbm,
    sent_ref, early_ref, more_ref, q_late_ref, k_ref, v_ref, cotangent_ref, stashed_ref,
    offsets_ref, bias, sems, offsets_sem,
):
    half = rows // 2
    head, tail = pl.ds(0, half), pl.ds(half, half)
    offsets_copy = load(offsets_hbm, offsets_ref, offsets_sem.at[0])
    arrays = (
        (k_hbm.at[head], k_ref.at[head]),
        (q_hbm.at[head], sent_ref.at[head]),
        (v_hbm.at[head], v_ref.at[head]),
    )
    copies = load_chunks(arrays, chunks, sems)
    later = (
        (k_hbm.at[tail], k_ref.at[tail]),
        (v_hbm.at[tail], v_ref.at[tail]),
        (q_hbm.at[tail], q_late_ref),
        (cotangent_hbm, cotangent_ref),
        (stashed_hbm, stashed_ref),
    )
    rest = []
    offsets_copy.wait()
    start = lax.axis_index("seq") * rows
    bias[...] = mask_bias(offsets_ref, start, start, lambda key, query: key <= query)
    pairs = k_ref.shape[1] // LANES
    split = early_ref.shape[0] // LANES

    def arrive(pair):
        per_chunk = pairs // chunks
        if pair % per_chunk == 0:
            for copy in copies[pair // per_chunk]:
                copy.wait()
        if pair == per_chunk:
            for i, (source, target) in enumerate(later):
                rest.append(load(source, target, offsets_sem.at[i + 1]))

    def score(pair):
        scores = dot_nt(k_ref[head, at(pair)], split_heads(sent_ref[head, at(pair)]))
        return scores, with_ones(jnp.transpose(v_ref[head, at(pair)]))

    def top(pair, scores, values_t):
        return scores, tops(scores + bias[...]), values_t

    def weigh(pair, scores, top, values_t):
        return top, jnp.exp((scores + bias[...]) - top).astype(jnp.bfloat16), values_t

    def mix(pair, top, weights, values_t):
        return top, dot_nn(values_t, weights)

    def finish(pair, top, mixed):
        total = mixed[LANES : LANES + 1]
        target, place = (early_ref, pair) if pair < split else (more_ref, pair - split)
        target[at(place), :] = own_heads(mixed, 1.0 / total).astype(jnp.bfloat16)
        lse = top + jnp.log(total)
        terms = three_terms(lse[:, :half]) + three_terms(lse[:, half:])
        terms.append(jnp.zeros((EXTRA - 6, LANES), jnp.float32))
        sent_ref[pl.ds(half, EXTRA), at(pair)] = jnp.concatenate(terms, axis=0).astype(jnp.bfloat16)
        return ()

    over_pairs(pairs, (score, top, weigh, mix, finish), LAGS, arrive)
    for copy in rest:
        copy.wait()


def late_kernel(
    rows, offsets_hbm, weight_hbm, q_ref, k_ref, v_ref, early_ref, both_ref, next_ref, weight_ref,
    offsets_ref, own_bias, other_bias, own, other, sems,
):
    offsets_copy = load(offsets_hbm, offsets_ref, sems.at[8])
    block = weight_ref.shape[0] // 8
    copies = []
    for i in range(8):
        place = pl.ds(i * block, block)
        copies.append(load(weight_hbm.at[place], weight_ref.at[place], sems.at[i]))
    half = q_ref.shape[0]
    key = lax.broadcasted_iota(jnp.int32, own.shape, 0)
    query = lax.broadcasted_iota(jnp.int32, own.shape, 1) % half
    own[...] = jnp.where(key <= query, 1.0, 0.0).astype(jnp.bfloat16)
    other[...] = jnp.where(key <= query, 0.0, 1.0).astype(jnp.bfloat16)
    pooling = pool_matrix(half)
    molecules = half // POOL
    features = early_ref.shape[0]
    both_ref[pl.ds(0, features), :] = early_ref[...]
    pairs = k_ref.shape[1] // LANES
    offsets_copy.wait()
    start = lax.axis_index("seq") * rows
    own_bias[...] = mask_bias(offsets_ref, start + half, start + half, lambda key, query: key <= query)
    other_bias[...] = mask_bias(offsets_ref, start + half, start, lambda key, query: key > query)
    next_ref[...] = mask_bias(offsets_ref, start + rows, start + half, lambda key, query: key > query)
    parts = []

    def score(pair):
        scores = dot_nt(k_ref[:, at(pair)], split_heads(q_ref[:, at(pair)]))
        return scores, with_ones(jnp.transpose(v_ref[:, at(pair)]))

    def top(pair, scores, values_t):
        scores = jnp.maximum(scores[:half] + other_bias[...], scores[half:] + own_bias[...])
        return scores, tops(scores), values_t

    def weigh(pair, scores, top, values_t):
        weights = jnp.exp(scores - top).astype(jnp.bfloat16)
        return jnp.concatenate([weights * other[...], weights * own[...]], axis=0), values_t

    def mix(pair, weights, values_t):
        return (dot_nn(values_t, weights),)

    def finish(pair, mixed):
        inverse = 1.0 / mixed[LANES : LANES + 1]
        parts.append(own_heads(mixed, inverse).astype(jnp.bfloat16))
        if len(parts) == 4:
            pooled = dot_nt(pooling, jnp.concatenate(parts, axis=0)).astype(jnp.bfloat16)
            for i in range(4):
                place = features + (pair - 3 + i) * molecules
                both_ref[pl.ds(place, molecules), :] = pooled[:, i * LANES : (i + 1) * LANES]
            parts.clear()
        return ()

    over_pairs(pairs, (score, top, weigh, mix, finish), LAGS, lambda pair: None)
    for copy in copies:
        copy.wait()


def halo_kernel(q_ref, k_ref, v_ref, bias, after_ref, out_ref, share_ref):
    half = bias.shape[0]
    molecules = half // POOL
    tail = pl.ds(half, half)
    pooling = pool_matrix(half)
    pairs = k_ref.shape[1] // LANES
    parts = []

    def score(pair):
        queries = split_heads(q_ref[pl.ds(0, half), at(pair)])
        scores = dot_nt(k_ref[tail, at(pair)], queries)
        return scores, with_ones(jnp.transpose(v_ref[tail, at(pair)]))

    def top(pair, scores, values_t):
        terms = q_ref[pl.ds(half, EXTRA), at(pair)].astype(jnp.float32)
        lse = jnp.concatenate(
            [terms[0:1] + terms[1:2] + terms[2:3], terms[3:4] + terms[4:5] + terms[5:6]], axis=1
        )
        return scores, jnp.maximum(tops(scores + bias[...]), lse), lse, values_t

    def weigh(pair, scores, top, lse, values_t):
        weights = jnp.exp((scores + bias[...]) - top).astype(jnp.bfloat16)
        return weights, jnp.exp(lse - top), values_t

    def mix(pair, weights, kept, values_t):
        return dot_nn(values_t, weights), kept

    def finish(pair, mixed, kept):
        inverse = 1.0 / (mixed[LANES : LANES + 1] + kept)
        parts.append(own_heads(mixed, inverse).astype(jnp.bfloat16))
        if len(parts) == 4:
            pooled = dot_nt(pooling, jnp.concatenate(parts, axis=0)).astype(jnp.bfloat16)
            for i in range(4):
                place = pl.ds((pair - 3 + i) * molecules, molecules)
                out_ref[place, :] = pooled[:, i * LANES : (i + 1) * LANES]
            parts.clear()
        share_ref[pl.ds(pair, 1), :] = kept * inverse
        return ()

    over_pairs(pairs, (score, top, weigh, mix, finish), LAGS, lambda pair: None)
    share = share_ref[...].astype(jnp.bfloat16)
    out_ref[pl.ds(pairs * molecules, pairs), :] = share[:, :half]
    out_ref[pl.ds(pairs * (molecules + 1), pairs), :] = share[:, half:]


def back_kernel(
    slot_ref, cotangent_ref, weight_ref, gain_ref, stashed_ref, after_ref, dinput_ref, term_ref, grad, held_ref
):
    held = stashed_ref[0]
    for i in range(1, stashed_ref.shape[0]):
        held = jnp.where(slot_ref[0:1, 0:1] == i, stashed_ref[i].astype(jnp.float32), held.astype(jnp.float32))
    held_ref[...] = held.astype(jnp.bfloat16)
    features = weight_ref.shape[0]
    block = 512
    for begin in range(0, features, block):
        columns = pl.ds(begin, block)
        grad[:, columns] = dot_nt(cotangent_ref[...], weight_ref[columns, :])
    held = held_ref[...].astype(jnp.float32)
    inv_rms = lax.rsqrt(jnp.sum(held * held, axis=1, keepdims=True) / features + EPS_NORM)
    along = jnp.zeros_like(inv_rms)
    for begin in range(0, features, block):
        columns = pl.ds(begin, block)
        product = grad[:, columns] * (held_ref[:, columns].astype(jnp.float32) * inv_rms)
        term_ref[:, columns] = jnp.sum(product, axis=0, keepdims=True)
        along += jnp.sum(product * gain_ref[:, columns], axis=1, keepdims=True)
    along = along / features
    for begin in range(0, features, block):
        columns = pl.ds(begin, block)
        whitened = held_ref[:, columns].astype(jnp.float32) * inv_rms
        scaled = grad[:, columns] * gain_ref[:, columns]
        dinput_ref[:, columns] = (inv_rms * (scaled - whitened * along)).astype(jnp.bfloat16)


def project_kernel(
    early_ref, both_ref, halo_ref, gain_ref, weight_ref, term_ref, other_ref, upstream_hbm,
    out_ref, update_ref, passed_hbm, scaled_ref, share_ref, sem,
):
    passing = load(upstream_hbm, passed_hbm, sem)
    half = both_ref.shape[1]
    features = gain_ref.shape[1]
    first_part = early_ref.shape[0]
    molecules = half // POOL
    pooling = pool_matrix(half)
    first = lax.axis_index("seq") == 0
    squares, parts, pairs = 0.0, [], features // LANES
    shares = halo_ref[pl.ds(pairs * molecules, 2 * pairs), :].astype(jnp.float32)
    share_ref[...] = jnp.where(first, 1.0, shares)
    for pair in range(pairs):
        share_a, share_b = share_ref[pl.ds(pair, 1), :], share_ref[pl.ds(pairs + pair, 1), :]
        begin = pair * LANES
        if begin < first_part:
            early = early_ref[pl.ds(begin, LANES), :].astype(jnp.float32)
        else:
            early = both_ref[pl.ds(begin - first_part, LANES), :].astype(jnp.float32)
        parts += [early[:HEAD_DIM] * share_a, early[HEAD_DIM:] * share_b]
        if len(parts) == 8:
            columns = pl.ds((pair - 3) * LANES, 4 * LANES)
            mean = dot_nt(pooling, jnp.concatenate(parts, axis=0).astype(jnp.bfloat16))
            halo = [halo_ref[pl.ds((pair - 3 + i) * molecules, molecules), :] for i in range(4)]
            upper = mean + jnp.concatenate(halo, axis=1).astype(jnp.float32)
            place = features - first_part + (pair - 3) * molecules
            lower = [both_ref[pl.ds(place + i * molecules, molecules), :] for i in range(4)]
            lower = jnp.concatenate(lower, axis=1)
            arrived = jnp.concatenate([upper.astype(jnp.bfloat16), lower], axis=0).astype(jnp.float32)
            squares += jnp.sum(arrived * arrived, axis=1, keepdims=True)
            scaled_ref[:, columns] = (arrived * gain_ref[:, columns]).astype(jnp.bfloat16)
            parts = []
    product = dot_nn(scaled_ref[...], weight_ref[...])
    out_ref[...] = (product * lax.rsqrt(squares / features + EPS_NORM)).astype(jnp.bfloat16)
    total = term_ref[...] + other_ref[...]
    mean = jnp.sum(total * total, axis=1, keepdims=True) / features
    update_ref[...] = total / jnp.sqrt(mean + EPS_STEP)
    passing.wait()


def cost(flops, read, exps=0):
    return pl.CostEstimate(flops=flops, bytes_accessed=read, transcendentals=exps)


SMEM = pl.BlockSpec(memory_space=pltpu.SMEM)
HBM = pl.BlockSpec(memory_space=pltpu.HBM)
ANY = pl.BlockSpec(memory_space=pl.ANY)
VMEM = pl.BlockSpec(memory_space=pltpu.VMEM)


def in_hbm(*arrays):
    return [pltpu.with_memory_space_constraint(x, pltpu.HBM) for x in arrays]


def params():
    return pltpu.CompilerParams(vmem_limit_bytes=24 * 2**20)


def attend_early(queries, keys, values, offsets, cotangent, stashed, chunks):
    rows, width = queries.shape
    half = rows // 2
    soon = width // (4 * LANES) * 3 // 4 * 4 * LANES
    bf16 = lambda *shape: jax.ShapeDtypeStruct(shape, jnp.bfloat16)
    return pl.pallas_call(
        functools.partial(early_kernel, rows, chunks),
        in_specs=[HBM] * 6,
        out_specs=[VMEM] * 8,
        out_shape=[
            bf16(half + EXTRA, width),
            bf16(soon, half),
            bf16(width - soon, half),
            bf16(half, width),
            bf16(rows, width),
            bf16(rows, width),
            bf16(*cotangent.shape),
            bf16(*stashed.shape),
        ],
        scratch_shapes=[
            pltpu.SMEM(offsets.shape, jnp.int32),
            pltpu.VMEM((half, 2 * half), jnp.float32),
            pltpu.SemaphoreType.DMA((3, chunks)),
            pltpu.SemaphoreType.DMA((6,)),
        ],
        cost_estimate=cost(4 * half * half * width, 6 * rows * width, half * half * width // 64),
        compiler_params=params(),
        name="attend_early",
    )(*in_hbm(offsets, queries, keys, values, cotangent, stashed))


def attend_late(queries, keys, values, offsets, weight, early):
    half, width = queries.shape
    rows = 2 * half
    return pl.pallas_call(
        functools.partial(late_kernel, rows),
        in_specs=[HBM] * 2 + [VMEM] * 4,
        out_specs=[VMEM] * 3,
        out_shape=[
            jax.ShapeDtypeStruct((early.shape[0] + width // POOL, half), jnp.bfloat16),
            jax.ShapeDtypeStruct((half, rows), jnp.float32),
            jax.ShapeDtypeStruct(weight.shape, weight.dtype),
        ],
        scratch_shapes=[
            pltpu.SMEM(offsets.shape, jnp.int32),
            pltpu.VMEM((half, rows), jnp.float32),
            pltpu.VMEM((half, rows), jnp.float32),
            pltpu.VMEM((half, rows), jnp.bfloat16),
            pltpu.VMEM((half, rows), jnp.bfloat16),
            pltpu.SemaphoreType.DMA((9,)),
        ],
        cost_estimate=cost(8 * half * half * width, 10 * half * width, half * half * width // 64),
        compiler_params=params(),
        name="attend_late",
    )(*in_hbm(offsets, weight), queries, keys, values, early)


def attend_halo(sent, keys, values, bias, after):
    half, width = bias.shape[0], keys.shape[1]
    return pl.pallas_call(
        halo_kernel,
        in_specs=[VMEM] * 4 + [ANY],
        out_specs=VMEM,
        out_shape=jax.ShapeDtypeStruct((width // LANES * (half // POOL + 2), LANES), jnp.bfloat16),
        scratch_shapes=[pltpu.VMEM((width // LANES, 2 * half), jnp.float32)],
        cost_estimate=cost(4 * half * half * width, 6 * half * width, half * half * width // 64),
        compiler_params=params(),
        name="attend_halo",
    )(sent, keys, values, bias, after)


def backward(slot, cotangent, weight, gain, stashed, after):
    rows, width = stashed.shape[1:]
    depth = weight.shape[1]
    return pl.pallas_call(
        back_kernel,
        in_specs=[VMEM] * 5 + [ANY],
        out_specs=[VMEM] * 2,
        scratch_shapes=[
            pltpu.VMEM((rows, width), jnp.float32),
            pltpu.VMEM((rows, width), jnp.bfloat16),
        ],
        out_shape=[
            jax.ShapeDtypeStruct((rows, width), jnp.bfloat16),
            jax.ShapeDtypeStruct((1, width), jnp.float32),
        ],
        cost_estimate=cost(2 * rows * width * depth, 2 * width * depth),
        compiler_params=params(),
        name="backward",
    )(slot, cotangent, weight, gain, stashed, after)


def project(early, both, halo, gain, weight, term, other, upstream):
    rows = upstream.shape[0]
    width, depth = weight.shape
    return pl.pallas_call(
        project_kernel,
        in_specs=[VMEM] * 7 + [ANY],
        out_specs=[VMEM, VMEM, HBM],
        out_shape=[
            jax.ShapeDtypeStruct((rows, depth), jnp.bfloat16),
            jax.ShapeDtypeStruct(term.shape, term.dtype),
            jax.ShapeDtypeStruct(upstream.shape, upstream.dtype),
        ],
        scratch_shapes=[
            pltpu.VMEM((rows, width), jnp.bfloat16),
            pltpu.VMEM((2 * width // LANES, LANES), jnp.float32),
            pltpu.SemaphoreType.DMA,
        ],
        cost_estimate=cost(2 * rows * width * depth, 2 * width * depth),
        compiler_params=params(),
        name="project",
    )(early, both, halo, gain, weight, term, other, upstream)


def swapped(value, axis, distance):
    return lax.ppermute(value, axis, [(i, i ^ distance) for i in range(lax.axis_size(axis))])


def sum_rounds():
    rounds = []
    for axis in ("rep", "seq"):
        count = lax.axis_size(axis)
        if count & (count - 1):
            return []
        rounds += [(axis, 1 << i) for i in range(count.bit_length() - 1)]
    return rounds if len(rounds) == 3 else []


def onward(value):
    sections, shards = lax.axis_size("section"), lax.axis_size("seq")
    route = [
        (s * shards + k, (s + 1) % sections * shards + k + 1)
        for s in range(sections)
        for k in range(shards - 1)
    ]
    return lax.ppermute(value, ("section", "seq"), route)


def local(queries, keys, values, doc_starts, weight, gain, stashed, cotangent, slot):
    queries, keys, values, offsets = queries[0, 0], keys[0, 0], values[0, 0], doc_starts[0]
    rounds = sum_rounds()

    def partner(term, index):
        return swapped(term, *rounds[index]) if rounds else jnp.zeros_like(term)

    sent, early, more, q_late, keys, values, cotangent, stashed = attend_early(
        queries, keys, values, offsets, cotangent[0, 0], stashed[0, 0], 4
    )
    arrived = shifted(sent, "seq", -1)
    early = passed_along(early, "section", 1)
    both, next_bias, weight = attend_late(q_late, keys, values, offsets, weight[0], more)
    slot = jnp.broadcast_to(slot, (1, LANES))
    dinput, term = backward(slot, cotangent, weight, gain, stashed, both)
    both = passed_along(both, "section", 1)
    upstream = passed_along(dinput, "section", -1)
    term = term if rounds else lax.psum(term, ("rep", "seq"))
    term = term + partner(term, 0)
    term = term + partner(term, 1)
    halo = onward(attend_halo(arrived, keys, values, next_bias, term))
    mol_keys, update, upstream = project(
        early, both, halo, gain, weight, term, partner(term, 2), upstream
    )
    return mol_keys[None, None], upstream[None, None], update


def solution(mesh):
    in_specs = (
        P("rep", "section", "seq", None),
        P("rep", "section", "seq", None),
        P("rep", "section", "seq", None),
        P("rep", "section", None),
        P("section", None, None),
        P("section", None),
        P("rep", "section", None, "seq", None),
        P("rep", "section", "seq", None),
        P("rep", "section"),
    )
    out_specs = (
        P("rep", "section", "seq", None),
        P("rep", "section", "seq", None),
        P("section", None),
    )
    return jax.shard_map(local, mesh=mesh, in_specs=in_specs, out_specs=out_specs, check_vma=False)
```

```python
import functools
import math

import jax
import jax.numpy as jnp
from jax import lax
from jax.experimental import pallas as pl
from jax.experimental.pallas import tpu as pltpu
from jax.sharding import PartitionSpec as P

HEAD_DIM = 64
POOL = 4
WINDOW = 128
LANES = 128
EPS_NORM = 1e-05
EPS_STEP = 1e-06
MASKED = -1e30
LAGS = (0, 3, 5, 6, 8)

NT = (((1,), (1,)), ((), ()))


def dot_nt(a, b):
    return lax.dot_general(a, b, NT, preferred_element_type=jnp.float32)


def dot_nn(a, b):
    return jnp.dot(a, b, preferred_element_type=jnp.float32)


def shifted(value, axis, steps):
    count = lax.axis_size(axis)
    first, last = max(0, -steps), min(count, count - steps)
    return lax.ppermute(value, axis, [(i, i + steps) for i in range(first, last)])


def passed_along(value, axis, steps):
    count = lax.axis_size(axis)
    return lax.ppermute(value, axis, [(i, (i + steps) % count) for i in range(count)])


def earliest_key(offsets_ref, query_pos):
    start = jnp.zeros_like(query_pos)
    for d in range(offsets_ref.shape[1]):
        offset = offsets_ref[0, d]
        start = jnp.where(query_pos >= offset, offset, start)
    return jnp.maximum(start, query_pos - (WINDOW - 1))


def mask_bias(offsets_ref, query_start, key_start, keep):
    key = lax.broadcasted_iota(jnp.int32, (WINDOW, 2 * WINDOW), 0)
    query = lax.broadcasted_iota(jnp.int32, (WINDOW, 2 * WINDOW), 1) % WINDOW
    lane = lax.broadcasted_iota(jnp.int32, (1, 2 * WINDOW), 1) % WINDOW
    lowest = earliest_key(offsets_ref, query_start + lane)
    allowed = (key_start + key >= lowest) & keep(key, query)
    return jnp.where(allowed, 0.0, MASKED).astype(jnp.float32)


def split_heads(queries):
    lane = lax.broadcasted_iota(jnp.int32, (1, LANES), 1)
    scale = 1.0 / math.sqrt(HEAD_DIM)
    first = jnp.where(lane < HEAD_DIM, scale, 0.0).astype(jnp.bfloat16)
    second = jnp.where(lane < HEAD_DIM, 0.0, scale).astype(jnp.bfloat16)
    return jnp.concatenate([queries * first, queries * second], axis=0)


def pool_matrix(queries):
    molecule = lax.broadcasted_iota(jnp.int32, (queries // POOL, queries), 0)
    query = lax.broadcasted_iota(jnp.int32, (queries // POOL, queries), 1)
    return jnp.where(query // POOL == molecule, 1.0 / POOL, 0.0).astype(jnp.bfloat16)


def own_heads(mixed, scale):
    count = mixed.shape[1] // 2
    return jnp.concatenate(
        [
            mixed[:HEAD_DIM, :count] * scale[:, :count],
            mixed[HEAD_DIM:LANES, count:] * scale[:, count:],
        ],
        axis=0,
    )


def load(source, target, sem):
    copy = pltpu.make_async_copy(source, target, sem)
    copy.start()
    return copy


def at(pair):
    return pl.ds(pair * LANES, LANES)


def over_pairs(pairs, stages, lags, before):
    results = {}
    for step in range(pairs + lags[-1]):
        if step < pairs:
            before(step)
        for stage, lag in zip(stages, lags):
            pair = step - lag
            if 0 <= pair < pairs:
                results[pair] = stage(pair, *results.get(pair, ()))


def tops(scores):
    rows = scores.shape[0]
    while rows > 8:
        rows //= 2
        scores = jnp.maximum(scores[:rows], scores[rows:])
    return jnp.max(scores, axis=0, keepdims=True)


def with_ones(values_t):
    return jnp.concatenate([values_t, jnp.ones((16, values_t.shape[1]), jnp.bfloat16)], axis=0)


def three_terms(value):
    high = value.astype(jnp.bfloat16).astype(jnp.float32)
    middle = (value - high).astype(jnp.bfloat16).astype(jnp.float32)
    return [high, middle, value - high - middle]


def early_kernel(
    rows, chunks, offsets_hbm, q_hbm, k_hbm, v_hbm, cotangent_hbm, stashed_hbm,
    sent_ref, early_ref, more_ref, q_late_ref, k_ref, v_ref, cotangent_ref, stashed_ref,
    offsets_ref, bias, lse_ref, sems, offsets_sem,
):
    half = rows // 2
    head, tail = pl.ds(0, half), pl.ds(half, half)
    offsets_copy = load(offsets_hbm, offsets_ref, offsets_sem.at[0])
    block = k_ref.shape[1] // chunks
    pairs, per_chunk = k_ref.shape[1] // LANES, block // LANES
    copies = {}

    def fetch(chunk):
        columns = pl.ds(chunk * block, block)
        copies[chunk] = [
            load(k_hbm.at[head, columns], k_ref.at[head, columns], sems.at[0, chunk]),
            load(v_hbm.at[head, columns], v_ref.at[head, columns], sems.at[1, chunk]),
        ]
        for pair in range(chunk * per_chunk, (chunk + 1) * per_chunk):
            copies[chunk].append(
                load(q_hbm.at[head, at(pair)], sent_ref.at[pl.ds(pair * half, half)], sems.at[2 + pair % per_chunk, chunk])
            )

    fetch(0)
    fetch(1)
    later = (
        (k_hbm.at[tail], k_ref.at[tail]),
        (v_hbm.at[tail], v_ref.at[tail]),
        (q_hbm.at[tail], q_late_ref),
        (cotangent_hbm, cotangent_ref),
        (stashed_hbm, stashed_ref),
    )
    rest = []
    offsets_copy.wait()
    start = lax.axis_index("seq") * rows
    bias[...] = mask_bias(offsets_ref, start, start, lambda key, query: key <= query)
    split = early_ref.shape[0] // LANES

    def arrive(pair):
        if pair % per_chunk == 0:
            chunk = pair // per_chunk
            for copy in copies[chunk]:
                copy.wait()
            if chunk + 2 < chunks:
                fetch(chunk + 2)
        if pair == per_chunk:
            for i, (source, target) in enumerate(later):
                rest.append(load(source, target, offsets_sem.at[i + 1]))

    def score(pair):
        scores = dot_nt(k_ref[head, at(pair)], split_heads(sent_ref[pl.ds(pair * half, half), :]))
        return scores, with_ones(jnp.transpose(v_ref[head, at(pair)]))

    def top(pair, scores, values_t):
        return scores, tops(scores + bias[...]), values_t

    def weigh(pair, scores, top, values_t):
        return top, jnp.exp((scores + bias[...]) - top).astype(jnp.bfloat16), values_t

    def mix(pair, top, weights, values_t):
        return top, dot_nn(values_t, weights)

    def finish(pair, top, mixed):
        total = mixed[LANES : LANES + 1]
        target, place = (early_ref, pair) if pair < split else (more_ref, pair - split)
        target[at(place), :] = own_heads(mixed, 1.0 / total).astype(jnp.bfloat16)
        lse_ref[pl.ds(pair, 1), :] = top + jnp.log(total)
        return ()

    over_pairs(pairs, (score, top, weigh, mix, finish), LAGS, arrive)
    for i, term in enumerate(three_terms(lse_ref[...])):
        for j in range(2):
            place = pl.ds(pairs * (half + 2 * i + j), pairs)
            sent_ref[place, :] = term[:, j * half : (j + 1) * half].astype(jnp.bfloat16)
    for copy in rest:
        copy.wait()


def late_kernel(
    rows, offsets_hbm, weight_hbm, q_ref, k_ref, v_ref, early_ref, both_ref, next_ref, weight_ref,
    offsets_ref, own_bias, other_bias, own, other, sems,
):
    offsets_copy = load(offsets_hbm, offsets_ref, sems.at[8])
    block = weight_ref.shape[0] // 8
    copies = []
    for i in range(8):
        place = pl.ds(i * block, block)
        copies.append(load(weight_hbm.at[place], weight_ref.at[place], sems.at[i]))
    half = q_ref.shape[0]
    key = lax.broadcasted_iota(jnp.int32, own.shape, 0)
    query = lax.broadcasted_iota(jnp.int32, own.shape, 1) % half
    own[...] = jnp.where(key <= query, 1.0, 0.0).astype(jnp.bfloat16)
    other[...] = jnp.where(key <= query, 0.0, 1.0).astype(jnp.bfloat16)
    pooling = pool_matrix(half)
    molecules = half // POOL
    features = early_ref.shape[0]
    both_ref[pl.ds(0, features), :] = early_ref[...]
    pairs = k_ref.shape[1] // LANES
    offsets_copy.wait()
    start = lax.axis_index("seq") * rows
    own_bias[...] = mask_bias(offsets_ref, start + half, start + half, lambda key, query: key <= query)
    other_bias[...] = mask_bias(offsets_ref, start + half, start, lambda key, query: key > query)
    next_ref[...] = mask_bias(offsets_ref, start + rows, start + half, lambda key, query: key > query)
    parts = []

    def score(pair):
        scores = dot_nt(k_ref[:, at(pair)], split_heads(q_ref[:, at(pair)]))
        return scores, with_ones(jnp.transpose(v_ref[:, at(pair)]))

    def top(pair, scores, values_t):
        scores = jnp.maximum(scores[:half] + other_bias[...], scores[half:] + own_bias[...])
        return scores, tops(scores), values_t

    def weigh(pair, scores, top, values_t):
        weights = jnp.exp(scores - top).astype(jnp.bfloat16)
        return jnp.concatenate([weights * other[...], weights * own[...]], axis=0), values_t

    def mix(pair, weights, values_t):
        return (dot_nn(values_t, weights),)

    def finish(pair, mixed):
        inverse = 1.0 / mixed[LANES : LANES + 1]
        parts.append(own_heads(mixed, inverse).astype(jnp.bfloat16))
        if len(parts) == 4:
            pooled = dot_nt(pooling, jnp.concatenate(parts, axis=0)).astype(jnp.bfloat16)
            for i in range(4):
                place = features + (pair - 3 + i) * molecules
                both_ref[pl.ds(place, molecules), :] = pooled[:, i * LANES : (i + 1) * LANES]
            parts.clear()
        return ()

    over_pairs(pairs, (score, top, weigh, mix, finish), LAGS, lambda pair: None)
    for copy in copies:
        copy.wait()


def halo_kernel(q_ref, k_ref, v_ref, bias, after_ref, out_ref, lse_ref, share_ref):
    half = bias.shape[0]
    molecules = half // POOL
    tail = pl.ds(half, half)
    pooling = pool_matrix(half)
    pairs = k_ref.shape[1] // LANES
    parts = []
    for j in range(2):
        places = [pl.ds(pairs * (half + 2 * i + j), pairs) for i in range(3)]
        high, middle, low = [q_ref[place, :].astype(jnp.float32) for place in places]
        lse_ref[:, pl.ds(j * half, half)] = high + middle + low

    def score(pair):
        queries = split_heads(q_ref[pl.ds(pair * half, half), :])
        scores = dot_nt(k_ref[tail, at(pair)], queries)
        return scores, with_ones(jnp.transpose(v_ref[tail, at(pair)]))

    def top(pair, scores, values_t):
        lse = lse_ref[pl.ds(pair, 1), :]
        return scores, jnp.maximum(tops(scores + bias[...]), lse), lse, values_t

    def weigh(pair, scores, top, lse, values_t):
        weights = jnp.exp((scores + bias[...]) - top).astype(jnp.bfloat16)
        return weights, jnp.exp(lse - top), values_t

    def mix(pair, weights, kept, values_t):
        return dot_nn(values_t, weights), kept

    def finish(pair, mixed, kept):
        inverse = 1.0 / (mixed[LANES : LANES + 1] + kept)
        parts.append(own_heads(mixed, inverse).astype(jnp.bfloat16))
        if len(parts) == 4:
            pooled = dot_nt(pooling, jnp.concatenate(parts, axis=0)).astype(jnp.bfloat16)
            for i in range(4):
                place = pl.ds((pair - 3 + i) * molecules, molecules)
                out_ref[place, :] = pooled[:, i * LANES : (i + 1) * LANES]
            parts.clear()
        share_ref[pl.ds(pair, 1), :] = kept * inverse
        return ()

    over_pairs(pairs, (score, top, weigh, mix, finish), LAGS, lambda pair: None)
    share = share_ref[...].astype(jnp.bfloat16)
    out_ref[pl.ds(pairs * molecules, pairs), :] = share[:, :half]
    out_ref[pl.ds(pairs * (molecules + 1), pairs), :] = share[:, half:]


def back_kernel(
    slot_ref, cotangent_ref, weight_ref, gain_ref, stashed_ref, after_ref, dinput_ref, term_ref, grad, held_ref
):
    held = stashed_ref[0]
    for i in range(1, stashed_ref.shape[0]):
        held = jnp.where(slot_ref[0:1, 0:1] == i, stashed_ref[i].astype(jnp.float32), held.astype(jnp.float32))
    held_ref[...] = held.astype(jnp.bfloat16)
    features = weight_ref.shape[0]
    block = 512
    for begin in range(0, features, block):
        columns = pl.ds(begin, block)
        grad[:, columns] = dot_nt(cotangent_ref[...], weight_ref[columns, :])
    held = held_ref[...].astype(jnp.float32)
    inv_rms = lax.rsqrt(jnp.sum(held * held, axis=1, keepdims=True) / features + EPS_NORM)
    along = jnp.zeros_like(inv_rms)
    for begin in range(0, features, block):
        columns = pl.ds(begin, block)
        product = grad[:, columns] * (held_ref[:, columns].astype(jnp.float32) * inv_rms)
        term_ref[:, columns] = jnp.sum(product, axis=0, keepdims=True)
        along += jnp.sum(product * gain_ref[:, columns], axis=1, keepdims=True)
    along = along / features
    for begin in range(0, features, block):
        columns = pl.ds(begin, block)
        whitened = held_ref[:, columns].astype(jnp.float32) * inv_rms
        scaled = grad[:, columns] * gain_ref[:, columns]
        dinput_ref[:, columns] = (inv_rms * (scaled - whitened * along)).astype(jnp.bfloat16)


def project_kernel(
    early_ref, both_ref, halo_ref, gain_ref, weight_ref, term_ref, other_ref, upstream_hbm,
    out_ref, update_ref, passed_hbm, scaled_ref, share_ref, sem,
):
    passing = load(upstream_hbm, passed_hbm, sem)
    half = both_ref.shape[1]
    features = gain_ref.shape[1]
    first_part = early_ref.shape[0]
    molecules = half // POOL
    pooling = pool_matrix(half)
    first = lax.axis_index("seq") == 0
    squares, parts, pairs = 0.0, [], features // LANES
    shares = halo_ref[pl.ds(pairs * molecules, 2 * pairs), :].astype(jnp.float32)
    share_ref[...] = jnp.where(first, 1.0, shares)
    for pair in range(pairs):
        share_a, share_b = share_ref[pl.ds(pair, 1), :], share_ref[pl.ds(pairs + pair, 1), :]
        begin = pair * LANES
        if begin < first_part:
            early = early_ref[pl.ds(begin, LANES), :].astype(jnp.float32)
        else:
            early = both_ref[pl.ds(begin - first_part, LANES), :].astype(jnp.float32)
        parts += [early[:HEAD_DIM] * share_a, early[HEAD_DIM:] * share_b]
        if len(parts) == 8:
            columns = pl.ds((pair - 3) * LANES, 4 * LANES)
            mean = dot_nt(pooling, jnp.concatenate(parts, axis=0).astype(jnp.bfloat16))
            halo = [halo_ref[pl.ds((pair - 3 + i) * molecules, molecules), :] for i in range(4)]
            upper = mean + jnp.concatenate(halo, axis=1).astype(jnp.float32)
            place = features - first_part + (pair - 3) * molecules
            lower = [both_ref[pl.ds(place + i * molecules, molecules), :] for i in range(4)]
            lower = jnp.concatenate(lower, axis=1)
            arrived = jnp.concatenate([upper.astype(jnp.bfloat16), lower], axis=0).astype(jnp.float32)
            squares += jnp.sum(arrived * arrived, axis=1, keepdims=True)
            scaled_ref[:, columns] = (arrived * gain_ref[:, columns]).astype(jnp.bfloat16)
            parts = []
    product = dot_nn(scaled_ref[...], weight_ref[...])
    out_ref[...] = (product * lax.rsqrt(squares / features + EPS_NORM)).astype(jnp.bfloat16)
    total = term_ref[...] + other_ref[...]
    mean = jnp.sum(total * total, axis=1, keepdims=True) / features
    update_ref[...] = total / jnp.sqrt(mean + EPS_STEP)
    passing.wait()


def cost(flops, read, exps=0):
    return pl.CostEstimate(flops=flops, bytes_accessed=read, transcendentals=exps)


SMEM = pl.BlockSpec(memory_space=pltpu.SMEM)
HBM = pl.BlockSpec(memory_space=pltpu.HBM)
ANY = pl.BlockSpec(memory_space=pl.ANY)
VMEM = pl.BlockSpec(memory_space=pltpu.VMEM)


def in_hbm(*arrays):
    return [pltpu.with_memory_space_constraint(x, pltpu.HBM) for x in arrays]


def params():
    return pltpu.CompilerParams(vmem_limit_bytes=24 * 2**20)


def attend_early(queries, keys, values, offsets, cotangent, stashed, chunks):
    rows, width = queries.shape
    half = rows // 2
    soon = width // (4 * LANES) * 3 // 4 * 4 * LANES
    bf16 = lambda *shape: jax.ShapeDtypeStruct(shape, jnp.bfloat16)
    return pl.pallas_call(
        functools.partial(early_kernel, rows, chunks),
        in_specs=[HBM] * 6,
        out_specs=[VMEM] * 8,
        out_shape=[
            bf16(width // LANES * (half + 6), LANES),
            bf16(soon, half),
            bf16(width - soon, half),
            bf16(half, width),
            bf16(rows, width),
            bf16(rows, width),
            bf16(*cotangent.shape),
            bf16(*stashed.shape),
        ],
        scratch_shapes=[
            pltpu.SMEM(offsets.shape, jnp.int32),
            pltpu.VMEM((half, 2 * half), jnp.float32),
            pltpu.VMEM((width // LANES, 2 * half), jnp.float32),
            pltpu.SemaphoreType.DMA((2 + width // LANES // chunks, chunks)),
            pltpu.SemaphoreType.DMA((6,)),
        ],
        cost_estimate=cost(4 * half * half * width, 6 * rows * width, half * half * width // 64),
        compiler_params=params(),
        name="attend_early",
    )(*in_hbm(offsets, queries, keys, values, cotangent, stashed))


def attend_late(queries, keys, values, offsets, weight, early):
    half, width = queries.shape
    rows = 2 * half
    return pl.pallas_call(
        functools.partial(late_kernel, rows),
        in_specs=[HBM] * 2 + [VMEM] * 4,
        out_specs=[VMEM] * 3,
        out_shape=[
            jax.ShapeDtypeStruct((early.shape[0] + width // POOL, half), jnp.bfloat16),
            jax.ShapeDtypeStruct((half, rows), jnp.float32),
            jax.ShapeDtypeStruct(weight.shape, weight.dtype),
        ],
        scratch_shapes=[
            pltpu.SMEM(offsets.shape, jnp.int32),
            pltpu.VMEM((half, rows), jnp.float32),
            pltpu.VMEM((half, rows), jnp.float32),
            pltpu.VMEM((half, rows), jnp.bfloat16),
            pltpu.VMEM((half, rows), jnp.bfloat16),
            pltpu.SemaphoreType.DMA((9,)),
        ],
        cost_estimate=cost(8 * half * half * width, 10 * half * width, half * half * width // 64),
        compiler_params=params(),
        name="attend_late",
    )(*in_hbm(offsets, weight), queries, keys, values, early)


def attend_halo(sent, keys, values, bias, after):
    half, width = bias.shape[0], keys.shape[1]
    return pl.pallas_call(
        halo_kernel,
        in_specs=[VMEM] * 4 + [ANY],
        out_specs=VMEM,
        out_shape=jax.ShapeDtypeStruct((width // LANES * (half // POOL + 2), LANES), jnp.bfloat16),
        scratch_shapes=[pltpu.VMEM((width // LANES, 2 * half), jnp.float32)] * 2,
        cost_estimate=cost(4 * half * half * width, 6 * half * width, half * half * width // 64),
        compiler_params=params(),
        name="attend_halo",
    )(sent, keys, values, bias, after)


def backward(slot, cotangent, weight, gain, stashed, after):
    rows, width = stashed.shape[1:]
    depth = weight.shape[1]
    return pl.pallas_call(
        back_kernel,
        in_specs=[VMEM] * 5 + [ANY],
        out_specs=[VMEM] * 2,
        scratch_shapes=[
            pltpu.VMEM((rows, width), jnp.float32),
            pltpu.VMEM((rows, width), jnp.bfloat16),
        ],
        out_shape=[
            jax.ShapeDtypeStruct((rows, width), jnp.bfloat16),
            jax.ShapeDtypeStruct((1, width), jnp.float32),
        ],
        cost_estimate=cost(2 * rows * width * depth, 2 * width * depth),
        compiler_params=params(),
        name="backward",
    )(slot, cotangent, weight, gain, stashed, after)


def project(early, both, halo, gain, weight, term, other, upstream):
    rows = upstream.shape[0]
    width, depth = weight.shape
    return pl.pallas_call(
        project_kernel,
        in_specs=[VMEM] * 7 + [ANY],
        out_specs=[VMEM, VMEM, HBM],
        out_shape=[
            jax.ShapeDtypeStruct((rows, depth), jnp.bfloat16),
            jax.ShapeDtypeStruct(term.shape, term.dtype),
            jax.ShapeDtypeStruct(upstream.shape, upstream.dtype),
        ],
        scratch_shapes=[
            pltpu.VMEM((rows, width), jnp.bfloat16),
            pltpu.VMEM((2 * width // LANES, LANES), jnp.float32),
            pltpu.SemaphoreType.DMA,
        ],
        cost_estimate=cost(2 * rows * width * depth, 2 * width * depth),
        compiler_params=params(),
        name="project",
    )(early, both, halo, gain, weight, term, other, upstream)


def swapped(value, axis, distance):
    return lax.ppermute(value, axis, [(i, i ^ distance) for i in range(lax.axis_size(axis))])


def sum_rounds():
    rounds = []
    for axis in ("rep", "seq"):
        count = lax.axis_size(axis)
        if count & (count - 1):
            return []
        rounds += [(axis, 1 << i) for i in range(count.bit_length() - 1)]
    return rounds if len(rounds) == 3 else []


def onward(value):
    sections, shards = lax.axis_size("section"), lax.axis_size("seq")
    route = [
        (s * shards + k, (s + 1) % sections * shards + k + 1)
        for s in range(sections)
        for k in range(shards - 1)
    ]
    return lax.ppermute(value, ("section", "seq"), route)


def local(queries, keys, values, doc_starts, weight, gain, stashed, cotangent, slot):
    queries, keys, values, offsets = queries[0, 0], keys[0, 0], values[0, 0], doc_starts[0]
    rounds = sum_rounds()

    def partner(term, index):
        return swapped(term, *rounds[index]) if rounds else jnp.zeros_like(term)

    sent, early, more, q_late, keys, values, cotangent, stashed = attend_early(
        queries, keys, values, offsets, cotangent[0, 0], stashed[0, 0], 4
    )
    arrived = shifted(sent, "seq", -1)
    early = passed_along(early, "section", 1)
    both, next_bias, weight = attend_late(q_late, keys, values, offsets, weight[0], more)
    slot = jnp.broadcast_to(slot, (1, LANES))
    dinput, term = backward(slot, cotangent, weight, gain, stashed, both)
    both = passed_along(both, "section", 1)
    upstream = passed_along(dinput, "section", -1)
    term = term if rounds else lax.psum(term, ("rep", "seq"))
    term = term + partner(term, 0)
    term = term + partner(term, 1)
    halo = onward(attend_halo(arrived, keys, values, next_bias, term))
    mol_keys, update, upstream = project(
        early, both, halo, gain, weight, term, partner(term, 2), upstream
    )
    return mol_keys[None, None], upstream[None, None], update


def solution(mesh):
    in_specs = (
        P("rep", "section", "seq", None),
        P("rep", "section", "seq", None),
        P("rep", "section", "seq", None),
        P("rep", "section", None),
        P("section", None, None),
        P("section", None),
        P("rep", "section", None, "seq", None),
        P("rep", "section", "seq", None),
        P("rep", "section"),
    )
    out_specs = (
        P("rep", "section", "seq", None),
        P("rep", "section", "seq", None),
        P("section", None),
    )
    return jax.shard_map(local, mesh=mesh, in_specs=in_specs, out_specs=out_specs, check_vma=False)
```

```python
import functools
import math

import jax
import jax.numpy as jnp
from jax import lax
from jax.experimental import pallas as pl
from jax.experimental.pallas import tpu as pltpu
from jax.sharding import PartitionSpec as P

HEAD_DIM = 64
POOL = 4
WINDOW = 128
LANES = 128
EPS_NORM = 1e-05
EPS_STEP = 1e-06
MASKED = -1e30
LAGS = (0, 3, 5, 6, 8)
EXTRA = 8

NT = (((1,), (1,)), ((), ()))


def dot_nt(a, b):
    return lax.dot_general(a, b, NT, preferred_element_type=jnp.float32)


def dot_nn(a, b):
    return jnp.dot(a, b, preferred_element_type=jnp.float32)


def shifted(value, axis, steps):
    count = lax.axis_size(axis)
    first, last = max(0, -steps), min(count, count - steps)
    return lax.ppermute(value, axis, [(i, i + steps) for i in range(first, last)])


def passed_along(value, axis, steps):
    count = lax.axis_size(axis)
    return lax.ppermute(value, axis, [(i, (i + steps) % count) for i in range(count)])


def earliest_key(offsets_ref, query_pos):
    start = jnp.zeros_like(query_pos)
    for d in range(offsets_ref.shape[1]):
        offset = offsets_ref[0, d]
        start = jnp.where(query_pos >= offset, offset, start)
    return jnp.maximum(start, query_pos - (WINDOW - 1))


def mask_bias(offsets_ref, query_start, key_start, keep):
    key = lax.broadcasted_iota(jnp.int32, (WINDOW, 2 * WINDOW), 0)
    query = lax.broadcasted_iota(jnp.int32, (WINDOW, 2 * WINDOW), 1) % WINDOW
    lane = lax.broadcasted_iota(jnp.int32, (1, 2 * WINDOW), 1) % WINDOW
    lowest = earliest_key(offsets_ref, query_start + lane)
    allowed = (key_start + key >= lowest) & keep(key, query)
    return jnp.where(allowed, 0.0, MASKED).astype(jnp.float32)


def split_heads(queries):
    lane = lax.broadcasted_iota(jnp.int32, (1, LANES), 1)
    scale = 1.0 / math.sqrt(HEAD_DIM)
    first = jnp.where(lane < HEAD_DIM, scale, 0.0).astype(jnp.bfloat16)
    second = jnp.where(lane < HEAD_DIM, 0.0, scale).astype(jnp.bfloat16)
    return jnp.concatenate([queries * first, queries * second], axis=0)


def pool_matrix(queries):
    molecule = lax.broadcasted_iota(jnp.int32, (queries // POOL, queries), 0)
    query = lax.broadcasted_iota(jnp.int32, (queries // POOL, queries), 1)
    return jnp.where(query // POOL == molecule, 1.0 / POOL, 0.0).astype(jnp.bfloat16)


def own_heads(mixed, scale):
    count = mixed.shape[1] // 2
    return jnp.concatenate(
        [
            mixed[:HEAD_DIM, :count] * scale[:, :count],
            mixed[HEAD_DIM:LANES, count:] * scale[:, count:],
        ],
        axis=0,
    )


def load(source, target, sem):
    copy = pltpu.make_async_copy(source, target, sem)
    copy.start()
    return copy


def load_chunks(arrays, chunks, sems, between):
    block = arrays[0][1].shape[1] // chunks
    copies, extra = [], None
    for chunk in range(chunks):
        columns = pl.ds(chunk * block, block)
        copies.append(
            [
                load(source.at[:, columns], target.at[:, columns], sems.at[i, chunk])
                for i, (source, target) in enumerate(arrays)
            ]
        )
        if chunk == 0:
            extra = between()
    return copies, extra


def at(pair):
    return pl.ds(pair * LANES, LANES)


def over_pairs(pairs, stages, lags, before):
    results = {}
    for step in range(pairs + lags[-1]):
        if step < pairs:
            before(step)
        for stage, lag in zip(stages, lags):
            pair = step - lag
            if 0 <= pair < pairs:
                results[pair] = stage(pair, *results.get(pair, ()))


def tops(scores):
    rows = scores.shape[0]
    while rows > 8:
        rows //= 2
        scores = jnp.maximum(scores[:rows], scores[rows:])
    return jnp.max(scores, axis=0, keepdims=True)


def with_ones(values_t):
    return jnp.concatenate([values_t, jnp.ones((16, values_t.shape[1]), jnp.bfloat16)], axis=0)


def three_terms(value):
    high = value.astype(jnp.bfloat16).astype(jnp.float32)
    middle = (value - high).astype(jnp.bfloat16).astype(jnp.float32)
    return [high, middle, value - high - middle]


def early_kernel(
    rows, chunks, offsets_hbm, q_hbm, k_hbm, v_hbm, cotangent_hbm, stashed_hbm,
    sent_ref, early_ref, more_ref, q_late_ref, k_ref, v_ref, cotangent_ref, stashed_ref,
    offsets_ref, bias, sems, offsets_sem,
):
    half = rows // 2
    head, tail = pl.ds(0, half), pl.ds(half, half)
    arrays = (
        (k_hbm.at[head], k_ref.at[head]),
        (q_hbm.at[head], sent_ref.at[head]),
        (v_hbm.at[head], v_ref.at[head]),
    )
    copies = load_chunks(arrays, chunks, sems, lambda: load(offsets_hbm, offsets_ref, offsets_sem.at[0]))
    copies, offsets_copy = copies
    later = (
        (k_hbm.at[tail], k_ref.at[tail]),
        (v_hbm.at[tail], v_ref.at[tail]),
        (q_hbm.at[tail], q_late_ref),
        (cotangent_hbm, cotangent_ref),
        (stashed_hbm, stashed_ref),
    )
    rest = []
    start = lax.axis_index("seq") * rows
    pairs = k_ref.shape[1] // LANES
    split = early_ref.shape[0] // LANES

    def arrive(pair):
        per_chunk = pairs // chunks
        if pair % per_chunk == 0:
            for copy in copies[pair // per_chunk]:
                copy.wait()
        if pair == 0:
            offsets_copy.wait()
            bias[...] = mask_bias(offsets_ref, start, start, lambda key, query: key <= query)
        if pair == per_chunk:
            for i, (source, target) in enumerate(later):
                rest.append(load(source, target, offsets_sem.at[i + 1]))

    def score(pair):
        scores = dot_nt(k_ref[head, at(pair)], split_heads(sent_ref[head, at(pair)]))
        return scores, with_ones(jnp.transpose(v_ref[head, at(pair)]))

    def top(pair, scores, values_t):
        return scores, tops(scores + bias[...]), values_t

    def weigh(pair, scores, top, values_t):
        return top, jnp.exp((scores + bias[...]) - top).astype(jnp.bfloat16), values_t

    def mix(pair, top, weights, values_t):
        return top, dot_nn(values_t, weights)

    def finish(pair, top, mixed):
        total = mixed[LANES : LANES + 1]
        target, place = (early_ref, pair) if pair < split else (more_ref, pair - split)
        target[at(place), :] = own_heads(mixed, 1.0 / total).astype(jnp.bfloat16)
        lse = top + jnp.log(total)
        terms = three_terms(lse[:, :half]) + three_terms(lse[:, half:])
        terms.append(jnp.zeros((EXTRA - 6, LANES), jnp.float32))
        sent_ref[pl.ds(half, EXTRA), at(pair)] = jnp.concatenate(terms, axis=0).astype(jnp.bfloat16)
        return ()

    over_pairs(pairs, (score, top, weigh, mix, finish), LAGS, arrive)
    for copy in rest:
        copy.wait()


def late_kernel(
    rows, offsets_hbm, weight_hbm, q_ref, k_ref, v_ref, early_ref, both_ref, next_ref, weight_ref,
    offsets_ref, own_bias, other_bias, own, other, sems,
):
    offsets_copy = load(offsets_hbm, offsets_ref, sems.at[8])
    block = weight_ref.shape[0] // 8
    copies = []
    for i in range(8):
        place = pl.ds(i * block, block)
        copies.append(load(weight_hbm.at[place], weight_ref.at[place], sems.at[i]))
    half = q_ref.shape[0]
    key = lax.broadcasted_iota(jnp.int32, own.shape, 0)
    query = lax.broadcasted_iota(jnp.int32, own.shape, 1) % half
    own[...] = jnp.where(key <= query, 1.0, 0.0).astype(jnp.bfloat16)
    other[...] = jnp.where(key <= query, 0.0, 1.0).astype(jnp.bfloat16)
    pooling = pool_matrix(half)
    molecules = half // POOL
    features = early_ref.shape[0]
    both_ref[pl.ds(0, features), :] = early_ref[...]
    pairs = k_ref.shape[1] // LANES
    offsets_copy.wait()
    start = lax.axis_index("seq") * rows
    own_bias[...] = mask_bias(offsets_ref, start + half, start + half, lambda key, query: key <= query)
    other_bias[...] = mask_bias(offsets_ref, start + half, start, lambda key, query: key > query)
    next_ref[...] = mask_bias(offsets_ref, start + rows, start + half, lambda key, query: key > query)
    parts = []

    def score(pair):
        scores = dot_nt(k_ref[:, at(pair)], split_heads(q_ref[:, at(pair)]))
        return scores, with_ones(jnp.transpose(v_ref[:, at(pair)]))

    def top(pair, scores, values_t):
        scores = jnp.maximum(scores[:half] + other_bias[...], scores[half:] + own_bias[...])
        return scores, tops(scores), values_t

    def weigh(pair, scores, top, values_t):
        weights = jnp.exp(scores - top).astype(jnp.bfloat16)
        return jnp.concatenate([weights * other[...], weights * own[...]], axis=0), values_t

    def mix(pair, weights, values_t):
        return (dot_nn(values_t, weights),)

    def finish(pair, mixed):
        inverse = 1.0 / mixed[LANES : LANES + 1]
        parts.append(own_heads(mixed, inverse).astype(jnp.bfloat16))
        if len(parts) == 4:
            pooled = dot_nt(pooling, jnp.concatenate(parts, axis=0)).astype(jnp.bfloat16)
            for i in range(4):
                place = features + (pair - 3 + i) * molecules
                both_ref[pl.ds(place, molecules), :] = pooled[:, i * LANES : (i + 1) * LANES]
            parts.clear()
        return ()

    over_pairs(pairs, (score, top, weigh, mix, finish), LAGS, lambda pair: None)
    for copy in copies:
        copy.wait()


def halo_kernel(q_ref, k_ref, v_ref, bias, after_ref, out_ref, share_ref):
    half = bias.shape[0]
    molecules = half // POOL
    tail = pl.ds(half, half)
    pooling = pool_matrix(half)
    pairs = k_ref.shape[1] // LANES
    parts = []

    def score(pair):
        queries = split_heads(q_ref[pl.ds(0, half), at(pair)])
        scores = dot_nt(k_ref[tail, at(pair)], queries)
        return scores, with_ones(jnp.transpose(v_ref[tail, at(pair)]))

    def top(pair, scores, values_t):
        terms = q_ref[pl.ds(half, EXTRA), at(pair)].astype(jnp.float32)
        lse = jnp.concatenate(
            [terms[0:1] + terms[1:2] + terms[2:3], terms[3:4] + terms[4:5] + terms[5:6]], axis=1
        )
        return scores, jnp.maximum(tops(scores + bias[...]), lse), lse, values_t

    def weigh(pair, scores, top, lse, values_t):
        weights = jnp.exp((scores + bias[...]) - top).astype(jnp.bfloat16)
        return weights, jnp.exp(lse - top), values_t

    def mix(pair, weights, kept, values_t):
        return dot_nn(values_t, weights), kept

    def finish(pair, mixed, kept):
        inverse = 1.0 / (mixed[LANES : LANES + 1] + kept)
        parts.append(own_heads(mixed, inverse).astype(jnp.bfloat16))
        if len(parts) == 4:
            pooled = dot_nt(pooling, jnp.concatenate(parts, axis=0)).astype(jnp.bfloat16)
            for i in range(4):
                place = pl.ds((pair - 3 + i) * molecules, molecules)
                out_ref[place, :] = pooled[:, i * LANES : (i + 1) * LANES]
            parts.clear()
        share_ref[pl.ds(pair, 1), :] = kept * inverse
        return ()

    over_pairs(pairs, (score, top, weigh, mix, finish), LAGS, lambda pair: None)
    share = share_ref[...].astype(jnp.bfloat16)
    out_ref[pl.ds(pairs * molecules, pairs), :] = share[:, :half]
    out_ref[pl.ds(pairs * (molecules + 1), pairs), :] = share[:, half:]


def back_kernel(
    slot_ref, cotangent_ref, weight_ref, gain_ref, stashed_ref, after_ref, dinput_ref, term_ref, grad, held_ref
):
    held = stashed_ref[0]
    for i in range(1, stashed_ref.shape[0]):
        held = jnp.where(slot_ref[0:1, 0:1] == i, stashed_ref[i].astype(jnp.float32), held.astype(jnp.float32))
    held_ref[...] = held.astype(jnp.bfloat16)
    features = weight_ref.shape[0]
    block = 512
    for begin in range(0, features, block):
        columns = pl.ds(begin, block)
        grad[:, columns] = dot_nt(cotangent_ref[...], weight_ref[columns, :])
    held = held_ref[...].astype(jnp.float32)
    inv_rms = lax.rsqrt(jnp.sum(held * held, axis=1, keepdims=True) / features + EPS_NORM)
    along = jnp.zeros_like(inv_rms)
    for begin in range(0, features, block):
        columns = pl.ds(begin, block)
        product = grad[:, columns] * (held_ref[:, columns].astype(jnp.float32) * inv_rms)
        term_ref[:, columns] = jnp.sum(product, axis=0, keepdims=True)
        along += jnp.sum(product * gain_ref[:, columns], axis=1, keepdims=True)
    along = along / features
    for begin in range(0, features, block):
        columns = pl.ds(begin, block)
        whitened = held_ref[:, columns].astype(jnp.float32) * inv_rms
        scaled = grad[:, columns] * gain_ref[:, columns]
        dinput_ref[:, columns] = (inv_rms * (scaled - whitened * along)).astype(jnp.bfloat16)


def project_kernel(
    early_ref, both_ref, halo_ref, gain_ref, weight_ref, term_ref, other_ref, upstream_hbm,
    out_ref, update_ref, passed_hbm, scaled_ref, share_ref, sem,
):
    passing = load(upstream_hbm, passed_hbm, sem)
    half = both_ref.shape[1]
    features = gain_ref.shape[1]
    first_part = early_ref.shape[0]
    molecules = half // POOL
    pooling = pool_matrix(half)
    first = lax.axis_index("seq") == 0
    squares, parts, pairs = 0.0, [], features // LANES
    shares = halo_ref[pl.ds(pairs * molecules, 2 * pairs), :].astype(jnp.float32)
    share_ref[...] = jnp.where(first, 1.0, shares)
    for pair in range(pairs):
        share_a, share_b = share_ref[pl.ds(pair, 1), :], share_ref[pl.ds(pairs + pair, 1), :]
        begin = pair * LANES
        if begin < first_part:
            early = early_ref[pl.ds(begin, LANES), :].astype(jnp.float32)
        else:
            early = both_ref[pl.ds(begin - first_part, LANES), :].astype(jnp.float32)
        parts += [early[:HEAD_DIM] * share_a, early[HEAD_DIM:] * share_b]
        if len(parts) == 8:
            columns = pl.ds((pair - 3) * LANES, 4 * LANES)
            mean = dot_nt(pooling, jnp.concatenate(parts, axis=0).astype(jnp.bfloat16))
            halo = [halo_ref[pl.ds((pair - 3 + i) * molecules, molecules), :] for i in range(4)]
            upper = mean + jnp.concatenate(halo, axis=1).astype(jnp.float32)
            place = features - first_part + (pair - 3) * molecules
            lower = [both_ref[pl.ds(place + i * molecules, molecules), :] for i in range(4)]
            lower = jnp.concatenate(lower, axis=1)
            arrived = jnp.concatenate([upper.astype(jnp.bfloat16), lower], axis=0).astype(jnp.float32)
            squares += jnp.sum(arrived * arrived, axis=1, keepdims=True)
            scaled_ref[:, columns] = (arrived * gain_ref[:, columns]).astype(jnp.bfloat16)
            parts = []
    product = dot_nn(scaled_ref[...], weight_ref[...])
    out_ref[...] = (product * lax.rsqrt(squares / features + EPS_NORM)).astype(jnp.bfloat16)
    total = term_ref[...] + other_ref[...]
    mean = jnp.sum(total * total, axis=1, keepdims=True) / features
    update_ref[...] = total / jnp.sqrt(mean + EPS_STEP)
    passing.wait()


def cost(flops, read, exps=0):
    return pl.CostEstimate(flops=flops, bytes_accessed=read, transcendentals=exps)


SMEM = pl.BlockSpec(memory_space=pltpu.SMEM)
HBM = pl.BlockSpec(memory_space=pltpu.HBM)
ANY = pl.BlockSpec(memory_space=pl.ANY)
VMEM = pl.BlockSpec(memory_space=pltpu.VMEM)


def in_hbm(*arrays):
    return [pltpu.with_memory_space_constraint(x, pltpu.HBM) for x in arrays]


def params():
    return pltpu.CompilerParams(vmem_limit_bytes=24 * 2**20)


def attend_early(queries, keys, values, offsets, cotangent, stashed, chunks):
    rows, width = queries.shape
    half = rows // 2
    soon = width // (4 * LANES) * 3 // 4 * 4 * LANES
    bf16 = lambda *shape: jax.ShapeDtypeStruct(shape, jnp.bfloat16)
    return pl.pallas_call(
        functools.partial(early_kernel, rows, chunks),
        in_specs=[HBM] * 6,
        out_specs=[VMEM] * 8,
        out_shape=[
            bf16(half + EXTRA, width),
            bf16(soon, half),
            bf16(width - soon, half),
            bf16(half, width),
            bf16(rows, width),
            bf16(rows, width),
            bf16(*cotangent.shape),
            bf16(*stashed.shape),
        ],
        scratch_shapes=[
            pltpu.SMEM(offsets.shape, jnp.int32),
            pltpu.VMEM((half, 2 * half), jnp.float32),
            pltpu.SemaphoreType.DMA((3, chunks)),
            pltpu.SemaphoreType.DMA((6,)),
        ],
        cost_estimate=cost(4 * half * half * width, 6 * rows * width, half * half * width // 64),
        compiler_params=params(),
        name="attend_early",
    )(*in_hbm(offsets, queries, keys, values, cotangent, stashed))


def attend_late(queries, keys, values, offsets, weight, early):
    half, width = queries.shape
    rows = 2 * half
    return pl.pallas_call(
        functools.partial(late_kernel, rows),
        in_specs=[HBM] * 2 + [VMEM] * 4,
        out_specs=[VMEM] * 3,
        out_shape=[
            jax.ShapeDtypeStruct((early.shape[0] + width // POOL, half), jnp.bfloat16),
            jax.ShapeDtypeStruct((half, rows), jnp.float32),
            jax.ShapeDtypeStruct(weight.shape, weight.dtype),
        ],
        scratch_shapes=[
            pltpu.SMEM(offsets.shape, jnp.int32),
            pltpu.VMEM((half, rows), jnp.float32),
            pltpu.VMEM((half, rows), jnp.float32),
            pltpu.VMEM((half, rows), jnp.bfloat16),
            pltpu.VMEM((half, rows), jnp.bfloat16),
            pltpu.SemaphoreType.DMA((9,)),
        ],
        cost_estimate=cost(8 * half * half * width, 10 * half * width, half * half * width // 64),
        compiler_params=params(),
        name="attend_late",
    )(*in_hbm(offsets, weight), queries, keys, values, early)


def attend_halo(sent, keys, values, bias, after):
    half, width = bias.shape[0], keys.shape[1]
    return pl.pallas_call(
        halo_kernel,
        in_specs=[VMEM] * 4 + [ANY],
        out_specs=VMEM,
        out_shape=jax.ShapeDtypeStruct((width // LANES * (half // POOL + 2), LANES), jnp.bfloat16),
        scratch_shapes=[pltpu.VMEM((width // LANES, 2 * half), jnp.float32)],
        cost_estimate=cost(4 * half * half * width, 6 * half * width, half * half * width // 64),
        compiler_params=params(),
        name="attend_halo",
    )(sent, keys, values, bias, after)


def backward(slot, cotangent, weight, gain, stashed, after):
    rows, width = stashed.shape[1:]
    depth = weight.shape[1]
    return pl.pallas_call(
        back_kernel,
        in_specs=[VMEM] * 5 + [ANY],
        out_specs=[VMEM] * 2,
        scratch_shapes=[
            pltpu.VMEM((rows, width), jnp.float32),
            pltpu.VMEM((rows, width), jnp.bfloat16),
        ],
        out_shape=[
            jax.ShapeDtypeStruct((rows, width), jnp.bfloat16),
            jax.ShapeDtypeStruct((1, width), jnp.float32),
        ],
        cost_estimate=cost(2 * rows * width * depth, 2 * width * depth),
        compiler_params=params(),
        name="backward",
    )(slot, cotangent, weight, gain, stashed, after)


def project(early, both, halo, gain, weight, term, other, upstream):
    rows = upstream.shape[0]
    width, depth = weight.shape
    return pl.pallas_call(
        project_kernel,
        in_specs=[VMEM] * 7 + [ANY],
        out_specs=[VMEM, VMEM, HBM],
        out_shape=[
            jax.ShapeDtypeStruct((rows, depth), jnp.bfloat16),
            jax.ShapeDtypeStruct(term.shape, term.dtype),
            jax.ShapeDtypeStruct(upstream.shape, upstream.dtype),
        ],
        scratch_shapes=[
            pltpu.VMEM((rows, width), jnp.bfloat16),
            pltpu.VMEM((2 * width // LANES, LANES), jnp.float32),
            pltpu.SemaphoreType.DMA,
        ],
        cost_estimate=cost(2 * rows * width * depth, 2 * width * depth),
        compiler_params=params(),
        name="project",
    )(early, both, halo, gain, weight, term, other, upstream)


def swapped(value, axis, distance):
    return lax.ppermute(value, axis, [(i, i ^ distance) for i in range(lax.axis_size(axis))])


def sum_rounds():
    rounds = []
    for axis in ("rep", "seq"):
        count = lax.axis_size(axis)
        if count & (count - 1):
            return []
        rounds += [(axis, 1 << i) for i in range(count.bit_length() - 1)]
    return rounds if len(rounds) == 3 else []


def onward(value):
    sections, shards = lax.axis_size("section"), lax.axis_size("seq")
    route = [
        (s * shards + k, (s + 1) % sections * shards + k + 1)
        for s in range(sections)
        for k in range(shards - 1)
    ]
    return lax.ppermute(value, ("section", "seq"), route)


def local(queries, keys, values, doc_starts, weight, gain, stashed, cotangent, slot):
    queries, keys, values, offsets = queries[0, 0], keys[0, 0], values[0, 0], doc_starts[0]
    rounds = sum_rounds()

    def partner(term, index):
        return swapped(term, *rounds[index]) if rounds else jnp.zeros_like(term)

    sent, early, more, q_late, keys, values, cotangent, stashed = attend_early(
        queries, keys, values, offsets, cotangent[0, 0], stashed[0, 0], 4
    )
    arrived = shifted(sent, "seq", -1)
    early = passed_along(early, "section", 1)
    both, next_bias, weight = attend_late(q_late, keys, values, offsets, weight[0], more)
    slot = jnp.broadcast_to(slot, (1, LANES))
    dinput, term = backward(slot, cotangent, weight, gain, stashed, both)
    both = passed_along(both, "section", 1)
    upstream = passed_along(dinput, "section", -1)
    term = term if rounds else lax.psum(term, ("rep", "seq"))
    term = term + partner(term, 0)
    term = term + partner(term, 1)
    halo = onward(attend_halo(arrived, keys, values, next_bias, term))
    mol_keys, update, upstream = project(
        early, both, halo, gain, weight, term, partner(term, 2), upstream
    )
    return mol_keys[None, None], upstream[None, None], update


def solution(mesh):
    in_specs = (
        P("rep", "section", "seq", None),
        P("rep", "section", "seq", None),
        P("rep", "section", "seq", None),
        P("rep", "section", None),
        P("section", None, None),
        P("section", None),
        P("rep", "section", None, "seq", None),
        P("rep", "section", "seq", None),
        P("rep", "section"),
    )
    out_specs = (
        P("rep", "section", "seq", None),
        P("rep", "section", "seq", None),
        P("section", None),
    )
    return jax.shard_map(local, mesh=mesh, in_specs=in_specs, out_specs=out_specs, check_vma=False)
```

```python
import functools
import math

import jax
import jax.numpy as jnp
from jax import lax
from jax.experimental import pallas as pl
from jax.experimental.pallas import tpu as pltpu
from jax.sharding import PartitionSpec as P

HEAD_DIM = 64
POOL = 4
WINDOW = 128
LANES = 128
EPS_NORM = 1e-05
EPS_STEP = 1e-06
MASKED = -1e30
LAGS = (0, 3, 5, 6, 8)
EXTRA = 8

NT = (((1,), (1,)), ((), ()))


def dot_nt(a, b):
    return lax.dot_general(a, b, NT, preferred_element_type=jnp.float32)


def dot_nn(a, b):
    return jnp.dot(a, b, preferred_element_type=jnp.float32)


def shifted(value, axis, steps):
    count = lax.axis_size(axis)
    first, last = max(0, -steps), min(count, count - steps)
    return lax.ppermute(value, axis, [(i, i + steps) for i in range(first, last)])


def passed_along(value, axis, steps):
    count = lax.axis_size(axis)
    return lax.ppermute(value, axis, [(i, (i + steps) % count) for i in range(count)])


def earliest_key(offsets_ref, query_pos):
    start = jnp.zeros_like(query_pos)
    for d in range(offsets_ref.shape[1]):
        offset = offsets_ref[0, d]
        start = jnp.where(query_pos >= offset, offset, start)
    return jnp.maximum(start, query_pos - (WINDOW - 1))


def mask_bias(offsets_ref, query_start, key_start, keep):
    key = lax.broadcasted_iota(jnp.int32, (WINDOW, 2 * WINDOW), 0)
    query = lax.broadcasted_iota(jnp.int32, (WINDOW, 2 * WINDOW), 1) % WINDOW
    lane = lax.broadcasted_iota(jnp.int32, (1, 2 * WINDOW), 1) % WINDOW
    lowest = earliest_key(offsets_ref, query_start + lane)
    allowed = (key_start + key >= lowest) & keep(key, query)
    return jnp.where(allowed, 0.0, MASKED).astype(jnp.float32)


def split_heads(queries):
    lane = lax.broadcasted_iota(jnp.int32, (1, LANES), 1)
    scale = 1.0 / math.sqrt(HEAD_DIM)
    first = jnp.where(lane < HEAD_DIM, scale, 0.0).astype(jnp.bfloat16)
    second = jnp.where(lane < HEAD_DIM, 0.0, scale).astype(jnp.bfloat16)
    return jnp.concatenate([queries * first, queries * second], axis=0)


def pool_matrix(queries):
    molecule = lax.broadcasted_iota(jnp.int32, (queries // POOL, queries), 0)
    query = lax.broadcasted_iota(jnp.int32, (queries // POOL, queries), 1)
    return jnp.where(query // POOL == molecule, 1.0 / POOL, 0.0).astype(jnp.bfloat16)


def own_heads(mixed, scale):
    count = mixed.shape[1] // 2
    return jnp.concatenate(
        [
            mixed[:HEAD_DIM, :count] * scale[:, :count],
            mixed[HEAD_DIM:LANES, count:] * scale[:, count:],
        ],
        axis=0,
    )


def load(source, target, sem):
    copy = pltpu.make_async_copy(source, target, sem)
    copy.start()
    return copy


def load_chunks(arrays, chunks, sems, between):
    block = arrays[0][1].shape[1] // chunks
    copies, extra = [], None
    for chunk in range(chunks):
        columns = pl.ds(chunk * block, block)
        copies.append(
            [
                load(source.at[:, columns], target.at[:, columns], sems.at[i, chunk])
                for i, (source, target) in enumerate(arrays)
            ]
        )
        if chunk == 0:
            extra = between()
    return copies, extra


def at(pair):
    return pl.ds(pair * LANES, LANES)


def over_pairs(pairs, stages, lags, before):
    results = {}
    for step in range(pairs + lags[-1]):
        if step < pairs:
            before(step)
        for stage, lag in zip(stages, lags):
            pair = step - lag
            if 0 <= pair < pairs:
                results[pair] = stage(pair, *results.get(pair, ()))


def tops(scores):
    rows = scores.shape[0]
    while rows > 8:
        rows //= 2
        scores = jnp.maximum(scores[:rows], scores[rows:])
    return jnp.max(scores, axis=0, keepdims=True)


def with_ones(values_t):
    return jnp.concatenate([values_t, jnp.ones((16, values_t.shape[1]), jnp.bfloat16)], axis=0)


def three_terms(value):
    high = value.astype(jnp.bfloat16).astype(jnp.float32)
    middle = (value - high).astype(jnp.bfloat16).astype(jnp.float32)
    return [high, middle, value - high - middle]


def early_kernel(
    rows, chunks, offsets_hbm, q_hbm, k_hbm, v_hbm, cotangent_hbm, stashed_hbm,
    sent_ref, early_ref, more_ref, q_late_ref, k_ref, v_ref, cotangent_ref, stashed_ref,
    offsets_ref, bias, sems, offsets_sem,
):
    half = rows // 2
    head, tail = pl.ds(0, half), pl.ds(half, half)
    arrays = (
        (k_hbm.at[head], k_ref.at[head]),
        (q_hbm.at[head], sent_ref.at[head]),
        (v_hbm.at[head], v_ref.at[head]),
    )
    copies = load_chunks(arrays, chunks, sems, lambda: load(offsets_hbm, offsets_ref, offsets_sem.at[0]))
    copies, offsets_copy = copies
    later = (
        (k_hbm.at[tail], k_ref.at[tail]),
        (v_hbm.at[tail], v_ref.at[tail]),
        (q_hbm.at[tail], q_late_ref),
        (cotangent_hbm, cotangent_ref),
        (stashed_hbm, stashed_ref),
    )
    rest = []
    start = lax.axis_index("seq") * rows
    pairs = k_ref.shape[1] // LANES
    split = early_ref.shape[0] // LANES

    def arrive(pair):
        per_chunk = pairs // chunks
        if pair % per_chunk == 0:
            for copy in copies[pair // per_chunk]:
                copy.wait()
        if pair == 0:
            offsets_copy.wait()
            bias[...] = mask_bias(offsets_ref, start, start, lambda key, query: key <= query)
        if pair == per_chunk:
            for i, (source, target) in enumerate(later):
                rest.append(load(source, target, offsets_sem.at[i + 1]))

    def score(pair):
        scores = dot_nt(k_ref[head, at(pair)], split_heads(sent_ref[head, at(pair)]))
        return scores, with_ones(jnp.transpose(v_ref[head, at(pair)]))

    def top(pair, scores, values_t):
        return scores, tops(scores + bias[...]), values_t

    def weigh(pair, scores, top, values_t):
        return top, jnp.exp((scores + bias[...]) - top).astype(jnp.bfloat16), values_t

    def mix(pair, top, weights, values_t):
        return top, dot_nn(values_t, weights)

    def finish(pair, top, mixed):
        total = mixed[LANES : LANES + 1]
        target, place = (early_ref, pair) if pair < split else (more_ref, pair - split)
        target[at(place), :] = own_heads(mixed, 1.0 / total).astype(jnp.bfloat16)
        lse = top + jnp.log(total)
        terms = three_terms(lse[:, :half]) + three_terms(lse[:, half:])
        terms.append(jnp.zeros((EXTRA - 6, LANES), jnp.float32))
        sent_ref[pl.ds(half, EXTRA), at(pair)] = jnp.concatenate(terms, axis=0).astype(jnp.bfloat16)
        return ()

    over_pairs(pairs, (score, top, weigh, mix, finish), LAGS, arrive)
    for copy in rest:
        copy.wait()


def late_kernel(
    rows, offsets_hbm, weight_hbm, q_ref, k_ref, v_ref, early_ref, both_ref, next_ref, weight_ref,
    offsets_ref, own_bias, other_bias, own, other, sems,
):
    offsets_copy = load(offsets_hbm, offsets_ref, sems.at[8])
    block = weight_ref.shape[0] // 8
    copies = []
    for i in range(8):
        place = pl.ds(i * block, block)
        copies.append(load(weight_hbm.at[place], weight_ref.at[place], sems.at[i]))
    half = q_ref.shape[0]
    key = lax.broadcasted_iota(jnp.int32, own.shape, 0)
    query = lax.broadcasted_iota(jnp.int32, own.shape, 1) % half
    own[...] = jnp.where(key <= query, 1.0, 0.0).astype(jnp.bfloat16)
    other[...] = jnp.where(key <= query, 0.0, 1.0).astype(jnp.bfloat16)
    pooling = pool_matrix(half)
    molecules = half // POOL
    features = early_ref.shape[0]
    both_ref[pl.ds(0, features), :] = early_ref[...]
    pairs = k_ref.shape[1] // LANES
    offsets_copy.wait()
    start = lax.axis_index("seq") * rows
    own_bias[...] = mask_bias(offsets_ref, start + half, start + half, lambda key, query: key <= query)
    other_bias[...] = mask_bias(offsets_ref, start + half, start, lambda key, query: key > query)
    next_ref[...] = mask_bias(offsets_ref, start + rows, start + half, lambda key, query: key > query)
    parts = []

    def score(pair):
        scores = dot_nt(k_ref[:, at(pair)], split_heads(q_ref[:, at(pair)]))
        return scores, with_ones(jnp.transpose(v_ref[:, at(pair)]))

    def top(pair, scores, values_t):
        scores = jnp.maximum(scores[:half] + other_bias[...], scores[half:] + own_bias[...])
        return scores, tops(scores), values_t

    def weigh(pair, scores, top, values_t):
        weights = jnp.exp(scores - top).astype(jnp.bfloat16)
        return jnp.concatenate([weights * other[...], weights * own[...]], axis=0), values_t

    def mix(pair, weights, values_t):
        return (dot_nn(values_t, weights),)

    def finish(pair, mixed):
        inverse = 1.0 / mixed[LANES : LANES + 1]
        parts.append(own_heads(mixed, inverse).astype(jnp.bfloat16))
        if len(parts) == 4:
            pooled = dot_nt(pooling, jnp.concatenate(parts, axis=0)).astype(jnp.bfloat16)
            for i in range(4):
                place = features + (pair - 3 + i) * molecules
                both_ref[pl.ds(place, molecules), :] = pooled[:, i * LANES : (i + 1) * LANES]
            parts.clear()
        return ()

    over_pairs(pairs, (score, top, weigh, mix, finish), LAGS, lambda pair: None)
    for copy in copies:
        copy.wait()


def halo_kernel(q_ref, k_ref, v_ref, bias, after_ref, out_ref, share_ref):
    half = bias.shape[0]
    molecules = half // POOL
    tail = pl.ds(half, half)
    pooling = pool_matrix(half)
    pairs = k_ref.shape[1] // LANES
    parts = []

    def score(pair):
        queries = split_heads(q_ref[pl.ds(0, half), at(pair)])
        scores = dot_nt(k_ref[tail, at(pair)], queries)
        return scores, with_ones(jnp.transpose(v_ref[tail, at(pair)]))

    def top(pair, scores, values_t):
        terms = q_ref[pl.ds(half, EXTRA), at(pair)].astype(jnp.float32)
        lse = jnp.concatenate(
            [terms[0:1] + terms[1:2] + terms[2:3], terms[3:4] + terms[4:5] + terms[5:6]], axis=1
        )
        return scores, jnp.maximum(tops(scores + bias[...]), lse), lse, values_t

    def weigh(pair, scores, top, lse, values_t):
        weights = jnp.exp((scores + bias[...]) - top).astype(jnp.bfloat16)
        return weights, jnp.exp(lse - top), values_t

    def mix(pair, weights, kept, values_t):
        return dot_nn(values_t, weights), kept

    def finish(pair, mixed, kept):
        inverse = 1.0 / (mixed[LANES : LANES + 1] + kept)
        parts.append(own_heads(mixed, inverse).astype(jnp.bfloat16))
        if len(parts) == 4:
            pooled = dot_nt(pooling, jnp.concatenate(parts, axis=0)).astype(jnp.bfloat16)
            for i in range(4):
                place = pl.ds((pair - 3 + i) * molecules, molecules)
                out_ref[place, :] = pooled[:, i * LANES : (i + 1) * LANES]
            parts.clear()
        share_ref[pl.ds(pair, 1), :] = kept * inverse
        return ()

    over_pairs(pairs, (score, top, weigh, mix, finish), LAGS, lambda pair: None)
    share = share_ref[...].astype(jnp.bfloat16)
    out_ref[pl.ds(pairs * molecules, pairs), :] = share[:, :half]
    out_ref[pl.ds(pairs * (molecules + 1), pairs), :] = share[:, half:]


def back_kernel(
    slot_ref, cotangent_ref, weight_ref, gain_ref, stashed_ref, after_ref, dinput_ref, term_ref, grad, held_ref
):
    held = stashed_ref[0]
    for i in range(1, stashed_ref.shape[0]):
        held = jnp.where(slot_ref[0:1, 0:1] == i, stashed_ref[i].astype(jnp.float32), held.astype(jnp.float32))
    held_ref[...] = held.astype(jnp.bfloat16)
    features = weight_ref.shape[0]
    block = 512
    for begin in range(0, features, block):
        columns = pl.ds(begin, block)
        grad[:, columns] = dot_nt(cotangent_ref[...], weight_ref[columns, :])
    held = held_ref[...].astype(jnp.float32)
    inv_rms = lax.rsqrt(jnp.sum(held * held, axis=1, keepdims=True) / features + EPS_NORM)
    along = jnp.zeros_like(inv_rms)
    for begin in range(0, features, block):
        columns = pl.ds(begin, block)
        product = grad[:, columns] * (held_ref[:, columns].astype(jnp.float32) * inv_rms)
        term_ref[:, columns] = jnp.sum(product, axis=0, keepdims=True)
        along += jnp.sum(product * gain_ref[:, columns], axis=1, keepdims=True)
    along = along / features
    for begin in range(0, features, block):
        columns = pl.ds(begin, block)
        whitened = held_ref[:, columns].astype(jnp.float32) * inv_rms
        scaled = grad[:, columns] * gain_ref[:, columns]
        dinput_ref[:, columns] = (inv_rms * (scaled - whitened * along)).astype(jnp.bfloat16)


def project_kernel(
    early_ref, both_ref, halo_ref, gain_ref, weight_ref, term_ref, other_ref, upstream_hbm,
    out_ref, update_ref, passed_hbm, scaled_ref, share_ref, sem,
):
    passing = load(upstream_hbm, passed_hbm, sem)
    half = both_ref.shape[1]
    features = gain_ref.shape[1]
    first_part = early_ref.shape[0]
    molecules = half // POOL
    pooling = pool_matrix(half)
    first = lax.axis_index("seq") == 0
    squares, parts, pairs = 0.0, [], features // LANES
    shares = halo_ref[pl.ds(pairs * molecules, 2 * pairs), :].astype(jnp.float32)
    share_ref[...] = jnp.where(first, 1.0, shares)
    for pair in range(pairs):
        share_a, share_b = share_ref[pl.ds(pair, 1), :], share_ref[pl.ds(pairs + pair, 1), :]
        begin = pair * LANES
        if begin < first_part:
            early = early_ref[pl.ds(begin, LANES), :].astype(jnp.float32)
        else:
            early = both_ref[pl.ds(begin - first_part, LANES), :].astype(jnp.float32)
        parts += [early[:HEAD_DIM] * share_a, early[HEAD_DIM:] * share_b]
        if len(parts) == 8:
            columns = pl.ds((pair - 3) * LANES, 4 * LANES)
            mean = dot_nt(pooling, jnp.concatenate(parts, axis=0).astype(jnp.bfloat16))
            halo = [halo_ref[pl.ds((pair - 3 + i) * molecules, molecules), :] for i in range(4)]
            upper = mean + jnp.concatenate(halo, axis=1).astype(jnp.float32)
            place = features - first_part + (pair - 3) * molecules
            lower = [both_ref[pl.ds(place + i * molecules, molecules), :] for i in range(4)]
            lower = jnp.concatenate(lower, axis=1)
            arrived = jnp.concatenate([upper.astype(jnp.bfloat16), lower], axis=0).astype(jnp.float32)
            squares += jnp.sum(arrived * arrived, axis=1, keepdims=True)
            scaled_ref[:, columns] = (arrived * gain_ref[:, columns]).astype(jnp.bfloat16)
            parts = []
    product = dot_nn(scaled_ref[...], weight_ref[...])
    out_ref[...] = (product * lax.rsqrt(squares / features + EPS_NORM)).astype(jnp.bfloat16)
    total = term_ref[...] + other_ref[...]
    mean = jnp.sum(total * total, axis=1, keepdims=True) / features
    update_ref[...] = total / jnp.sqrt(mean + EPS_STEP)
    passing.wait()


def cost(flops, read, exps=0):
    return pl.CostEstimate(flops=flops, bytes_accessed=read, transcendentals=exps)


SMEM = pl.BlockSpec(memory_space=pltpu.SMEM)
HBM = pl.BlockSpec(memory_space=pltpu.HBM)
ANY = pl.BlockSpec(memory_space=pl.ANY)
VMEM = pl.BlockSpec(memory_space=pltpu.VMEM)


def in_hbm(*arrays):
    return [pltpu.with_memory_space_constraint(x, pltpu.HBM) for x in arrays]


def params():
    return pltpu.CompilerParams(vmem_limit_bytes=24 * 2**20)


def attend_early(queries, keys, values, offsets, cotangent, stashed, chunks):
    rows, width = queries.shape
    half = rows // 2
    soon = width // (4 * LANES) * 3 // 4 * 4 * LANES
    bf16 = lambda *shape: jax.ShapeDtypeStruct(shape, jnp.bfloat16)
    return pl.pallas_call(
        functools.partial(early_kernel, rows, chunks),
        in_specs=[HBM] * 6,
        out_specs=[VMEM] * 8,
        out_shape=[
            bf16(half + EXTRA, width),
            bf16(soon, half),
            bf16(width - soon, half),
            bf16(half, width),
            bf16(rows, width),
            bf16(rows, width),
            bf16(*cotangent.shape),
            bf16(*stashed.shape),
        ],
        scratch_shapes=[
            pltpu.SMEM(offsets.shape, jnp.int32),
            pltpu.VMEM((half, 2 * half), jnp.float32),
            pltpu.SemaphoreType.DMA((3, chunks)),
            pltpu.SemaphoreType.DMA((6,)),
        ],
        cost_estimate=cost(4 * half * half * width, 6 * rows * width, half * half * width // 64),
        compiler_params=params(),
        name="attend_early",
    )(*in_hbm(offsets, queries, keys, values, cotangent, stashed))


def attend_late(queries, keys, values, offsets, weight, early):
    half, width = queries.shape
    rows = 2 * half
    return pl.pallas_call(
        functools.partial(late_kernel, rows),
        in_specs=[HBM] * 2 + [VMEM] * 4,
        out_specs=[VMEM] * 3,
        out_shape=[
            jax.ShapeDtypeStruct((early.shape[0] + width // POOL, half), jnp.bfloat16),
            jax.ShapeDtypeStruct((half, rows), jnp.float32),
            jax.ShapeDtypeStruct(weight.shape, weight.dtype),
        ],
        scratch_shapes=[
            pltpu.SMEM(offsets.shape, jnp.int32),
            pltpu.VMEM((half, rows), jnp.float32),
            pltpu.VMEM((half, rows), jnp.float32),
            pltpu.VMEM((half, rows), jnp.bfloat16),
            pltpu.VMEM((half, rows), jnp.bfloat16),
            pltpu.SemaphoreType.DMA((9,)),
        ],
        cost_estimate=cost(8 * half * half * width, 10 * half * width, half * half * width // 64),
        compiler_params=params(),
        name="attend_late",
    )(*in_hbm(offsets, weight), queries, keys, values, early)


def attend_halo(sent, keys, values, bias, after):
    half, width = bias.shape[0], keys.shape[1]
    return pl.pallas_call(
        halo_kernel,
        in_specs=[VMEM] * 4 + [ANY],
        out_specs=VMEM,
        out_shape=jax.ShapeDtypeStruct((width // LANES * (half // POOL + 2), LANES), jnp.bfloat16),
        scratch_shapes=[pltpu.VMEM((width // LANES, 2 * half), jnp.float32)],
        cost_estimate=cost(4 * half * half * width, 6 * half * width, half * half * width // 64),
        compiler_params=params(),
        name="attend_halo",
    )(sent, keys, values, bias, after)


def backward(slot, cotangent, weight, gain, stashed, after):
    rows, width = stashed.shape[1:]
    depth = weight.shape[1]
    return pl.pallas_call(
        back_kernel,
        in_specs=[VMEM] * 5 + [ANY],
        out_specs=[VMEM] * 2,
        scratch_shapes=[
            pltpu.VMEM((rows, width), jnp.float32),
            pltpu.VMEM((rows, width), jnp.bfloat16),
        ],
        out_shape=[
            jax.ShapeDtypeStruct((rows, width), jnp.bfloat16),
            jax.ShapeDtypeStruct((1, width), jnp.float32),
        ],
        cost_estimate=cost(2 * rows * width * depth, 2 * width * depth),
        compiler_params=params(),
        name="backward",
    )(slot, cotangent, weight, gain, stashed, after)


def project(early, both, halo, gain, weight, term, other, upstream):
    rows = upstream.shape[0]
    width, depth = weight.shape
    return pl.pallas_call(
        project_kernel,
        in_specs=[VMEM] * 7 + [ANY],
        out_specs=[VMEM, VMEM, HBM],
        out_shape=[
            jax.ShapeDtypeStruct((rows, depth), jnp.bfloat16),
            jax.ShapeDtypeStruct(term.shape, term.dtype),
            jax.ShapeDtypeStruct(upstream.shape, upstream.dtype),
        ],
        scratch_shapes=[
            pltpu.VMEM((rows, width), jnp.bfloat16),
            pltpu.VMEM((2 * width // LANES, LANES), jnp.float32),
            pltpu.SemaphoreType.DMA,
        ],
        cost_estimate=cost(2 * rows * width * depth, 2 * width * depth),
        compiler_params=params(),
        name="project",
    )(early, both, halo, gain, weight, term, other, upstream)


def swapped(value, axis, distance):
    return lax.ppermute(value, axis, [(i, i ^ distance) for i in range(lax.axis_size(axis))])


def sum_rounds():
    rounds = []
    for axis in ("rep", "seq"):
        count = lax.axis_size(axis)
        if count & (count - 1):
            return []
        rounds += [(axis, (2 << i) - 1) for i in range(count.bit_length() - 1)]
    return rounds if len(rounds) == 3 else []


def onward(value):
    sections, shards = lax.axis_size("section"), lax.axis_size("seq")
    route = [
        (s * shards + k, (s + 1) % sections * shards + k + 1)
        for s in range(sections)
        for k in range(shards - 1)
    ]
    return lax.ppermute(value, ("section", "seq"), route)


def local(queries, keys, values, doc_starts, weight, gain, stashed, cotangent, slot):
    queries, keys, values, offsets = queries[0, 0], keys[0, 0], values[0, 0], doc_starts[0]
    rounds = sum_rounds()

    def partner(term, index):
        return swapped(term, *rounds[index]) if rounds else jnp.zeros_like(term)

    sent, early, more, q_late, keys, values, cotangent, stashed = attend_early(
        queries, keys, values, offsets, cotangent[0, 0], stashed[0, 0], 4
    )
    arrived = shifted(sent, "seq", -1)
    early = passed_along(early, "section", 1)
    both, next_bias, weight = attend_late(q_late, keys, values, offsets, weight[0], more)
    slot = jnp.broadcast_to(slot, (1, LANES))
    dinput, term = backward(slot, cotangent, weight, gain, stashed, both)
    both = passed_along(both, "section", 1)
    upstream = passed_along(dinput, "section", -1)
    term = term if rounds else lax.psum(term, ("rep", "seq"))
    term = term + partner(term, 0)
    term = term + partner(term, 1)
    halo = onward(attend_halo(arrived, keys, values, next_bias, term))
    mol_keys, update, upstream = project(
        early, both, halo, gain, weight, term, partner(term, 2), upstream
    )
    return mol_keys[None, None], upstream[None, None], update


def solution(mesh):
    in_specs = (
        P("rep", "section", "seq", None),
        P("rep", "section", "seq", None),
        P("rep", "section", "seq", None),
        P("rep", "section", None),
        P("section", None, None),
        P("section", None),
        P("rep", "section", None, "seq", None),
        P("rep", "section", "seq", None),
        P("rep", "section"),
    )
    out_specs = (
        P("rep", "section", "seq", None),
        P("rep", "section", "seq", None),
        P("section", None),
    )
    return jax.shard_map(local, mesh=mesh, in_specs=in_specs, out_specs=out_specs, check_vma=False)
```

```python
import functools
import math

import jax
import jax.numpy as jnp
from jax import lax
from jax.experimental import pallas as pl
from jax.experimental.pallas import tpu as pltpu
from jax.sharding import PartitionSpec as P

HEAD_DIM = 64
POOL = 4
WINDOW = 128
LANES = 128
EPS_NORM = 1e-05
EPS_STEP = 1e-06
MASKED = -1e30
LAGS = (0, 3, 5, 6, 8)
EXTRA = 8

NT = (((1,), (1,)), ((), ()))


def dot_nt(a, b):
    return lax.dot_general(a, b, NT, preferred_element_type=jnp.float32)


def dot_nn(a, b):
    return jnp.dot(a, b, preferred_element_type=jnp.float32)


def shifted(value, axis, steps):
    count = lax.axis_size(axis)
    first, last = max(0, -steps), min(count, count - steps)
    return lax.ppermute(value, axis, [(i, i + steps) for i in range(first, last)])


def passed_along(value, axis, steps):
    count = lax.axis_size(axis)
    return lax.ppermute(value, axis, [(i, (i + steps) % count) for i in range(count)])


def earliest_key(offsets_ref, query_pos):
    start = jnp.zeros_like(query_pos)
    for d in range(offsets_ref.shape[1]):
        offset = offsets_ref[0, d]
        start = jnp.where(query_pos >= offset, offset, start)
    return jnp.maximum(start, query_pos - (WINDOW - 1))


def mask_bias(offsets_ref, query_start, key_start, keep):
    key = lax.broadcasted_iota(jnp.int32, (WINDOW, 2 * WINDOW), 0)
    query = lax.broadcasted_iota(jnp.int32, (WINDOW, 2 * WINDOW), 1) % WINDOW
    lane = lax.broadcasted_iota(jnp.int32, (1, 2 * WINDOW), 1) % WINDOW
    lowest = earliest_key(offsets_ref, query_start + lane)
    allowed = (key_start + key >= lowest) & keep(key, query)
    return jnp.where(allowed, 0.0, MASKED).astype(jnp.float32)


def split_heads(queries):
    lane = lax.broadcasted_iota(jnp.int32, (1, LANES), 1)
    scale = 1.0 / math.sqrt(HEAD_DIM)
    first = jnp.where(lane < HEAD_DIM, scale, 0.0).astype(jnp.bfloat16)
    second = jnp.where(lane < HEAD_DIM, 0.0, scale).astype(jnp.bfloat16)
    return jnp.concatenate([queries * first, queries * second], axis=0)


def pool_matrix(queries):
    molecule = lax.broadcasted_iota(jnp.int32, (queries // POOL, queries), 0)
    query = lax.broadcasted_iota(jnp.int32, (queries // POOL, queries), 1)
    return jnp.where(query // POOL == molecule, 1.0 / POOL, 0.0).astype(jnp.bfloat16)


def own_heads(mixed, scale):
    count = mixed.shape[1] // 2
    return jnp.concatenate(
        [
            mixed[:HEAD_DIM, :count] * scale[:, :count],
            mixed[HEAD_DIM:LANES, count:] * scale[:, count:],
        ],
        axis=0,
    )


def load(source, target, sem):
    copy = pltpu.make_async_copy(source, target, sem)
    copy.start()
    return copy


def load_chunks(arrays, begins, sems, between):
    width = arrays[0][1].shape[1]
    copies, extra = [], None
    for chunk, (begin, end) in enumerate(zip(begins, begins[1:] + [width])):
        columns = pl.ds(begin, end - begin)
        copies.append(
            [
                load(source.at[:, columns], target.at[:, columns], sems.at[i, chunk])
                for i, (source, target) in enumerate(arrays)
            ]
        )
        if chunk == 0:
            extra = between()
    return copies, extra


def at(pair):
    return pl.ds(pair * LANES, LANES)


def over_pairs(pairs, stages, lags, before):
    results = {}
    for step in range(pairs + lags[-1]):
        if step < pairs:
            before(step)
        for stage, lag in zip(stages, lags):
            pair = step - lag
            if 0 <= pair < pairs:
                results[pair] = stage(pair, *results.get(pair, ()))


def tops(scores):
    rows = scores.shape[0]
    while rows > 8:
        rows //= 2
        scores = jnp.maximum(scores[:rows], scores[rows:])
    return jnp.max(scores, axis=0, keepdims=True)


def with_ones(values_t):
    return jnp.concatenate([values_t, jnp.ones((16, values_t.shape[1]), jnp.bfloat16)], axis=0)


def three_terms(value):
    high = value.astype(jnp.bfloat16).astype(jnp.float32)
    middle = (value - high).astype(jnp.bfloat16).astype(jnp.float32)
    return [high, middle, value - high - middle]


def early_kernel(
    rows, chunks, offsets_hbm, q_hbm, k_hbm, v_hbm, cotangent_hbm, stashed_hbm,
    sent_ref, early_ref, more_ref, q_late_ref, k_ref, v_ref, cotangent_ref, stashed_ref,
    offsets_ref, bias, sems, offsets_sem,
):
    half = rows // 2
    head, tail = pl.ds(0, half), pl.ds(half, half)
    arrays = (
        (k_hbm.at[head], k_ref.at[head]),
        (q_hbm.at[head], sent_ref.at[head]),
        (v_hbm.at[head], v_ref.at[head]),
    )
    begins = [0, k_ref.shape[1] // chunks]
    copies, offsets_copy = load_chunks(
        arrays, begins, sems, lambda: load(offsets_hbm, offsets_ref, offsets_sem.at[0])
    )
    later = (
        (k_hbm.at[tail], k_ref.at[tail]),
        (v_hbm.at[tail], v_ref.at[tail]),
        (q_hbm.at[tail], q_late_ref),
        (cotangent_hbm, cotangent_ref),
        (stashed_hbm, stashed_ref),
    )
    rest = []
    start = lax.axis_index("seq") * rows
    pairs = k_ref.shape[1] // LANES
    split = early_ref.shape[0] // LANES

    def arrive(pair):
        if pair * LANES in begins:
            for copy in copies[begins.index(pair * LANES)]:
                copy.wait()
        if pair == 0:
            offsets_copy.wait()
            bias[...] = mask_bias(offsets_ref, start, start, lambda key, query: key <= query)
        if pair * LANES == begins[1]:
            for i, (source, target) in enumerate(later):
                rest.append(load(source, target, offsets_sem.at[i + 1]))

    def score(pair):
        scores = dot_nt(k_ref[head, at(pair)], split_heads(sent_ref[head, at(pair)]))
        return scores, with_ones(jnp.transpose(v_ref[head, at(pair)]))

    def top(pair, scores, values_t):
        return scores, tops(scores + bias[...]), values_t

    def weigh(pair, scores, top, values_t):
        return top, jnp.exp((scores + bias[...]) - top).astype(jnp.bfloat16), values_t

    def mix(pair, top, weights, values_t):
        return top, dot_nn(values_t, weights)

    def finish(pair, top, mixed):
        total = mixed[LANES : LANES + 1]
        target, place = (early_ref, pair) if pair < split else (more_ref, pair - split)
        target[at(place), :] = own_heads(mixed, 1.0 / total).astype(jnp.bfloat16)
        lse = top + jnp.log(total)
        terms = three_terms(lse[:, :half]) + three_terms(lse[:, half:])
        terms.append(jnp.zeros((EXTRA - 6, LANES), jnp.float32))
        sent_ref[pl.ds(half, EXTRA), at(pair)] = jnp.concatenate(terms, axis=0).astype(jnp.bfloat16)
        return ()

    over_pairs(pairs, (score, top, weigh, mix, finish), LAGS, arrive)
    for copy in rest:
        copy.wait()


def late_kernel(
    rows, offsets_hbm, weight_hbm, q_ref, k_ref, v_ref, early_ref, both_ref, next_ref, weight_ref,
    offsets_ref, own_bias, other_bias, own, other, sems,
):
    offsets_copy = load(offsets_hbm, offsets_ref, sems.at[8])
    block = weight_ref.shape[0] // 8
    copies = []
    for i in range(8):
        place = pl.ds(i * block, block)
        copies.append(load(weight_hbm.at[place], weight_ref.at[place], sems.at[i]))
    half = q_ref.shape[0]
    key = lax.broadcasted_iota(jnp.int32, own.shape, 0)
    query = lax.broadcasted_iota(jnp.int32, own.shape, 1) % half
    own[...] = jnp.where(key <= query, 1.0, 0.0).astype(jnp.bfloat16)
    other[...] = jnp.where(key <= query, 0.0, 1.0).astype(jnp.bfloat16)
    pooling = pool_matrix(half)
    molecules = half // POOL
    features = early_ref.shape[0]
    both_ref[pl.ds(0, features), :] = early_ref[...]
    pairs = k_ref.shape[1] // LANES
    offsets_copy.wait()
    start = lax.axis_index("seq") * rows
    own_bias[...] = mask_bias(offsets_ref, start + half, start + half, lambda key, query: key <= query)
    other_bias[...] = mask_bias(offsets_ref, start + half, start, lambda key, query: key > query)
    next_ref[...] = mask_bias(offsets_ref, start + rows, start + half, lambda key, query: key > query)
    parts = []

    def score(pair):
        scores = dot_nt(k_ref[:, at(pair)], split_heads(q_ref[:, at(pair)]))
        return scores, with_ones(jnp.transpose(v_ref[:, at(pair)]))

    def top(pair, scores, values_t):
        scores = jnp.maximum(scores[:half] + other_bias[...], scores[half:] + own_bias[...])
        return scores, tops(scores), values_t

    def weigh(pair, scores, top, values_t):
        weights = jnp.exp(scores - top).astype(jnp.bfloat16)
        return jnp.concatenate([weights * other[...], weights * own[...]], axis=0), values_t

    def mix(pair, weights, values_t):
        return (dot_nn(values_t, weights),)

    def finish(pair, mixed):
        inverse = 1.0 / mixed[LANES : LANES + 1]
        parts.append(own_heads(mixed, inverse).astype(jnp.bfloat16))
        if len(parts) == 4:
            pooled = dot_nt(pooling, jnp.concatenate(parts, axis=0)).astype(jnp.bfloat16)
            for i in range(4):
                place = features + (pair - 3 + i) * molecules
                both_ref[pl.ds(place, molecules), :] = pooled[:, i * LANES : (i + 1) * LANES]
            parts.clear()
        return ()

    over_pairs(pairs, (score, top, weigh, mix, finish), LAGS, lambda pair: None)
    for copy in copies:
        copy.wait()


def halo_kernel(q_ref, k_ref, v_ref, bias, after_ref, out_ref, share_ref):
    half = bias.shape[0]
    molecules = half // POOL
    tail = pl.ds(half, half)
    pooling = pool_matrix(half)
    pairs = k_ref.shape[1] // LANES
    parts = []

    def score(pair):
        queries = split_heads(q_ref[pl.ds(0, half), at(pair)])
        scores = dot_nt(k_ref[tail, at(pair)], queries)
        return scores, with_ones(jnp.transpose(v_ref[tail, at(pair)]))

    def top(pair, scores, values_t):
        terms = q_ref[pl.ds(half, EXTRA), at(pair)].astype(jnp.float32)
        lse = jnp.concatenate(
            [terms[0:1] + terms[1:2] + terms[2:3], terms[3:4] + terms[4:5] + terms[5:6]], axis=1
        )
        return scores, jnp.maximum(tops(scores + bias[...]), lse), lse, values_t

    def weigh(pair, scores, top, lse, values_t):
        weights = jnp.exp((scores + bias[...]) - top).astype(jnp.bfloat16)
        return weights, jnp.exp(lse - top), values_t

    def mix(pair, weights, kept, values_t):
        return dot_nn(values_t, weights), kept

    def finish(pair, mixed, kept):
        inverse = 1.0 / (mixed[LANES : LANES + 1] + kept)
        parts.append(own_heads(mixed, inverse).astype(jnp.bfloat16))
        if len(parts) == 4:
            pooled = dot_nt(pooling, jnp.concatenate(parts, axis=0)).astype(jnp.bfloat16)
            for i in range(4):
                place = pl.ds((pair - 3 + i) * molecules, molecules)
                out_ref[place, :] = pooled[:, i * LANES : (i + 1) * LANES]
            parts.clear()
        share_ref[pl.ds(pair, 1), :] = kept * inverse
        return ()

    over_pairs(pairs, (score, top, weigh, mix, finish), LAGS, lambda pair: None)
    share = share_ref[...].astype(jnp.bfloat16)
    out_ref[pl.ds(pairs * molecules, pairs), :] = share[:, :half]
    out_ref[pl.ds(pairs * (molecules + 1), pairs), :] = share[:, half:]


def back_kernel(
    slot_ref, cotangent_ref, weight_ref, gain_ref, stashed_ref, after_ref, dinput_ref, term_ref, grad, held_ref
):
    held = stashed_ref[0]
    for i in range(1, stashed_ref.shape[0]):
        held = jnp.where(slot_ref[0:1, 0:1] == i, stashed_ref[i].astype(jnp.float32), held.astype(jnp.float32))
    held_ref[...] = held.astype(jnp.bfloat16)
    features = weight_ref.shape[0]
    block = 512
    for begin in range(0, features, block):
        columns = pl.ds(begin, block)
        grad[:, columns] = dot_nt(cotangent_ref[...], weight_ref[columns, :])
    held = held_ref[...].astype(jnp.float32)
    inv_rms = lax.rsqrt(jnp.sum(held * held, axis=1, keepdims=True) / features + EPS_NORM)
    along = jnp.zeros_like(inv_rms)
    for begin in range(0, features, block):
        columns = pl.ds(begin, block)
        product = grad[:, columns] * (held_ref[:, columns].astype(jnp.float32) * inv_rms)
        term_ref[:, columns] = jnp.sum(product, axis=0, keepdims=True)
        along += jnp.sum(product * gain_ref[:, columns], axis=1, keepdims=True)
    along = along / features
    for begin in range(0, features, block):
        columns = pl.ds(begin, block)
        whitened = held_ref[:, columns].astype(jnp.float32) * inv_rms
        scaled = grad[:, columns] * gain_ref[:, columns]
        dinput_ref[:, columns] = (inv_rms * (scaled - whitened * along)).astype(jnp.bfloat16)


def project_kernel(
    early_ref, both_ref, halo_ref, gain_ref, weight_ref, term_ref, other_ref, upstream_hbm,
    out_ref, update_ref, passed_hbm, scaled_ref, share_ref, sem,
):
    passing = load(upstream_hbm, passed_hbm, sem)
    half = both_ref.shape[1]
    features = gain_ref.shape[1]
    first_part = early_ref.shape[0]
    molecules = half // POOL
    pooling = pool_matrix(half)
    first = lax.axis_index("seq") == 0
    squares, parts, pairs = 0.0, [], features // LANES
    shares = halo_ref[pl.ds(pairs * molecules, 2 * pairs), :].astype(jnp.float32)
    share_ref[...] = jnp.where(first, 1.0, shares)
    for pair in range(pairs):
        share_a, share_b = share_ref[pl.ds(pair, 1), :], share_ref[pl.ds(pairs + pair, 1), :]
        begin = pair * LANES
        if begin < first_part:
            early = early_ref[pl.ds(begin, LANES), :].astype(jnp.float32)
        else:
            early = both_ref[pl.ds(begin - first_part, LANES), :].astype(jnp.float32)
        parts += [early[:HEAD_DIM] * share_a, early[HEAD_DIM:] * share_b]
        if len(parts) == 8:
            columns = pl.ds((pair - 3) * LANES, 4 * LANES)
            mean = dot_nt(pooling, jnp.concatenate(parts, axis=0).astype(jnp.bfloat16))
            halo = [halo_ref[pl.ds((pair - 3 + i) * molecules, molecules), :] for i in range(4)]
            upper = mean + jnp.concatenate(halo, axis=1).astype(jnp.float32)
            place = features - first_part + (pair - 3) * molecules
            lower = [both_ref[pl.ds(place + i * molecules, molecules), :] for i in range(4)]
            lower = jnp.concatenate(lower, axis=1)
            arrived = jnp.concatenate([upper.astype(jnp.bfloat16), lower], axis=0).astype(jnp.float32)
            squares += jnp.sum(arrived * arrived, axis=1, keepdims=True)
            scaled_ref[:, columns] = (arrived * gain_ref[:, columns]).astype(jnp.bfloat16)
            parts = []
    product = dot_nn(scaled_ref[...], weight_ref[...])
    out_ref[...] = (product * lax.rsqrt(squares / features + EPS_NORM)).astype(jnp.bfloat16)
    total = term_ref[...] + other_ref[...]
    mean = jnp.sum(total * total, axis=1, keepdims=True) / features
    update_ref[...] = total / jnp.sqrt(mean + EPS_STEP)
    passing.wait()


def cost(flops, read, exps=0):
    return pl.CostEstimate(flops=flops, bytes_accessed=read, transcendentals=exps)


SMEM = pl.BlockSpec(memory_space=pltpu.SMEM)
HBM = pl.BlockSpec(memory_space=pltpu.HBM)
ANY = pl.BlockSpec(memory_space=pl.ANY)
VMEM = pl.BlockSpec(memory_space=pltpu.VMEM)


def in_hbm(*arrays):
    return [pltpu.with_memory_space_constraint(x, pltpu.HBM) for x in arrays]


def params():
    return pltpu.CompilerParams(vmem_limit_bytes=24 * 2**20)


def attend_early(queries, keys, values, offsets, cotangent, stashed, chunks):
    rows, width = queries.shape
    half = rows // 2
    soon = width // (4 * LANES) * 3 // 4 * 4 * LANES
    bf16 = lambda *shape: jax.ShapeDtypeStruct(shape, jnp.bfloat16)
    return pl.pallas_call(
        functools.partial(early_kernel, rows, chunks),
        in_specs=[HBM] * 6,
        out_specs=[VMEM] * 8,
        out_shape=[
            bf16(half + EXTRA, width),
            bf16(soon, half),
            bf16(width - soon, half),
            bf16(half, width),
            bf16(rows, width),
            bf16(rows, width),
            bf16(*cotangent.shape),
            bf16(*stashed.shape),
        ],
        scratch_shapes=[
            pltpu.SMEM(offsets.shape, jnp.int32),
            pltpu.VMEM((half, 2 * half), jnp.float32),
            pltpu.SemaphoreType.DMA((3, 2)),
            pltpu.SemaphoreType.DMA((6,)),
        ],
        cost_estimate=cost(4 * half * half * width, 6 * rows * width, half * half * width // 64),
        compiler_params=params(),
        name="attend_early",
    )(*in_hbm(offsets, queries, keys, values, cotangent, stashed))


def attend_late(queries, keys, values, offsets, weight, early):
    half, width = queries.shape
    rows = 2 * half
    return pl.pallas_call(
        functools.partial(late_kernel, rows),
        in_specs=[HBM] * 2 + [VMEM] * 4,
        out_specs=[VMEM] * 3,
        out_shape=[
            jax.ShapeDtypeStruct((early.shape[0] + width // POOL, half), jnp.bfloat16),
            jax.ShapeDtypeStruct((half, rows), jnp.float32),
            jax.ShapeDtypeStruct(weight.shape, weight.dtype),
        ],
        scratch_shapes=[
            pltpu.SMEM(offsets.shape, jnp.int32),
            pltpu.VMEM((half, rows), jnp.float32),
            pltpu.VMEM((half, rows), jnp.float32),
            pltpu.VMEM((half, rows), jnp.bfloat16),
            pltpu.VMEM((half, rows), jnp.bfloat16),
            pltpu.SemaphoreType.DMA((9,)),
        ],
        cost_estimate=cost(8 * half * half * width, 10 * half * width, half * half * width // 64),
        compiler_params=params(),
        name="attend_late",
    )(*in_hbm(offsets, weight), queries, keys, values, early)


def attend_halo(sent, keys, values, bias, after):
    half, width = bias.shape[0], keys.shape[1]
    return pl.pallas_call(
        halo_kernel,
        in_specs=[VMEM] * 4 + [ANY],
        out_specs=VMEM,
        out_shape=jax.ShapeDtypeStruct((width // LANES * (half // POOL + 2), LANES), jnp.bfloat16),
        scratch_shapes=[pltpu.VMEM((width // LANES, 2 * half), jnp.float32)],
        cost_estimate=cost(4 * half * half * width, 6 * half * width, half * half * width // 64),
        compiler_params=params(),
        name="attend_halo",
    )(sent, keys, values, bias, after)


def backward(slot, cotangent, weight, gain, stashed, after):
    rows, width = stashed.shape[1:]
    depth = weight.shape[1]
    return pl.pallas_call(
        back_kernel,
        in_specs=[VMEM] * 5 + [ANY],
        out_specs=[VMEM] * 2,
        scratch_shapes=[
            pltpu.VMEM((rows, width), jnp.float32),
            pltpu.VMEM((rows, width), jnp.bfloat16),
        ],
        out_shape=[
            jax.ShapeDtypeStruct((rows, width), jnp.bfloat16),
            jax.ShapeDtypeStruct((1, width), jnp.float32),
        ],
        cost_estimate=cost(2 * rows * width * depth, 2 * width * depth),
        compiler_params=params(),
        name="backward",
    )(slot, cotangent, weight, gain, stashed, after)


def project(early, both, halo, gain, weight, term, other, upstream):
    rows = upstream.shape[0]
    width, depth = weight.shape
    return pl.pallas_call(
        project_kernel,
        in_specs=[VMEM] * 7 + [ANY],
        out_specs=[VMEM, VMEM, HBM],
        out_shape=[
            jax.ShapeDtypeStruct((rows, depth), jnp.bfloat16),
            jax.ShapeDtypeStruct(term.shape, term.dtype),
            jax.ShapeDtypeStruct(upstream.shape, upstream.dtype),
        ],
        scratch_shapes=[
            pltpu.VMEM((rows, width), jnp.bfloat16),
            pltpu.VMEM((2 * width // LANES, LANES), jnp.float32),
            pltpu.SemaphoreType.DMA,
        ],
        cost_estimate=cost(2 * rows * width * depth, 2 * width * depth),
        compiler_params=params(),
        name="project",
    )(early, both, halo, gain, weight, term, other, upstream)


def swapped(value, axis, distance):
    return lax.ppermute(value, axis, [(i, i ^ distance) for i in range(lax.axis_size(axis))])


def sum_rounds():
    rounds = []
    for axis in ("rep", "seq"):
        count = lax.axis_size(axis)
        if count & (count - 1):
            return []
        rounds += [(axis, 1 << i) for i in range(count.bit_length() - 1)]
    return rounds if len(rounds) == 3 else []


def onward(value):
    sections, shards = lax.axis_size("section"), lax.axis_size("seq")
    route = [
        (s * shards + k, (s + 1) % sections * shards + k + 1)
        for s in range(sections)
        for k in range(shards - 1)
    ]
    return lax.ppermute(value, ("section", "seq"), route)


def local(queries, keys, values, doc_starts, weight, gain, stashed, cotangent, slot):
    queries, keys, values, offsets = queries[0, 0], keys[0, 0], values[0, 0], doc_starts[0]
    rounds = sum_rounds()

    def partner(term, index):
        return swapped(term, *rounds[index]) if rounds else jnp.zeros_like(term)

    sent, early, more, q_late, keys, values, cotangent, stashed = attend_early(
        queries, keys, values, offsets, cotangent[0, 0], stashed[0, 0], 4
    )
    arrived = shifted(sent, "seq", -1)
    early = passed_along(early, "section", 1)
    both, next_bias, weight = attend_late(q_late, keys, values, offsets, weight[0], more)
    slot = jnp.broadcast_to(slot, (1, LANES))
    dinput, term = backward(slot, cotangent, weight, gain, stashed, both)
    both = passed_along(both, "section", 1)
    upstream = passed_along(dinput, "section", -1)
    term = term if rounds else lax.psum(term, ("rep", "seq"))
    term = term + partner(term, 0)
    term = term + partner(term, 1)
    halo = onward(attend_halo(arrived, keys, values, next_bias, term))
    mol_keys, update, upstream = project(
        early, both, halo, gain, weight, term, partner(term, 2), upstream
    )
    return mol_keys[None, None], upstream[None, None], update


def solution(mesh):
    in_specs = (
        P("rep", "section", "seq", None),
        P("rep", "section", "seq", None),
        P("rep", "section", "seq", None),
        P("rep", "section", None),
        P("section", None, None),
        P("section", None),
        P("rep", "section", None, "seq", None),
        P("rep", "section", "seq", None),
        P("rep", "section"),
    )
    out_specs = (
        P("rep", "section", "seq", None),
        P("rep", "section", "seq", None),
        P("section", None),
    )
    return jax.shard_map(local, mesh=mesh, in_specs=in_specs, out_specs=out_specs, check_vma=False)
```

```python
import functools
import math

import jax
import jax.numpy as jnp
from jax import lax
from jax.experimental import pallas as pl
from jax.experimental.pallas import tpu as pltpu
from jax.sharding import PartitionSpec as P

HEAD_DIM = 64
POOL = 4
WINDOW = 128
LANES = 128
EPS_NORM = 1e-05
EPS_STEP = 1e-06
MASKED = -1e30
LAGS = (0, 3, 5, 6, 8)
EXTRA = 8

NT = (((1,), (1,)), ((), ()))


def dot_nt(a, b):
    return lax.dot_general(a, b, NT, preferred_element_type=jnp.float32)


def dot_nn(a, b):
    return jnp.dot(a, b, preferred_element_type=jnp.float32)


def shifted(value, axis, steps):
    count = lax.axis_size(axis)
    first, last = max(0, -steps), min(count, count - steps)
    return lax.ppermute(value, axis, [(i, i + steps) for i in range(first, last)])


def passed_along(value, axis, steps):
    count = lax.axis_size(axis)
    return lax.ppermute(value, axis, [(i, (i + steps) % count) for i in range(count)])


def earliest_key(offsets_ref, query_pos):
    start = jnp.zeros_like(query_pos)
    for d in range(offsets_ref.shape[1]):
        offset = offsets_ref[0, d]
        start = jnp.where(query_pos >= offset, offset, start)
    return jnp.maximum(start, query_pos - (WINDOW - 1))


def mask_bias(offsets_ref, query_start, key_start, keep):
    key = lax.broadcasted_iota(jnp.int32, (WINDOW, 2 * WINDOW), 0)
    query = lax.broadcasted_iota(jnp.int32, (WINDOW, 2 * WINDOW), 1) % WINDOW
    lane = lax.broadcasted_iota(jnp.int32, (1, 2 * WINDOW), 1) % WINDOW
    lowest = earliest_key(offsets_ref, query_start + lane)
    allowed = (key_start + key >= lowest) & keep(key, query)
    return jnp.where(allowed, 0.0, MASKED).astype(jnp.float32)


def split_heads(queries):
    lane = lax.broadcasted_iota(jnp.int32, (1, LANES), 1)
    scale = 1.0 / math.sqrt(HEAD_DIM)
    first = jnp.where(lane < HEAD_DIM, scale, 0.0).astype(jnp.bfloat16)
    second = jnp.where(lane < HEAD_DIM, 0.0, scale).astype(jnp.bfloat16)
    return jnp.concatenate([queries * first, queries * second], axis=0)


def pool_matrix(queries):
    molecule = lax.broadcasted_iota(jnp.int32, (queries // POOL, queries), 0)
    query = lax.broadcasted_iota(jnp.int32, (queries // POOL, queries), 1)
    return jnp.where(query // POOL == molecule, 1.0 / POOL, 0.0).astype(jnp.bfloat16)


def own_heads(mixed, scale):
    count = mixed.shape[1] // 2
    return jnp.concatenate(
        [
            mixed[:HEAD_DIM, :count] * scale[:, :count],
            mixed[HEAD_DIM:LANES, count:] * scale[:, count:],
        ],
        axis=0,
    )


def load(source, target, sem):
    copy = pltpu.make_async_copy(source, target, sem)
    copy.start()
    return copy


def load_chunks(arrays, chunks, sems, between):
    block = arrays[0][1].shape[1] // chunks
    copies, extra = [], None
    for chunk in range(chunks):
        columns = pl.ds(chunk * block, block)
        copies.append(
            [
                load(source.at[:, columns], target.at[:, columns], sems.at[i, chunk])
                for i, (source, target) in enumerate(arrays)
            ]
        )
        if chunk == 0:
            extra = between()
    return copies, extra


def at(pair):
    return pl.ds(pair * LANES, LANES)


def over_pairs(pairs, stages, lags, before):
    results = {}
    for step in range(pairs + lags[-1]):
        if step < pairs:
            before(step)
        for stage, lag in zip(stages, lags):
            pair = step - lag
            if 0 <= pair < pairs:
                results[pair] = stage(pair, *results.get(pair, ()))


def tops(scores):
    rows = scores.shape[0]
    while rows > 8:
        rows //= 2
        scores = jnp.maximum(scores[:rows], scores[rows:])
    return jnp.max(scores, axis=0, keepdims=True)


def with_ones(values_t):
    return jnp.concatenate([values_t, jnp.ones((16, values_t.shape[1]), jnp.bfloat16)], axis=0)


def three_terms(value):
    high = value.astype(jnp.bfloat16).astype(jnp.float32)
    middle = (value - high).astype(jnp.bfloat16).astype(jnp.float32)
    return [high, middle, value - high - middle]


def early_kernel(
    rows, chunks, offsets_hbm, q_hbm, k_hbm, v_hbm, cotangent_hbm, stashed_hbm,
    sent_ref, early_ref, more_ref, q_late_ref, k_ref, v_ref, cotangent_ref, stashed_ref,
    offsets_ref, bias, sems, offsets_sem,
):
    half = rows // 2
    head, tail = pl.ds(0, half), pl.ds(half, half)
    arrays = (
        (k_hbm.at[head], k_ref.at[head]),
        (q_hbm.at[head], sent_ref.at[head]),
        (v_hbm.at[head], v_ref.at[head]),
    )
    copies = load_chunks(arrays, chunks, sems, lambda: load(offsets_hbm, offsets_ref, offsets_sem.at[0]))
    copies, offsets_copy = copies
    later = (
        (k_hbm.at[tail], k_ref.at[tail]),
        (v_hbm.at[tail], v_ref.at[tail]),
        (q_hbm.at[tail], q_late_ref),
        (cotangent_hbm, cotangent_ref),
        (stashed_hbm, stashed_ref),
    )
    rest = []
    start = lax.axis_index("seq") * rows
    pairs = k_ref.shape[1] // LANES
    split = early_ref.shape[0] // LANES

    def arrive(pair):
        per_chunk = pairs // chunks
        if pair % per_chunk == 0:
            for copy in copies[pair // per_chunk]:
                copy.wait()
        if pair == 0:
            offsets_copy.wait()
            bias[...] = mask_bias(offsets_ref, start, start, lambda key, query: key <= query)
        if pair == per_chunk:
            for i, (source, target) in enumerate(later):
                rest.append(load(source, target, offsets_sem.at[i + 1]))

    def score(pair):
        scores = dot_nt(k_ref[head, at(pair)], split_heads(sent_ref[head, at(pair)]))
        return scores, with_ones(jnp.transpose(v_ref[head, at(pair)]))

    def top(pair, scores, values_t):
        return scores, tops(scores + bias[...]), values_t

    def weigh(pair, scores, top, values_t):
        return top, jnp.exp((scores + bias[...]) - top).astype(jnp.bfloat16), values_t

    def mix(pair, top, weights, values_t):
        return top, dot_nn(values_t, weights)

    def finish(pair, top, mixed):
        total = mixed[LANES : LANES + 1]
        target, place = (early_ref, pair) if pair < split else (more_ref, pair - split)
        target[at(place), :] = own_heads(mixed, 1.0 / total).astype(jnp.bfloat16)
        lse = top + jnp.log(total)
        terms = three_terms(lse[:, :half]) + three_terms(lse[:, half:])
        terms.append(jnp.zeros((EXTRA - 6, LANES), jnp.float32))
        sent_ref[pl.ds(half, EXTRA), at(pair)] = jnp.concatenate(terms, axis=0).astype(jnp.bfloat16)
        return ()

    over_pairs(pairs, (score, top, weigh, mix, finish), LAGS, arrive)
    for copy in rest:
        copy.wait()


def late_kernel(
    rows, offsets_hbm, weight_hbm, q_ref, k_ref, v_ref, early_ref, both_ref, next_ref, weight_ref,
    offsets_ref, own_bias, other_bias, own, other, sems,
):
    offsets_copy = load(offsets_hbm, offsets_ref, sems.at[8])
    block = weight_ref.shape[0] // 8
    copies = []
    for i in range(8):
        place = pl.ds(i * block, block)
        copies.append(load(weight_hbm.at[place], weight_ref.at[place], sems.at[i]))
    half = q_ref.shape[0]
    key = lax.broadcasted_iota(jnp.int32, own.shape, 0)
    query = lax.broadcasted_iota(jnp.int32, own.shape, 1) % half
    own[...] = jnp.where(key <= query, 1.0, 0.0).astype(jnp.bfloat16)
    other[...] = jnp.where(key <= query, 0.0, 1.0).astype(jnp.bfloat16)
    pooling = pool_matrix(half)
    molecules = half // POOL
    features = early_ref.shape[0]
    both_ref[pl.ds(0, features), :] = early_ref[...]
    pairs = k_ref.shape[1] // LANES
    offsets_copy.wait()
    start = lax.axis_index("seq") * rows
    own_bias[...] = mask_bias(offsets_ref, start + half, start + half, lambda key, query: key <= query)
    other_bias[...] = mask_bias(offsets_ref, start + half, start, lambda key, query: key > query)
    next_ref[...] = mask_bias(offsets_ref, start + rows, start + half, lambda key, query: key > query)
    parts = []

    def score(pair):
        scores = dot_nt(k_ref[:, at(pair)], split_heads(q_ref[:, at(pair)]))
        return scores, with_ones(jnp.transpose(v_ref[:, at(pair)]))

    def top(pair, scores, values_t):
        scores = jnp.maximum(scores[:half] + other_bias[...], scores[half:] + own_bias[...])
        return scores, tops(scores), values_t

    def weigh(pair, scores, top, values_t):
        weights = jnp.exp(scores - top).astype(jnp.bfloat16)
        return jnp.concatenate([weights * other[...], weights * own[...]], axis=0), values_t

    def mix(pair, weights, values_t):
        return (dot_nn(values_t, weights),)

    def finish(pair, mixed):
        inverse = 1.0 / mixed[LANES : LANES + 1]
        parts.append(own_heads(mixed, inverse).astype(jnp.bfloat16))
        if len(parts) == 4:
            pooled = dot_nt(pooling, jnp.concatenate(parts, axis=0)).astype(jnp.bfloat16)
            for i in range(4):
                place = features + (pair - 3 + i) * molecules
                both_ref[pl.ds(place, molecules), :] = pooled[:, i * LANES : (i + 1) * LANES]
            parts.clear()
        return ()

    over_pairs(pairs, (score, top, weigh, mix, finish), LAGS, lambda pair: None)
    for copy in copies:
        copy.wait()


def halo_kernel(q_ref, k_ref, v_ref, bias, after_ref, out_ref, share_ref):
    half = bias.shape[0]
    molecules = half // POOL
    tail = pl.ds(half, half)
    pooling = pool_matrix(half)
    pairs = k_ref.shape[1] // LANES
    parts = []

    def score(pair):
        queries = split_heads(q_ref[pl.ds(0, half), at(pair)])
        scores = dot_nt(k_ref[tail, at(pair)], queries)
        return scores, with_ones(jnp.transpose(v_ref[tail, at(pair)]))

    def top(pair, scores, values_t):
        terms = q_ref[pl.ds(half, EXTRA), at(pair)].astype(jnp.float32)
        lse = jnp.concatenate(
            [terms[0:1] + terms[1:2] + terms[2:3], terms[3:4] + terms[4:5] + terms[5:6]], axis=1
        )
        return scores, jnp.maximum(tops(scores + bias[...]), lse), lse, values_t

    def weigh(pair, scores, top, lse, values_t):
        weights = jnp.exp((scores + bias[...]) - top).astype(jnp.bfloat16)
        return weights, jnp.exp(lse - top), values_t

    def mix(pair, weights, kept, values_t):
        return dot_nn(values_t, weights), kept

    def finish(pair, mixed, kept):
        inverse = 1.0 / (mixed[LANES : LANES + 1] + kept)
        parts.append(own_heads(mixed, inverse).astype(jnp.bfloat16))
        if len(parts) == 4:
            pooled = dot_nt(pooling, jnp.concatenate(parts, axis=0)).astype(jnp.bfloat16)
            for i in range(4):
                place = pl.ds((pair - 3 + i) * molecules, molecules)
                out_ref[place, :] = pooled[:, i * LANES : (i + 1) * LANES]
            parts.clear()
        share_ref[pl.ds(pair, 1), :] = kept * inverse
        return ()

    over_pairs(pairs, (score, top, weigh, mix, finish), LAGS, lambda pair: None)
    share = share_ref[...].astype(jnp.bfloat16)
    out_ref[pl.ds(pairs * molecules, pairs), :] = share[:, :half]
    out_ref[pl.ds(pairs * (molecules + 1), pairs), :] = share[:, half:]


def back_kernel(
    slot_ref, cotangent_ref, weight_ref, gain_ref, stashed_ref, after_ref, dinput_ref, term_ref, grad, held_ref
):
    held = stashed_ref[0]
    for i in range(1, stashed_ref.shape[0]):
        held = jnp.where(slot_ref[0:1, 0:1] == i, stashed_ref[i].astype(jnp.float32), held.astype(jnp.float32))
    held_ref[...] = held.astype(jnp.bfloat16)
    features = weight_ref.shape[0]
    block = 512
    for begin in range(0, features, block):
        columns = pl.ds(begin, block)
        grad[:, columns] = dot_nt(cotangent_ref[...], weight_ref[columns, :])
    held = held_ref[...].astype(jnp.float32)
    inv_rms = lax.rsqrt(jnp.sum(held * held, axis=1, keepdims=True) / features + EPS_NORM)
    along = jnp.zeros_like(inv_rms)
    for begin in range(0, features, block):
        columns = pl.ds(begin, block)
        product = grad[:, columns] * (held_ref[:, columns].astype(jnp.float32) * inv_rms)
        term_ref[:, columns] = jnp.sum(product, axis=0, keepdims=True)
        along += jnp.sum(product * gain_ref[:, columns], axis=1, keepdims=True)
    along = along / features
    for begin in range(0, features, block):
        columns = pl.ds(begin, block)
        whitened = held_ref[:, columns].astype(jnp.float32) * inv_rms
        scaled = grad[:, columns] * gain_ref[:, columns]
        dinput_ref[:, columns] = (inv_rms * (scaled - whitened * along)).astype(jnp.bfloat16)


def project_kernel(
    early_ref, both_ref, halo_ref, gain_ref, weight_ref, term_ref, other_ref, upstream_hbm,
    out_ref, update_ref, passed_hbm, scaled_ref, share_ref, sem,
):
    passing = load(upstream_hbm, passed_hbm, sem)
    half = both_ref.shape[1]
    features = gain_ref.shape[1]
    first_part = early_ref.shape[0]
    molecules = half // POOL
    pooling = pool_matrix(half)
    first = lax.axis_index("seq") == 0
    squares, parts, pairs = 0.0, [], features // LANES
    shares = halo_ref[pl.ds(pairs * molecules, 2 * pairs), :].astype(jnp.float32)
    share_ref[...] = jnp.where(first, 1.0, shares)
    for pair in range(pairs):
        share_a = share_ref[pl.ds(pair, 1), :].astype(jnp.bfloat16)
        share_b = share_ref[pl.ds(pairs + pair, 1), :].astype(jnp.bfloat16)
        begin = pair * LANES
        if begin < first_part:
            early = early_ref[pl.ds(begin, LANES), :]
        else:
            early = both_ref[pl.ds(begin - first_part, LANES), :]
        parts += [early[:HEAD_DIM] * share_a, early[HEAD_DIM:] * share_b]
        if len(parts) == 8:
            columns = pl.ds((pair - 3) * LANES, 4 * LANES)
            mean = dot_nt(pooling, jnp.concatenate(parts, axis=0))
            halo = [halo_ref[pl.ds((pair - 3 + i) * molecules, molecules), :] for i in range(4)]
            upper = mean + jnp.concatenate(halo, axis=1).astype(jnp.float32)
            place = features - first_part + (pair - 3) * molecules
            lower = [both_ref[pl.ds(place + i * molecules, molecules), :] for i in range(4)]
            lower = jnp.concatenate(lower, axis=1)
            arrived = jnp.concatenate([upper.astype(jnp.bfloat16), lower], axis=0).astype(jnp.float32)
            squares += jnp.sum(arrived * arrived, axis=1, keepdims=True)
            scaled_ref[:, columns] = (arrived * gain_ref[:, columns]).astype(jnp.bfloat16)
            parts = []
    product = dot_nn(scaled_ref[...], weight_ref[...])
    out_ref[...] = (product * lax.rsqrt(squares / features + EPS_NORM)).astype(jnp.bfloat16)
    total = term_ref[...] + other_ref[...]
    mean = jnp.sum(total * total, axis=1, keepdims=True) / features
    update_ref[...] = total / jnp.sqrt(mean + EPS_STEP)
    passing.wait()


def cost(flops, read, exps=0):
    return pl.CostEstimate(flops=flops, bytes_accessed=read, transcendentals=exps)


SMEM = pl.BlockSpec(memory_space=pltpu.SMEM)
HBM = pl.BlockSpec(memory_space=pltpu.HBM)
ANY = pl.BlockSpec(memory_space=pl.ANY)
VMEM = pl.BlockSpec(memory_space=pltpu.VMEM)


def in_hbm(*arrays):
    return [pltpu.with_memory_space_constraint(x, pltpu.HBM) for x in arrays]


def params():
    return pltpu.CompilerParams(vmem_limit_bytes=24 * 2**20)


def attend_early(queries, keys, values, offsets, cotangent, stashed, chunks):
    rows, width = queries.shape
    half = rows // 2
    soon = width // (4 * LANES) * 3 // 4 * 4 * LANES
    bf16 = lambda *shape: jax.ShapeDtypeStruct(shape, jnp.bfloat16)
    return pl.pallas_call(
        functools.partial(early_kernel, rows, chunks),
        in_specs=[HBM] * 6,
        out_specs=[VMEM] * 8,
        out_shape=[
            bf16(half + EXTRA, width),
            bf16(soon, half),
            bf16(width - soon, half),
            bf16(half, width),
            bf16(rows, width),
            bf16(rows, width),
            bf16(*cotangent.shape),
            bf16(*stashed.shape),
        ],
        scratch_shapes=[
            pltpu.SMEM(offsets.shape, jnp.int32),
            pltpu.VMEM((half, 2 * half), jnp.float32),
            pltpu.SemaphoreType.DMA((3, chunks)),
            pltpu.SemaphoreType.DMA((6,)),
        ],
        cost_estimate=cost(4 * half * half * width, 6 * rows * width, half * half * width // 64),
        compiler_params=params(),
        name="attend_early",
    )(*in_hbm(offsets, queries, keys, values, cotangent, stashed))


def attend_late(queries, keys, values, offsets, weight, early):
    half, width = queries.shape
    rows = 2 * half
    return pl.pallas_call(
        functools.partial(late_kernel, rows),
        in_specs=[HBM] * 2 + [VMEM] * 4,
        out_specs=[VMEM] * 3,
        out_shape=[
            jax.ShapeDtypeStruct((early.shape[0] + width // POOL, half), jnp.bfloat16),
            jax.ShapeDtypeStruct((half, rows), jnp.float32),
            jax.ShapeDtypeStruct(weight.shape, weight.dtype),
        ],
        scratch_shapes=[
            pltpu.SMEM(offsets.shape, jnp.int32),
            pltpu.VMEM((half, rows), jnp.float32),
            pltpu.VMEM((half, rows), jnp.float32),
            pltpu.VMEM((half, rows), jnp.bfloat16),
            pltpu.VMEM((half, rows), jnp.bfloat16),
            pltpu.SemaphoreType.DMA((9,)),
        ],
        cost_estimate=cost(8 * half * half * width, 10 * half * width, half * half * width // 64),
        compiler_params=params(),
        name="attend_late",
    )(*in_hbm(offsets, weight), queries, keys, values, early)


def attend_halo(sent, keys, values, bias, after):
    half, width = bias.shape[0], keys.shape[1]
    return pl.pallas_call(
        halo_kernel,
        in_specs=[VMEM] * 4 + [ANY],
        out_specs=VMEM,
        out_shape=jax.ShapeDtypeStruct((width // LANES * (half // POOL + 2), LANES), jnp.bfloat16),
        scratch_shapes=[pltpu.VMEM((width // LANES, 2 * half), jnp.float32)],
        cost_estimate=cost(4 * half * half * width, 6 * half * width, half * half * width // 64),
        compiler_params=params(),
        name="attend_halo",
    )(sent, keys, values, bias, after)


def backward(slot, cotangent, weight, gain, stashed, after):
    rows, width = stashed.shape[1:]
    depth = weight.shape[1]
    return pl.pallas_call(
        back_kernel,
        in_specs=[VMEM] * 5 + [ANY],
        out_specs=[VMEM] * 2,
        scratch_shapes=[
            pltpu.VMEM((rows, width), jnp.float32),
            pltpu.VMEM((rows, width), jnp.bfloat16),
        ],
        out_shape=[
            jax.ShapeDtypeStruct((rows, width), jnp.bfloat16),
            jax.ShapeDtypeStruct((1, width), jnp.float32),
        ],
        cost_estimate=cost(2 * rows * width * depth, 2 * width * depth),
        compiler_params=params(),
        name="backward",
    )(slot, cotangent, weight, gain, stashed, after)


def project(early, both, halo, gain, weight, term, other, upstream):
    rows = upstream.shape[0]
    width, depth = weight.shape
    return pl.pallas_call(
        project_kernel,
        in_specs=[VMEM] * 7 + [ANY],
        out_specs=[VMEM, VMEM, HBM],
        out_shape=[
            jax.ShapeDtypeStruct((rows, depth), jnp.bfloat16),
            jax.ShapeDtypeStruct(term.shape, term.dtype),
            jax.ShapeDtypeStruct(upstream.shape, upstream.dtype),
        ],
        scratch_shapes=[
            pltpu.VMEM((rows, width), jnp.bfloat16),
            pltpu.VMEM((2 * width // LANES, LANES), jnp.float32),
            pltpu.SemaphoreType.DMA,
        ],
        cost_estimate=cost(2 * rows * width * depth, 2 * width * depth),
        compiler_params=params(),
        name="project",
    )(early, both, halo, gain, weight, term, other, upstream)


def swapped(value, axis, distance):
    return lax.ppermute(value, axis, [(i, i ^ distance) for i in range(lax.axis_size(axis))])


def sum_rounds():
    rounds = []
    for axis in ("rep", "seq"):
        count = lax.axis_size(axis)
        if count & (count - 1):
            return []
        rounds += [(axis, 1 << i) for i in range(count.bit_length() - 1)]
    return rounds if len(rounds) == 3 else []


def onward(value):
    sections, shards = lax.axis_size("section"), lax.axis_size("seq")
    route = [
        (s * shards + k, (s + 1) % sections * shards + k + 1)
        for s in range(sections)
        for k in range(shards - 1)
    ]
    return lax.ppermute(value, ("section", "seq"), route)


def local(queries, keys, values, doc_starts, weight, gain, stashed, cotangent, slot):
    queries, keys, values, offsets = queries[0, 0], keys[0, 0], values[0, 0], doc_starts[0]
    rounds = sum_rounds()

    def partner(term, index):
        return swapped(term, *rounds[index]) if rounds else jnp.zeros_like(term)

    sent, early, more, q_late, keys, values, cotangent, stashed = attend_early(
        queries, keys, values, offsets, cotangent[0, 0], stashed[0, 0], 4
    )
    arrived = shifted(sent, "seq", -1)
    early = passed_along(early, "section", 1)
    both, next_bias, weight = attend_late(q_late, keys, values, offsets, weight[0], more)
    slot = jnp.broadcast_to(slot, (1, LANES))
    dinput, term = backward(slot, cotangent, weight, gain, stashed, both)
    both = passed_along(both, "section", 1)
    upstream = passed_along(dinput, "section", -1)
    term = term if rounds else lax.psum(term, ("rep", "seq"))
    term = term + partner(term, 0)
    term = term + partner(term, 1)
    halo = onward(attend_halo(arrived, keys, values, next_bias, term))
    mol_keys, update, upstream = project(
        early, both, halo, gain, weight, term, partner(term, 2), upstream
    )
    return mol_keys[None, None], upstream[None, None], update


def solution(mesh):
    in_specs = (
        P("rep", "section", "seq", None),
        P("rep", "section", "seq", None),
        P("rep", "section", "seq", None),
        P("rep", "section", None),
        P("section", None, None),
        P("section", None),
        P("rep", "section", None, "seq", None),
        P("rep", "section", "seq", None),
        P("rep", "section"),
    )
    out_specs = (
        P("rep", "section", "seq", None),
        P("rep", "section", "seq", None),
        P("section", None),
    )
    return jax.shard_map(local, mesh=mesh, in_specs=in_specs, out_specs=out_specs, check_vma=False)
```

```python
import functools
import math

import jax
import jax.numpy as jnp
from jax import lax
from jax.experimental import pallas as pl
from jax.experimental.pallas import tpu as pltpu
from jax.sharding import PartitionSpec as P

HEAD_DIM = 64
POOL = 4
WINDOW = 128
LANES = 128
EPS_NORM = 1e-05
EPS_STEP = 1e-06
MASKED = -1e30
LAGS = (0, 3, 5, 6, 8)
EXTRA = 8

NT = (((1,), (1,)), ((), ()))


def dot_nt(a, b):
    return lax.dot_general(a, b, NT, preferred_element_type=jnp.float32)


def dot_nn(a, b):
    return jnp.dot(a, b, preferred_element_type=jnp.float32)


def shifted(value, axis, steps):
    count = lax.axis_size(axis)
    first, last = max(0, -steps), min(count, count - steps)
    return lax.ppermute(value, axis, [(i, i + steps) for i in range(first, last)])


def passed_along(value, axis, steps):
    count = lax.axis_size(axis)
    return lax.ppermute(value, axis, [(i, (i + steps) % count) for i in range(count)])


def earliest_key(offsets_ref, query_pos):
    start = jnp.zeros_like(query_pos)
    for d in range(offsets_ref.shape[1]):
        offset = offsets_ref[0, d]
        start = jnp.where(query_pos >= offset, offset, start)
    return jnp.maximum(start, query_pos - (WINDOW - 1))


def mask_bias(offsets_ref, query_start, key_start, keep):
    key = lax.broadcasted_iota(jnp.int32, (WINDOW, 2 * WINDOW), 0)
    query = lax.broadcasted_iota(jnp.int32, (WINDOW, 2 * WINDOW), 1) % WINDOW
    lane = lax.broadcasted_iota(jnp.int32, (1, 2 * WINDOW), 1) % WINDOW
    lowest = earliest_key(offsets_ref, query_start + lane)
    allowed = (key_start + key >= lowest) & keep(key, query)
    return jnp.where(allowed, 0.0, MASKED).astype(jnp.float32)


def split_heads(queries):
    lane = lax.broadcasted_iota(jnp.int32, (1, LANES), 1)
    scale = 1.0 / math.sqrt(HEAD_DIM)
    first = jnp.where(lane < HEAD_DIM, scale, 0.0).astype(jnp.bfloat16)
    second = jnp.where(lane < HEAD_DIM, 0.0, scale).astype(jnp.bfloat16)
    return jnp.concatenate([queries * first, queries * second], axis=0)


def pool_matrix(queries):
    molecule = lax.broadcasted_iota(jnp.int32, (queries // POOL, queries), 0)
    query = lax.broadcasted_iota(jnp.int32, (queries // POOL, queries), 1)
    return jnp.where(query // POOL == molecule, 1.0 / POOL, 0.0).astype(jnp.bfloat16)


def own_heads(mixed, scale):
    count = mixed.shape[1] // 2
    return jnp.concatenate(
        [
            mixed[:HEAD_DIM, :count] * scale[:, :count],
            mixed[HEAD_DIM:LANES, count:] * scale[:, count:],
        ],
        axis=0,
    )


def load(source, target, sem):
    copy = pltpu.make_async_copy(source, target, sem)
    copy.start()
    return copy


def load_chunks(arrays, chunks, sems, between):
    block = arrays[0][1].shape[1] // chunks
    copies, extra = [], None
    for chunk in range(chunks):
        columns = pl.ds(chunk * block, block)
        copies.append(
            [
                load(source.at[:, columns], target.at[:, columns], sems.at[i, chunk])
                for i, (source, target) in enumerate(arrays)
            ]
        )
        if chunk == 0:
            extra = between()
    return copies, extra


def at(pair):
    return pl.ds(pair * LANES, LANES)


def over_pairs(pairs, stages, lags, before):
    results = {}
    for step in range(pairs + lags[-1]):
        if step < pairs:
            before(step)
        for stage, lag in zip(stages, lags):
            pair = step - lag
            if 0 <= pair < pairs:
                results[pair] = stage(pair, *results.get(pair, ()))


def tops(scores):
    rows = scores.shape[0]
    while rows > 8:
        rows //= 2
        scores = jnp.maximum(scores[:rows], scores[rows:])
    return jnp.max(scores, axis=0, keepdims=True)


def with_ones(values_t):
    return jnp.concatenate([values_t, jnp.ones((16, values_t.shape[1]), jnp.bfloat16)], axis=0)


def three_terms(value):
    high = value.astype(jnp.bfloat16).astype(jnp.float32)
    middle = (value - high).astype(jnp.bfloat16).astype(jnp.float32)
    return [high, middle, value - high - middle]


def early_kernel(
    rows, chunks, offsets_hbm, q_hbm, k_hbm, v_hbm, cotangent_hbm, stashed_hbm,
    sent_ref, early_ref, more_ref, q_late_ref, k_ref, v_ref, cotangent_ref, stashed_ref,
    offsets_ref, bias, sems, offsets_sem,
):
    half = rows // 2
    head, tail = pl.ds(0, half), pl.ds(half, half)
    arrays = (
        (k_hbm.at[head], k_ref.at[head]),
        (q_hbm.at[head], sent_ref.at[head]),
        (v_hbm.at[head], v_ref.at[head]),
    )
    copies = load_chunks(arrays, chunks, sems, lambda: load(offsets_hbm, offsets_ref, offsets_sem.at[0]))
    copies, offsets_copy = copies
    later = (
        (k_hbm.at[tail], k_ref.at[tail]),
        (v_hbm.at[tail], v_ref.at[tail]),
        (q_hbm.at[tail], q_late_ref),
        (cotangent_hbm, cotangent_ref),
        (stashed_hbm, stashed_ref),
    )
    rest = []
    start = lax.axis_index("seq") * rows
    pairs = k_ref.shape[1] // LANES
    split = early_ref.shape[0] // LANES

    def arrive(pair):
        per_chunk = pairs // chunks
        if pair % per_chunk == 0:
            for copy in copies[pair // per_chunk]:
                copy.wait()
        if pair == 0:
            offsets_copy.wait()
            bias[...] = mask_bias(offsets_ref, start, start, lambda key, query: key <= query)
        if pair == per_chunk:
            for i, (source, target) in enumerate(later):
                rest.append(load(source, target, offsets_sem.at[i + 1]))

    def score(pair):
        scores = dot_nt(k_ref[head, at(pair)], split_heads(sent_ref[head, at(pair)]))
        return scores, with_ones(jnp.transpose(v_ref[head, at(pair)]))

    def top(pair, scores, values_t):
        return scores, tops(scores + bias[...]), values_t

    def weigh(pair, scores, top, values_t):
        return top, jnp.exp((scores + bias[...]) - top).astype(jnp.bfloat16), values_t

    def mix(pair, top, weights, values_t):
        return top, dot_nn(values_t, weights)

    def finish(pair, top, mixed):
        total = mixed[LANES : LANES + 1]
        target, place = (early_ref, pair) if pair < split else (more_ref, pair - split)
        target[at(place), :] = own_heads(mixed, 1.0 / total).astype(jnp.bfloat16)
        lse = top + jnp.log(total)
        terms = three_terms(lse[:, :half]) + three_terms(lse[:, half:])
        terms.append(jnp.zeros((EXTRA - 6, LANES), jnp.float32))
        sent_ref[pl.ds(half, EXTRA), at(pair)] = jnp.concatenate(terms, axis=0).astype(jnp.bfloat16)
        return ()

    over_pairs(pairs, (score, top, weigh, mix, finish), LAGS, arrive)
    for copy in rest:
        copy.wait()


def late_kernel(
    rows, offsets_hbm, weight_hbm, q_ref, k_ref, v_ref, early_ref, both_ref, next_ref, weight_ref,
    offsets_ref, own_bias, other_bias, own, other, sems,
):
    offsets_copy = load(offsets_hbm, offsets_ref, sems.at[8])
    block = weight_ref.shape[0] // 8
    copies = []
    for i in range(8):
        place = pl.ds(i * block, block)
        copies.append(load(weight_hbm.at[place], weight_ref.at[place], sems.at[i]))
    half = q_ref.shape[0]
    key = lax.broadcasted_iota(jnp.int32, own.shape, 0)
    query = lax.broadcasted_iota(jnp.int32, own.shape, 1) % half
    own[...] = jnp.where(key <= query, 1.0, 0.0).astype(jnp.bfloat16)
    other[...] = jnp.where(key <= query, 0.0, 1.0).astype(jnp.bfloat16)
    pooling = pool_matrix(half)
    molecules = half // POOL
    features = early_ref.shape[0]
    both_ref[pl.ds(0, features), :] = early_ref[...]
    pairs = k_ref.shape[1] // LANES
    offsets_copy.wait()
    start = lax.axis_index("seq") * rows
    own_bias[...] = mask_bias(offsets_ref, start + half, start + half, lambda key, query: key <= query)
    other_bias[...] = mask_bias(offsets_ref, start + half, start, lambda key, query: key > query)
    next_ref[...] = mask_bias(offsets_ref, start + rows, start + half, lambda key, query: key > query)
    parts = []

    def score(pair):
        scores = dot_nt(k_ref[:, at(pair)], split_heads(q_ref[:, at(pair)]))
        return scores, with_ones(jnp.transpose(v_ref[:, at(pair)]))

    def top(pair, scores, values_t):
        scores = jnp.maximum(scores[:half] + other_bias[...], scores[half:] + own_bias[...])
        return scores, tops(scores), values_t

    def weigh(pair, scores, top, values_t):
        weights = jnp.exp(scores - top).astype(jnp.bfloat16)
        return jnp.concatenate([weights * other[...], weights * own[...]], axis=0), values_t

    def mix(pair, weights, values_t):
        return (dot_nn(values_t, weights),)

    def finish(pair, mixed):
        inverse = 1.0 / mixed[LANES : LANES + 1]
        parts.append(own_heads(mixed, inverse).astype(jnp.bfloat16))
        if len(parts) == 4:
            pooled = dot_nt(pooling, jnp.concatenate(parts, axis=0)).astype(jnp.bfloat16)
            for i in range(4):
                place = features + (pair - 3 + i) * molecules
                both_ref[pl.ds(place, molecules), :] = pooled[:, i * LANES : (i + 1) * LANES]
            parts.clear()
        return ()

    over_pairs(pairs, (score, top, weigh, mix, finish), LAGS, lambda pair: None)
    for copy in copies:
        copy.wait()


def halo_kernel(q_ref, k_ref, v_ref, bias, after_ref, out_ref, share_ref):
    half = bias.shape[0]
    molecules = half // POOL
    tail = pl.ds(half, half)
    pooling = pool_matrix(half)
    pairs = k_ref.shape[1] // LANES
    parts = []

    def score(pair):
        queries = split_heads(q_ref[pl.ds(0, half), at(pair)])
        scores = dot_nt(k_ref[tail, at(pair)], queries)
        return scores, with_ones(jnp.transpose(v_ref[tail, at(pair)]))

    def top(pair, scores, values_t):
        terms = q_ref[pl.ds(half, EXTRA), at(pair)].astype(jnp.float32)
        lse = jnp.concatenate(
            [terms[0:1] + terms[1:2] + terms[2:3], terms[3:4] + terms[4:5] + terms[5:6]], axis=1
        )
        return scores, jnp.maximum(tops(scores + bias[...]), lse), lse, values_t

    def weigh(pair, scores, top, lse, values_t):
        weights = jnp.exp((scores + bias[...]) - top).astype(jnp.bfloat16)
        return weights, jnp.exp(lse - top), values_t

    def mix(pair, weights, kept, values_t):
        return dot_nn(values_t, weights), kept

    def finish(pair, mixed, kept):
        inverse = 1.0 / (mixed[LANES : LANES + 1] + kept)
        parts.append(own_heads(mixed, inverse).astype(jnp.bfloat16))
        if len(parts) == 4:
            pooled = dot_nt(pooling, jnp.concatenate(parts, axis=0)).astype(jnp.bfloat16)
            for i in range(4):
                place = pl.ds((pair - 3 + i) * molecules, molecules)
                out_ref[place, :] = pooled[:, i * LANES : (i + 1) * LANES]
            parts.clear()
        share_ref[pl.ds(pair, 1), :] = kept * inverse
        return ()

    over_pairs(pairs, (score, top, weigh, mix, finish), LAGS, lambda pair: None)
    share = share_ref[...].astype(jnp.bfloat16)
    out_ref[pl.ds(pairs * molecules, pairs), :] = share[:, :half]
    out_ref[pl.ds(pairs * (molecules + 1), pairs), :] = share[:, half:]


def back_kernel(
    slot_ref, cotangent_ref, weight_ref, gain_ref, stashed_ref, after_ref, dinput_ref, term_ref, grad, held_ref
):
    held = stashed_ref[0]
    for i in range(1, stashed_ref.shape[0]):
        held = jnp.where(slot_ref[0:1, 0:1] == i, stashed_ref[i].astype(jnp.float32), held.astype(jnp.float32))
    held_ref[...] = held.astype(jnp.bfloat16)
    features = weight_ref.shape[0]
    block = 512
    for begin in range(0, features, block):
        columns = pl.ds(begin, block)
        grad[:, columns] = dot_nt(cotangent_ref[...], weight_ref[columns, :])
    held = held_ref[...].astype(jnp.float32)
    inv_rms = lax.rsqrt(jnp.sum(held * held, axis=1, keepdims=True) / features + EPS_NORM)
    along = jnp.zeros_like(inv_rms)
    for begin in range(0, features, block):
        columns = pl.ds(begin, block)
        product = grad[:, columns] * (held_ref[:, columns].astype(jnp.float32) * inv_rms)
        term_ref[:, columns] = jnp.sum(product, axis=0, keepdims=True)
        along += jnp.sum(product * gain_ref[:, columns], axis=1, keepdims=True)
    along = along / features
    for begin in range(0, features, block):
        columns = pl.ds(begin, block)
        whitened = held_ref[:, columns].astype(jnp.float32) * inv_rms
        scaled = grad[:, columns] * gain_ref[:, columns]
        dinput_ref[:, columns] = (inv_rms * (scaled - whitened * along)).astype(jnp.bfloat16)


def project_kernel(
    early_ref, both_ref, halo_ref, gain_ref, weight_ref, term_ref, other_ref, upstream_hbm,
    out_hbm, update_ref, passed_hbm, scaled_ref, share_ref, out_ref, sems,
):
    passing = load(upstream_hbm, passed_hbm, sems.at[0])
    half = both_ref.shape[1]
    features = gain_ref.shape[1]
    first_part = early_ref.shape[0]
    molecules = half // POOL
    pooling = pool_matrix(half)
    first = lax.axis_index("seq") == 0
    squares, parts, pairs = 0.0, [], features // LANES
    shares = halo_ref[pl.ds(pairs * molecules, 2 * pairs), :].astype(jnp.float32)
    share_ref[...] = jnp.where(first, 1.0, shares)
    for pair in range(pairs):
        share_a, share_b = share_ref[pl.ds(pair, 1), :], share_ref[pl.ds(pairs + pair, 1), :]
        begin = pair * LANES
        if begin < first_part:
            early = early_ref[pl.ds(begin, LANES), :].astype(jnp.float32)
        else:
            early = both_ref[pl.ds(begin - first_part, LANES), :].astype(jnp.float32)
        parts += [early[:HEAD_DIM] * share_a, early[HEAD_DIM:] * share_b]
        if len(parts) == 8:
            columns = pl.ds((pair - 3) * LANES, 4 * LANES)
            mean = dot_nt(pooling, jnp.concatenate(parts, axis=0).astype(jnp.bfloat16))
            halo = [halo_ref[pl.ds((pair - 3 + i) * molecules, molecules), :] for i in range(4)]
            upper = mean + jnp.concatenate(halo, axis=1).astype(jnp.float32)
            place = features - first_part + (pair - 3) * molecules
            lower = [both_ref[pl.ds(place + i * molecules, molecules), :] for i in range(4)]
            lower = jnp.concatenate(lower, axis=1)
            arrived = jnp.concatenate([upper.astype(jnp.bfloat16), lower], axis=0).astype(jnp.float32)
            squares += jnp.sum(arrived * arrived, axis=1, keepdims=True)
            scaled_ref[:, columns] = (arrived * gain_ref[:, columns]).astype(jnp.bfloat16)
            parts = []
    inverse = lax.rsqrt(squares / features + EPS_NORM)
    width = out_ref.shape[1] // 2
    leaving = []
    for i in range(2):
        columns = pl.ds(i * width, width)
        product = dot_nn(scaled_ref[...], weight_ref[:, columns])
        out_ref[:, columns] = (product * inverse).astype(jnp.bfloat16)
        leaving.append(load(out_ref.at[:, columns], out_hbm.at[:, columns], sems.at[1 + i]))
    total = term_ref[...] + other_ref[...]
    mean = jnp.sum(total * total, axis=1, keepdims=True) / features
    update_ref[...] = total / jnp.sqrt(mean + EPS_STEP)
    for copy in (passing, *leaving):
        copy.wait()


def cost(flops, read, exps=0):
    return pl.CostEstimate(flops=flops, bytes_accessed=read, transcendentals=exps)


SMEM = pl.BlockSpec(memory_space=pltpu.SMEM)
HBM = pl.BlockSpec(memory_space=pltpu.HBM)
ANY = pl.BlockSpec(memory_space=pl.ANY)
VMEM = pl.BlockSpec(memory_space=pltpu.VMEM)


def in_hbm(*arrays):
    return [pltpu.with_memory_space_constraint(x, pltpu.HBM) for x in arrays]


def params():
    return pltpu.CompilerParams(vmem_limit_bytes=24 * 2**20)


def attend_early(queries, keys, values, offsets, cotangent, stashed, chunks):
    rows, width = queries.shape
    half = rows // 2
    soon = width // (4 * LANES) * 3 // 4 * 4 * LANES
    bf16 = lambda *shape: jax.ShapeDtypeStruct(shape, jnp.bfloat16)
    return pl.pallas_call(
        functools.partial(early_kernel, rows, chunks),
        in_specs=[HBM] * 6,
        out_specs=[VMEM] * 8,
        out_shape=[
            bf16(half + EXTRA, width),
            bf16(soon, half),
            bf16(width - soon, half),
            bf16(half, width),
            bf16(rows, width),
            bf16(rows, width),
            bf16(*cotangent.shape),
            bf16(*stashed.shape),
        ],
        scratch_shapes=[
            pltpu.SMEM(offsets.shape, jnp.int32),
            pltpu.VMEM((half, 2 * half), jnp.float32),
            pltpu.SemaphoreType.DMA((3, chunks)),
            pltpu.SemaphoreType.DMA((6,)),
        ],
        cost_estimate=cost(4 * half * half * width, 6 * rows * width, half * half * width // 64),
        compiler_params=params(),
        name="attend_early",
    )(*in_hbm(offsets, queries, keys, values, cotangent, stashed))


def attend_late(queries, keys, values, offsets, weight, early):
    half, width = queries.shape
    rows = 2 * half
    return pl.pallas_call(
        functools.partial(late_kernel, rows),
        in_specs=[HBM] * 2 + [VMEM] * 4,
        out_specs=[VMEM] * 3,
        out_shape=[
            jax.ShapeDtypeStruct((early.shape[0] + width // POOL, half), jnp.bfloat16),
            jax.ShapeDtypeStruct((half, rows), jnp.float32),
            jax.ShapeDtypeStruct(weight.shape, weight.dtype),
        ],
        scratch_shapes=[
            pltpu.SMEM(offsets.shape, jnp.int32),
            pltpu.VMEM((half, rows), jnp.float32),
            pltpu.VMEM((half, rows), jnp.float32),
            pltpu.VMEM((half, rows), jnp.bfloat16),
            pltpu.VMEM((half, rows), jnp.bfloat16),
            pltpu.SemaphoreType.DMA((9,)),
        ],
        cost_estimate=cost(8 * half * half * width, 10 * half * width, half * half * width // 64),
        compiler_params=params(),
        name="attend_late",
    )(*in_hbm(offsets, weight), queries, keys, values, early)


def attend_halo(sent, keys, values, bias, after):
    half, width = bias.shape[0], keys.shape[1]
    return pl.pallas_call(
        halo_kernel,
        in_specs=[VMEM] * 4 + [ANY],
        out_specs=VMEM,
        out_shape=jax.ShapeDtypeStruct((width // LANES * (half // POOL + 2), LANES), jnp.bfloat16),
        scratch_shapes=[pltpu.VMEM((width // LANES, 2 * half), jnp.float32)],
        cost_estimate=cost(4 * half * half * width, 6 * half * width, half * half * width // 64),
        compiler_params=params(),
        name="attend_halo",
    )(sent, keys, values, bias, after)


def backward(slot, cotangent, weight, gain, stashed, after):
    rows, width = stashed.shape[1:]
    depth = weight.shape[1]
    return pl.pallas_call(
        back_kernel,
        in_specs=[VMEM] * 5 + [ANY],
        out_specs=[VMEM] * 2,
        scratch_shapes=[
            pltpu.VMEM((rows, width), jnp.float32),
            pltpu.VMEM((rows, width), jnp.bfloat16),
        ],
        out_shape=[
            jax.ShapeDtypeStruct((rows, width), jnp.bfloat16),
            jax.ShapeDtypeStruct((1, width), jnp.float32),
        ],
        cost_estimate=cost(2 * rows * width * depth, 2 * width * depth),
        compiler_params=params(),
        name="backward",
    )(slot, cotangent, weight, gain, stashed, after)


def project(early, both, halo, gain, weight, term, other, upstream):
    rows = upstream.shape[0]
    width, depth = weight.shape
    return pl.pallas_call(
        project_kernel,
        in_specs=[VMEM] * 7 + [ANY],
        out_specs=[HBM, VMEM, HBM],
        out_shape=[
            jax.ShapeDtypeStruct((rows, depth), jnp.bfloat16),
            jax.ShapeDtypeStruct(term.shape, term.dtype),
            jax.ShapeDtypeStruct(upstream.shape, upstream.dtype),
        ],
        scratch_shapes=[
            pltpu.VMEM((rows, width), jnp.bfloat16),
            pltpu.VMEM((2 * width // LANES, LANES), jnp.float32),
            pltpu.VMEM((rows, depth), jnp.bfloat16),
            pltpu.SemaphoreType.DMA((3,)),
        ],
        cost_estimate=cost(2 * rows * width * depth, 2 * width * depth),
        compiler_params=params(),
        name="project",
    )(early, both, halo, gain, weight, term, other, upstream)


def swapped(value, axis, distance):
    return lax.ppermute(value, axis, [(i, i ^ distance) for i in range(lax.axis_size(axis))])


def sum_rounds():
    rounds = []
    for axis in ("rep", "seq"):
        count = lax.axis_size(axis)
        if count & (count - 1):
            return []
        rounds += [(axis, 1 << i) for i in range(count.bit_length() - 1)]
    return rounds if len(rounds) == 3 else []


def onward(value):
    sections, shards = lax.axis_size("section"), lax.axis_size("seq")
    route = [
        (s * shards + k, (s + 1) % sections * shards + k + 1)
        for s in range(sections)
        for k in range(shards - 1)
    ]
    return lax.ppermute(value, ("section", "seq"), route)


def local(queries, keys, values, doc_starts, weight, gain, stashed, cotangent, slot):
    queries, keys, values, offsets = queries[0, 0], keys[0, 0], values[0, 0], doc_starts[0]
    rounds = sum_rounds()

    def partner(term, index):
        return swapped(term, *rounds[index]) if rounds else jnp.zeros_like(term)

    sent, early, more, q_late, keys, values, cotangent, stashed = attend_early(
        queries, keys, values, offsets, cotangent[0, 0], stashed[0, 0], 4
    )
    arrived = shifted(sent, "seq", -1)
    early = passed_along(early, "section", 1)
    both, next_bias, weight = attend_late(q_late, keys, values, offsets, weight[0], more)
    slot = jnp.broadcast_to(slot, (1, LANES))
    dinput, term = backward(slot, cotangent, weight, gain, stashed, both)
    both = passed_along(both, "section", 1)
    upstream = passed_along(dinput, "section", -1)
    term = term if rounds else lax.psum(term, ("rep", "seq"))
    term = term + partner(term, 0)
    term = term + partner(term, 1)
    halo = onward(attend_halo(arrived, keys, values, next_bias, term))
    mol_keys, update, upstream = project(
        early, both, halo, gain, weight, term, partner(term, 2), upstream
    )
    return mol_keys[None, None], upstream[None, None], update


def solution(mesh):
    in_specs = (
        P("rep", "section", "seq", None),
        P("rep", "section", "seq", None),
        P("rep", "section", "seq", None),
        P("rep", "section", None),
        P("section", None, None),
        P("section", None),
        P("rep", "section", None, "seq", None),
        P("rep", "section", "seq", None),
        P("rep", "section"),
    )
    out_specs = (
        P("rep", "section", "seq", None),
        P("rep", "section", "seq", None),
        P("section", None),
    )
    return jax.shard_map(local, mesh=mesh, in_specs=in_specs, out_specs=out_specs, check_vma=False)
```
